32 devices in a mesh: dp: 2 (over y), seq: 4 (over z), tensor: 4 (over x, core).
Axes of the slice: x: 2, y: 2, z: 4, core: 2. Of those that a mesh axis runs over, the one named last changes fastest.
Arguments:
- tokens: bfloat16 [8192, 2048], P(('dp', 'seq')), may hold values from -6 to 6
- sequence_lengths: int32 [2, 3], P('dp'), may hold values from 1 to 4094, as said below
- output_cotangent: bfloat16 [8192, 2048], P(('dp', 'seq')), may hold values from -6 to 6
- query_weight: bfloat16 [2048, 2048], P(('dp', 'seq'), 'tensor'), may hold values from -0.125 to 0.125
- key_weight: bfloat16 [2048, 512], P(('dp', 'seq'), 'tensor'), may hold values from -0.125 to 0.125
- value_weight: bfloat16 [2048, 512], P(('dp', 'seq'), 'tensor'), may hold values from -0.125 to 0.125
- output_weight: bfloat16 [2048, 2048], P('tensor', ('dp', 'seq')), may hold values from -2 to 2
- gate_weight: bfloat16 [2048, 8192], P(('dp', 'seq'), 'tensor'), may hold values from -0.125 to 0.125
- up_weight: bfloat16 [2048, 8192], P(('dp', 'seq'), 'tensor'), may hold values from -0.125 to 0.125
- down_weight: bfloat16 [8192, 2048], P('tensor', ('dp', 'seq')), may hold values from -0.0625 to 0.0625
- attention_norm_gain: bfloat16 [2048], replicated, may hold values from 0.5 to 1.5
- feedforward_norm_gain: bfloat16 [2048], replicated, may hold values from 0.5 to 1.5
- query_adapter_down: bfloat16 [2048, 8], replicated, may hold values from -0.125 to 0.125
- key_adapter_down: bfloat16 [2048, 8], replicated, may hold values from -0.125 to 0.125
- value_adapter_down: bfloat16 [2048, 8], replicated, may hold values from -0.125 to 0.125
- output_adapter_up: bfloat16 [2048, 8], replicated, may hold values from -0.75 to 0.75
- query_adapter_up: bfloat16 [32, 64, 8], P('tensor'), may hold values from -0.75 to 0.75
- key_adapter_up: bfloat16 [8, 64, 8], P('tensor'), may hold values from -0.75 to 0.75
- value_adapter_up: bfloat16 [8, 64, 8], P('tensor'), may hold values from -0.75 to 0.75
- output_adapter_down: bfloat16 [32, 64, 8], P('tensor'), may hold values from -2 to 2
- feature_map_query: bfloat16 [32, 64, 64], P('tensor'), may hold values from -1 to 1
- feature_map_key: bfloat16 [8, 64, 64], P('tensor'), may hold values from -1 to 1
Outputs:
- block_out: bfloat16 [8192, 2048], P(('dp', 'seq'))
- grad_tokens: float32 [8192, 2048], P(('dp', 'seq'))
- grad_q_down: float32 [2048, 8], P(('dp', 'seq', 'tensor'))
- grad_k_down: float32 [2048, 8], P(('dp', 'seq', 'tensor'))
- grad_v_down: float32 [2048, 8], P(('dp', 'seq', 'tensor'))
- grad_o_up: float32 [2048, 8], P(('dp', 'seq', 'tensor'))
- query_up_gradient: float32 [32, 64, 8], P('tensor', ('dp', 'seq'))
- grad_k_up: float32 [8, 64, 8], P('tensor', ('dp', 'seq'))
- value_up_gradient: float32 [8, 64, 8], P('tensor', ('dp', 'seq'))
- grad_o_down: float32 [32, 64, 8], P('tensor', ('dp', 'seq'))
- grad_fmap_q: float32 [32, 64, 64], P('tensor', ('dp', 'seq'))
- grad_fmap_k: float32 [8, 64, 64], P('tensor', ('dp', 'seq'))
The draws below stay inside these ranges and needn't reach their ends.
Inputs may be any that keep to these rules, and one draw needn't show every extreme that they name: `sequence_lengths`: in each group the 3 lengths add up to 4096; one of them, in a place drawn from the seed, is longer than 3072. The first group holds one sequence of 4094 tokens and two of 1 token.
All inputs are finite; a program needn't handle non-finite values.
Results may differ from the reference program's by a relative error of at most 0.014.
Values may be sent and summed in bfloat16 or wider, within the bound.
No kernel may reach another device: no remote copies, remote signals or barrier semaphores. Data moves between devices by JAX's collectives and lax.ppermute only.
A program may use at most 256 MiB of HBM per device.

```python
import math
import jax
import jax.numpy as jnp
from jax import lax

MODEL_WIDTH = 2048
QUERY_HEADS = 32
KEY_VALUE_HEADS = 8
HEAD_SIZE = 64
FF = 8192
ADAPTER_RANK = 8
WIN = 64
TOK_DEV = 1024
GROUP = 4096
GROUPS = 2
TOKENS = 8192


def draw_sequence_lengths(key, part):
    key = jax.random.fold_in(key, 7)
    key_long, key_split, key_place = jax.random.split(key, 3)
    group_marks = jnp.arange(GROUPS).astype(jnp.int32)
    drawn_long = GROUP - TOK_DEV + 1 + jax.random.randint(key_long, (GROUPS,), 0, TOK_DEV - 2)
    longest = jnp.where(group_marks == 0, GROUP - 2, drawn_long).astype(jnp.int32)
    leftover = GROUP - longest
    first_short = 1 + jax.random.randint(key_split, (GROUPS,), 0, leftover - 1)
    second_short = leftover - first_short
    slot_index = jax.random.randint(key_place, (GROUPS,), 0, 3)
    first_col = jnp.where(slot_index == 0, longest, first_short)
    middle_col = jnp.where(slot_index == 1, longest, jnp.where(slot_index == 0, first_short, second_short))
    last_col = jnp.where(slot_index == 2, longest, second_short)
    return jnp.stack([first_col, middle_col, last_col], axis=1).astype(jnp.int32)


def strengthened(array, stream_key, source, target, shards_of, factor):
    def block_of(position):
        return (jnp.arange(array.shape[position]) // (array.shape[position] // shards_of)).reshape((-1,) + (1,) * (array.ndim - 1 - position))

    first = jax.random.permutation(stream_key, shards_of)[block_of(target)]
    far = (block_of(target) + shards_of // 2) % shards_of
    return jnp.where((block_of(source) == first) | (block_of(source) == far), factor * array, array)


def shard_levels(stream_key, extent, cuts, low, high):
    factor_of = 1.0
    for position, parts in cuts:
        heights = jax.random.uniform(jax.random.fold_in(jax.random.fold_in(stream_key, 6), position), (parts,), jnp.float32, low / len(cuts), high / len(cuts))
        factor_of = factor_of * jnp.repeat(jnp.exp(heights), extent[position] // parts).reshape((-1,) + (1,) * (len(extent) - 1 - position))
    return factor_of


def scatter_about(own_key, extent, spread, most, cuts=(), held_as=jnp.bfloat16):
    level = shard_levels(own_key, extent, cuts, -0.22, 0.18) if cuts else 1.0
    values = jax.random.normal(own_key, extent, jnp.float32) * spread * level
    return jnp.minimum(jnp.maximum(values, -most), most).astype(held_as)


def noise_with(rng, extent, spread, limit, cuts, heavy, kind=jnp.bfloat16):
    values = spread * jax.random.normal(rng, extent, jnp.float32)
    if cuts:
        values = values * shard_levels(rng, extent, cuts, -0.22, 0.18)
    return jnp.clip(strengthened(values, jax.random.fold_in(rng, 3), *heavy), -limit, limit).astype(kind)


def setup_inputs(seed: int = 0) -> dict:
    streams_of = jax.random.split(jax.random.key(seed), 23)
    return {
        "tokens": noise_with(streams_of[0], (TOKENS, MODEL_WIDTH), 1.0, 6.0, ((0, 8),), (0, 1, 8, 2.0)),
        "sequence_lengths": draw_sequence_lengths(jax.random.fold_in(streams_of[22], 71), 0),
        "output_cotangent": scatter_about(streams_of[2], (TOKENS, MODEL_WIDTH), 1.0, 6.0, ((0, 8),)),
        "query_weight": scatter_about(streams_of[3], (MODEL_WIDTH, QUERY_HEADS * HEAD_SIZE), MODEL_WIDTH ** -0.5, 0.125, ((0, 8), (1, 4))),
        "key_weight": scatter_about(streams_of[4], (MODEL_WIDTH, KEY_VALUE_HEADS * HEAD_SIZE), MODEL_WIDTH ** -0.5, 0.125, ((0, 8), (1, 4))),
        "value_weight": scatter_about(streams_of[5], (MODEL_WIDTH, KEY_VALUE_HEADS * HEAD_SIZE), MODEL_WIDTH ** -0.5, 0.125, ((0, 8), (1, 4))),
        "output_weight": scatter_about(streams_of[6], (QUERY_HEADS * HEAD_SIZE, MODEL_WIDTH), (QUERY_HEADS * HEAD_SIZE // 256) ** -0.5, 2.0, ((0, 4), (1, 8))),
        "gate_weight": scatter_about(streams_of[7], (MODEL_WIDTH, FF), MODEL_WIDTH ** -0.5, 0.125, ((0, 8), (1, 4))),
        "up_weight": scatter_about(streams_of[8], (MODEL_WIDTH, FF), MODEL_WIDTH ** -0.5, 0.125, ((0, 8), (1, 4))),
        "down_weight": scatter_about(streams_of[9], (FF, MODEL_WIDTH), FF ** -0.5, 0.0625, ((0, 4), (1, 8))),
        "attention_norm_gain": jnp.clip(1.0 + 0.1 * jax.random.normal(streams_of[10], (MODEL_WIDTH,), jnp.float32), 0.5, 1.5).astype(jnp.bfloat16),
        "feedforward_norm_gain": jnp.clip(1.0 + 0.1 * jax.random.normal(streams_of[11], (MODEL_WIDTH,), jnp.float32), 0.5, 1.5).astype(jnp.bfloat16),
        "query_adapter_down": scatter_about(streams_of[12], (MODEL_WIDTH, ADAPTER_RANK), MODEL_WIDTH ** -0.5, 0.125),
        "key_adapter_down": scatter_about(streams_of[13], (MODEL_WIDTH, ADAPTER_RANK), MODEL_WIDTH ** -0.5, 0.125),
        "value_adapter_down": scatter_about(streams_of[14], (MODEL_WIDTH, ADAPTER_RANK), MODEL_WIDTH ** -0.5, 0.125),
        "output_adapter_up": scatter_about(streams_of[15], (MODEL_WIDTH, ADAPTER_RANK), (ADAPTER_RANK * 8) ** -0.5, 0.75),
        "query_adapter_up": scatter_about(streams_of[16], (QUERY_HEADS, HEAD_SIZE, ADAPTER_RANK), (ADAPTER_RANK * 8) ** -0.5, 0.75, ((0, 4),)),
        "key_adapter_up": scatter_about(streams_of[17], (KEY_VALUE_HEADS, HEAD_SIZE, ADAPTER_RANK), (ADAPTER_RANK * 8) ** -0.5, 0.75, ((0, 4),)),
        "value_adapter_up": scatter_about(streams_of[18], (KEY_VALUE_HEADS, HEAD_SIZE, ADAPTER_RANK), (ADAPTER_RANK * 8) ** -0.5, 0.75, ((0, 4),)),
        "output_adapter_down": scatter_about(streams_of[19], (QUERY_HEADS, HEAD_SIZE, ADAPTER_RANK), (QUERY_HEADS * HEAD_SIZE // 256) ** -0.5, 2.0, ((0, 4),)),
        "feature_map_query": scatter_about(streams_of[20], (QUERY_HEADS, HEAD_SIZE, HEAD_SIZE), (HEAD_SIZE // 2) ** -0.5, 1.0, ((0, 4),)),
        "feature_map_key": scatter_about(streams_of[21], (KEY_VALUE_HEADS, HEAD_SIZE, HEAD_SIZE), (HEAD_SIZE // 2) ** -0.5, 1.0, ((0, 4),)),
    }


epsilon = 1e-05
rope_base = 500000.0
highest = lax.Precision.HIGHEST

@jax.custom_vjp
def lowered_input(v):
    return lax.optimization_barrier(v.astype(jnp.bfloat16)).astype(jnp.float32)

@jax.custom_vjp
def low_back(v):
    return v

def low_keep(v):
    return (lowered_input(v), None)

def low_pass(kept, grad):
    return (grad,)

def back_keep(v):
    return (v, None)

def back_low(kept, grad):
    return (lowered_input(grad),)
lowered_input.defvjp(low_keep, low_pass)
low_back.defvjp(back_keep, back_low)

def matrix_product(left, right):
    return jnp.dot(left, right, precision=highest)

def rms_scale(value_rows_all, gain):
    return value_rows_all * lax.rsqrt(lax.optimization_barrier(jnp.mean(value_rows_all * value_rows_all, axis=-1, keepdims=True)) + epsilon) * gain

def rope_tables(relative, head_columns):
    half_width = head_columns // 2
    ladder = jnp.arange(half_width).astype(jnp.float32)
    inverse = jnp.exp(ladder * (-2.0 * math.log(rope_base) / head_columns))
    angles = relative.astype(jnp.float32)[:, None] * inverse[None, :]
    return (jnp.cos(angles), jnp.sin(angles))

def apply_rotation(value_rows_all, cosine_table, sine_table):
    half_width = value_rows_all.shape[-1] // 2
    first_half = value_rows_all[..., :half_width]
    second_half = value_rows_all[..., half_width:]
    cos_rows = cosine_table[:, None, :]
    sin_rows = sine_table[:, None, :]
    return jnp.concatenate([first_half * cos_rows - second_half * sin_rows, second_half * cos_rows + first_half * sin_rows], axis=-1)

def doc_layout(lengths, positions):
    ends_at = jnp.cumsum(lengths).astype(jnp.int32)
    starts_at = (ends_at - lengths).astype(jnp.int32)
    doc_index = lax.optimization_barrier(jnp.sum((positions[:, None] >= ends_at[None, :]).astype(jnp.int32), axis=1)).astype(jnp.int32)
    marks = jnp.arange(lengths.shape[0]).astype(jnp.int32)
    start_of = lax.optimization_barrier(jnp.sum(jnp.where(doc_index[:, None] == marks[None, :], starts_at[None, :], 0), axis=1)).astype(jnp.int32)
    return (doc_index, (positions - start_of).astype(jnp.int32))

def hedgehog(value_rows_all, maps):
    logits = low_back(jnp.einsum('thd,hde->the', value_rows_all, maps, precision=highest))
    return jnp.concatenate([jax.nn.softmax(logits, axis=-1), jax.nn.softmax(-logits, axis=-1)], axis=-1)

def group_forward(inputs, lengths, frozen, training_step):
    query_weight, key_weight, value_weight, output_weight, gate_weight, up_weight, down_weight, attention_norm_gain, feedforward_norm_gain = frozen
    query_adapter_down, key_adapter_down, value_adapter_down, output_adapter_up, query_adapter_up, key_adapter_up, value_adapter_up, output_adapter_down, feature_map_query, feature_map_key = training_step
    num_tokens = inputs.shape[0]
    head_count, head_columns, adapter_rank = query_adapter_up.shape
    key_value_heads = key_adapter_up.shape[0]
    grouping = head_count // key_value_heads
    score_scale = head_columns ** (-0.5)
    positions = jnp.arange(num_tokens).astype(jnp.int32)
    doc_index, relative = doc_layout(lengths, positions)
    cosine_table, sine_table = rope_tables(relative, head_columns)
    normed = lowered_input(rms_scale(inputs, attention_norm_gain))

    def apply_projection(weight, down_side, up_product, item_count):
        flattened_up = up_product.reshape(item_count * head_columns, adapter_rank)
        mixed = matrix_product(normed, weight) + matrix_product(matrix_product(normed, down_side), flattened_up.T)
        return low_back(mixed).reshape(num_tokens, item_count, head_columns)
    query_vectors = lowered_input(apply_rotation(apply_projection(query_weight, query_adapter_down, query_adapter_up, head_count), cosine_table, sine_table))
    key_rows_all = lowered_input(apply_rotation(apply_projection(key_weight, key_adapter_down, key_adapter_up, key_value_heads), cosine_table, sine_table))
    value_rows_all = lowered_input(apply_projection(value_weight, value_adapter_down, value_adapter_up, key_value_heads))
    phi_q = lowered_input(hedgehog(query_vectors, feature_map_query))
    phi_k = lowered_input(hedgehog(key_rows_all, feature_map_key))
    front = ((WIN, 0), (0, 0), (0, 0))
    keys_pad = jnp.pad(key_rows_all, front)
    values_pad = jnp.pad(value_rows_all, front)
    phi_k_pad = jnp.pad(phi_k, front)
    key_positions = (jnp.arange(num_tokens + WIN) - WIN).astype(jnp.int32)
    key_docs, key_relative = doc_layout(lengths, key_positions)

    def block(carried, block_index, query_vectors, keys_pad, values_pad, phi_q, phi_k_pad):
        state, norm_sum = carried
        q_start = (block_index * TOK_DEV).astype(jnp.int32)
        key_rows = TOK_DEV + WIN
        q_block = lax.dynamic_slice_in_dim(query_vectors, q_start, TOK_DEV, 0).reshape(TOK_DEV, key_value_heads, grouping, head_columns)
        phi_block = lax.dynamic_slice_in_dim(phi_q, q_start, TOK_DEV, 0).reshape(TOK_DEV, key_value_heads, grouping, 2 * head_columns)
        k_block = lax.dynamic_slice_in_dim(keys_pad, q_start, key_rows, 0)
        v_block = lax.dynamic_slice_in_dim(values_pad, q_start, key_rows, 0)
        f_block = lax.dynamic_slice_in_dim(phi_k_pad, q_start, key_rows, 0)
        q_pos = q_start + jnp.arange(TOK_DEV).astype(jnp.int32)
        k_pos = q_start - WIN + jnp.arange(key_rows).astype(jnp.int32)
        q_doc = lax.dynamic_slice_in_dim(doc_index, q_start, TOK_DEV, 0)
        k_doc = lax.dynamic_slice_in_dim(key_docs, q_start, key_rows, 0)
        k_rel = lax.dynamic_slice_in_dim(key_relative, q_start, key_rows, 0)
        k_valid = k_pos >= 0
        same_doc = (q_doc[:, None] == k_doc[None, :]) & k_valid[None, :]
        gaps = q_pos[:, None] - k_pos[None, :]
        mask_win = same_doc & (gaps >= 0) & (gaps < WIN)
        mask_lin = same_doc & (gaps >= WIN)
        raw_scores = low_back(jnp.einsum('tkgd,ekd->kgte', q_block, k_block, precision=highest) * score_scale)
        weights_win = jnp.where(mask_win, jnp.exp(raw_scores), 0.0)
        weights_lin = jnp.where(mask_lin, low_back(jnp.einsum('tkgf,ekf->kgte', phi_block, f_block, precision=highest)), 0.0)
        weights = weights_win + weights_lin
        prior = q_start - WIN - 1
        prior_doc, unused_rel = doc_layout(lengths, jnp.reshape(prior, (1,)).astype(jnp.int32))
        use_state = ((q_doc == prior_doc[0]) & (prior >= 0)).astype(jnp.float32)
        totals = lax.optimization_barrier(jnp.sum(weights, axis=-1)) + jnp.einsum('tkgf,kf->kgt', phi_block, norm_sum, precision=highest) * use_state
        numer = jnp.einsum('kgte,ekd->kgtd', lowered_input(weights), v_block, precision=highest) + jnp.einsum('tkgf,kfd->kgtd', phi_block, state, precision=highest) * use_state[:, None]
        attended = low_back(numer) / totals[..., None]
        attended = jnp.transpose(attended, (2, 0, 1, 3)).reshape(TOK_DEV, head_count * head_columns)
        include = (k_valid[:TOK_DEV] & (k_doc[:TOK_DEV] == k_doc[TOK_DEV - 1])).astype(jnp.float32)
        opens = jnp.any(k_valid[:TOK_DEV] & (k_rel[:TOK_DEV] == 0))
        passing = 1.0 - opens.astype(jnp.float32)
        masked_phi = f_block[:TOK_DEV] * include[:, None, None]
        contrib = jnp.einsum('ekf,ekd->kfd', masked_phi, v_block[:TOK_DEV], precision=highest)
        contrib_norm = lax.optimization_barrier(jnp.sum(masked_phi, axis=0))
        return ((contrib + passing * state, contrib_norm + passing * norm_sum), attended)
    stepper = jax.checkpoint(block)

    def advance(carried, block_index):
        return stepper(carried, block_index, query_vectors, keys_pad, values_pad, phi_q, phi_k_pad)
    start_state = (jnp.zeros((key_value_heads, 2 * head_columns, head_columns), jnp.float32), jnp.zeros((key_value_heads, 2 * head_columns), jnp.float32))
    unused_carry, attended_all = lax.scan(advance, start_state, jnp.arange(num_tokens // TOK_DEV).astype(jnp.int32))
    attended_bfloat = lowered_input(attended_all.reshape(num_tokens, head_count * head_columns))
    output_flattened = output_adapter_down.reshape(head_count * head_columns, adapter_rank)
    adapter_branch = matrix_product(attended_bfloat, output_weight) + matrix_product(matrix_product(attended_bfloat, output_flattened), output_adapter_up.T)
    hidden = inputs + low_back(adapter_branch)
    normed_mlp = lowered_input(rms_scale(hidden, feedforward_norm_gain))
    gate_value = low_back(matrix_product(normed_mlp, gate_weight))
    up_value = low_back(matrix_product(normed_mlp, up_weight))
    activated = lowered_input(jax.nn.silu(gate_value) * up_value)
    return hidden + matrix_product(activated, down_weight)

def reference(tokens, sequence_lengths, output_cotangent, query_weight, key_weight, value_weight, output_weight, gate_weight, up_weight, down_weight, attention_norm_gain, feedforward_norm_gain, query_adapter_down, key_adapter_down, value_adapter_down, output_adapter_up, query_adapter_up, key_adapter_up, value_adapter_up, output_adapter_down, feature_map_query, feature_map_key):
    frozen = tuple((make_array.astype(jnp.float32) for make_array in (query_weight, key_weight, value_weight, output_weight, gate_weight, up_weight, down_weight, attention_norm_gain, feedforward_norm_gain)))
    training_step = tuple((make_array.astype(jnp.float32) for make_array in (query_adapter_down, key_adapter_down, value_adapter_down, output_adapter_up, query_adapter_up, key_adapter_up, value_adapter_up, output_adapter_down, feature_map_query, feature_map_key)))
    model_width = tokens.shape[1]
    stacked = (tokens.reshape(GROUPS, GROUP, model_width), sequence_lengths, output_cotangent.reshape(GROUPS, GROUP, model_width))

    def one_group(summed, batch_item):
        group_rows, lengths, cotangent = batch_item

        def forward(inputs, *params):
            return group_forward(inputs, lengths, frozen, params)
        result, pullback = jax.vjp(forward, group_rows.astype(jnp.float32), *training_step)
        gradients = pullback(cotangent.astype(jnp.float32))
        updated = tuple((total + grad_part for total, grad_part in zip(summed, gradients[1:])))
        return (updated, (result.astype(jnp.bfloat16), gradients[0]))
    initial = tuple((jnp.zeros_like(make_array) for make_array in training_step))
    sums, (outputs, input_grads) = lax.scan(one_group, initial, stacked)
    return (outputs.reshape(TOKENS, model_width), input_grads.reshape(TOKENS, model_width), sums[0], sums[1], sums[2], sums[3], sums[4], sums[5], sums[6], sums[7], sums[8], sums[9])
```

```python
import math

import jax
import jax.numpy as jnp
from jax import lax
from jax.experimental import pallas as pl
from jax.experimental.pallas import tpu as pltpu
from jax.sharding import PartitionSpec as P

WIN = 64
CHUNK = 128
AUG = 80
RING = 8
FFN_PARTS = 4

epsilon = 1e-05
rope_base = 500000.0
bf16, f32, i32 = jnp.bfloat16, jnp.float32, jnp.int32
MIB = 1 << 20


def nn(a, b):
    return lax.dot_general(a, b, (((1,), (0,)), ((), ())), preferred_element_type=f32)


def nt(a, b):
    return lax.dot_general(a, b, (((1,), (1,)), ((), ())), preferred_element_type=f32)


def tn(a, b):
    return lax.dot_general(a, b, (((0,), (0,)), ((), ())), preferred_element_type=f32)


def halves(x, axis):
    high = x.astype(bf16)
    return jnp.concatenate([high, (x - high.astype(f32)).astype(bf16)], axis=axis)


def halves_outside(x, axis):
    high = lax.reduce_precision(x, 8, 7)
    return jnp.concatenate([high, x - high], axis=axis).astype(bf16)


def exchange(x, axis, bit):
    count = lax.axis_size(axis)
    return lax.ppermute(x, axis, [(i, i ^ bit) for i in range(count)])


def shifted(x, axis, by):
    count = lax.axis_size(axis)
    return lax.ppermute(x, axis, [(i, i + by) for i in range(count) if 0 <= i + by < count])


def place_of(index, seq):
    row, col = index // seq, index % seq
    return row * seq + (col if row % 2 == 0 else seq - 1 - col)


def place_of_traced(index, seq):
    row, col = index // seq, index % seq
    return row * seq + jnp.where(row % 2 == 0, col, seq - 1 - col)


def weight_ring(block, after):
    dp, seq = lax.axis_size("dp"), lax.axis_size("seq")
    count = dp * seq
    if count > RING:
        return [lax.all_gather(block, ("dp", "seq"), axis=0, tiled=True)]
    order = [place_of(i, seq) for i in range(count)]
    up = [(order[i], order[(i + 1) % count]) for i in range(count)]
    half = block.shape[0] // 2
    a, b = block[:half], block[half:]
    if after:
        a, b = lax.optimization_barrier((a, b, *after))[:2]
    first, second = [a], [b]
    for _ in range(count - 1):
        a = lax.ppermute(a, ("dp", "seq"), up)
        b = lax.ppermute(b, ("dp", "seq"), [(j, i) for i, j in up])
        first.append(a)
        second.append(b)
    return first + second


def ring_offsets(rows):
    dp, seq = lax.axis_size("dp"), lax.axis_size("seq")
    count = dp * seq
    if count > RING:
        return jnp.zeros((1,), i32)
    place = place_of_traced(lax.axis_index("dp") * seq + lax.axis_index("seq"), seq)
    steps = jnp.arange(count)
    first = place_of_traced((place - steps) % count, seq) * rows
    second = place_of_traced((place + steps) % count, seq) * rows + rows // 2
    return jnp.concatenate([first, second]).astype(i32)


def reduce_to_own(x, axis):
    size, index = lax.axis_size(axis), lax.axis_index(axis)
    while size > 1:
        half = size // 2
        bit = (index // half) % 2
        x = x.reshape((2, half) + x.shape[1:])
        send = lax.dynamic_index_in_dim(x, 1 - bit, 0, keepdims=False)
        keep = lax.dynamic_index_in_dim(x, bit, 0, keepdims=False)
        x = keep + exchange(send, axis, half)
        size = half
    return x[0]


def reduce_quarters(far, near):
    far_mine = far[1].astype(f32) + exchange(far[0], "tensor", 1).astype(f32)
    crossed = exchange(far_mine.astype(bf16), "tensor", 2)
    near_mine = near[1].astype(f32) + exchange(near[0], "tensor", 1).astype(f32)
    return near_mine + crossed.astype(f32)


def gather_quarters(own):
    across = exchange(own, "tensor", 2)
    beside = exchange(own, "tensor", 1)
    last = exchange(across, "tensor", 1)
    return jnp.stack([own, beside, across, last])


def load_pieces(pieces, offsets, held, sems):
    copies = [
        pltpu.make_async_copy(
            piece,
            held.at[pl.ds(pl.multiple_of(offsets[i], 16), piece.shape[0])],
            sems.at[i],
        )
        for i, piece in enumerate(pieces)
    ]
    for copy in copies:
        copy.start()
    for copy in copies:
        copy.wait()


def params(limit):
    return pltpu.CompilerParams(vmem_limit_bytes=limit * MIB)


def cost(flops, moved, exps=0):
    return pl.CostEstimate(flops=int(flops), bytes_accessed=int(moved), transcendentals=int(exps))


ANY = pl.BlockSpec(memory_space=pl.ANY)


def whole(shape):
    return pl.BlockSpec(shape, lambda *_: (0,) * len(shape))


def rope(x, cos, sin):
    width = 2 * cos.shape[0]
    half = width // 2
    out = []
    for at in range(0, x.shape[0], width):
        x1, x2 = x[at : at + half], x[at + half : at + width]
        out += [x1 * cos - x2 * sin, x2 * cos + x1 * sin]
    return jnp.concatenate(out, axis=0)


def hedgehog(a, width):
    out = []
    for at in range(0, a.shape[0], width):
        one = a[at : at + width]
        for e in (
            jnp.exp(one - jnp.max(one, axis=0, keepdims=True)),
            jnp.exp(jnp.min(one, axis=0, keepdims=True) - one),
        ):
            out.append(e * (1.0 / jnp.sum(e, axis=0, keepdims=True)))
    return jnp.concatenate(out, axis=0).astype(bf16)


def hedgehog_back(phi, grad, width):
    out = []
    for at in range(0, phi.shape[0], 2 * width):
        p1, p2 = phi[at : at + width].astype(f32), phi[at + width : at + 2 * width].astype(f32)
        d1, d2 = grad[at : at + width], grad[at + width : at + 2 * width]
        out.append(
            p1 * (d1 - jnp.sum(p1 * d1, axis=0, keepdims=True))
            - p2 * (d2 - jnp.sum(p2 * d2, axis=0, keepdims=True))
        )
    return jnp.concatenate(out, axis=0).astype(bf16)


def prep_body(dims, offsets, last_docs, nx, low_up, cos_q, sin_q, cos_k, sin_k, map_q, map_k, doc_row, *rest):
    tokens, ext, q_width, kv_width, head, n_pieces, chunks = dims
    pieces, rest = rest[:n_pieces], rest[n_pieces:]
    q_t, phi_q, k_n, k_t, v_n, v_a, phi_kn, phi_kt, contrib, held, sems = rest
    load_pieces(pieces, offsets, held, sems)
    kv_heads = kv_width // head
    step = ext // 3
    v_a[...] = jnp.zeros(v_a.shape, bf16)
    for at in range(0, ext, step):
        rows = pl.ds(at, step)
        raw = nn(nx[rows, :], held[:, q_width:]) + low_up[rows, q_width:]
        v = raw[:, kv_width:].astype(bf16)
        v_n[rows, :] = v
        v_tr = raw[:, kv_width:].T.astype(bf16)
        for k in range(kv_heads):
            v_a[k * AUG : k * AUG + head, rows] = v_tr[k * head : (k + 1) * head]
            v_a[k * AUG + head : (k + 1) * AUG, rows] = (
                lax.broadcasted_iota(i32, (AUG - head, step), 0) < 2
            ).astype(f32).astype(bf16)
        k_rot = rope(raw[:, :kv_width].T, cos_k[:, rows], sin_k[:, rows])
        k_bf = k_rot.astype(bf16)
        k_t[:, rows] = k_bf
        k_n[rows, :] = k_rot.T.astype(bf16)
        phi = hedgehog(nn(map_k[...], k_bf), head)
        phi_kt[:, rows] = phi
        phi_kn[rows, :] = phi.astype(f32).T.astype(bf16)
    incl = (doc_row[:, :tokens] == last_docs[chunks]).astype(f32).astype(bf16)
    for k in range(kv_heads):
        masked = v_a[k * AUG : (k + 1) * AUG, :tokens] * incl
        contrib[k] = nn(masked, phi_kn[:tokens, k * 2 * head : (k + 1) * 2 * head])
    step = tokens // 2
    group = q_width // kv_heads
    for at in range(0, tokens, step):
        rows = pl.ds(at, step)
        raw = nn(nx[pl.ds(WIN + at, step), :], held[:, :q_width])
        raw = raw + low_up[pl.ds(WIN + at, step), :q_width]
        q_bf = rope(raw.T, cos_q[:, rows], sin_q[:, rows]).astype(bf16)
        q_t[:, rows] = q_bf
        for k in range(kv_heads):
            logits = nn(map_q[k], q_bf[k * group : (k + 1) * group])
            phi_q[2 * k * group : 2 * (k + 1) * group, rows] = hedgehog(logits, head)


def masks(q_doc, k_doc, heads):
    keys = CHUNK + WIN
    j = lax.broadcasted_iota(i32, (keys, CHUNK), 0)
    t = lax.broadcasted_iota(i32, (keys, CHUNK), 1)
    same = k_doc == q_doc
    win = same & (j > t) & (j <= t + WIN)
    lin = (same & (j <= t))[:CHUNK]
    win_f = jnp.concatenate([win.astype(f32)] * heads, axis=1)
    lin_f = jnp.concatenate([lin.astype(f32)] * heads, axis=1)
    return win_f > 0.5, lin_f > 0.5


def side(ref, first, count, size):
    return jnp.concatenate([ref[first + g * size : first + (g + 1) * size, :] for g in range(count)], axis=1)


def window_weights(q, phi_q, k_win, phi_k, win, lin, scale):
    scores = nn(k_win, q)
    weights_win = jnp.where(win, jnp.exp(scores * scale), 0.0)
    linear = jnp.where(lin, nn(phi_k, phi_q), 0.0)
    return weights_win, jnp.concatenate([weights_win[:CHUNK] + linear, weights_win[CHUNK:]], axis=0)


def forward_body(dims, last_docs, q_t, phi_q, k_n, v_a, phi_kn, doc_col, doc_row, q_doc, state_in, att, att_t, totals, states, state):
    kv_heads, group, head = dims
    chunk = pl.program_id(0)
    start = pl.multiple_of(chunk * CHUNK, CHUNK)

    @pl.when(chunk == 0)
    def _():
        state[...] = state_in[...]

    keys = CHUNK + WIN
    win, lin = masks(q_doc[...], doc_col[pl.ds(start, keys), :], group)
    use = (q_doc[...] == last_docs[chunk]).astype(f32)
    use = jnp.concatenate([use] * group, axis=1)
    incl = (doc_row[:, pl.ds(start, CHUNK)] == last_docs[chunk + 1]).astype(f32).astype(bf16)
    passing = (last_docs[chunk] == last_docs[chunk + 1]).astype(f32)
    scale = head**-0.5
    out = []
    for k in range(kv_heads):
        q = side(q_t, k * group * head, group, head)
        phi = side(phi_q, 2 * k * group * head, group, 2 * head)
        k_win = k_n[pl.ds(start, keys), k * head : (k + 1) * head]
        phi_k = phi_kn[pl.ds(start, CHUNK), 2 * k * head : 2 * (k + 1) * head]
        v_win = v_a[k * AUG : (k + 1) * AUG, pl.ds(start, 2 * CHUNK)]
        _, weights = window_weights(q, phi, k_win, phi_k, win, lin, scale)
        before = state[k]
        from_state = nn(before.astype(bf16), phi) * use
        total = jnp.sum(weights, axis=0, keepdims=True) + from_state[head : head + 1]
        numer = nn(v_win[:, :keys], weights.astype(bf16))[:head] + from_state[:head]
        attended = numer * (1.0 / total)
        for g in range(group):
            out.append(attended[:, g * CHUNK : (g + 1) * CHUNK])
            totals[k * group + g : k * group + g + 1, :] = total[:, g * CHUNK : (g + 1) * CHUNK]
        states[0, k] = before.T.astype(bf16)
        state[k] = nn(v_win[:, :CHUNK] * incl, phi_k) + passing * before
    attended = jnp.concatenate(out, axis=0)
    att_t[...] = attended
    att[...] = attended.T.astype(bf16)


def o_body(n_pieces, offsets, nat, att, down, up, *rest):
    pieces = rest[:n_pieces]
    part, lowered, held, sems = rest[n_pieces:]

    @pl.when(pl.program_id(0) == 0)
    def _():
        load_pieces(pieces, offsets, held, sems)

    low = nn(att[...], down[...])
    lowered[0] = low
    part[0] = (nt(att[...], held[...]) + nn(halves(low, 1), up[...])).astype(bf16)


def ffn_body(n_pieces, units, first, offsets, order, nat, n2, cot, *rest):
    pieces, rest = rest[:n_pieces], rest[n_pieces:]
    if first:
        mlp, grad, held, sems = rest
    else:
        mlp_in, grad_in, mlp, grad, held, sems = rest

    @pl.when(pl.program_id(0) == 0)
    def _():
        load_pieces(pieces, offsets, held, sems)

    gate = nn(n2[0], held[:, :units])
    up = nn(n2[0], held[:, units : 2 * units])
    grad_act = nn(cot[...], held[:, 2 * units :])
    s = 1.0 / (1.0 + jnp.exp(-gate))
    silu = gate * s
    act = (silu * up).astype(bf16)
    grad_gate = (grad_act * up * s * (1.0 + gate * (1.0 - s))).astype(bf16)
    grad_up = (grad_act * silu).astype(bf16)
    down_sum = nt(act, held[:, 2 * units :])
    grad_sum = nt(grad_gate, held[:, :units]) + nt(grad_up, held[:, units : 2 * units])
    if not first:
        down_sum = down_sum + mlp_in[0]
        grad_sum = grad_sum + grad_in[0]
    mlp[0] = down_sum.astype(mlp.dtype)
    grad[0] = grad_sum.astype(grad.dtype)


def go_body(dims, offsets, nat, before_doc, branch, o_up, o_down, att_t, totals, phi_q, q_doc, *rest):
    n_pieces, kv_heads, group, head = dims
    pieces = rest[:n_pieces]
    numer, grad_totals, up_product, dstate, held, sems = rest[n_pieces:]

    @pl.when(pl.program_id(0) == 0)
    def _():
        load_pieces(pieces, offsets, held, sems)
        dstate[...] = jnp.zeros(dstate.shape, f32)

    up = nn(branch[0], o_up[...])
    up_product[...] = up
    grad = (nn(branch[0], held[...]) + nn(halves(up, 1), o_down[...])).T
    use = (q_doc[...] == before_doc[0]).astype(f32)
    columns = grad.shape[1]
    for k in range(kv_heads):
        total = jnp.zeros((2 * head, AUG), f32)
        for g in range(group):
            h = k * group + g
            rows = slice(h * head, (h + 1) * head)
            inverse = 1.0 / totals[h : h + 1, :]
            one = grad[rows]
            g_total = -jnp.sum(one * att_t[rows, :], axis=0, keepdims=True) * inverse
            g_numer = (one * inverse).astype(bf16)
            numer[rows, :] = g_numer
            grad_totals[h : h + 1, :] = g_total
            aug = augmented(g_numer, g_total * use, columns, head, use)
            total = total + nt(phi_q[2 * h * head : 2 * (h + 1) * head, :], aug)
        dstate[k] += total


def augmented(g_numer, g_total, columns, head, use=None):
    top = g_numer if use is None else g_numer * use.astype(bf16)
    high = g_total.astype(bf16).astype(f32)
    row = lax.broadcasted_iota(i32, (AUG - head, columns), 0)
    below = jnp.where(row == 0, high, jnp.where(row == 1, g_total - high, 0.0))
    return jnp.concatenate([top, below.astype(bf16)], axis=0)


def backward_body(
    dims, last_docs, q_t, phi_q, numer, grad_totals, k_n, k_t, v_n, v_a, phi_kn, phi_kt, doc_col, doc_row, q_doc,
    states, later_in, cos_q, sin_q, map_q, map_k,
    g_nat, g_kt, g_vt, g_map_q, g_map_k, later, acc_phi,
):
    kv_heads, group, head, chunks = dims
    step = pl.program_id(0)
    chunk = chunks - 1 - step
    start = pl.multiple_of(chunk * CHUNK, CHUNK)
    keys = CHUNK + WIN

    @pl.when(step == 0)
    def _():
        later[...] = later_in[...]
        g_kt[...] = jnp.zeros(g_kt.shape, f32)
        g_vt[...] = jnp.zeros(g_vt.shape, f32)
        acc_phi[...] = jnp.zeros(acc_phi.shape, f32)
        g_map_q[...] = jnp.zeros(g_map_q.shape, f32)

    win, lin = masks(q_doc[...], doc_col[pl.ds(start, keys), :], group)
    use1 = (q_doc[...] == last_docs[chunk]).astype(f32)
    use = jnp.concatenate([use1] * group, axis=1)
    incl = (doc_row[:, pl.ds(start, CHUNK)] == last_docs[chunk + 1]).astype(f32)
    passing = (last_docs[chunk] == last_docs[chunk + 1]).astype(f32)
    scale = head**-0.5
    two = pl.ds(start, 2 * CHUNK)
    one = pl.ds(start, CHUNK)
    pad = jnp.zeros((head, 2 * CHUNK - keys), f32)
    grads = []
    for k in range(kv_heads):
        lanes = slice(k * head, (k + 1) * head)
        wide = slice(2 * k * head, 2 * (k + 1) * head)
        q = side(q_t, k * group * head, group, head)
        phi = side(phi_q, 2 * k * group * head, group, 2 * head)
        gn = side(numer, k * group * head, group, head)
        gt = side(grad_totals, k * group, group, 1)
        weights_win, weights = window_weights(
            q, phi, k_n[pl.ds(start, keys), lanes], phi_kn[one, wide], win, lin, scale
        )
        grad_w = nn(v_n[pl.ds(start, keys), lanes], gn) + gt
        gs = (grad_w * weights_win).astype(bf16)
        gl = jnp.where(lin, grad_w[:CHUNK], 0.0).astype(bf16)
        gq = nn(k_t[lanes, two][:, :keys], gs) * scale
        gk = nt(q, gs) * scale
        gv = nt(gn, weights.astype(bf16))
        aug = augmented(gn, gt, group * CHUNK, head)
        gphi_q = nn(phi_kt[wide, one], gl) + use * nn(states[0, k], aug)
        gphi_k = nt(phi, gl)
        after = later[k]
        after_bf = after.astype(bf16)
        v_aug = v_a[k * AUG : (k + 1) * AUG, one]
        gphi_k = gphi_k + incl * nn(after_bf, v_aug)
        from_later = incl * nn(after.T.astype(bf16), phi_kt[wide, one])[:head]
        gv = gv + jnp.concatenate([from_later, jnp.zeros((head, keys - CHUNK), f32)], axis=1)
        later[k] = nt(phi, augmented(gn, gt * use, group * CHUNK, head, use)) + passing * after
        g_kt[lanes, two] += jnp.concatenate([gk, pad], axis=1)
        g_vt[lanes, two] += jnp.concatenate([gv, pad], axis=1)
        acc_phi[wide, one] += gphi_k
        heads = [slice(g * CHUNK, (g + 1) * CHUNK) for g in range(group)]
        rows = slice(k * group * head, (k + 1) * group * head)
        grad_phi = jnp.concatenate([gphi_q[:, at] for at in heads], axis=0)
        phi_rows = phi_q[2 * k * group * head : 2 * (k + 1) * group * head, :]
        ga = hedgehog_back(phi_rows, grad_phi, head)
        gq_rows = jnp.concatenate([gq[:, at] for at in heads], axis=0) + tn(map_q[k], ga)
        g_map_q[k] += nt(q_t[rows, :], ga)
        grads.append(rope(gq_rows, cos_q[...], -sin_q[...]))
    g_nat[...] = jnp.concatenate(grads, axis=0).T.astype(bf16)

    @pl.when(step == chunks - 1)
    def _():
        ga = hedgehog_back(phi_kt[...], acc_phi[...], head)
        g_kt[...] += tn(map_k[...], ga)
        g_map_k[...] = nt(k_t[...], ga)


def gn_body(n_pieces, offsets, nat, g_q, g_kv, ups_q, ups_kv, downs, *rest):
    pieces = rest[:n_pieces]
    part, ups, held, sems = rest[n_pieces:]

    @pl.when(pl.program_id(0) == 0)
    def _():
        load_pieces(pieces, offsets, held, sems)

    q_width = g_q.shape[1]
    up = nn(g_q[...], ups_q[...]) + nn(g_kv[...], ups_kv[...])
    ups[0] = up
    total = nt(g_q[...], held[:, :q_width]) + nt(g_kv[...], held[:, q_width:])
    part[0] = (total + nn(halves(up, 1), downs[...])).astype(bf16)


def place_body(nat, x, out):
    out[...] = x[0].astype(out.dtype)


def place(x, nat, dtype):
    count, rows, width = x.shape
    return pl.pallas_call(
        place_body,
        grid_spec=pltpu.PrefetchScalarGridSpec(
            num_scalar_prefetch=1,
            grid=(count,),
            in_specs=[pl.BlockSpec((1, rows, width), lambda i, nat: (i, 0, 0))],
            out_specs=pl.BlockSpec((rows, width), lambda i, nat: (nat[i], 0)),
        ),
        out_shape=jax.ShapeDtypeStruct((count * rows, width), dtype),
        compiler_params=params(32),
        cost_estimate=cost(0, x.size * 6),
        name="place",
    )(nat, x)


def rms_factor(x):
    return lax.rsqrt(jnp.mean(x * x, axis=-1, keepdims=True) + epsilon)


def rms_back(x, gain, grads):
    factor = rms_factor(x)
    unit = x * factor
    scaled = grads * gain
    return factor * (scaled - unit * jnp.mean(unit * scaled, axis=-1, keepdims=True))


def block_diagonal(blocks):
    count, rows, cols = blocks.shape
    eye = jnp.eye(count, dtype=blocks.dtype)
    return (blocks[:, :, None, :] * eye[:, None, :, None]).reshape(count * rows, count * cols)


def diagonal_blocks(x, count):
    size = x.shape[0] // count
    return jnp.stack([x[i * size : (i + 1) * size, i * size : (i + 1) * size] for i in range(count)])


def per_device(
    tokens,
    sequence_lengths,
    output_cotangent,
    query_weight,
    key_weight,
    value_weight,
    output_weight,
    gate_weight,
    up_weight,
    down_weight,
    attention_norm_gain,
    feedforward_norm_gain,
    query_adapter_down,
    key_adapter_down,
    value_adapter_down,
    output_adapter_up,
    query_adapter_up,
    key_adapter_up,
    value_adapter_up,
    output_adapter_down,
    feature_map_query,
    feature_map_key,
):
    rows, model = tokens.shape
    heads, head, rank = query_adapter_up.shape
    kv_heads = key_adapter_up.shape[0]
    group = heads // kv_heads
    q_width, kv_width = heads * head, kv_heads * head
    seq, ring = lax.axis_size("seq"), lax.axis_size("dp") * lax.axis_size("seq")
    here = lax.axis_index("seq")
    chunks = rows // CHUNK
    ext = -(-(rows + WIN) // CHUNK) * CHUNK
    quarter = rows // 4
    units = gate_weight.shape[1] // FFN_PARTS

    core, far = lax.axis_index("tensor") % 2, lax.axis_index("tensor") // 2
    nat = jnp.stack([core * 2 + far, (1 - core) * 2 + far, core * 2 + 1 - far, (1 - core) * 2 + 1 - far]).astype(i32)
    own_rows = lambda x: lax.dynamic_slice_in_dim(x, nat[0] * quarter, quarter, 0)

    offsets = ring_offsets(query_weight.shape[0])
    n_pieces = offsets.shape[0]
    qkv_pieces = weight_ring(jnp.concatenate([query_weight, key_weight, value_weight], axis=1), ())
    o_pieces = weight_ring(output_weight.T, qkv_pieces[n_pieces // 2 - 2 : n_pieces // 2 - 1] if n_pieces > 1 else ())
    ffn_pieces, chain = [], [qkv_pieces, o_pieces]
    for j in range(FFN_PARTS):
        cols = slice(j * units, (j + 1) * units)
        packed = jnp.concatenate([gate_weight[:, cols], up_weight[:, cols], down_weight[cols].T], axis=1)
        behind = chain[-2]
        after = (behind[n_pieces // 2 - 1], behind[-1]) if n_pieces > 1 else ()
        ffn_pieces.append(weight_ring(packed, after))
        chain.append(ffn_pieces[-1])

    lengths = sequence_lengths[0]
    ends = jnp.cumsum(lengths)
    first_row = here * rows

    def docs_of(at):
        return jnp.where(at >= 0, jnp.sum((at[:, None] >= ends[None, :]).astype(i32), axis=1), -1)

    def angles_of(at):
        doc = docs_of(at)
        starts = ends - lengths
        start = jnp.sum(jnp.where(doc[:, None] == jnp.arange(lengths.shape[0])[None, :], starts[None, :], 0), axis=1)
        ladder = jnp.arange(head // 2).astype(f32)
        inverse = jnp.exp(ladder * (-2.0 * math.log(rope_base) / head))
        angles = inverse[:, None] * (at - start).astype(f32)[None, :]
        return jnp.cos(angles), jnp.sin(angles)

    q_at = first_row + jnp.arange(rows)
    k_index = jnp.arange(ext)
    k_at = first_row - WIN + k_index
    q_doc = docs_of(q_at)[None, :]
    k_doc = jnp.where(k_index < rows + WIN, docs_of(k_at), -2)
    doc_col, doc_row = k_doc[:, None], k_doc[None, :]
    last_docs = docs_of(first_row - WIN - 1 + CHUNK * jnp.arange(chunks + 1))
    block_docs = docs_of(rows * jnp.arange(seq + 1) - WIN - 1)
    passes = (block_docs[:-1] == block_docs[1:]).astype(f32)
    cos_q, sin_q = angles_of(q_at)
    cos_k, sin_k = angles_of(k_at)

    halo = shifted(tokens[rows - WIN :], "seq", 1)
    spare = jnp.zeros((ext - rows - WIN, model), bf16)
    seen = jnp.concatenate([halo, tokens, spare], axis=0).astype(f32)
    gain_attn = attention_norm_gain.astype(f32)
    gain_mlp = feedforward_norm_gain.astype(f32)
    normed = (seen * rms_factor(seen) * gain_attn).astype(bf16)
    downs = jnp.concatenate([query_adapter_down, key_adapter_down, value_adapter_down], axis=1)
    low = nn(normed, downs)
    ups = jnp.zeros((q_width + 2 * kv_width, 3 * rank), bf16)
    ups = ups.at[:q_width, :rank].set(query_adapter_up.reshape(q_width, rank))
    ups = ups.at[q_width : q_width + kv_width, rank : 2 * rank].set(key_adapter_up.reshape(kv_width, rank))
    ups = ups.at[q_width + kv_width :, 2 * rank :].set(value_adapter_up.reshape(kv_width, rank))
    low_up = nt(halves_outside(low, 1), jnp.concatenate([ups, ups], axis=1))
    maps_q = jnp.stack(
        [block_diagonal(feature_map_query[k * group : (k + 1) * group].transpose(0, 2, 1)) for k in range(kv_heads)]
    )
    maps_k = block_diagonal(feature_map_key.transpose(0, 2, 1))

    sems = pltpu.SemaphoreType.DMA((n_pieces,))
    qkv_width = q_width + 2 * kv_width
    held_qkv = pltpu.VMEM((model, qkv_width), bf16)
    held_o = pltpu.VMEM((model, q_width), bf16)

    dims = (rows, ext, q_width, kv_width, head, n_pieces, chunks)
    shapes = [
        ((q_width, rows), bf16),
        ((2 * q_width, rows), bf16),
        ((ext, kv_width), bf16),
        ((kv_width, ext), bf16),
        ((ext, kv_width), bf16),
        ((kv_heads * AUG, ext), bf16),
        ((ext, 2 * kv_width), bf16),
        ((2 * kv_width, ext), bf16),
        ((kv_heads, AUG, 2 * head), f32),
    ]
    prep_in = (normed, low_up, cos_q, sin_q, cos_k, sin_k, maps_q, maps_k, doc_row)
    q_t, phi_q, k_n, k_t, v_n, v_a, phi_kn, phi_kt, contrib = pl.pallas_call(
        lambda *refs: prep_body(dims, *refs),
        grid_spec=pltpu.PrefetchScalarGridSpec(
            num_scalar_prefetch=2,
            grid=(1,),
            in_specs=[whole(x.shape) for x in prep_in] + [ANY] * n_pieces,
            out_specs=[whole(s) for s, _ in shapes],
            scratch_shapes=[held_qkv, sems],
        ),
        out_shape=[jax.ShapeDtypeStruct(s, d) for s, d in shapes],
        compiler_params=params(56),
        cost_estimate=cost(2 * rows * model * qkv_width, 20 * MIB, 3 * rows * q_width),
        name="prep",
    )(offsets, last_docs, *prep_in, *qkv_pieces)

    state_in = jnp.zeros_like(contrib)
    factor = jnp.ones((), f32)
    for by in range(1, seq):
        state_in = state_in + factor * shifted(contrib, "seq", by)
        factor = factor * passes[jnp.maximum(here - by, 0)]

    column = lambda r: pl.BlockSpec((r, CHUNK), lambda c, *_: (0, c))
    att, att_t, totals, states = pl.pallas_call(
        lambda *refs: forward_body((kv_heads, group, head), *refs),
        grid_spec=pltpu.PrefetchScalarGridSpec(
            num_scalar_prefetch=1,
            grid=(chunks,),
            in_specs=[
                column(q_width),
                column(2 * q_width),
                whole(k_n.shape),
                whole(v_a.shape),
                whole(phi_kn.shape),
                whole(doc_col.shape),
                whole(doc_row.shape),
                column(1),
                whole(state_in.shape),
            ],
            out_specs=[
                pl.BlockSpec((CHUNK, q_width), lambda c, *_: (c, 0)),
                column(q_width),
                column(heads),
                pl.BlockSpec((1, kv_heads, 2 * head, AUG), lambda c, *_: (c, 0, 0, 0)),
            ],
            scratch_shapes=[pltpu.VMEM(state_in.shape, f32)],
        ),
        out_shape=[
            jax.ShapeDtypeStruct((rows, q_width), bf16),
            jax.ShapeDtypeStruct((q_width, rows), f32),
            jax.ShapeDtypeStruct((heads, rows), f32),
            jax.ShapeDtypeStruct((chunks, kv_heads, 2 * head, AUG), bf16),
        ],
        compiler_params=params(48),
        cost_estimate=cost(2 * heads * rows * 256 * 256, 10 * MIB, rows * heads * 192),
        name="attend",
    )(last_docs, q_t, phi_q, k_n, v_a, phi_kn, doc_col, doc_row, q_doc, state_in)

    o_down = output_adapter_down.reshape(q_width, rank)
    o_up_t = jnp.concatenate([output_adapter_up.T, output_adapter_up.T], axis=0)
    order_far, order_near = jnp.array([3, 2], i32), jnp.array([1, 0], i32)

    def o_part(which):
        return pl.pallas_call(
            lambda *refs: o_body(n_pieces, *refs),
            grid_spec=pltpu.PrefetchScalarGridSpec(
                num_scalar_prefetch=2,
                grid=(2,),
                in_specs=[
                    pl.BlockSpec((quarter, q_width), lambda i, off, nat: (nat[i], 0)),
                    whole(o_down.shape),
                    whole(o_up_t.shape),
                ]
                + [ANY] * n_pieces,
                out_specs=[
                    pl.BlockSpec((1, quarter, model), lambda i, *_: (i, 0, 0)),
                    pl.BlockSpec((1, quarter, rank), lambda i, *_: (i, 0, 0)),
                ],
                scratch_shapes=[held_o, sems],
            ),
            out_shape=[
                jax.ShapeDtypeStruct((2, quarter, model), bf16),
                jax.ShapeDtypeStruct((2, quarter, rank), f32),
            ],
            compiler_params=params(32),
            cost_estimate=cost(2 * rows * model * q_width / 2, 5 * MIB),
            name="project",
        )(offsets, nat[which], att, o_down, o_up_t, *o_pieces)

    o_far, low_far = o_part(order_far)
    o_near, low_near = o_part(order_near)
    lowered = jnp.concatenate([low_near[1], low_near[0], low_far[1], low_far[0]], axis=0)
    hidden = own_rows(tokens).astype(f32) + reduce_quarters(o_far, o_near)
    normed_mlp = gather_quarters((hidden * rms_factor(hidden) * gain_mlp).astype(bf16))

    def ffn(pieces, which, sums, out_type):
        count = which.shape[0]
        block = lambda: pl.BlockSpec((1, quarter, model), lambda i, off, order, nat: (order[i], 0, 0))
        in_order = pl.BlockSpec((1, quarter, model), lambda i, *_: (i, 0, 0))
        out = jax.ShapeDtypeStruct((count, quarter, model), out_type)
        share = count / 4
        aliases = {5 + n_pieces: 0, 6 + n_pieces: 1} if sums and out_type == f32 else {}
        return pl.pallas_call(
            lambda *refs: ffn_body(n_pieces, units, not sums, *refs),
            grid_spec=pltpu.PrefetchScalarGridSpec(
                num_scalar_prefetch=3,
                grid=(count,),
                in_specs=[
                    block(),
                    pl.BlockSpec((quarter, model), lambda i, off, order, nat: (nat[i], 0)),
                ]
                + [ANY] * n_pieces
                + [block() for _ in sums],
                out_specs=[in_order, in_order],
                scratch_shapes=[pltpu.VMEM((model, 3 * units), bf16), sems],
            ),
            out_shape=[out, out],
            input_output_aliases=aliases,
            compiler_params=params(52),
            cost_estimate=cost(12 * rows * model * units * share, 46 * MIB * share, rows * units * share),
            name="feed_forward",
        )(offsets, which, nat[which], normed_mlp, output_cotangent, *pieces, *sums)

    every = jnp.arange(4).astype(i32)
    sums = ()
    for pieces in ffn_pieces[:-1]:
        sums = tuple(ffn(pieces, every, sums, f32))
    mlp_far, grad_far = ffn(ffn_pieces[-1], order_far, sums, bf16)
    mlp_near, grad_near = ffn(ffn_pieces[-1], order_near, sums, bf16)
    grad_normed_mlp = reduce_quarters(grad_far, grad_near)
    grad_hidden = own_rows(output_cotangent).astype(f32) + rms_back(hidden, gain_mlp, grad_normed_mlp)
    branch = gather_quarters(grad_hidden.astype(bf16))

    o_down_t = jnp.concatenate([o_down.T, o_down.T], axis=0)
    by_quarter = lambda r: pl.BlockSpec((r, quarter), lambda i, off, nat, before: (0, nat[i]))
    numer, grad_totals, up_product, dstate = pl.pallas_call(
        lambda *refs: go_body((n_pieces, kv_heads, group, head), *refs),
        grid_spec=pltpu.PrefetchScalarGridSpec(
            num_scalar_prefetch=3,
            grid=(4,),
            in_specs=[
                pl.BlockSpec((1, quarter, model), lambda i, *_: (i, 0, 0)),
                whole((model, rank)),
                whole(o_down_t.shape),
                by_quarter(q_width),
                by_quarter(heads),
                by_quarter(2 * q_width),
                by_quarter(1),
            ]
            + [ANY] * n_pieces,
            out_specs=[
                by_quarter(q_width),
                by_quarter(heads),
                pl.BlockSpec((quarter, rank), lambda i, off, nat, before: (nat[i], 0)),
                whole((kv_heads, 2 * head, AUG)),
            ],
            scratch_shapes=[held_o, sems],
        ),
        out_shape=[
            jax.ShapeDtypeStruct((q_width, rows), bf16),
            jax.ShapeDtypeStruct((heads, rows), f32),
            jax.ShapeDtypeStruct((rows, rank), f32),
            jax.ShapeDtypeStruct((kv_heads, 2 * head, AUG), f32),
        ],
        compiler_params=params(48),
        cost_estimate=cost(2 * rows * model * q_width, 14 * MIB),
        name="project_back",
    )(offsets, nat, last_docs[:1], branch, output_adapter_up, o_down_t, att_t, totals, phi_q, q_doc, *o_pieces)

    later_in = jnp.zeros_like(dstate)
    factor = jnp.ones((), f32)
    for by in range(1, seq):
        later_in = later_in + factor * shifted(dstate, "seq", -by)
        factor = factor * passes[jnp.minimum(here + by, seq - 1)]

    back_column = lambda r: pl.BlockSpec((r, CHUNK), lambda c, *_: (0, chunks - 1 - c))
    back_in = (
        (q_t, back_column(q_width)),
        (phi_q, back_column(2 * q_width)),
        (numer, back_column(q_width)),
        (grad_totals, back_column(heads)),
        (k_n, None),
        (k_t, None),
        (v_n, None),
        (v_a, None),
        (phi_kn, None),
        (phi_kt, None),
        (doc_col, None),
        (doc_row, None),
        (q_doc, back_column(1)),
        (states, pl.BlockSpec((1, kv_heads, 2 * head, AUG), lambda c, *_: (chunks - 1 - c, 0, 0, 0))),
        (later_in, None),
        (cos_q, back_column(head // 2)),
        (sin_q, back_column(head // 2)),
        (maps_q, None),
        (maps_k, None),
    )
    g_q, g_kt, g_vt, g_map_q, g_map_k = pl.pallas_call(
        lambda *refs: backward_body((kv_heads, group, head, chunks), *refs),
        grid_spec=pltpu.PrefetchScalarGridSpec(
            num_scalar_prefetch=1,
            grid=(chunks,),
            in_specs=[whole(x.shape) if spec is None else spec for x, spec in back_in],
            out_specs=[
                pl.BlockSpec((CHUNK, q_width), lambda c, *_: (chunks - 1 - c, 0)),
                whole((kv_width, ext)),
                whole((kv_width, ext)),
                whole((kv_heads, group * head, group * head)),
                whole((kv_width, kv_width)),
            ],
            scratch_shapes=[pltpu.VMEM(dstate.shape, f32), pltpu.VMEM((2 * kv_width, ext), f32)],
        ),
        out_shape=[
            jax.ShapeDtypeStruct((rows, q_width), bf16),
            jax.ShapeDtypeStruct((kv_width, ext), f32),
            jax.ShapeDtypeStruct((kv_width, ext), f32),
            jax.ShapeDtypeStruct((kv_heads, group * head, group * head), f32),
            jax.ShapeDtypeStruct((kv_width, kv_width), f32),
        ],
        compiler_params=params(52),
        cost_estimate=cost(6 * heads * rows * 256 * 256, 12 * MIB, rows * heads * 192),
        name="attend_back",
    )(last_docs, *[x for x, _ in back_in])

    returned = shifted(jnp.concatenate([g_kt[:, :WIN], g_vt[:, :WIN]], axis=0), "seq", -1)
    lead = ((0, 0), (rows - WIN, 0))
    g_k = g_kt[:, WIN : WIN + rows] + jnp.pad(returned[:kv_width], lead)
    g_v = g_vt[:, WIN : WIN + rows] + jnp.pad(returned[kv_width:], lead)
    g_k = rope(g_k, cos_q, -sin_q)
    g_kv = jnp.concatenate([g_k, g_v], axis=0).astype(bf16).T

    downs_t = jnp.concatenate([downs.T, downs.T], axis=0)

    def gn_part(which):
        by_rows = lambda w: pl.BlockSpec((quarter, w), lambda i, off, nat: (nat[i], 0))
        return pl.pallas_call(
            lambda *refs: gn_body(n_pieces, *refs),
            grid_spec=pltpu.PrefetchScalarGridSpec(
                num_scalar_prefetch=2,
                grid=(2,),
                in_specs=[
                    by_rows(q_width),
                    by_rows(2 * kv_width),
                    whole((q_width, 3 * rank)),
                    whole((2 * kv_width, 3 * rank)),
                    whole(downs_t.shape),
                ]
                + [ANY] * n_pieces,
                out_specs=[
                    pl.BlockSpec((1, quarter, model), lambda i, *_: (i, 0, 0)),
                    pl.BlockSpec((1, quarter, 3 * rank), lambda i, *_: (i, 0, 0)),
                ],
                scratch_shapes=[held_qkv, sems],
            ),
            out_shape=[
                jax.ShapeDtypeStruct((2, quarter, model), bf16),
                jax.ShapeDtypeStruct((2, quarter, 3 * rank), f32),
            ],
            compiler_params=params(32),
            cost_estimate=cost(rows * model * qkv_width, 7 * MIB),
            name="norm_back",
        )(offsets, nat[which], g_q, g_kv, ups[:q_width], ups[q_width:], downs_t, *qkv_pieces)

    gn_far, ups_far = gn_part(order_far)
    gn_near, ups_near = gn_part(order_near)
    grad_normed = reduce_quarters(gn_far, gn_near)
    grad_rows = grad_hidden + rms_back(own_rows(tokens).astype(f32), gain_attn, grad_normed)
    grad_tokens = place(gather_quarters(grad_rows.astype(bf16)), nat, f32)
    mlp = reduce_quarters(mlp_far, mlp_near)
    block_out = place(gather_quarters((hidden + mlp).astype(bf16)), nat, bf16)

    def joined(x):
        return x[:, : x.shape[1] // 2] + x[:, x.shape[1] // 2 :]

    low_own = halves_outside(low[WIN : WIN + rows], 1)
    g_q_up = joined(tn(g_q, low_own))[:, :rank]
    g_kv_up = joined(tn(g_kv, low_own))
    g_k_up = g_kv_up[:kv_width, rank : 2 * rank]
    g_v_up = g_kv_up[kv_width:, 2 * rank :]
    ups_rel = jnp.stack([ups_near[1], ups_near[0], ups_far[1], ups_far[0]])
    ups_nat = jnp.zeros_like(ups_rel).at[nat].set(ups_rel).reshape(rows, 3 * rank)
    g_downs = joined(tn(normed[WIN : WIN + rows], halves_outside(ups_nat, 1)))
    g_o_up = joined(tn(branch.reshape(rows, model), halves_outside(lowered, 1)))
    g_o_down = joined(tn(att, halves_outside(up_product, 1)))
    shared = jnp.concatenate([g_downs, g_o_up], axis=1).reshape(ring, 4, model // ring // 4, 4 * rank)
    shared = reduce_to_own(shared.transpose(1, 0, 2, 3), "tensor")

    def by_rows_of_head(x, count):
        return x.reshape(count, ring, head // ring, -1).transpose(1, 0, 2, 3)

    per_head = [
        by_rows_of_head(g_q_up, heads),
        by_rows_of_head(g_k_up, kv_heads),
        by_rows_of_head(g_v_up, kv_heads),
        by_rows_of_head(g_o_down, heads),
        by_rows_of_head(jnp.concatenate([diagonal_blocks(g_map_q[k], group) for k in range(kv_heads)]), heads),
        by_rows_of_head(diagonal_blocks(g_map_k, kv_heads), kv_heads),
    ]
    parts = [shared] + per_head
    flat = jnp.concatenate([x.reshape(ring, -1) for x in parts], axis=1)
    flat = reduce_to_own(flat.reshape(-1, seq, flat.shape[1]), "dp")
    flat = reduce_to_own(flat, "seq")
    out, at = [], 0
    for x in parts:
        size = x.size // ring
        out.append(flat[at : at + size].reshape(x.shape[1:]))
        at += size
    shared_out = out[0]
    return (
        block_out,
        grad_tokens,
        shared_out[:, :rank],
        shared_out[:, rank : 2 * rank],
        shared_out[:, 2 * rank : 3 * rank],
        shared_out[:, 3 * rank :],
        *out[1:],
    )


def solution(mesh):
    return jax.shard_map(
        per_device,
        mesh=mesh,
        in_specs=(
            P(("dp", "seq"), None),
            P("dp", None),
            P(("dp", "seq"), None),
            P(("dp", "seq"), "tensor"),
            P(("dp", "seq"), "tensor"),
            P(("dp", "seq"), "tensor"),
            P("tensor", ("dp", "seq")),
            P(("dp", "seq"), "tensor"),
            P(("dp", "seq"), "tensor"),
            P("tensor", ("dp", "seq")),
            P(),
            P(),
            P(),
            P(),
            P(),
            P(),
            P("tensor", None, None),
            P("tensor", None, None),
            P("tensor", None, None),
            P("tensor", None, None),
            P("tensor", None, None),
            P("tensor", None, None),
        ),
        out_specs=(
            P(("dp", "seq"), None),
            P(("dp", "seq"), None),
            P(("dp", "seq", "tensor"), None),
            P(("dp", "seq", "tensor"), None),
            P(("dp", "seq", "tensor"), None),
            P(("dp", "seq", "tensor"), None),
            P("tensor", ("dp", "seq"), None),
            P("tensor", ("dp", "seq"), None),
            P("tensor", ("dp", "seq"), None),
            P("tensor", ("dp", "seq"), None),
            P("tensor", ("dp", "seq"), None),
            P("tensor", ("dp", "seq"), None),
        ),
        check_vma=False,
    )
```

```python
import math

import jax
import jax.numpy as jnp
from jax import lax
from jax.experimental import pallas as pl
from jax.experimental.pallas import tpu as pltpu
from jax.sharding import PartitionSpec as P

WIN = 64
CHUNK = 128
AUG = 80
RING = 8
FFN_UNITS = ((384, 384), (640, 640))
BIG = 60

epsilon = 1e-05
rope_base = 500000.0
bf16, f32, i32 = jnp.bfloat16, jnp.float32, jnp.int32
MIB = 1 << 20


def nn(a, b):
    return lax.dot_general(a, b, (((1,), (0,)), ((), ())), preferred_element_type=f32)


def nt(a, b):
    return lax.dot_general(a, b, (((1,), (1,)), ((), ())), preferred_element_type=f32)


def tn(a, b):
    return lax.dot_general(a, b, (((0,), (0,)), ((), ())), preferred_element_type=f32)


def halves(x, axis):
    high = x.astype(bf16)
    return jnp.concatenate([high, (x - high.astype(f32)).astype(bf16)], axis=axis)


def halves_outside(x, axis):
    high = lax.reduce_precision(x, 8, 7)
    return jnp.concatenate([high, x - high], axis=axis).astype(bf16)


def exchange(x, axis, bit):
    count = lax.axis_size(axis)
    return lax.ppermute(x, axis, [(i, i ^ bit) for i in range(count)])


def shifted(x, axis, by):
    count = lax.axis_size(axis)
    return lax.ppermute(x, axis, [(i, i + by) for i in range(count) if 0 <= i + by < count])


def place_of(index, seq):
    row, col = index // seq, index % seq
    return row * seq + (col if row % 2 == 0 else seq - 1 - col)


def place_of_traced(index, seq):
    row, col = index // seq, index % seq
    return row * seq + jnp.where(row % 2 == 0, col, seq - 1 - col)


class Clock:
    def __init__(self):
        self.now = jnp.zeros((), i32)

    def wait(self, *arrays):
        *out, self.now = lax.optimization_barrier((*arrays, self.now))
        return out

    def tie(self, x):
        return self.wait(x)[0]


class Chain:
    def __init__(self, clock, way, pack, *blocks):
        block = pack(*clock.wait(*blocks))
        dp, seq = lax.axis_size("dp"), lax.axis_size("seq")
        self.clock, self.count = clock, dp * seq
        self.ringed = self.count <= RING
        rows = block.shape[0]
        if not self.ringed:
            self.lanes = [[lax.all_gather(block, ("dp", "seq"), axis=0, tiled=True)]]
            self.offsets = jnp.zeros((1,), i32)
            return
        order = [place_of(i, seq) for i in range(self.count)]
        up = [(order[i], order[(i + 1) % self.count]) for i in range(self.count)]
        down = [(j, i) for i, j in up]
        place = place_of_traced(lax.axis_index("dp") * seq + lax.axis_index("seq"), seq)
        steps = jnp.arange(self.count)
        came_up = place_of_traced((place - steps) % self.count, seq) * rows
        came_down = place_of_traced((place + steps) % self.count, seq) * rows
        if way:
            self.lanes, self.ways = [[block]], [up if way > 0 else down]
            self.offsets = (came_up if way > 0 else came_down).astype(i32)
        else:
            half = rows // 2
            self.lanes, self.ways = [[block[:half]], [block[half:]]], [up, down]
            self.offsets = jnp.concatenate([came_up, came_down + half]).astype(i32)

    def settle(self):
        if self.ringed:
            came = self.clock.wait(*[lane[-1] for lane in self.lanes])
            for lane, x in zip(self.lanes, came):
                lane[-1] = x

    def step(self):
        if self.ringed:
            self.settle()
            for lane, way in zip(self.lanes, self.ways):
                lane.append(lax.ppermute(lane[-1], ("dp", "seq"), way))

    def pieces(self):
        self.settle()
        return [piece for lane in self.lanes for piece in lane]


def load_pieces(pieces, offsets, held, sems):
    copies = [
        pltpu.make_async_copy(
            piece,
            held.at[pl.ds(pl.multiple_of(offsets[i], 16), piece.shape[0])],
            sems.at[i],
        )
        for i, piece in enumerate(pieces)
    ]
    for copy in copies:
        copy.start()
    for copy in copies:
        copy.wait()


def params(limit):
    return pltpu.CompilerParams(vmem_limit_bytes=limit * MIB)


SMALL = pl.CostEstimate(flops=1, bytes_accessed=1, transcendentals=0)


ANY = pl.BlockSpec(memory_space=pl.ANY)


def whole(shape):
    return pl.BlockSpec(shape, lambda *_: (0,) * len(shape))


def rope(x, cos, sin):
    width = 2 * cos.shape[0]
    half = width // 2
    out = []
    for at in range(0, x.shape[0], width):
        x1, x2 = x[at : at + half], x[at + half : at + width]
        out += [x1 * cos - x2 * sin, x2 * cos + x1 * sin]
    return jnp.concatenate(out, axis=0)


def hedgehog(a, width):
    out = []
    for at in range(0, a.shape[0], width):
        one = a[at : at + width]
        for e in (
            jnp.exp(one - jnp.max(one, axis=0, keepdims=True)),
            jnp.exp(jnp.min(one, axis=0, keepdims=True) - one),
        ):
            out.append(e * (1.0 / jnp.sum(e, axis=0, keepdims=True)))
    return jnp.concatenate(out, axis=0).astype(bf16)


def hedgehog_back(phi, grad, width):
    out = []
    for at in range(0, phi.shape[0], 2 * width):
        p1, p2 = phi[at : at + width].astype(f32), phi[at + width : at + 2 * width].astype(f32)
        d1, d2 = grad[at : at + width], grad[at + width : at + 2 * width]
        out.append(
            p1 * (d1 - jnp.sum(p1 * d1, axis=0, keepdims=True))
            - p2 * (d2 - jnp.sum(p2 * d2, axis=0, keepdims=True))
        )
    return jnp.concatenate(out, axis=0).astype(bf16)


def prep_body(dims, offsets, last_docs, nx, low_up, cos_q, sin_q, cos_k, sin_k, map_q, map_k, doc_row, *rest):
    tokens, ext, q_width, kv_width, head, n_pieces, chunks = dims
    pieces, rest = rest[:n_pieces], rest[n_pieces:]
    q_t, phi_q, k_n, k_t, v_n, v_a, phi_kn, phi_kt, contrib, held, sems = rest
    load_pieces(pieces, offsets, held, sems)
    kv_heads = kv_width // head
    step = ext // 3
    v_a[...] = jnp.zeros(v_a.shape, bf16)
    for at in range(0, ext, step):
        rows = pl.ds(at, step)
        raw = nn(nx[rows, :], held[:, q_width:]) + low_up[rows, q_width:]
        v = raw[:, kv_width:].astype(bf16)
        v_n[rows, :] = v
        v_tr = raw[:, kv_width:].T.astype(bf16)
        for k in range(kv_heads):
            v_a[k * AUG : k * AUG + head, rows] = v_tr[k * head : (k + 1) * head]
            v_a[k * AUG + head : (k + 1) * AUG, rows] = (
                lax.broadcasted_iota(i32, (AUG - head, step), 0) < 2
            ).astype(f32).astype(bf16)
        k_rot = rope(raw[:, :kv_width].T, cos_k[:, rows], sin_k[:, rows])
        k_bf = k_rot.astype(bf16)
        k_t[:, rows] = k_bf
        k_n[rows, :] = k_rot.T.astype(bf16)
        phi = hedgehog(nn(map_k[...], k_bf), head)
        phi_kt[:, rows] = phi
        phi_kn[rows, :] = phi.astype(f32).T.astype(bf16)
    incl = (doc_row[:, :tokens] == last_docs[chunks]).astype(f32).astype(bf16)
    for k in range(kv_heads):
        masked = v_a[k * AUG : (k + 1) * AUG, :tokens] * incl
        contrib[k] = nn(masked, phi_kn[:tokens, k * 2 * head : (k + 1) * 2 * head])
    step = tokens // 2
    group = q_width // kv_heads
    for at in range(0, tokens, step):
        rows = pl.ds(at, step)
        raw = nn(nx[pl.ds(WIN + at, step), :], held[:, :q_width])
        raw = raw + low_up[pl.ds(WIN + at, step), :q_width]
        q_bf = rope(raw.T, cos_q[:, rows], sin_q[:, rows]).astype(bf16)
        q_t[:, rows] = q_bf
        for k in range(kv_heads):
            logits = nn(map_q[k], q_bf[k * group : (k + 1) * group])
            phi_q[2 * k * group : 2 * (k + 1) * group, rows] = hedgehog(logits, head)


def masks(q_doc, k_doc, heads):
    keys = CHUNK + WIN
    j = lax.broadcasted_iota(i32, (keys, CHUNK), 0)
    t = lax.broadcasted_iota(i32, (keys, CHUNK), 1)
    same = k_doc == q_doc
    win = same & (j > t) & (j <= t + WIN)
    lin = (same & (j <= t))[:CHUNK]
    win_f = jnp.concatenate([win.astype(f32)] * heads, axis=1)
    lin_f = jnp.concatenate([lin.astype(f32)] * heads, axis=1)
    return win_f > 0.5, lin_f > 0.5


def side(ref, first, count, size):
    return jnp.concatenate([ref[first + g * size : first + (g + 1) * size, :] for g in range(count)], axis=1)


def window_weights(q, phi_q, k_win, phi_k, win, lin, scale):
    scores = nn(k_win, q)
    weights_win = jnp.where(win, jnp.exp(scores * scale), 0.0)
    linear = jnp.where(lin, nn(phi_k, phi_q), 0.0)
    return weights_win, jnp.concatenate([weights_win[:CHUNK] + linear, weights_win[CHUNK:]], axis=0)


def forward_body(dims, last_docs, q_t, phi_q, k_n, v_a, phi_kn, doc_col, doc_row, q_doc, state_in, att, att_t, totals, states, state):
    kv_heads, group, head = dims
    chunk = pl.program_id(0)
    start = pl.multiple_of(chunk * CHUNK, CHUNK)

    @pl.when(chunk == 0)
    def _():
        state[...] = state_in[...]

    keys = CHUNK + WIN
    win, lin = masks(q_doc[...], doc_col[pl.ds(start, keys), :], group)
    use = (q_doc[...] == last_docs[chunk]).astype(f32)
    use = jnp.concatenate([use] * group, axis=1)
    incl = (doc_row[:, pl.ds(start, CHUNK)] == last_docs[chunk + 1]).astype(f32).astype(bf16)
    passing = (last_docs[chunk] == last_docs[chunk + 1]).astype(f32)
    scale = head**-0.5
    out = []
    for k in range(kv_heads):
        q = side(q_t, k * group * head, group, head)
        phi = side(phi_q, 2 * k * group * head, group, 2 * head)
        k_win = k_n[pl.ds(start, keys), k * head : (k + 1) * head]
        phi_k = phi_kn[pl.ds(start, CHUNK), 2 * k * head : 2 * (k + 1) * head]
        v_win = v_a[k * AUG : (k + 1) * AUG, pl.ds(start, 2 * CHUNK)]
        _, weights = window_weights(q, phi, k_win, phi_k, win, lin, scale)
        before = state[k]
        from_state = nn(before.astype(bf16), phi) * use
        total = jnp.sum(weights, axis=0, keepdims=True) + from_state[head : head + 1]
        numer = nn(v_win[:, :keys], weights.astype(bf16))[:head] + from_state[:head]
        attended = numer * (1.0 / total)
        for g in range(group):
            out.append(attended[:, g * CHUNK : (g + 1) * CHUNK])
            totals[k * group + g : k * group + g + 1, :] = total[:, g * CHUNK : (g + 1) * CHUNK]
        states[0, k] = before.T.astype(bf16)
        state[k] = nn(v_win[:, :CHUNK] * incl, phi_k) + passing * before
    attended = jnp.concatenate(out, axis=0)
    att_t[...] = attended
    att[...] = attended.T.astype(bf16)


def store_at(step, value, outs):
    for i, out in enumerate(outs):

        @pl.when(step == i)
        def _(out=out):
            out[...] = value.astype(out.dtype)


def o_body(n_pieces, offsets, nat, att, down, up, *rest):
    pieces = rest[:n_pieces]
    part0, part1, lowered, held, sems = rest[-5:]
    step = pl.program_id(0)

    @pl.when(step == 0)
    def _():
        load_pieces(pieces, offsets, held, sems)

    low = nn(att[...], down[...])
    lowered[...] = low
    store_at(step, nt(att[...], held[...]) + nn(halves(low, 1), up[...]), (part0, part1))


def quarter_copies(quarters, held, sems, first=0):
    return [pltpu.make_async_copy(x, held.at[first + i], sems.at[first + i]) for i, x in enumerate(quarters)]


def quarter_of(step, quarters, held, sems):
    for i, copy in enumerate(quarter_copies(quarters, held, sems)):

        @pl.when(step == i)
        def _(copy=copy):
            copy.wait()

    return held[step]


def ffn_body(lots, units, summed, last, offsets, nat, cot, *rest):
    count, n_out = sum(lots), 4 if last else 2
    quarters, pieces, rest = rest[:2], rest[2 : 2 + count], rest[2 + count :]
    sums, outs, rest = rest[: 2 * summed], rest[2 * summed : 2 * summed + n_out], rest[2 * summed + n_out :]
    rows, rows_sems, held, sems, out_held, out_sems, *rest = rest
    step = pl.program_id(0)

    def at_first(act):
        pl.when(step == 0)(act)

    def copies(which):
        made, at, i = [], 0, 0
        for lot, size in zip(lots, units):
            for _ in range(lot):
                made.append(
                    pltpu.make_async_copy(
                        pieces[i].at[:, pl.ds(which * size, size)],
                        held.at[which, pl.ds(pl.multiple_of(offsets[i], 16), pieces[i].shape[0]), pl.ds(at, size)],
                        sems.at[which, i],
                    )
                )
                i += 1
            at += size
        return made

    def sum_copy(i, kind):
        return pltpu.make_async_copy(sums[kind].at[i], rest[0].at[i, kind], rest[1].at[i, kind])

    def out_copy(i, kind):
        out = outs[2 * (1 - kind) + i] if last else outs[kind].at[i]
        return pltpu.make_async_copy(out_held.at[i, kind], out, out_sems.at[i, kind])

    @at_first
    def _():
        first = copies(0)
        for copy in quarter_copies(quarters[:1], rows, rows_sems) + first:
            copy.start()
        for copy in quarter_copies(quarters[1:], rows, rows_sems, 1):
            copy.start()
        for copy in first:
            copy.wait()
        for copy in copies(1):
            copy.start()

    n2 = quarter_of(step, quarters, rows, rows_sems)
    gate = nn(n2, held[0])

    @at_first
    def _():
        for copy in copies(1):
            copy.wait()
        for copy in copies(2):
            copy.start()

    up = nn(n2, held[1])

    @at_first
    def _():
        for copy in copies(2):
            copy.wait()
        for i in range(2 if summed else 0):
            for kind in (1, 0):
                sum_copy(i, kind).start()

    grad_act = nn(cot[...], held[2])
    s = 1.0 / (1.0 + jnp.exp(-gate))
    silu = gate * s
    act = (silu * up).astype(bf16)
    grad_gate = (grad_act * up * s * (1.0 + gate * (1.0 - s))).astype(bf16)
    grad_up = (grad_act * silu).astype(bf16)

    def finish(kind, total):
        if summed:
            sum_copy(step, kind).wait()
            total = total + rest[0][step, kind]
        out_held[step, kind] = total.astype(out_held.dtype)
        for i in range(2):

            @pl.when(step == i)
            def _(i=i):
                out_copy(i, kind).start()

    finish(1, nt(grad_gate, held[0]) + nt(grad_up, held[1]))
    finish(0, nt(act, held[2]))

    @pl.when(step == 1)
    def _():
        for i in range(2):
            for kind in range(2):
                out_copy(i, kind).wait()


def go_body(dims, offsets, nat, before_doc, o_up, o_down, att_t, totals, phi_q, q_doc, *rest):
    n_pieces, kv_heads, group, head, later = dims
    quarters, pieces, rest = rest[:2], rest[2 : 2 + n_pieces], rest[2 + n_pieces :]
    earlier, rest = rest[: 4 * later], rest[4 * later :]
    numer, grad_totals, up_product, dstate, rows_held, rows_sems, held, sems = rest
    step = pl.program_id(0)

    @pl.when(step == 0)
    def _():
        for copy in quarter_copies(quarters, rows_held, rows_sems):
            copy.start()
        load_pieces(pieces, offsets, held, sems)
        dstate[...] = earlier[3][...] if later else jnp.zeros(dstate.shape, f32)

    branch = quarter_of(step, quarters, rows_held, rows_sems)
    up = nn(branch, o_up[...])
    up_product[...] = up
    grad = (nn(branch, held[...]) + nn(halves(up, 1), o_down[...])).T
    use = (q_doc[...] == before_doc[0]).astype(f32)
    columns = grad.shape[1]
    for k in range(kv_heads):
        total = jnp.zeros((2 * head, AUG), f32)
        for g in range(group):
            h = k * group + g
            rows = slice(h * head, (h + 1) * head)
            inverse = 1.0 / totals[h : h + 1, :]
            one = grad[rows]
            g_total = -jnp.sum(one * att_t[rows, :], axis=0, keepdims=True) * inverse
            g_numer = (one * inverse).astype(bf16)
            numer[rows, :] = g_numer
            grad_totals[h : h + 1, :] = g_total
            aug = augmented(g_numer, g_total * use, columns, head, use)
            total = total + nt(phi_q[2 * h * head : 2 * (h + 1) * head, :], aug)
        dstate[k] += total


def augmented(g_numer, g_total, columns, head, use=None):
    top = g_numer if use is None else g_numer * use.astype(bf16)
    high = g_total.astype(bf16).astype(f32)
    row = lax.broadcasted_iota(i32, (AUG - head, columns), 0)
    below = jnp.where(row == 0, high, jnp.where(row == 1, g_total - high, 0.0))
    return jnp.concatenate([top, below.astype(bf16)], axis=0)


def backward_body(
    dims, last_docs, q_t, phi_q, numer, grad_totals, k_n, k_t, v_n, v_a, phi_kn, phi_kt, doc_col, doc_row, q_doc,
    states, cos_q, sin_q, map_q,
    g_nat, g_kt, g_vt, acc_phi, g_map_q, later,
):
    kv_heads, group, head, chunks = dims
    step = pl.program_id(0)
    chunk = chunks - 1 - step
    start = pl.multiple_of(chunk * CHUNK, CHUNK)
    keys = CHUNK + WIN

    @pl.when(step == 0)
    def _():
        later[...] = jnp.zeros(later.shape, f32)
        g_kt[...] = jnp.zeros(g_kt.shape, f32)
        g_vt[...] = jnp.zeros(g_vt.shape, f32)
        acc_phi[...] = jnp.zeros(acc_phi.shape, f32)
        g_map_q[...] = jnp.zeros(g_map_q.shape, f32)

    win, lin = masks(q_doc[...], doc_col[pl.ds(start, keys), :], group)
    use1 = (q_doc[...] == last_docs[chunk]).astype(f32)
    use = jnp.concatenate([use1] * group, axis=1)
    incl = (doc_row[:, pl.ds(start, CHUNK)] == last_docs[chunk + 1]).astype(f32)
    passing = (last_docs[chunk] == last_docs[chunk + 1]).astype(f32)
    scale = head**-0.5
    two = pl.ds(start, 2 * CHUNK)
    one = pl.ds(start, CHUNK)
    pad = jnp.zeros((head, 2 * CHUNK - keys), f32)
    grads = []
    for k in range(kv_heads):
        lanes = slice(k * head, (k + 1) * head)
        wide = slice(2 * k * head, 2 * (k + 1) * head)
        q = side(q_t, k * group * head, group, head)
        phi = side(phi_q, 2 * k * group * head, group, 2 * head)
        gn = side(numer, k * group * head, group, head)
        gt = side(grad_totals, k * group, group, 1)
        weights_win, weights = window_weights(
            q, phi, k_n[pl.ds(start, keys), lanes], phi_kn[one, wide], win, lin, scale
        )
        grad_w = nn(v_n[pl.ds(start, keys), lanes], gn) + gt
        gs = (grad_w * weights_win).astype(bf16)
        gl = jnp.where(lin, grad_w[:CHUNK], 0.0).astype(bf16)
        gq = nn(k_t[lanes, two][:, :keys], gs) * scale
        gk = nt(q, gs) * scale
        gv = nt(gn, weights.astype(bf16))
        aug = augmented(gn, gt, group * CHUNK, head)
        gphi_q = nn(phi_kt[wide, one], gl) + use * nn(states[0, k], aug)
        gphi_k = nt(phi, gl)
        after = later[k]
        after_bf = after.astype(bf16)
        v_aug = v_a[k * AUG : (k + 1) * AUG, one]
        gphi_k = gphi_k + incl * nn(after_bf, v_aug)
        from_later = incl * nn(after.T.astype(bf16), phi_kt[wide, one])[:head]
        gv = gv + jnp.concatenate([from_later, jnp.zeros((head, keys - CHUNK), f32)], axis=1)
        later[k] = nt(phi, augmented(gn, gt * use, group * CHUNK, head, use)) + passing * after
        g_kt[lanes, two] += jnp.concatenate([gk, pad], axis=1)
        g_vt[lanes, two] += jnp.concatenate([gv, pad], axis=1)
        acc_phi[wide, one] += gphi_k
        heads = [slice(g * CHUNK, (g + 1) * CHUNK) for g in range(group)]
        rows = slice(k * group * head, (k + 1) * group * head)
        grad_phi = jnp.concatenate([gphi_q[:, at] for at in heads], axis=0)
        phi_rows = phi_q[2 * k * group * head : 2 * (k + 1) * group * head, :]
        ga = hedgehog_back(phi_rows, grad_phi, head)
        gq_rows = jnp.concatenate([gq[:, at] for at in heads], axis=0) + tn(map_q[k], ga)
        g_map_q[k] += nt(q_t[rows, :], ga)
        grads.append(rope(gq_rows, cos_q[...], -sin_q[...]))
    g_nat[...] = jnp.concatenate(grads, axis=0).T.astype(bf16)


def keys_back_body(dims, last_docs, factors, g_kt, g_vt, g_phi, v_a, phi_kt, k_t, doc_row, map_k, *rest):
    kv_heads, head, chunks, rows = dims
    later, (g_own, g_halo, g_map_k) = rest[:-3], rest[-3:]
    ext = g_kt.shape[1]
    incl = (doc_row[...] == last_docs[chunks]) & (lax.broadcasted_iota(i32, (1, ext), 1) < rows)
    incl = incl.astype(f32)
    phi_grads, v_grads = [], []
    for k in range(kv_heads):
        wide = slice(2 * k * head, 2 * (k + 1) * head)
        after = jnp.zeros(later[0].shape[1:], f32)
        for i, x in enumerate(later):
            after = after + factors[i] * x[k]
        phi_grads.append(g_phi[wide, :] + incl * nn(after.astype(bf16), v_a[k * AUG : (k + 1) * AUG, :]))
        from_later = nn(after.T.astype(bf16), phi_kt[wide, :])[:head]
        v_grads.append(g_vt[k * head : (k + 1) * head, :] + incl * from_later)
    ga = hedgehog_back(phi_kt[...], jnp.concatenate(phi_grads, axis=0), head)
    g_map_k[...] = nt(k_t[...], ga)
    g_k = g_kt[...] + tn(map_k[...], ga)
    for i, grad in enumerate((g_k, jnp.concatenate(v_grads, axis=0))):
        mine = slice(i * kv_heads * head, (i + 1) * kv_heads * head)
        g_own[mine, :] = grad[:, WIN : WIN + rows]
        g_halo[mine, :] = jnp.concatenate([jnp.zeros((kv_heads * head, CHUNK - WIN), f32), grad[:, :WIN]], axis=1)


def adapters_body(
    dims, nat, g_q, g_own, g_halo, cos, sin, ups, low, normed, lowered, att, up_product, g_map_q, g_map_k, *rest
):
    rows, window, head, rank = dims
    branch, (g_kv, low_back, by_head, shared) = rest[:4], rest[4:]
    half = g_own.shape[0] // 2
    wide = rows - g_halo.shape[1]
    k = jnp.concatenate([g_own[:half, :wide], g_own[:half, wide:] + g_halo[:half]], axis=1)
    v = jnp.concatenate([g_own[half:, :wide], g_own[half:, wide:] + g_halo[half:]], axis=1)
    kv = jnp.concatenate([rope(k, cos[...], -sin[...]), v], axis=0).T.astype(bf16)
    g_kv[...] = kv
    q_width = g_q.shape[1]
    up = nn(g_q[...], ups[:q_width]) + nn(kv, ups[q_width:])
    up_halves = halves(up, 1)
    low_back[...] = up_halves

    def joined(x, axis):
        one, other = jnp.split(x, 2, axis=axis)
        return one + other

    low_halves = halves(low[...], 1)
    g_q_up = joined(tn(g_q[...], low_halves), 1)[:, :rank]
    g_kv_up = joined(tn(kv, low_halves), 1)
    g_o_down = joined(tn(att[...], halves(up_product[...], 1)), 1)
    by_head[...] = jnp.zeros(by_head.shape, f32)
    q_heads, kv_heads = q_width // head, half // head
    group = q_heads // kv_heads
    for h in range(q_heads):
        mine, at = slice(h * head, (h + 1) * head), (h % group) * head
        by_head[h, :, :head] = g_map_q[h // group, at : at + head, at : at + head]
        by_head[h, :, head : head + rank] = g_q_up[mine]
        by_head[h, :, head + rank : head + 2 * rank] = g_o_down[mine]
    for h in range(kv_heads):
        mine = slice(h * head, (h + 1) * head)
        by_head[q_heads + h, :, :head] = g_map_k[mine, mine]
        by_head[q_heads + h, :, head : head + rank] = g_kv_up[mine, rank : 2 * rank]
        by_head[q_heads + h, :, head + rank : head + 2 * rank] = g_kv_up[half + h * head : half + (h + 1) * head, 2 * rank :]
    shared[: 3 * rank, :] = joined(tn(up_halves, normed[window : window + rows, :]), 0)
    o_up = 0.0
    for i, x in enumerate(branch):
        part = lowered[pl.ds(pl.multiple_of(nat[i] * x.shape[0], x.shape[0]), x.shape[0]), :]
        o_up = o_up + tn(halves(part, 1), x[...])
    shared[3 * rank :, :] = joined(o_up, 0)


def gn_body(n_pieces, offsets, nat, g_q, g_kv, low_back, downs, *rest):
    pieces = rest[:n_pieces]
    part0, part1, held, sems = rest[n_pieces:]
    step = pl.program_id(0)

    @pl.when(step == 0)
    def _():
        load_pieces(pieces, offsets, held, sems)

    q_width = g_q.shape[1]
    total = nt(g_q[...], held[:, :q_width]) + nt(g_kv[...], held[:, q_width:])
    store_at(step, total + nn(low_back[...], downs[...]), (part0, part1))


def place_body(nat, *refs):
    quarters, (out, held, sems) = refs[:4], refs[4:]
    step = pl.program_id(0)

    @pl.when(step == 0)
    def _():
        for copy in quarter_copies(quarters, held, sems):
            copy.start()

    out[...] = quarter_of(step, quarters, held, sems).astype(out.dtype)


def place(quarters, nat, dtype):
    rows, width = quarters[0].shape
    return pl.pallas_call(
        place_body,
        grid_spec=pltpu.PrefetchScalarGridSpec(
            num_scalar_prefetch=1,
            grid=(4,),
            in_specs=[ANY] * 4,
            out_specs=pl.BlockSpec((rows, width), lambda i, nat: (nat[i], 0)),
            scratch_shapes=[pltpu.VMEM((4, rows, width), bf16), pltpu.SemaphoreType.DMA((4,))],
        ),
        out_shape=jax.ShapeDtypeStruct((4 * rows, width), dtype),
        compiler_params=params(32),
        cost_estimate=SMALL,
        name="place",
    )(nat, *quarters)


def rms_factor(x):
    return lax.rsqrt(jnp.mean(x * x, axis=-1, keepdims=True) + epsilon)


def rms_back(x, gain, grads):
    factor = rms_factor(x)
    unit = x * factor
    scaled = grads * gain
    return factor * (scaled - unit * jnp.mean(unit * scaled, axis=-1, keepdims=True))


def block_diagonal(blocks):
    count, rows, cols = blocks.shape
    eye = jnp.eye(count, dtype=blocks.dtype)
    return (blocks[:, :, None, :] * eye[:, None, :, None]).reshape(count * rows, count * cols)


def diagonal_blocks(x, count):
    size = x.shape[0] // count
    return jnp.stack([x[i * size : (i + 1) * size, i * size : (i + 1) * size] for i in range(count)])


def per_device(
    tokens,
    sequence_lengths,
    output_cotangent,
    query_weight,
    key_weight,
    value_weight,
    output_weight,
    gate_weight,
    up_weight,
    down_weight,
    attention_norm_gain,
    feedforward_norm_gain,
    query_adapter_down,
    key_adapter_down,
    value_adapter_down,
    output_adapter_up,
    query_adapter_up,
    key_adapter_up,
    value_adapter_up,
    output_adapter_down,
    feature_map_query,
    feature_map_key,
):
    rows, model = tokens.shape
    heads, head, rank = query_adapter_up.shape
    kv_heads = key_adapter_up.shape[0]
    group = heads // kv_heads
    q_width, kv_width = heads * head, kv_heads * head
    seq, ring = lax.axis_size("seq"), lax.axis_size("dp") * lax.axis_size("seq")
    here = lax.axis_index("seq")
    chunks = rows // CHUNK
    ext = -(-(rows + WIN) // CHUNK) * CHUNK
    quarter = rows // 4

    core, far = lax.axis_index("tensor") % 2, lax.axis_index("tensor") // 2
    nat = jnp.stack([core * 2 + far, (1 - core) * 2 + far, core * 2 + 1 - far, (1 - core) * 2 + 1 - far]).astype(i32)
    own_rows = lambda x: lax.dynamic_slice_in_dim(x, nat[0] * quarter, quarter, 0)

    clock = Clock()
    beside_each_other = lambda *blocks: jnp.concatenate(blocks, axis=1)
    qkv_chain = Chain(clock, 0, beside_each_other, query_weight, key_weight, value_weight)
    qkv_chain.step()
    o_chain = Chain(clock, 0, jnp.transpose, output_weight)
    o_chain.step()
    offsets = qkv_chain.offsets
    n_pieces = offsets.shape[0]
    assert sum(map(sum, FFN_UNITS)) == gate_weight.shape[1]

    def ffn_chains(part):
        made = []
        at = sum(map(sum, FFN_UNITS[:part]))
        for units, way in zip(FFN_UNITS[part], (1, -1)):
            cols = slice(at, at + units)
            pack = lambda gate, up, down, cols=cols: jnp.concatenate([gate[:, cols], up[:, cols], down[cols].T], axis=1)
            made.append(Chain(clock, way, pack, gate_weight, up_weight, down_weight))
            at += units
        return made

    def turn(part):
        for chain in chains[part]:
            chain.settle()
        for chain in chains[part]:
            chain.step()

    def round_qkv_o():
        qkv_chain.step()
        o_chain.step()

    lengths = sequence_lengths[0]
    ends = jnp.cumsum(lengths)
    first_row = here * rows

    def docs_of(at):
        return jnp.where(at >= 0, jnp.sum((at[:, None] >= ends[None, :]).astype(i32), axis=1), -1)

    def angles_of(at):
        doc = docs_of(at)
        starts = ends - lengths
        start = jnp.sum(jnp.where(doc[:, None] == jnp.arange(lengths.shape[0])[None, :], starts[None, :], 0), axis=1)
        ladder = jnp.arange(head // 2).astype(f32)
        inverse = jnp.exp(ladder * (-2.0 * math.log(rope_base) / head))
        angles = inverse[:, None] * (at - start).astype(f32)[None, :]
        return jnp.cos(angles), jnp.sin(angles)

    q_at = first_row + jnp.arange(rows)
    k_index = jnp.arange(ext)
    k_at = first_row - WIN + k_index
    q_doc = docs_of(q_at)[None, :]
    k_doc = jnp.where(k_index < rows + WIN, docs_of(k_at), -2)
    doc_col, doc_row = k_doc[:, None], k_doc[None, :]
    last_docs = docs_of(first_row - WIN - 1 + CHUNK * jnp.arange(chunks + 1))
    block_docs = docs_of(rows * jnp.arange(seq + 1) - WIN - 1)
    passes = (block_docs[:-1] == block_docs[1:]).astype(f32)
    cos_q, sin_q = angles_of(q_at)
    cos_k, sin_k = angles_of(k_at)
    cos_q, sin_q, cos_k, sin_k = clock.wait(cos_q, sin_q, cos_k, sin_k)

    halo = shifted(tokens[rows - WIN :], "seq", 1)
    round_qkv_o()
    (halo,) = clock.wait(halo)
    spare = jnp.zeros((ext - rows - WIN, model), bf16)
    seen = jnp.concatenate([halo, tokens, spare], axis=0).astype(f32)
    gain_attn = attention_norm_gain.astype(f32)
    gain_mlp = feedforward_norm_gain.astype(f32)
    factor = clock.tie(rms_factor(seen))
    round_qkv_o()
    normed = clock.tie((seen * factor * gain_attn).astype(bf16))
    downs = jnp.concatenate([query_adapter_down, key_adapter_down, value_adapter_down], axis=1)
    low = clock.tie(nn(normed, downs))
    round_qkv_o()
    ups = jnp.zeros((q_width + 2 * kv_width, 3 * rank), bf16)
    ups = ups.at[:q_width, :rank].set(query_adapter_up.reshape(q_width, rank))
    ups = ups.at[q_width : q_width + kv_width, rank : 2 * rank].set(key_adapter_up.reshape(kv_width, rank))
    ups = ups.at[q_width + kv_width :, 2 * rank :].set(value_adapter_up.reshape(kv_width, rank))
    low_up = clock.tie(nt(halves_outside(low, 1), jnp.concatenate([ups, ups], axis=1)))
    round_qkv_o()
    maps_q = jnp.stack(
        [block_diagonal(feature_map_query[k * group : (k + 1) * group].transpose(0, 2, 1)) for k in range(kv_heads)]
    )
    maps_k = block_diagonal(feature_map_key.transpose(0, 2, 1))
    maps_q, maps_k = clock.wait(maps_q, maps_k)
    round_qkv_o()
    chains = [ffn_chains(0)]
    for chain in chains[0]:
        chain.settle()
    for _ in range(ring - 7):
        round_qkv_o()
    qkv_pieces = qkv_chain.pieces()
    turn(0)

    sems = pltpu.SemaphoreType.DMA((n_pieces,))
    qkv_width = q_width + 2 * kv_width
    held_qkv = pltpu.VMEM((model, qkv_width), bf16)
    held_o = pltpu.VMEM((model, q_width), bf16)

    dims = (rows, ext, q_width, kv_width, head, n_pieces, chunks)
    shapes = [
        ((q_width, rows), bf16),
        ((2 * q_width, rows), bf16),
        ((ext, kv_width), bf16),
        ((kv_width, ext), bf16),
        ((ext, kv_width), bf16),
        ((kv_heads * AUG, ext), bf16),
        ((ext, 2 * kv_width), bf16),
        ((2 * kv_width, ext), bf16),
        ((kv_heads, AUG, 2 * head), f32),
    ]
    prep_in = (normed, low_up, cos_q, sin_q, cos_k, sin_k, maps_q, maps_k, doc_row)
    q_t, phi_q, k_n, k_t, v_n, v_a, phi_kn, phi_kt, contrib = pl.pallas_call(
        lambda *refs: prep_body(dims, *refs),
        grid_spec=pltpu.PrefetchScalarGridSpec(
            num_scalar_prefetch=2,
            grid=(1,),
            in_specs=[whole(x.shape) for x in prep_in] + [ANY] * n_pieces,
            out_specs=[whole(s) for s, _ in shapes],
            scratch_shapes=[held_qkv, sems],
        ),
        out_shape=[jax.ShapeDtypeStruct(s, d) for s, d in shapes],
        compiler_params=params(56),
        cost_estimate=SMALL,
        name="prep",
    )(clock.tie(offsets), last_docs, *prep_in, *qkv_pieces)
    (contrib,) = clock.wait(contrib)
    turn(0)

    coming = clock.wait(*[shifted(contrib, "seq", by) for by in range(1, seq)])
    state_in = jnp.zeros_like(contrib)
    factor = jnp.ones((), f32)
    for by in range(1, seq):
        state_in = state_in + factor * coming[by - 1]
        factor = factor * passes[jnp.maximum(here - by, 0)]
    state_in = clock.tie(state_in)
    turn(0)

    column = lambda r: pl.BlockSpec((r, CHUNK), lambda c, *_: (0, c))
    att, att_t, totals, states = pl.pallas_call(
        lambda *refs: forward_body((kv_heads, group, head), *refs),
        grid_spec=pltpu.PrefetchScalarGridSpec(
            num_scalar_prefetch=1,
            grid=(chunks,),
            in_specs=[
                column(q_width),
                column(2 * q_width),
                whole(k_n.shape),
                whole(v_a.shape),
                whole(phi_kn.shape),
                whole(doc_col.shape),
                whole(doc_row.shape),
                column(1),
                whole(state_in.shape),
            ],
            out_specs=[
                pl.BlockSpec((CHUNK, q_width), lambda c, *_: (c, 0)),
                column(q_width),
                column(heads),
                pl.BlockSpec((1, kv_heads, 2 * head, AUG), lambda c, *_: (c, 0, 0, 0)),
            ],
            scratch_shapes=[pltpu.VMEM(state_in.shape, f32)],
        ),
        out_shape=[
            jax.ShapeDtypeStruct((rows, q_width), bf16),
            jax.ShapeDtypeStruct((q_width, rows), f32),
            jax.ShapeDtypeStruct((heads, rows), f32),
            jax.ShapeDtypeStruct((chunks, kv_heads, 2 * head, AUG), bf16),
        ],
        compiler_params=params(48),
        cost_estimate=SMALL,
        name="attend",
    )(last_docs, q_t, phi_q, k_n, v_a, phi_kn, doc_col, doc_row, q_doc, state_in)
    att = clock.tie(att)

    o_pieces = o_chain.pieces()
    o_down = output_adapter_down.reshape(q_width, rank)
    o_up_t = jnp.concatenate([output_adapter_up.T, output_adapter_up.T], axis=0)
    one_quarter = jax.ShapeDtypeStruct((quarter, model), bf16)

    def o_part(first, earlier):
        return pl.pallas_call(
            lambda *refs: o_body(n_pieces, *refs),
            grid_spec=pltpu.PrefetchScalarGridSpec(
                num_scalar_prefetch=2,
                grid=(2,),
                in_specs=[
                    pl.BlockSpec((quarter, q_width), lambda i, off, nat: (nat[first - i], 0)),
                    whole(o_down.shape),
                    whole(o_up_t.shape),
                ]
                + [ANY] * (n_pieces + len(earlier)),
                out_specs=[whole((quarter, model))] * 2
                + [pl.BlockSpec((quarter, rank), lambda i, off, nat: (nat[first - i], 0))],
                scratch_shapes=[held_o, sems],
            ),
            out_shape=[one_quarter, one_quarter, jax.ShapeDtypeStruct((rows, rank), f32)],
            input_output_aliases={5 + n_pieces: 2} if earlier else {},
            compiler_params=params(BIG),
            cost_estimate=SMALL,
            name="project",
        )(clock.tie(offsets), nat, att, o_down, o_up_t, *o_pieces, *earlier)

    o_far0, o_far1, lowered = o_part(3, ())
    (o_far0,) = clock.wait(o_far0)
    turn(0)
    beside = exchange(clock.tie(o_far0), "tensor", 1)
    o_near0, o_near1, lowered = o_part(1, (lowered,))
    (beside,) = clock.wait(beside)
    o_far = clock.tie((o_far1.astype(f32) + beside.astype(f32)).astype(bf16))
    across = exchange(o_far, "tensor", 2)
    (o_near0,) = clock.wait(o_near0)
    beside = exchange(o_near0, "tensor", 1)
    (beside,) = clock.wait(beside)
    chains.append(ffn_chains(1))
    turn(0)
    (across,) = clock.wait(across)
    hidden = own_rows(tokens).astype(f32) + (o_near1.astype(f32) + beside.astype(f32) + across.astype(f32))
    (hidden,) = clock.wait(hidden)
    normed_mlp = clock.tie((hidden * rms_factor(hidden) * gain_mlp).astype(bf16))
    across, beside = exchange(normed_mlp, "tensor", 2), exchange(normed_mlp, "tensor", 1)
    (beside,) = clock.wait(beside)
    turn(0)
    turn(0)
    (across,) = clock.wait(across)
    last = clock.tie(exchange(across, "tensor", 1))
    normed_mlp = [normed_mlp, beside, across, last]

    def ffn(part, quarters, sums):
        units, last = FFN_UNITS[part], part == len(FFN_UNITS) - 1
        lots = [chain.pieces() for chain in chains[part]]
        sizes = tuple(map(len, lots))
        pieces = [piece for lot in lots for piece in lot]
        ring_offsets = jnp.concatenate([chain.offsets for chain in chains[part]])
        first = quarters[0]
        summed = jax.ShapeDtypeStruct((2, quarter, model), f32)
        return pl.pallas_call(
            lambda *refs: ffn_body(sizes, units, bool(sums), last, *refs),
            grid_spec=pltpu.PrefetchScalarGridSpec(
                num_scalar_prefetch=2,
                grid=(2,),
                in_specs=[pl.BlockSpec((quarter, model), lambda i, off, nat: (nat[first - i], 0))]
                + [ANY] * (2 + len(pieces) + len(sums)),
                out_specs=[ANY] * (4 if last else 2),
                scratch_shapes=[
                    pltpu.VMEM((2, quarter, model), bf16),
                    pltpu.SemaphoreType.DMA((2,)),
                    pltpu.VMEM((3, model, sum(units)), bf16),
                    pltpu.SemaphoreType.DMA((3, len(pieces))),
                    pltpu.VMEM((2, 2, quarter, model), bf16 if last else f32),
                    pltpu.SemaphoreType.DMA((2, 2)),
                ]
                + [pltpu.VMEM((2, 2, quarter, model), f32), pltpu.SemaphoreType.DMA((2, 2))] * bool(sums),
            ),
            out_shape=[one_quarter] * 4 if last else [summed] * 2,
            compiler_params=params(BIG),
            cost_estimate=SMALL,
            name="feed_forward",
        )(clock.tie(ring_offsets), nat, output_cotangent, *[normed_mlp[q] for q in quarters], *pieces, *sums)

    for chain in chains[0]:
        chain.settle()
    turn(1)
    sums_far = clock.wait(*ffn(0, (3, 2), ()))
    turn(1)
    sums_near = clock.wait(*ffn(0, (1, 0), ()))
    for _ in range(ring - 3):
        turn(1)
    gn_far0, gn_far1, mlp_far0, mlp_far1 = ffn(1, (3, 2), sums_far)
    gn_far0, mlp_far0 = clock.wait(gn_far0, mlp_far0)
    beside = exchange(gn_far0, "tensor", 1)
    mlp_beside_far = exchange(mlp_far0, "tensor", 1)
    (beside,) = clock.wait(beside)
    across = exchange(clock.tie((gn_far1.astype(f32) + beside.astype(f32)).astype(bf16)), "tensor", 2)
    gn_near0, gn_near1, mlp_near0, mlp_near1 = ffn(1, (1, 0), sums_near)
    gn_near0, mlp_near0 = clock.wait(gn_near0, mlp_near0)
    (mlp_beside_far,) = clock.wait(mlp_beside_far)
    mlp_far = clock.tie((mlp_far1.astype(f32) + mlp_beside_far.astype(f32)).astype(bf16))
    across, gn_near0 = clock.wait(across, gn_near0)
    beside = exchange(gn_near0, "tensor", 1)
    (beside,) = clock.wait(beside)
    grad_normed_mlp = gn_near1.astype(f32) + beside.astype(f32) + across.astype(f32)
    grad_hidden = own_rows(output_cotangent).astype(f32) + rms_back(hidden, gain_mlp, grad_normed_mlp)
    grad_hidden = clock.tie(grad_hidden)
    branch = clock.tie(grad_hidden.astype(bf16))
    across, beside = exchange(branch, "tensor", 2), exchange(branch, "tensor", 1)
    mlp_beside = exchange(clock.tie(mlp_near0), "tensor", 1)
    (beside,) = clock.wait(beside)

    o_down_t = jnp.concatenate([o_down.T, o_down.T], axis=0)
    sizes = [((q_width, rows), bf16), ((heads, rows), f32), ((rows, rank), f32), ((kv_heads, 2 * head, AUG), f32)]

    def go_part(first, quarters, earlier):
        by_quarter = lambda r: pl.BlockSpec((r, quarter), lambda i, off, nat, before: (0, nat[first + i]))
        late = bool(earlier)
        return pl.pallas_call(
            lambda *refs: go_body((n_pieces, kv_heads, group, head, late), *refs),
            grid_spec=pltpu.PrefetchScalarGridSpec(
                num_scalar_prefetch=3,
                grid=(2,),
                in_specs=[
                    whole((model, rank)),
                    whole(o_down_t.shape),
                    by_quarter(q_width),
                    by_quarter(heads),
                    by_quarter(2 * q_width),
                    by_quarter(1),
                ]
                + [ANY] * (2 + n_pieces)
                + ([ANY] * 3 + [whole(sizes[3][0])]) * late,
                out_specs=[
                    by_quarter(q_width),
                    by_quarter(heads),
                    pl.BlockSpec((quarter, rank), lambda i, off, nat, before: (nat[first + i], 0)),
                    whole(sizes[3][0]),
                ],
                scratch_shapes=[
                    pltpu.VMEM((2, quarter, model), bf16),
                    pltpu.SemaphoreType.DMA((2,)),
                    held_o,
                    sems,
                ],
            ),
            out_shape=[jax.ShapeDtypeStruct(s, d) for s, d in sizes],
            input_output_aliases={11 + n_pieces + i: i for i in range(3)} if late else {},
            compiler_params=params(BIG),
            cost_estimate=SMALL,
            name="project_back",
        )(
            clock.tie(offsets), nat, last_docs[:1], output_adapter_up, o_down_t, att_t, totals, phi_q, q_doc,
            *quarters, *o_pieces, *earlier,
        )

    near = clock.wait(*go_part(0, (branch, beside), ()))
    (mlp_beside,) = clock.wait(mlp_beside)
    mlp_near = clock.tie(hidden + (mlp_near1.astype(f32) + mlp_beside.astype(f32)))
    (across,) = clock.wait(across)
    last = clock.tie(exchange(across, "tensor", 1))
    mlp_across = exchange(clock.tie(mlp_far), "tensor", 2)
    branch = [branch, beside, across, last]
    numer, grad_totals, up_product, dstate = clock.wait(*go_part(2, branch[2:], near))

    coming = [shifted(dstate, "seq", -by) for by in range(1, seq)]

    back_column = lambda r: pl.BlockSpec((r, CHUNK), lambda c, *_: (0, chunks - 1 - c))
    back_in = (
        (q_t, back_column(q_width)),
        (phi_q, back_column(2 * q_width)),
        (numer, back_column(q_width)),
        (grad_totals, back_column(heads)),
        (k_n, None),
        (k_t, None),
        (v_n, None),
        (v_a, None),
        (phi_kn, None),
        (phi_kt, None),
        (doc_col, None),
        (doc_row, None),
        (q_doc, back_column(1)),
        (states, pl.BlockSpec((1, kv_heads, 2 * head, AUG), lambda c, *_: (chunks - 1 - c, 0, 0, 0))),
        (cos_q, back_column(head // 2)),
        (sin_q, back_column(head // 2)),
        (maps_q, None),
    )
    g_q, g_kt, g_vt, g_phi, g_map_q = pl.pallas_call(
        lambda *refs: backward_body((kv_heads, group, head, chunks), *refs),
        grid_spec=pltpu.PrefetchScalarGridSpec(
            num_scalar_prefetch=1,
            grid=(chunks,),
            in_specs=[whole(x.shape) if spec is None else spec for x, spec in back_in],
            out_specs=[
                pl.BlockSpec((CHUNK, q_width), lambda c, *_: (chunks - 1 - c, 0)),
                whole((kv_width, ext)),
                whole((kv_width, ext)),
                whole((2 * kv_width, ext)),
                whole((kv_heads, group * head, group * head)),
            ],
            scratch_shapes=[pltpu.VMEM(dstate.shape, f32)],
        ),
        out_shape=[
            jax.ShapeDtypeStruct((rows, q_width), bf16),
            jax.ShapeDtypeStruct((kv_width, ext), f32),
            jax.ShapeDtypeStruct((kv_width, ext), f32),
            jax.ShapeDtypeStruct((2 * kv_width, ext), f32),
            jax.ShapeDtypeStruct((kv_heads, group * head, group * head), f32),
        ],
        compiler_params=params(52),
        cost_estimate=SMALL,
        name="attend_back",
    )(clock.tie(last_docs), *[x for x, _ in back_in])

    g_q, g_kt, g_vt, g_phi, g_map_q = clock.wait(g_q, g_kt, g_vt, g_phi, g_map_q)
    (mlp_across,) = clock.wait(mlp_across)
    out_rows = clock.tie((mlp_near + mlp_across.astype(f32)).astype(bf16))
    out_across, out_beside = exchange(out_rows, "tensor", 2), exchange(out_rows, "tensor", 1)
    coming = clock.wait(*coming)
    factors = [jnp.ones((), f32)]
    for by in range(1, seq - 1):
        factors.append(factors[-1] * passes[jnp.minimum(here + by, seq - 1)])
    g_own, g_halo, g_map_k = pl.pallas_call(
        lambda *refs: keys_back_body((kv_heads, head, chunks, rows), *refs),
        grid_spec=pltpu.PrefetchScalarGridSpec(
            num_scalar_prefetch=2,
            grid=(1,),
            in_specs=[whole(x.shape) for x in (g_kt, g_vt, g_phi, v_a, phi_kt, k_t, doc_row, maps_k, *coming)],
            out_specs=[whole((2 * kv_width, rows)), whole((2 * kv_width, CHUNK)), whole((kv_width, kv_width))],
        ),
        out_shape=[
            jax.ShapeDtypeStruct((2 * kv_width, rows), f32),
            jax.ShapeDtypeStruct((2 * kv_width, CHUNK), f32),
            jax.ShapeDtypeStruct((kv_width, kv_width), f32),
        ],
        compiler_params=params(BIG),
        cost_estimate=SMALL,
        name="keys_back",
    )(clock.tie(last_docs), jnp.stack(factors), g_kt, g_vt, g_phi, v_a, phi_kt, k_t, doc_row, maps_k, *coming)

    g_own, g_halo, g_map_k = clock.wait(g_own, g_halo, g_map_k)
    g_halo = shifted(g_halo, "seq", -1)
    (g_halo,) = clock.wait(g_halo)

    downs_t = jnp.concatenate([downs.T, downs.T], axis=0)

    adapters_in = (g_q, g_own, g_halo, cos_q, sin_q, ups, low[WIN : WIN + rows], normed, lowered, att, up_product, g_map_q, g_map_k, *branch)
    sizes = [
        ((rows, 2 * kv_width), bf16),
        ((rows, 6 * rank), bf16),
        ((heads + kv_heads, head, 2 * head), f32),
        ((4 * rank, model), f32),
    ]
    g_kv, low_back, by_head, shared = pl.pallas_call(
        lambda *refs: adapters_body((rows, WIN, head, rank), *refs),
        grid_spec=pltpu.PrefetchScalarGridSpec(
            num_scalar_prefetch=1,
            grid=(1,),
            in_specs=[whole(x.shape) for x in adapters_in],
            out_specs=[whole(x) for x, _ in sizes],
        ),
        out_shape=[jax.ShapeDtypeStruct(x, d) for x, d in sizes],
        compiler_params=params(BIG),
        cost_estimate=SMALL,
        name="adapters",
    )(clock.tie(nat), *adapters_in)
    g_kv, low_back, by_head, shared = clock.wait(g_kv, low_back, by_head, shared)
    out_across, out_beside = clock.wait(out_across, out_beside)

    def gn_part(first):
        by_rows = lambda w: pl.BlockSpec((quarter, w), lambda i, off, nat: (nat[first - i], 0))
        return pl.pallas_call(
            lambda *refs: gn_body(n_pieces, *refs),
            grid_spec=pltpu.PrefetchScalarGridSpec(
                num_scalar_prefetch=2,
                grid=(2,),
                in_specs=[by_rows(q_width), by_rows(2 * kv_width), by_rows(6 * rank), whole(downs_t.shape)]
                + [ANY] * n_pieces,
                out_specs=[whole((quarter, model))] * 2,
                scratch_shapes=[held_qkv, sems],
            ),
            out_shape=[one_quarter, one_quarter],
            compiler_params=params(BIG),
            cost_estimate=SMALL,
            name="norm_back",
        )(clock.tie(offsets), nat, g_q, g_kv, low_back, downs_t, *qkv_pieces)

    gn_far0, gn_far1 = gn_part(3)
    (gn_far0,) = clock.wait(gn_far0)
    beside = exchange(gn_far0, "tensor", 1)

    by_head = by_head.reshape(heads + kv_heads, ring, head // ring, 2 * head).transpose(1, 0, 2, 3)
    shared = shared.reshape(4 * rank, ring, model // ring).transpose(1, 0, 2)
    by_head, shared = clock.wait(by_head, shared)

    def halved(x, axis, half, bit, over=0):
        x = x.reshape(x.shape[:over] + (2, half) + x.shape[over + 1 :])
        send = lax.dynamic_index_in_dim(x, 1 - bit, over, keepdims=False)
        return lax.dynamic_index_in_dim(x, bit, over, keepdims=False), exchange(send, axis, half)

    def summed_over(axis, size, xs):
        while size > 1:
            half = size // 2
            both = [halved(x, axis, half, (lax.axis_index(axis) // half) % 2) for x in xs]
            coming = clock.wait(*[coming for _, coming in both])
            xs = [kept + x for (kept, _), x in zip(both, coming)]
            size = half
            yield xs

    (beside,) = clock.wait(beside)
    gn_far = clock.tie((gn_far1.astype(f32) + beside.astype(f32)).astype(bf16))
    across = exchange(gn_far, "tensor", 2)
    parts = [by_head, shared]
    dp = ring // seq
    parts = [x.reshape((dp, seq) + x.shape[1:]) for x in parts]
    for parts in summed_over("dp", dp, parts):
        pass
    along_seq = summed_over("seq", seq, [x[0] for x in parts])
    parts = next(along_seq)
    gn_near0, gn_near1 = gn_part(1)
    gn_near0, gn_near1 = clock.wait(gn_near0, gn_near1)
    across, gn_near0 = clock.wait(across, gn_near0)
    beside = exchange(gn_near0, "tensor", 1)
    (beside,) = clock.wait(beside)
    grad_normed = gn_near1.astype(f32) + beside.astype(f32) + across.astype(f32)
    grad_rows = grad_hidden + rms_back(own_rows(tokens).astype(f32), gain_attn, grad_normed)
    grad_rows = clock.tie(grad_rows.astype(bf16))
    across, beside = exchange(grad_rows, "tensor", 2), exchange(grad_rows, "tensor", 1)
    out_last = clock.tie(exchange(out_across, "tensor", 1))
    for parts in along_seq:
        pass
    by_head, shared = [x[0] for x in parts]
    shared = shared.reshape(4 * rank, 2, 2, model // ring // 4)
    kept, sent = halved(shared.reshape(4 * rank, 4, -1), "tensor", 2, far, 1)
    shared = kept.reshape(4 * rank, 2, -1)
    sent = sent.reshape(4 * rank, 2, -1)
    block_out = clock.tie(place([out_rows, out_beside, out_across, out_last], nat, bf16))
    beside, across, sent = clock.wait(beside, across, sent)
    last = exchange(across, "tensor", 1)
    kept, sent = halved(shared + sent, "tensor", 1, core, 1)
    last, sent = clock.wait(last, sent)
    shared = (kept + sent).reshape(4 * rank, -1).T
    grad_tokens = clock.tie(place([grad_rows, beside, across, last], nat, f32))
    of_q, of_kv = by_head[:heads], by_head[heads:]
    first, second = slice(head, head + rank), slice(head + rank, head + 2 * rank)
    out = [of_q[..., first], of_kv[..., first], of_kv[..., second], of_q[..., second], of_q[..., :head], of_kv[..., :head]]
    return (
        block_out,
        grad_tokens,
        shared[:, :rank] + clock.now.astype(f32),
        shared[:, rank : 2 * rank],
        shared[:, 2 * rank : 3 * rank],
        shared[:, 3 * rank :],
        *out,
    )


def solution(mesh):
    return jax.shard_map(
        per_device,
        mesh=mesh,
        in_specs=(
            P(("dp", "seq"), None),
            P("dp", None),
            P(("dp", "seq"), None),
            P(("dp", "seq"), "tensor"),
            P(("dp", "seq"), "tensor"),
            P(("dp", "seq"), "tensor"),
            P("tensor", ("dp", "seq")),
            P(("dp", "seq"), "tensor"),
            P(("dp", "seq"), "tensor"),
            P("tensor", ("dp", "seq")),
            P(),
            P(),
            P(),
            P(),
            P(),
            P(),
            P("tensor", None, None),
            P("tensor", None, None),
            P("tensor", None, None),
            P("tensor", None, None),
            P("tensor", None, None),
            P("tensor", None, None),
        ),
        out_specs=(
            P(("dp", "seq"), None),
            P(("dp", "seq"), None),
            P(("dp", "seq", "tensor"), None),
            P(("dp", "seq", "tensor"), None),
            P(("dp", "seq", "tensor"), None),
            P(("dp", "seq", "tensor"), None),
            P("tensor", ("dp", "seq"), None),
            P("tensor", ("dp", "seq"), None),
            P("tensor", ("dp", "seq"), None),
            P("tensor", ("dp", "seq"), None),
            P("tensor", ("dp", "seq"), None),
            P("tensor", ("dp", "seq"), None),
        ),
        check_vma=False,
    )
```

```python
import math

import jax
import jax.numpy as jnp
from jax import lax
from jax.experimental import pallas as pl
from jax.experimental.pallas import tpu as pltpu
from jax.sharding import PartitionSpec as P

WIN = 64
CHUNK = 128
AUG = 80
RING = 8
FFN_UNITS = ((512, 512), (512, 512))
BIG = 60

epsilon = 1e-05
rope_base = 500000.0
bf16, f32, i32 = jnp.bfloat16, jnp.float32, jnp.int32
MIB = 1 << 20


def nn(a, b):
    return lax.dot_general(a, b, (((1,), (0,)), ((), ())), preferred_element_type=f32)


def nt(a, b):
    return lax.dot_general(a, b, (((1,), (1,)), ((), ())), preferred_element_type=f32)


def tn(a, b):
    return lax.dot_general(a, b, (((0,), (0,)), ((), ())), preferred_element_type=f32)


def halves(x, axis):
    high = x.astype(bf16)
    return jnp.concatenate([high, (x - high.astype(f32)).astype(bf16)], axis=axis)


def exchange(x, axis, bit):
    count = lax.axis_size(axis)
    return lax.ppermute(x, axis, [(i, i ^ bit) for i in range(count)])


def shifted(x, axis, by):
    count = lax.axis_size(axis)
    return lax.ppermute(x, axis, [(i, i + by) for i in range(count) if 0 <= i + by < count])


def place_of(index, seq):
    row, col = index // seq, index % seq
    return row * seq + (col if row % 2 == 0 else seq - 1 - col)


def place_of_traced(index, seq):
    row, col = index // seq, index % seq
    return row * seq + jnp.where(row % 2 == 0, col, seq - 1 - col)


class Clock:
    def __init__(self):
        self.now = jnp.zeros((), i32)

    def wait(self, *arrays):
        *out, self.now = lax.optimization_barrier((*arrays, self.now))
        return out

    def tie(self, x):
        return self.wait(x)[0]


class Chain:
    def __init__(self, clock, way, pack, *blocks):
        block = pack(*clock.wait(*blocks))
        dp, seq = lax.axis_size("dp"), lax.axis_size("seq")
        self.clock, self.count = clock, dp * seq
        self.ringed = self.count <= RING
        rows = block.shape[0]
        if not self.ringed:
            self.lanes = [[lax.all_gather(block, ("dp", "seq"), axis=0, tiled=True)]]
            self.offsets = jnp.zeros((1,), i32)
            return
        order = [place_of(i, seq) for i in range(self.count)]
        up = [(order[i], order[(i + 1) % self.count]) for i in range(self.count)]
        down = [(j, i) for i, j in up]
        place = place_of_traced(lax.axis_index("dp") * seq + lax.axis_index("seq"), seq)
        steps = jnp.arange(self.count)
        came_up = place_of_traced((place - steps) % self.count, seq) * rows
        came_down = place_of_traced((place + steps) % self.count, seq) * rows
        if way:
            self.lanes, self.ways = [[block]], [up if way > 0 else down]
            self.offsets = (came_up if way > 0 else came_down).astype(i32)
        else:
            half = rows // 2
            self.lanes, self.ways = [[block[:half]], [block[half:]]], [up, down]
            self.offsets = jnp.concatenate([came_up, came_down + half]).astype(i32)

    def settle(self):
        if self.ringed:
            came = self.clock.wait(*[lane[-1] for lane in self.lanes])
            for lane, x in zip(self.lanes, came):
                lane[-1] = x

    def step(self):
        if self.ringed:
            self.settle()
            for lane, way in zip(self.lanes, self.ways):
                lane.append(lax.ppermute(lane[-1], ("dp", "seq"), way))

    def pieces(self):
        self.settle()
        return [piece for lane in self.lanes for piece in lane]


def load_pieces(pieces, offsets, held, sems, first=0):
    copies = [
        pltpu.make_async_copy(
            piece.at[:, pl.ds(first, held.shape[1])],
            held.at[pl.ds(pl.multiple_of(offsets[i], 16), piece.shape[0])],
            sems.at[i],
        )
        for i, piece in enumerate(pieces)
    ]
    for copy in copies:
        copy.start()
    for copy in copies:
        copy.wait()


def params(limit):
    return pltpu.CompilerParams(vmem_limit_bytes=limit * MIB)


SMALL = pl.CostEstimate(flops=1, bytes_accessed=1, transcendentals=0)


ANY = pl.BlockSpec(memory_space=pl.ANY)


def whole(shape):
    return pl.BlockSpec(shape, lambda *_: (0,) * len(shape))


def rope(x, cos, sin):
    width = 2 * cos.shape[0]
    half = width // 2
    out = []
    for at in range(0, x.shape[0], width):
        x1, x2 = x[at : at + half], x[at + half : at + width]
        out += [x1 * cos - x2 * sin, x2 * cos + x1 * sin]
    return jnp.concatenate(out, axis=0)


def hedgehog(a, width):
    out = []
    for at in range(0, a.shape[0], width):
        one = a[at : at + width]
        for e in (
            jnp.exp(one - jnp.max(one, axis=0, keepdims=True)),
            jnp.exp(jnp.min(one, axis=0, keepdims=True) - one),
        ):
            out.append(e * (1.0 / jnp.sum(e, axis=0, keepdims=True)))
    return jnp.concatenate(out, axis=0).astype(bf16)


def hedgehog_back(phi, grad, width):
    out = []
    for at in range(0, phi.shape[0], 2 * width):
        p1, p2 = phi[at : at + width].astype(f32), phi[at + width : at + 2 * width].astype(f32)
        d1, d2 = grad[at : at + width], grad[at + width : at + 2 * width]
        out.append(
            p1 * (d1 - jnp.sum(p1 * d1, axis=0, keepdims=True))
            - p2 * (d2 - jnp.sum(p2 * d2, axis=0, keepdims=True))
        )
    return jnp.concatenate(out, axis=0).astype(bf16)


def norm_body(tokens, halo, gain, downs, normed, low, held, sems):
    rows, window = tokens.shape[0], halo.shape[0]
    part = rows // 4

    def copy(i):
        return pltpu.make_async_copy(
            tokens.at[pl.ds(i * part, part)], held.at[pl.ds(window + i * part, part)], sems.at[i]
        )

    for i in range(4):
        copy(i).start()
    held[:window, :] = halo[...]
    held[window + rows :, :] = jnp.zeros((held.shape[0] - window - rows, held.shape[1]), bf16)
    for i in range(4):
        copy(i).wait()
        first = window + i * part if i else 0
        last = window + (i + 1) * part if i < 3 else held.shape[0]
        x = held[first:last, :].astype(f32)
        out = (x * rms_factor(x) * gain[...]).astype(bf16)
        normed[first:last, :] = out
        low[first:last, :] = nn(out, downs[...])


def pack_body(units, gate, up, down, q_up, k_up, v_up, map_q, map_k, *outs):
    packed, (ups, twice, maps_q, maps_k) = outs[:-4], outs[-4:]
    at = 0
    for size, out in zip(units, packed):
        out[:, :size] = gate[:, at : at + size]
        out[:, size : 2 * size] = up[:, at : at + size]
        out[:, 2 * size :] = down[at : at + size, :].T
        at += size
    head, rank = q_up.shape[1:]
    at = 0
    for i, x in enumerate((q_up, k_up, v_up)):
        for h in range(x.shape[0]):
            row = jnp.concatenate(
                [jnp.zeros((head, rank), bf16)] * i + [x[h]] + [jnp.zeros((head, rank), bf16)] * (2 - i), axis=1
            )
            ups[at : at + head, :] = row
            twice[at : at + head, :] = jnp.concatenate([row, row], axis=1)
            at += head
    maps_q[...] = jnp.zeros(maps_q.shape, bf16)
    maps_k[...] = jnp.zeros(maps_k.shape, bf16)
    group = map_q.shape[0] // maps_q.shape[0]
    for h in range(map_q.shape[0]):
        mine = slice(h % group * head, (h % group + 1) * head)
        maps_q[h // group, mine, mine] = map_q[h].astype(f32).T.astype(bf16)
    for h in range(map_k.shape[0]):
        mine = slice(h * head, (h + 1) * head)
        maps_k[mine, mine] = map_k[h].astype(f32).T.astype(bf16)


def prep_body(dims, offsets, last_docs, nx, low, ups, cos_q, sin_q, cos_k, sin_k, map_q, map_k, doc_row, *rest):
    tokens, ext, q_width, kv_width, head, n_pieces, chunks = dims
    pieces, rest = rest[:n_pieces], rest[n_pieces:]
    q_t, phi_q, k_n, k_t, v_n, v_a, phi_kn, phi_kt, contrib, held, sems = rest
    load_pieces(pieces, offsets, held, sems)
    kv_heads = kv_width // head
    step = ext // 3
    v_a[...] = jnp.zeros(v_a.shape, bf16)
    for at in range(0, ext, step):
        rows = pl.ds(at, step)
        raw = nn(nx[rows, :], held[:, q_width:]) + nt(halves(low[rows, :], 1), ups[q_width:, :])
        v = raw[:, kv_width:].astype(bf16)
        v_n[rows, :] = v
        v_tr = raw[:, kv_width:].T.astype(bf16)
        for k in range(kv_heads):
            v_a[k * AUG : k * AUG + head, rows] = v_tr[k * head : (k + 1) * head]
            v_a[k * AUG + head : (k + 1) * AUG, rows] = (
                lax.broadcasted_iota(i32, (AUG - head, step), 0) < 2
            ).astype(f32).astype(bf16)
        k_rot = rope(raw[:, :kv_width].T, cos_k[:, rows], sin_k[:, rows])
        k_bf = k_rot.astype(bf16)
        k_t[:, rows] = k_bf
        k_n[rows, :] = k_rot.T.astype(bf16)
        phi = hedgehog(nn(map_k[...], k_bf), head)
        phi_kt[:, rows] = phi
        phi_kn[rows, :] = phi.astype(f32).T.astype(bf16)
    incl = (doc_row[:, :tokens] == last_docs[chunks]).astype(f32).astype(bf16)
    for k in range(kv_heads):
        masked = v_a[k * AUG : (k + 1) * AUG, :tokens] * incl
        contrib[k] = nn(masked, phi_kn[:tokens, k * 2 * head : (k + 1) * 2 * head])
    step = tokens // 2
    group = q_width // kv_heads
    for at in range(0, tokens, step):
        rows = pl.ds(at, step)
        raw = nn(nx[pl.ds(WIN + at, step), :], held[:, :q_width])
        raw = raw + nt(halves(low[pl.ds(WIN + at, step), :], 1), ups[:q_width, :])
        q_bf = rope(raw.T, cos_q[:, rows], sin_q[:, rows]).astype(bf16)
        q_t[:, rows] = q_bf
        for k in range(kv_heads):
            logits = nn(map_q[k], q_bf[k * group : (k + 1) * group])
            phi_q[2 * k * group : 2 * (k + 1) * group, rows] = hedgehog(logits, head)


def masks(q_doc, k_doc, heads):
    keys = CHUNK + WIN
    j = lax.broadcasted_iota(i32, (keys, CHUNK), 0)
    t = lax.broadcasted_iota(i32, (keys, CHUNK), 1)
    same = k_doc == q_doc
    win = same & (j > t) & (j <= t + WIN)
    lin = (same & (j <= t))[:CHUNK]
    win_f = jnp.concatenate([win.astype(f32)] * heads, axis=1)
    lin_f = jnp.concatenate([lin.astype(f32)] * heads, axis=1)
    return win_f > 0.5, lin_f > 0.5


def side(ref, first, count, size):
    return jnp.concatenate([ref[first + g * size : first + (g + 1) * size, :] for g in range(count)], axis=1)


def window_weights(q, phi_q, k_win, phi_k, win, lin, scale):
    scores = nn(k_win, q)
    weights_win = jnp.where(win, jnp.exp(scores * scale), 0.0)
    linear = jnp.where(lin, nn(phi_k, phi_q), 0.0)
    return weights_win, jnp.concatenate([weights_win[:CHUNK] + linear, weights_win[CHUNK:]], axis=0)


def forward_body(dims, last_docs, factors, q_t, phi_q, k_n, v_a, phi_kn, doc_col, doc_row, q_doc, *rest):
    kv_heads, group, head = dims
    earlier, (att, att_t, totals, states, state) = rest[:-5], rest[-5:]
    chunk = pl.program_id(0)
    start = pl.multiple_of(chunk * CHUNK, CHUNK)

    @pl.when(chunk == 0)
    def _():
        total = jnp.zeros(state.shape, f32)
        for i, x in enumerate(earlier):
            total = total + factors[i] * x[...]
        state[...] = total

    keys = CHUNK + WIN
    win, lin = masks(q_doc[...], doc_col[pl.ds(start, keys), :], group)
    use = (q_doc[...] == last_docs[chunk]).astype(f32)
    use = jnp.concatenate([use] * group, axis=1)
    incl = (doc_row[:, pl.ds(start, CHUNK)] == last_docs[chunk + 1]).astype(f32).astype(bf16)
    passing = (last_docs[chunk] == last_docs[chunk + 1]).astype(f32)
    scale = head**-0.5
    out = []
    for k in range(kv_heads):
        q = side(q_t, k * group * head, group, head)
        phi = side(phi_q, 2 * k * group * head, group, 2 * head)
        k_win = k_n[pl.ds(start, keys), k * head : (k + 1) * head]
        phi_k = phi_kn[pl.ds(start, CHUNK), 2 * k * head : 2 * (k + 1) * head]
        v_win = v_a[k * AUG : (k + 1) * AUG, pl.ds(start, 2 * CHUNK)]
        _, weights = window_weights(q, phi, k_win, phi_k, win, lin, scale)
        before = state[k]
        from_state = nn(before.astype(bf16), phi) * use
        total = jnp.sum(weights, axis=0, keepdims=True) + from_state[head : head + 1]
        numer = nn(v_win[:, :keys], weights.astype(bf16))[:head] + from_state[:head]
        attended = numer * (1.0 / total)
        for g in range(group):
            out.append(attended[:, g * CHUNK : (g + 1) * CHUNK])
            totals[k * group + g : k * group + g + 1, :] = total[:, g * CHUNK : (g + 1) * CHUNK]
        states[0, k] = before.T.astype(bf16)
        state[k] = nn(v_win[:, :CHUNK] * incl, phi_k) + passing * before
    attended = jnp.concatenate(out, axis=0)
    att_t[...] = attended
    att[...] = attended.T.astype(bf16)


def store_at(step, value, outs):
    for i, out in enumerate(outs):

        @pl.when(step == i)
        def _(out=out):
            out[...] = value.astype(out.dtype)


def o_body(n_pieces, first, offsets, nat, att, down, up, *rest):
    pieces, parts, (lowered, held, sems) = rest[:n_pieces], rest[n_pieces:-3], rest[-3:]
    step = pl.program_id(0)

    @pl.when(step == 0)
    def _():
        load_pieces(pieces, offsets, held, sems, first)

    low = nn(att[...], down[...])
    lowered[...] = low
    store_at(step, nt(att[...], held[...]) + nn(halves(low, 1), up[...]), parts)


def quarter_copies(quarters, held, sems, first=0):
    return [pltpu.make_async_copy(x, held.at[first + i], sems.at[first + i]) for i, x in enumerate(quarters)]


def quarter_of(step, quarters, held, sems):
    for i, copy in enumerate(quarter_copies(quarters, held, sems)):

        @pl.when(step == i)
        def _(copy=copy):
            copy.wait()

    return held[step]


def ffn_body(lots, units, summed, last, offsets, nat, cot, *rest):
    count, n_out = sum(lots), 4 if last else 2
    quarters, pieces, rest = rest[:2], rest[2 : 2 + count], rest[2 + count :]
    sums, outs, rest = rest[: 2 * summed], rest[2 * summed : 2 * summed + n_out], rest[2 * summed + n_out :]
    rows, rows_sems, held, sems, out_held, out_sems, *rest = rest
    step = pl.program_id(0)

    def at_first(act):
        pl.when(step == 0)(act)

    def copies(which):
        made, at, i = [], 0, 0
        for lot, size in zip(lots, units):
            for _ in range(lot):
                made.append(
                    pltpu.make_async_copy(
                        pieces[i].at[:, pl.ds(which * size, size)],
                        held.at[which, pl.ds(pl.multiple_of(offsets[i], 16), pieces[i].shape[0]), pl.ds(at, size)],
                        sems.at[which, i],
                    )
                )
                i += 1
            at += size
        return made

    def sum_copy(i, kind):
        return pltpu.make_async_copy(sums[kind].at[i], rest[0].at[i, kind], rest[1].at[i, kind])

    def out_copy(i, kind):
        out = outs[2 * (1 - kind) + i] if last else outs[kind].at[i]
        return pltpu.make_async_copy(out_held.at[i, kind], out, out_sems.at[i, kind])

    @at_first
    def _():
        first = copies(0)
        for copy in quarter_copies(quarters[:1], rows, rows_sems) + first:
            copy.start()
        for copy in quarter_copies(quarters[1:], rows, rows_sems, 1):
            copy.start()
        for copy in first:
            copy.wait()
        for copy in copies(1):
            copy.start()

    n2 = quarter_of(step, quarters, rows, rows_sems)
    gate = nn(n2, held[0])

    @at_first
    def _():
        for copy in copies(1):
            copy.wait()
        for copy in copies(2):
            copy.start()

    up = nn(n2, held[1])

    @at_first
    def _():
        for copy in copies(2):
            copy.wait()
        for i in range(2 if summed else 0):
            for kind in (1, 0):
                sum_copy(i, kind).start()

    grad_act = nn(cot[...], held[2])
    s = 1.0 / (1.0 + jnp.exp(-gate))
    silu = gate * s
    act = (silu * up).astype(bf16)
    grad_gate = (grad_act * up * s * (1.0 + gate * (1.0 - s))).astype(bf16)
    grad_up = (grad_act * silu).astype(bf16)

    def finish(kind, total):
        if summed:
            sum_copy(step, kind).wait()
            total = total + rest[0][step, kind]
        out_held[step, kind] = total.astype(out_held.dtype)
        for i in range(2):

            @pl.when(step == i)
            def _(i=i):
                out_copy(i, kind).start()

    finish(1, nt(grad_gate, held[0]) + nt(grad_up, held[1]))
    finish(0, nt(act, held[2]))

    @pl.when(step == 1)
    def _():
        for i in range(2):
            for kind in range(2):
                out_copy(i, kind).wait()


def go_body(dims, offsets, nat, before_doc, o_up, o_down, att_t, totals, phi_q, q_doc, *rest):
    n_pieces, first, kv_heads, group, head, later = dims
    quarters, pieces, rest = rest[:2], rest[2 : 2 + n_pieces], rest[2 + n_pieces :]
    earlier, rest = rest[: 4 * later], rest[4 * later :]
    numer, grad_totals, up_product, dstate, rows_held, rows_sems, held, sems = rest
    step = pl.program_id(0)

    @pl.when(step == 0)
    def _():
        for copy in quarter_copies(quarters, rows_held, rows_sems):
            copy.start()
        load_pieces(pieces, offsets, held, sems, first)
        dstate[...] = earlier[3][...] if later else jnp.zeros(dstate.shape, f32)

    branch = quarter_of(step, quarters, rows_held, rows_sems)
    up = nn(branch, o_up[...])
    up_product[...] = up
    grad = (nn(branch, held[...]) + nn(halves(up, 1), o_down[...])).T
    use = (q_doc[...] == before_doc[0]).astype(f32)
    columns = grad.shape[1]
    for k in range(kv_heads):
        total = jnp.zeros((2 * head, AUG), f32)
        for g in range(group):
            h = k * group + g
            rows = slice(h * head, (h + 1) * head)
            inverse = 1.0 / totals[h : h + 1, :]
            one = grad[rows]
            g_total = -jnp.sum(one * att_t[rows, :], axis=0, keepdims=True) * inverse
            g_numer = (one * inverse).astype(bf16)
            numer[rows, :] = g_numer
            grad_totals[h : h + 1, :] = g_total
            aug = augmented(g_numer, g_total * use, columns, head, use)
            total = total + nt(phi_q[2 * h * head : 2 * (h + 1) * head, :], aug)
        dstate[k] += total


def augmented(g_numer, g_total, columns, head, use=None):
    top = g_numer if use is None else g_numer * use.astype(bf16)
    high = g_total.astype(bf16).astype(f32)
    row = lax.broadcasted_iota(i32, (AUG - head, columns), 0)
    below = jnp.where(row == 0, high, jnp.where(row == 1, g_total - high, 0.0))
    return jnp.concatenate([top, below.astype(bf16)], axis=0)


def backward_body(
    dims, last_docs, q_t, phi_q, numer, grad_totals, k_n, k_t, v_n, v_a, phi_kn, phi_kt, doc_col, doc_row, q_doc,
    states, cos_q, sin_q, map_q,
    g_nat, g_kt, g_vt, acc_phi, g_map_q, later,
):
    kv_heads, group, head, chunks = dims
    step = pl.program_id(0)
    chunk = chunks - 1 - step
    start = pl.multiple_of(chunk * CHUNK, CHUNK)
    keys = CHUNK + WIN

    @pl.when(step == 0)
    def _():
        later[...] = jnp.zeros(later.shape, f32)
        g_kt[...] = jnp.zeros(g_kt.shape, f32)
        g_vt[...] = jnp.zeros(g_vt.shape, f32)
        acc_phi[...] = jnp.zeros(acc_phi.shape, f32)
        g_map_q[...] = jnp.zeros(g_map_q.shape, f32)

    win, lin = masks(q_doc[...], doc_col[pl.ds(start, keys), :], group)
    use1 = (q_doc[...] == last_docs[chunk]).astype(f32)
    use = jnp.concatenate([use1] * group, axis=1)
    incl = (doc_row[:, pl.ds(start, CHUNK)] == last_docs[chunk + 1]).astype(f32)
    passing = (last_docs[chunk] == last_docs[chunk + 1]).astype(f32)
    scale = head**-0.5
    two = pl.ds(start, 2 * CHUNK)
    one = pl.ds(start, CHUNK)
    pad = jnp.zeros((head, 2 * CHUNK - keys), f32)
    grads = []
    for k in range(kv_heads):
        lanes = slice(k * head, (k + 1) * head)
        wide = slice(2 * k * head, 2 * (k + 1) * head)
        q = side(q_t, k * group * head, group, head)
        phi = side(phi_q, 2 * k * group * head, group, 2 * head)
        gn = side(numer, k * group * head, group, head)
        gt = side(grad_totals, k * group, group, 1)
        weights_win, weights = window_weights(
            q, phi, k_n[pl.ds(start, keys), lanes], phi_kn[one, wide], win, lin, scale
        )
        grad_w = nn(v_n[pl.ds(start, keys), lanes], gn) + gt
        gs = (grad_w * weights_win).astype(bf16)
        gl = jnp.where(lin, grad_w[:CHUNK], 0.0).astype(bf16)
        gq = nn(k_t[lanes, two][:, :keys], gs) * scale
        gk = nt(q, gs) * scale
        gv = nt(gn, weights.astype(bf16))
        aug = augmented(gn, gt, group * CHUNK, head)
        gphi_q = nn(phi_kt[wide, one], gl) + use * nn(states[0, k], aug)
        gphi_k = nt(phi, gl)
        after = later[k]
        after_bf = after.astype(bf16)
        v_aug = v_a[k * AUG : (k + 1) * AUG, one]
        gphi_k = gphi_k + incl * nn(after_bf, v_aug)
        from_later = incl * nn(after.T.astype(bf16), phi_kt[wide, one])[:head]
        gv = gv + jnp.concatenate([from_later, jnp.zeros((head, keys - CHUNK), f32)], axis=1)
        later[k] = nt(phi, augmented(gn, gt * use, group * CHUNK, head, use)) + passing * after
        g_kt[lanes, two] += jnp.concatenate([gk, pad], axis=1)
        g_vt[lanes, two] += jnp.concatenate([gv, pad], axis=1)
        acc_phi[wide, one] += gphi_k
        heads = [slice(g * CHUNK, (g + 1) * CHUNK) for g in range(group)]
        rows = slice(k * group * head, (k + 1) * group * head)
        grad_phi = jnp.concatenate([gphi_q[:, at] for at in heads], axis=0)
        phi_rows = phi_q[2 * k * group * head : 2 * (k + 1) * group * head, :]
        ga = hedgehog_back(phi_rows, grad_phi, head)
        gq_rows = jnp.concatenate([gq[:, at] for at in heads], axis=0) + tn(map_q[k], ga)
        g_map_q[k] += nt(q_t[rows, :], ga)
        grads.append(rope(gq_rows, cos_q[...], -sin_q[...]))
    g_nat[...] = jnp.concatenate(grads, axis=0).T.astype(bf16)


def keys_back_body(dims, last_docs, factors, g_kt, g_vt, g_phi, v_a, phi_kt, k_t, doc_row, map_k, *rest):
    kv_heads, head, chunks, rows = dims
    later, (g_own, g_halo, g_map_k) = rest[:-3], rest[-3:]
    ext = g_kt.shape[1]
    incl = (doc_row[...] == last_docs[chunks]) & (lax.broadcasted_iota(i32, (1, ext), 1) < rows)
    incl = incl.astype(f32)
    phi_grads, v_grads = [], []
    for k in range(kv_heads):
        wide = slice(2 * k * head, 2 * (k + 1) * head)
        after = jnp.zeros(later[0].shape[1:], f32)
        for i, x in enumerate(later):
            after = after + factors[i] * x[k]
        phi_grads.append(g_phi[wide, :] + incl * nn(after.astype(bf16), v_a[k * AUG : (k + 1) * AUG, :]))
        from_later = nn(after.T.astype(bf16), phi_kt[wide, :])[:head]
        v_grads.append(g_vt[k * head : (k + 1) * head, :] + incl * from_later)
    ga = hedgehog_back(phi_kt[...], jnp.concatenate(phi_grads, axis=0), head)
    g_map_k[...] = nt(k_t[...], ga)
    g_k = g_kt[...] + tn(map_k[...], ga)
    for i, grad in enumerate((g_k, jnp.concatenate(v_grads, axis=0))):
        mine = slice(i * kv_heads * head, (i + 1) * kv_heads * head)
        g_own[mine, :] = grad[:, WIN : WIN + rows]
        g_halo[mine, :] = jnp.concatenate([jnp.zeros((kv_heads * head, CHUNK - WIN), f32), grad[:, :WIN]], axis=1)


def adapters_body(
    dims, nat, g_q, g_own, g_halo, cos, sin, ups, low, normed, lowered, att, up_product, g_map_q, g_map_k, *rest
):
    rows, window, head, rank = dims
    branch, (by_head, shared) = rest[:4], rest[4:]
    half = g_own.shape[0] // 2
    kv = keys_values(g_own[...], g_halo[...], cos[...], sin[...], 1.0)
    q_width = g_q.shape[1]
    up = nn(g_q[...], ups[:q_width]) + nn(kv, ups[q_width:])
    up_halves = halves(up, 1)

    def joined(x, axis):
        one, other = jnp.split(x, 2, axis=axis)
        return one + other

    low_halves = halves(low[...], 1)
    g_q_up = joined(tn(g_q[...], low_halves), 1)[:, :rank]
    g_kv_up = joined(tn(kv, low_halves), 1)
    g_o_down = joined(tn(att[...], halves(up_product[...], 1)), 1)
    by_head[...] = jnp.zeros(by_head.shape, f32)
    q_heads, kv_heads = q_width // head, half // head
    group = q_heads // kv_heads
    for h in range(q_heads):
        mine, at = slice(h * head, (h + 1) * head), (h % group) * head
        by_head[h, :, :head] = g_map_q[h // group, at : at + head, at : at + head]
        by_head[h, :, head : head + rank] = g_q_up[mine]
        by_head[h, :, head + rank : head + 2 * rank] = g_o_down[mine]
    for h in range(kv_heads):
        mine = slice(h * head, (h + 1) * head)
        by_head[q_heads + h, :, :head] = g_map_k[mine, mine]
        by_head[q_heads + h, :, head : head + rank] = g_kv_up[mine, rank : 2 * rank]
        by_head[q_heads + h, :, head + rank : head + 2 * rank] = g_kv_up[half + h * head : half + (h + 1) * head, 2 * rank :]
    shared[: 3 * rank, :] = joined(tn(up_halves, normed[window : window + rows, :]), 0)
    o_up = 0.0
    for i, x in enumerate(branch):
        part = lowered[pl.ds(pl.multiple_of(nat[i] * x.shape[0], x.shape[0]), x.shape[0]), :]
        o_up = o_up + tn(halves(part, 1), x[...])
    shared[3 * rank :, :] = joined(o_up, 0)


def keys_values(own, halo, cos, sin, last):
    half, wide = own.shape[0] // 2, own.shape[1] - halo.shape[1]
    total = jnp.concatenate([own[:, :wide], own[:, wide:] + halo * last], axis=1)
    return jnp.concatenate([rope(total[:half], cos, -sin), total[half:]], axis=0).T.astype(bf16)


def gn_body(n_pieces, offsets, nat, g_q, g_own, g_halo, cos, sin, ups, downs, *rest):
    pieces = rest[:n_pieces]
    part0, part1, held, sems = rest[n_pieces:]
    step = pl.program_id(0)

    @pl.when(step == 0)
    def _():
        load_pieces(pieces, offsets, held, sems)

    q_width = g_q.shape[1]
    kv = keys_values(g_own[...], g_halo[...], cos[...], sin[...], (nat[4 + step] == 3).astype(f32))
    up = nn(g_q[...], ups[:q_width]) + nn(kv, ups[q_width:])
    total = nt(g_q[...], held[:, :q_width]) + nt(kv, held[:, q_width:])
    store_at(step, total + nn(halves(up, 1), downs[...]), (part0, part1))


def rms_factor(x):
    return lax.rsqrt(jnp.mean(x * x, axis=-1, keepdims=True) + epsilon)


def rms_back(x, gain, grads):
    factor = rms_factor(x)
    unit = x * factor
    scaled = grads * gain
    return factor * (scaled - unit * jnp.mean(unit * scaled, axis=-1, keepdims=True))


def hidden_body(nat, near, beside, across, tokens, gain, hidden, normed):
    total = near[...].astype(f32) + beside[...].astype(f32) + across[...].astype(f32)
    hidden[...] = tokens[...].astype(f32) + total
    normed[...] = (hidden[...] * rms_factor(hidden[...]) * gain[...]).astype(bf16)


def grad_hidden_body(nat, near, beside, across, cotangent, hidden, gain, grad, rounded):
    total = near[...].astype(f32) + beside[...].astype(f32) + across[...].astype(f32)
    grad[...] = cotangent[...].astype(f32) + rms_back(hidden[...], gain[...], total)
    rounded[...] = grad[...].astype(bf16)


def grad_tokens_body(nat, near, beside, across, tokens, grad, gain, out):
    total = near[...].astype(f32) + beside[...].astype(f32) + across[...].astype(f32)
    out[...] = (grad[...] + rms_back(tokens[...].astype(f32), gain[...], total)).astype(bf16)


def on_own_rows(body, nat, near, beside, across, placed, owned, gain, out_types):
    rows, model = near.shape
    steps = 2
    block = pl.BlockSpec((rows // steps, model), lambda i, nat: (i, 0))
    return pl.pallas_call(
        body,
        grid_spec=pltpu.PrefetchScalarGridSpec(
            num_scalar_prefetch=1,
            grid=(steps,),
            in_specs=[block] * 3
            + [pl.BlockSpec((rows // steps, model), lambda i, nat: (nat[0] * steps + i, 0))]
            + [block] * len(owned)
            + [whole((1, model))],
            out_specs=[block] * len(out_types),
        ),
        out_shape=[jax.ShapeDtypeStruct((rows, model), x) for x in out_types],
        compiler_params=params(BIG),
        cost_estimate=SMALL,
        name="own_rows",
    )(nat, near, beside, across, placed, *owned, gain)


def place_body(count, nat, *refs):
    quarters, (out, held, sems) = refs[:count], refs[-3:]
    step = pl.program_id(0)

    @pl.when(step == 0)
    def _():
        for copy in quarter_copies(quarters, held, sems):
            copy.start()

    out[...] = quarter_of(step, quarters, held, sems).astype(out.dtype)


def place(quarters, first, nat, dtype, earlier=()):
    count, (rows, width) = len(quarters), quarters[0].shape
    return pl.pallas_call(
        lambda *refs: place_body(count, *refs),
        grid_spec=pltpu.PrefetchScalarGridSpec(
            num_scalar_prefetch=1,
            grid=(count,),
            in_specs=[ANY] * (count + len(earlier)),
            out_specs=pl.BlockSpec((rows, width), lambda i, nat: (nat[first + i], 0)),
            scratch_shapes=[pltpu.VMEM((count, rows, width), bf16), pltpu.SemaphoreType.DMA((count,))],
        ),
        out_shape=jax.ShapeDtypeStruct((4 * rows, width), dtype),
        input_output_aliases={1 + count: 0} if earlier else {},
        compiler_params=params(BIG),
        cost_estimate=SMALL,
        name="place",
    )(nat, *quarters, *earlier)


def per_device(
    tokens,
    sequence_lengths,
    output_cotangent,
    query_weight,
    key_weight,
    value_weight,
    output_weight,
    gate_weight,
    up_weight,
    down_weight,
    attention_norm_gain,
    feedforward_norm_gain,
    query_adapter_down,
    key_adapter_down,
    value_adapter_down,
    output_adapter_up,
    query_adapter_up,
    key_adapter_up,
    value_adapter_up,
    output_adapter_down,
    feature_map_query,
    feature_map_key,
):
    rows, model = tokens.shape
    heads, head, rank = query_adapter_up.shape
    kv_heads = key_adapter_up.shape[0]
    group = heads // kv_heads
    q_width, kv_width = heads * head, kv_heads * head
    seq, ring = lax.axis_size("seq"), lax.axis_size("dp") * lax.axis_size("seq")
    here = lax.axis_index("seq")
    chunks = rows // CHUNK
    ext = -(-(rows + WIN) // CHUNK) * CHUNK
    quarter = rows // 4

    core, far = lax.axis_index("tensor") % 2, lax.axis_index("tensor") // 2
    nat = jnp.stack([core * 2 + far, (1 - core) * 2 + far, core * 2 + 1 - far, (1 - core) * 2 + 1 - far]).astype(i32)
    turned_far = jnp.concatenate([nat, nat[3:], nat[2:3]])
    turned_near = jnp.concatenate([nat, nat[1:2], nat[:1]])

    clock = Clock()
    pack = lambda q, k, v, o: jnp.concatenate([q, k, v, o.T], axis=1)
    attn_chain = Chain(clock, 0, pack, query_weight, key_weight, value_weight, output_weight)
    attn_chain.step()
    offsets = attn_chain.offsets
    n_pieces = offsets.shape[0]
    assert sum(map(sum, FFN_UNITS)) == gate_weight.shape[1]

    def turn(part):
        for chain in chains[part]:
            chain.settle()
        for chain in chains[part]:
            chain.step()


    lengths = sequence_lengths[0]
    ends = jnp.cumsum(lengths)
    first_row = here * rows

    def docs_of(at):
        return jnp.where(at >= 0, jnp.sum((at[:, None] >= ends[None, :]).astype(i32), axis=1), -1)

    def angles_of(at):
        doc = docs_of(at)
        starts = ends - lengths
        start = jnp.sum(jnp.where(doc[:, None] == jnp.arange(lengths.shape[0])[None, :], starts[None, :], 0), axis=1)
        ladder = jnp.arange(head // 2).astype(f32)
        inverse = jnp.exp(ladder * (-2.0 * math.log(rope_base) / head))
        angles = inverse[:, None] * (at - start).astype(f32)[None, :]
        return jnp.cos(angles), jnp.sin(angles)

    q_at = first_row + jnp.arange(rows)
    k_index = jnp.arange(ext)
    k_at = first_row - WIN + k_index
    q_doc = docs_of(q_at)[None, :]
    k_doc = jnp.where(k_index < rows + WIN, docs_of(k_at), -2)
    doc_col, doc_row = k_doc[:, None], k_doc[None, :]
    last_docs = docs_of(first_row - WIN - 1 + CHUNK * jnp.arange(chunks + 1))
    block_docs = docs_of(rows * jnp.arange(seq + 1) - WIN - 1)
    passes = (block_docs[:-1] == block_docs[1:]).astype(f32)

    halo = shifted(tokens[rows - WIN :], "seq", 1)
    cos_q, sin_q = angles_of(q_at)
    cos_k, sin_k = angles_of(k_at)
    cos_q, sin_q, cos_k, sin_k = clock.wait(cos_q, sin_q, cos_k, sin_k)
    passed_before, passed_after = [jnp.ones((), f32)], [jnp.ones((), f32)]
    for by in range(1, seq - 1):
        passed_before.append(passed_before[-1] * passes[jnp.maximum(here - by, 0)])
        passed_after.append(passed_after[-1] * passes[jnp.minimum(here + by, seq - 1)])
    passed_before, passed_after = jnp.stack(passed_before), jnp.stack(passed_after)
    q_doc, doc_col, doc_row, last_docs, passed_before, passed_after = clock.wait(
        q_doc, doc_col, doc_row, last_docs, passed_before, passed_after
    )
    attn_chain.step()
    (halo,) = clock.wait(halo)
    attn_chain.step()
    gain_attn = attention_norm_gain.astype(f32)[None, :]
    gain_mlp = feedforward_norm_gain.astype(f32)[None, :]
    downs = jnp.concatenate([query_adapter_down, key_adapter_down, value_adapter_down], axis=1)
    normed, low = pl.pallas_call(
        norm_body,
        grid_spec=pltpu.PrefetchScalarGridSpec(
            num_scalar_prefetch=0,
            grid=(1,),
            in_specs=[ANY, whole((WIN, model)), whole((1, model)), whole((model, 3 * rank))],
            out_specs=[whole((ext, model)), whole((ext, 3 * rank))],
            scratch_shapes=[pltpu.VMEM((ext, model), bf16), pltpu.SemaphoreType.DMA((4,))],
        ),
        out_shape=[jax.ShapeDtypeStruct((ext, model), bf16), jax.ShapeDtypeStruct((ext, 3 * rank), f32)],
        compiler_params=params(BIG),
        cost_estimate=SMALL,
        name="norm",
    )(clock.tie(tokens), halo, gain_attn, downs)
    normed, low = clock.wait(normed, low)
    attn_chain.step()
    all_units = [x for part in FFN_UNITS for x in part]
    pack_in = (
        gate_weight, up_weight, down_weight, query_adapter_up, key_adapter_up, value_adapter_up,
        feature_map_query, feature_map_key,
    )
    pack_out = [(gate_weight.shape[0], 3 * x) for x in all_units] + [
        (q_width + 2 * kv_width, 3 * rank),
        (q_width + 2 * kv_width, 6 * rank),
        (kv_heads, group * head, group * head),
        (kv_width, kv_width),
    ]
    packed = pl.pallas_call(
        lambda *refs: pack_body(all_units, *refs),
        grid_spec=pltpu.PrefetchScalarGridSpec(
            num_scalar_prefetch=0,
            grid=(1,),
            in_specs=[whole(x.shape) for x in pack_in],
            out_specs=[whole(x) for x in pack_out],
        ),
        out_shape=[jax.ShapeDtypeStruct(x, bf16) for x in pack_out],
        compiler_params=params(BIG),
        cost_estimate=SMALL,
        name="pack",
    )(clock.tie(gate_weight), *pack_in[1:])
    *packed, ups, ups_twice, maps_q, maps_k = clock.wait(*packed)
    chains = [[Chain(clock, 1, lambda x: x, packed[2 * i]), Chain(clock, -1, lambda x: x, packed[2 * i + 1])] for i in range(2)]
    for _ in range(ring - 5):
        attn_chain.step()
    attn_pieces = attn_chain.pieces()
    turn(0)

    sems = pltpu.SemaphoreType.DMA((n_pieces,))
    qkv_width = q_width + 2 * kv_width
    held_qkv = pltpu.VMEM((model, qkv_width), bf16)
    held_o = pltpu.VMEM((model, q_width), bf16)

    dims = (rows, ext, q_width, kv_width, head, n_pieces, chunks)
    shapes = [
        ((q_width, rows), bf16),
        ((2 * q_width, rows), bf16),
        ((ext, kv_width), bf16),
        ((kv_width, ext), bf16),
        ((ext, kv_width), bf16),
        ((kv_heads * AUG, ext), bf16),
        ((ext, 2 * kv_width), bf16),
        ((2 * kv_width, ext), bf16),
        ((kv_heads, AUG, 2 * head), f32),
    ]
    prep_in = (normed, low, ups_twice, cos_q, sin_q, cos_k, sin_k, maps_q, maps_k, doc_row)
    q_t, phi_q, k_n, k_t, v_n, v_a, phi_kn, phi_kt, contrib = pl.pallas_call(
        lambda *refs: prep_body(dims, *refs),
        grid_spec=pltpu.PrefetchScalarGridSpec(
            num_scalar_prefetch=2,
            grid=(1,),
            in_specs=[whole(x.shape) for x in prep_in] + [ANY] * n_pieces,
            out_specs=[whole(s) for s, _ in shapes],
            scratch_shapes=[held_qkv, sems],
        ),
        out_shape=[jax.ShapeDtypeStruct(s, d) for s, d in shapes],
        compiler_params=params(56),
        cost_estimate=SMALL,
        name="prep",
    )(clock.tie(offsets), last_docs, *prep_in, *attn_pieces)
    (contrib,) = clock.wait(contrib)
    turn(0)

    coming = clock.wait(*[shifted(contrib, "seq", by) for by in range(1, seq)])
    column = lambda r: pl.BlockSpec((r, CHUNK), lambda c, *_: (0, c))
    att, att_t, totals, states = pl.pallas_call(
        lambda *refs: forward_body((kv_heads, group, head), *refs),
        grid_spec=pltpu.PrefetchScalarGridSpec(
            num_scalar_prefetch=2,
            grid=(chunks,),
            in_specs=[
                column(q_width),
                column(2 * q_width),
                whole(k_n.shape),
                whole(v_a.shape),
                whole(phi_kn.shape),
                whole(doc_col.shape),
                whole(doc_row.shape),
                column(1),
            ]
            + [whole(contrib.shape)] * len(coming),
            out_specs=[
                pl.BlockSpec((CHUNK, q_width), lambda c, *_: (c, 0)),
                column(q_width),
                column(heads),
                pl.BlockSpec((1, kv_heads, 2 * head, AUG), lambda c, *_: (c, 0, 0, 0)),
            ],
            scratch_shapes=[pltpu.VMEM(contrib.shape, f32)],
        ),
        out_shape=[
            jax.ShapeDtypeStruct((rows, q_width), bf16),
            jax.ShapeDtypeStruct((q_width, rows), f32),
            jax.ShapeDtypeStruct((heads, rows), f32),
            jax.ShapeDtypeStruct((chunks, kv_heads, 2 * head, AUG), bf16),
        ],
        compiler_params=params(BIG),
        cost_estimate=SMALL,
        name="attend",
    )(clock.tie(last_docs), passed_before, q_t, phi_q, k_n, v_a, phi_kn, doc_col, doc_row, q_doc, *coming)
    att = clock.tie(att)
    turn(0)

    o_down = output_adapter_down.reshape(q_width, rank)
    o_up_t = jnp.concatenate([output_adapter_up.T, output_adapter_up.T], axis=0)
    one_quarter = jax.ShapeDtypeStruct((quarter, model), bf16)

    *o_parts, lowered = pl.pallas_call(
        lambda *refs: o_body(n_pieces, qkv_width, *refs),
        grid_spec=pltpu.PrefetchScalarGridSpec(
            num_scalar_prefetch=2,
            grid=(4,),
            in_specs=[
                pl.BlockSpec((quarter, q_width), lambda i, off, nat: (nat[3 - i], 0)),
                whole(o_down.shape),
                whole(o_up_t.shape),
            ]
            + [ANY] * n_pieces,
            out_specs=[whole((quarter, model))] * 4
            + [pl.BlockSpec((quarter, rank), lambda i, off, nat: (nat[3 - i], 0))],
            scratch_shapes=[held_o, sems],
        ),
        out_shape=[one_quarter] * 4 + [jax.ShapeDtypeStruct((rows, rank), f32)],
        compiler_params=params(BIG),
        cost_estimate=SMALL,
        name="project",
    )(clock.tie(offsets), nat, att, o_down, o_up_t, *attn_pieces)
    o_far0, o_far1, o_near0, o_near1 = clock.wait(*o_parts)
    turn(0)
    o_far0, o_near0 = clock.wait(o_far0, o_near0)
    beside = exchange(o_far0, "tensor", 1)
    beside_near = exchange(o_near0, "tensor", 1)
    beside, beside_near = clock.wait(beside, beside_near)
    o_far = clock.tie((o_far1.astype(f32) + beside.astype(f32)).astype(bf16))
    across = exchange(o_far, "tensor", 2)
    turn(0)
    (across,) = clock.wait(across)
    beside = beside_near
    hidden, normed_mlp = on_own_rows(
        hidden_body, clock.tie(nat), o_near1, beside, across, tokens, (), gain_mlp, (f32, bf16)
    )
    hidden, normed_mlp = clock.wait(hidden, normed_mlp)
    for _ in range(ring - 7):
        turn(0)
    normed_mlp = clock.tie(normed_mlp)
    across, beside = exchange(normed_mlp, "tensor", 2), exchange(normed_mlp, "tensor", 1)
    (beside,) = clock.wait(beside)
    turn(0)
    (across,) = clock.wait(across)
    for chain in chains[0]:
        chain.settle()
    turn(1)
    last = clock.tie(exchange(clock.tie(across), "tensor", 1))
    normed_mlp = [normed_mlp, beside, across, last]

    def ffn(part, which, quarters, sums):
        units, last = FFN_UNITS[part][which], part == len(FFN_UNITS) - 1
        lots = [chain.pieces() for chain in chains[part][which]]
        sizes = tuple(map(len, lots))
        pieces = [piece for lot in lots for piece in lot]
        ring_offsets = jnp.concatenate([chain.offsets for chain in chains[part][which]])
        first = quarters[0]
        summed = jax.ShapeDtypeStruct((2, quarter, model), f32)
        return pl.pallas_call(
            lambda *refs: ffn_body(sizes, units, bool(sums), last, *refs),
            grid_spec=pltpu.PrefetchScalarGridSpec(
                num_scalar_prefetch=2,
                grid=(2,),
                in_specs=[pl.BlockSpec((quarter, model), lambda i, off, nat: (nat[first - i], 0))]
                + [ANY] * (2 + len(pieces) + len(sums)),
                out_specs=[ANY] * (4 if last else 2),
                scratch_shapes=[
                    pltpu.VMEM((2, quarter, model), bf16),
                    pltpu.SemaphoreType.DMA((2,)),
                    pltpu.VMEM((3, model, sum(units)), bf16),
                    pltpu.SemaphoreType.DMA((3, len(pieces))),
                    pltpu.VMEM((2, 2, quarter, model), bf16 if last else f32),
                    pltpu.SemaphoreType.DMA((2, 2)),
                ]
                + [pltpu.VMEM((2, 2, quarter, model), f32), pltpu.SemaphoreType.DMA((2, 2))] * bool(sums),
            ),
            out_shape=[one_quarter] * 4 if last else [summed] * 2,
            compiler_params=params(BIG),
            cost_estimate=SMALL,
            name="feed_forward",
        )(clock.tie(ring_offsets), nat, output_cotangent, *[normed_mlp[q] for q in quarters], *pieces, *sums)

    sums_far = sums_near = ()
    up, down, both = slice(0, 1), slice(1, 2), slice(0, 2)
    for way in (up, down):
        sums_far = clock.wait(*ffn(0, way, (3, 2), sums_far))
        turn(1)
        sums_near = clock.wait(*ffn(0, way, (1, 0), sums_near))
        turn(1)
    for _ in range(ring - 6):
        turn(1)
    gn_far0, gn_far1, mlp_far0, mlp_far1 = ffn(1, both, (3, 2), sums_far)
    gn_far0, mlp_far0 = clock.wait(gn_far0, mlp_far0)
    beside = exchange(gn_far0, "tensor", 1)
    mlp_beside_far = exchange(mlp_far0, "tensor", 1)
    (beside,) = clock.wait(beside)
    across = exchange(clock.tie((gn_far1.astype(f32) + beside.astype(f32)).astype(bf16)), "tensor", 2)
    gn_near0, gn_near1, mlp_near0, mlp_near1 = ffn(1, both, (1, 0), sums_near)
    gn_near0, mlp_near0 = clock.wait(gn_near0, mlp_near0)
    across, gn_near0 = clock.wait(across, gn_near0)
    beside = exchange(gn_near0, "tensor", 1)
    (beside,) = clock.wait(beside)
    grad_hidden, branch = on_own_rows(
        grad_hidden_body, clock.tie(nat), gn_near1, beside, across, output_cotangent, (hidden,), gain_mlp, (f32, bf16)
    )
    grad_hidden, branch = clock.wait(grad_hidden, branch)
    across, beside = exchange(branch, "tensor", 2), exchange(branch, "tensor", 1)
    mlp_beside = exchange(clock.tie(mlp_near0), "tensor", 1)
    (beside,) = clock.wait(beside)

    o_down_t = jnp.concatenate([o_down.T, o_down.T], axis=0)
    sizes = [((q_width, rows), bf16), ((heads, rows), f32), ((rows, rank), f32), ((kv_heads, 2 * head, AUG), f32)]

    def go_part(first, quarters, earlier):
        by_quarter = lambda r: pl.BlockSpec((r, quarter), lambda i, off, nat, before: (0, nat[first + i]))
        late = bool(earlier)
        return pl.pallas_call(
            lambda *refs: go_body((n_pieces, qkv_width, kv_heads, group, head, late), *refs),
            grid_spec=pltpu.PrefetchScalarGridSpec(
                num_scalar_prefetch=3,
                grid=(2,),
                in_specs=[
                    whole((model, rank)),
                    whole(o_down_t.shape),
                    by_quarter(q_width),
                    by_quarter(heads),
                    by_quarter(2 * q_width),
                    by_quarter(1),
                ]
                + [ANY] * (2 + n_pieces)
                + ([ANY] * 3 + [whole(sizes[3][0])]) * late,
                out_specs=[
                    by_quarter(q_width),
                    by_quarter(heads),
                    pl.BlockSpec((quarter, rank), lambda i, off, nat, before: (nat[first + i], 0)),
                    whole(sizes[3][0]),
                ],
                scratch_shapes=[
                    pltpu.VMEM((2, quarter, model), bf16),
                    pltpu.SemaphoreType.DMA((2,)),
                    held_o,
                    sems,
                ],
            ),
            out_shape=[jax.ShapeDtypeStruct(s, d) for s, d in sizes],
            input_output_aliases={11 + n_pieces + i: i for i in range(3)} if late else {},
            compiler_params=params(BIG),
            cost_estimate=SMALL,
            name="project_back",
        )(
            clock.tie(offsets), nat, last_docs[:1], output_adapter_up, o_down_t, att_t, totals, phi_q, q_doc,
            *quarters, *attn_pieces, *earlier,
        )

    near = clock.wait(*go_part(0, (branch, beside), ()))
    mlp_beside, mlp_beside_far = clock.wait(mlp_beside, mlp_beside_far)
    mlp_far = clock.tie((mlp_far1.astype(f32) + mlp_beside_far.astype(f32)).astype(bf16))
    mlp_near = clock.tie(hidden + (mlp_near1.astype(f32) + mlp_beside.astype(f32)))
    (across,) = clock.wait(across)
    last = clock.tie(exchange(across, "tensor", 1))
    mlp_across = exchange(clock.tie(mlp_far), "tensor", 2)
    branch = [branch, beside, across, last]
    numer, grad_totals, up_product, dstate = clock.wait(*go_part(2, branch[2:], near))

    coming = [shifted(dstate, "seq", -by) for by in range(1, seq)]

    back_column = lambda r: pl.BlockSpec((r, CHUNK), lambda c, *_: (0, chunks - 1 - c))
    back_in = (
        (q_t, back_column(q_width)),
        (phi_q, back_column(2 * q_width)),
        (numer, back_column(q_width)),
        (grad_totals, back_column(heads)),
        (k_n, None),
        (k_t, None),
        (v_n, None),
        (v_a, None),
        (phi_kn, None),
        (phi_kt, None),
        (doc_col, None),
        (doc_row, None),
        (q_doc, back_column(1)),
        (states, pl.BlockSpec((1, kv_heads, 2 * head, AUG), lambda c, *_: (chunks - 1 - c, 0, 0, 0))),
        (cos_q, back_column(head // 2)),
        (sin_q, back_column(head // 2)),
        (maps_q, None),
    )
    g_q, g_kt, g_vt, g_phi, g_map_q = pl.pallas_call(
        lambda *refs: backward_body((kv_heads, group, head, chunks), *refs),
        grid_spec=pltpu.PrefetchScalarGridSpec(
            num_scalar_prefetch=1,
            grid=(chunks,),
            in_specs=[whole(x.shape) if spec is None else spec for x, spec in back_in],
            out_specs=[
                pl.BlockSpec((CHUNK, q_width), lambda c, *_: (chunks - 1 - c, 0)),
                whole((kv_width, ext)),
                whole((kv_width, ext)),
                whole((2 * kv_width, ext)),
                whole((kv_heads, group * head, group * head)),
            ],
            scratch_shapes=[pltpu.VMEM(dstate.shape, f32)],
        ),
        out_shape=[
            jax.ShapeDtypeStruct((rows, q_width), bf16),
            jax.ShapeDtypeStruct((kv_width, ext), f32),
            jax.ShapeDtypeStruct((kv_width, ext), f32),
            jax.ShapeDtypeStruct((2 * kv_width, ext), f32),
            jax.ShapeDtypeStruct((kv_heads, group * head, group * head), f32),
        ],
        compiler_params=params(52),
        cost_estimate=SMALL,
        name="attend_back",
    )(clock.tie(last_docs), *[x for x, _ in back_in])

    g_q, g_kt, g_vt, g_phi, g_map_q = clock.wait(g_q, g_kt, g_vt, g_phi, g_map_q)
    coming = clock.wait(*coming)
    (mlp_across,) = clock.wait(mlp_across)
    out_rows = clock.tie((mlp_near + mlp_across.astype(f32)).astype(bf16))
    out_across, out_beside = exchange(out_rows, "tensor", 2), exchange(out_rows, "tensor", 1)
    g_own, g_halo, g_map_k = pl.pallas_call(
        lambda *refs: keys_back_body((kv_heads, head, chunks, rows), *refs),
        grid_spec=pltpu.PrefetchScalarGridSpec(
            num_scalar_prefetch=2,
            grid=(1,),
            in_specs=[whole(x.shape) for x in (g_kt, g_vt, g_phi, v_a, phi_kt, k_t, doc_row, maps_k, *coming)],
            out_specs=[whole((2 * kv_width, rows)), whole((2 * kv_width, CHUNK)), whole((kv_width, kv_width))],
        ),
        out_shape=[
            jax.ShapeDtypeStruct((2 * kv_width, rows), f32),
            jax.ShapeDtypeStruct((2 * kv_width, CHUNK), f32),
            jax.ShapeDtypeStruct((kv_width, kv_width), f32),
        ],
        compiler_params=params(BIG),
        cost_estimate=SMALL,
        name="keys_back",
    )(clock.tie(last_docs), passed_after, g_kt, g_vt, g_phi, v_a, phi_kt, k_t, doc_row, maps_k, *coming)

    g_own, g_halo, g_map_k = clock.wait(g_own, g_halo, g_map_k)
    g_halo = shifted(g_halo, "seq", -1)
    (g_halo,) = clock.wait(g_halo)

    downs_t = jnp.concatenate([downs.T, downs.T], axis=0)

    def gn_part(which):
        by_rows = lambda w: pl.BlockSpec((quarter, w), lambda i, off, nat: (nat[4 + i], 0))
        by_columns = lambda r: pl.BlockSpec((r, quarter), lambda i, off, nat: (0, nat[4 + i]))
        return pl.pallas_call(
            lambda *refs: gn_body(n_pieces, *refs),
            grid_spec=pltpu.PrefetchScalarGridSpec(
                num_scalar_prefetch=2,
                grid=(2,),
                in_specs=[
                    by_rows(q_width),
                    by_columns(2 * kv_width),
                    whole(g_halo.shape),
                    by_columns(head // 2),
                    by_columns(head // 2),
                    whole(ups.shape),
                    whole(downs_t.shape),
                ]
                + [ANY] * n_pieces,
                out_specs=[whole((quarter, model))] * 2,
                scratch_shapes=[held_qkv, sems],
            ),
            out_shape=[one_quarter, one_quarter],
            compiler_params=params(BIG),
            cost_estimate=SMALL,
            name="norm_back",
        )(clock.tie(offsets), which, g_q, g_own, g_halo, cos_q, sin_q, ups, downs_t, *attn_pieces)

    gn_far0, gn_far1 = gn_part(turned_far)
    (gn_far0,) = clock.wait(gn_far0)
    out_across, out_beside, gn_far0 = clock.wait(out_across, out_beside, gn_far0)
    beside = exchange(gn_far0, "tensor", 1)
    (beside,) = clock.wait(beside)
    gn_far = clock.tie((gn_far1.astype(f32) + beside.astype(f32)).astype(bf16))
    across = exchange(gn_far, "tensor", 2)

    adapters_in = (g_q, g_own, g_halo, cos_q, sin_q, ups, low[WIN : WIN + rows], normed, lowered, att, up_product, g_map_q, g_map_k, *branch)
    sizes = [
        ((heads + kv_heads, head, 2 * head), f32),
        ((4 * rank, model), f32),
    ]
    by_head, shared = pl.pallas_call(
        lambda *refs: adapters_body((rows, WIN, head, rank), *refs),
        grid_spec=pltpu.PrefetchScalarGridSpec(
            num_scalar_prefetch=1,
            grid=(1,),
            in_specs=[whole(x.shape) for x in adapters_in],
            out_specs=[whole(x) for x, _ in sizes],
        ),
        out_shape=[jax.ShapeDtypeStruct(x, d) for x, d in sizes],
        compiler_params=params(BIG),
        cost_estimate=SMALL,
        name="adapters",
    )(clock.tie(nat), *adapters_in)
    by_head, shared = clock.wait(by_head, shared)

    by_head = by_head.reshape(heads + kv_heads, ring, head // ring, 2 * head).transpose(1, 0, 2, 3)
    shared = shared.reshape(4 * rank, ring, model // ring).transpose(1, 0, 2)
    by_head, shared = clock.wait(by_head, shared)

    def halved(x, axis, half, bit, over=0):
        x = x.reshape(x.shape[:over] + (2, half) + x.shape[over + 1 :])
        send = lax.dynamic_index_in_dim(x, 1 - bit, over, keepdims=False)
        return lax.dynamic_index_in_dim(x, bit, over, keepdims=False), exchange(send, axis, half)

    def summed_over(axis, size, xs):
        while size > 1:
            half = size // 2
            both = [halved(x, axis, half, (lax.axis_index(axis) // half) % 2) for x in xs]
            coming = clock.wait(*[coming for _, coming in both])
            xs = [kept + x for (kept, _), x in zip(both, coming)]
            size = half
            yield xs

    parts = [by_head, shared]
    dp = ring // seq
    parts = [x.reshape((dp, seq) + x.shape[1:]) for x in parts]
    for parts in summed_over("dp", dp, parts):
        pass
    gn_near0, gn_near1 = gn_part(turned_near)
    gn_near0, gn_near1 = clock.wait(gn_near0, gn_near1)
    across, gn_near0 = clock.wait(across, gn_near0)
    beside = exchange(gn_near0, "tensor", 1)
    (beside,) = clock.wait(beside)
    (grad_rows,) = on_own_rows(
        grad_tokens_body, clock.tie(nat), gn_near1, beside, across, tokens, (grad_hidden,), gain_attn, (bf16,)
    )
    (grad_rows,) = clock.wait(grad_rows)
    across, beside = exchange(grad_rows, "tensor", 2), exchange(grad_rows, "tensor", 1)
    out_last = clock.tie(exchange(out_across, "tensor", 1))
    along_seq = summed_over("seq", seq, clock.wait(*[x[0] for x in parts]))
    (beside,) = clock.wait(beside)
    grad_tokens = clock.tie(place([grad_rows, beside], 0, nat, f32))
    for parts in along_seq:
        pass
    by_head, shared = [x[0] for x in parts]
    shared = shared.reshape(4 * rank, 2, 2, model // ring // 4)
    kept, sent = halved(shared.reshape(4 * rank, 4, -1), "tensor", 2, far, 1)
    shared = kept.reshape(4 * rank, 2, -1)
    sent = sent.reshape(4 * rank, 2, -1)
    block_out = clock.tie(place([out_rows, out_beside, out_across, out_last], 0, nat, bf16))
    across, sent = clock.wait(across, sent)
    last = exchange(across, "tensor", 1)
    kept, sent = halved(shared + sent, "tensor", 1, core, 1)
    last, sent = clock.wait(last, sent)
    shared = (kept + sent).reshape(4 * rank, -1).T
    grad_tokens = clock.tie(place([across, last], 2, nat, f32, (grad_tokens,)))
    of_q, of_kv = by_head[:heads], by_head[heads:]
    first, second = slice(head, head + rank), slice(head + rank, head + 2 * rank)
    out = [of_q[..., first], of_kv[..., first], of_kv[..., second], of_q[..., second], of_q[..., :head], of_kv[..., :head]]
    return (
        block_out,
        grad_tokens,
        shared[:, :rank] + clock.now.astype(f32),
        shared[:, rank : 2 * rank],
        shared[:, 2 * rank : 3 * rank],
        shared[:, 3 * rank :],
        *out,
    )


def solution(mesh):
    return jax.shard_map(
        per_device,
        mesh=mesh,
        in_specs=(
            P(("dp", "seq"), None),
            P("dp", None),
            P(("dp", "seq"), None),
            P(("dp", "seq"), "tensor"),
            P(("dp", "seq"), "tensor"),
            P(("dp", "seq"), "tensor"),
            P("tensor", ("dp", "seq")),
            P(("dp", "seq"), "tensor"),
            P(("dp", "seq"), "tensor"),
            P("tensor", ("dp", "seq")),
            P(),
            P(),
            P(),
            P(),
            P(),
            P(),
            P("tensor", None, None),
            P("tensor", None, None),
            P("tensor", None, None),
            P("tensor", None, None),
            P("tensor", None, None),
            P("tensor", None, None),
        ),
        out_specs=(
            P(("dp", "seq"), None),
            P(("dp", "seq"), None),
            P(("dp", "seq", "tensor"), None),
            P(("dp", "seq", "tensor"), None),
            P(("dp", "seq", "tensor"), None),
            P(("dp", "seq", "tensor"), None),
            P("tensor", ("dp", "seq"), None),
            P("tensor", ("dp", "seq"), None),
            P("tensor", ("dp", "seq"), None),
            P("tensor", ("dp", "seq"), None),
            P("tensor", ("dp", "seq"), None),
            P("tensor", ("dp", "seq"), None),
        ),
        check_vma=False,
    )
```

```python
import math

import jax
import jax.numpy as jnp
from jax import lax
from jax.experimental import pallas as pl
from jax.experimental.pallas import tpu as pltpu
from jax.sharding import PartitionSpec as P

WIN = 64
CHUNK = 128
AUG = 80
RING = 8
FFN_UNITS = ((512, 512), (512, 512))
BIG = 60

epsilon = 1e-05
rope_base = 500000.0
bf16, f32, i32 = jnp.bfloat16, jnp.float32, jnp.int32
MIB = 1 << 20


def nn(a, b):
    return lax.dot_general(a, b, (((1,), (0,)), ((), ())), preferred_element_type=f32)


def nt(a, b):
    return lax.dot_general(a, b, (((1,), (1,)), ((), ())), preferred_element_type=f32)


def tn(a, b):
    return lax.dot_general(a, b, (((0,), (0,)), ((), ())), preferred_element_type=f32)


def halves(x, axis):
    high = x.astype(bf16)
    return jnp.concatenate([high, (x - high.astype(f32)).astype(bf16)], axis=axis)


def exchange(x, axis, bit):
    count = lax.axis_size(axis)
    return lax.ppermute(x, axis, [(i, i ^ bit) for i in range(count)])


def shifted(x, axis, by):
    count = lax.axis_size(axis)
    return lax.ppermute(x, axis, [(i, i + by) for i in range(count) if 0 <= i + by < count])


def place_of(index, seq):
    row, col = index // seq, index % seq
    return row * seq + (col if row % 2 == 0 else seq - 1 - col)


def place_of_traced(index, seq):
    row, col = index // seq, index % seq
    return row * seq + jnp.where(row % 2 == 0, col, seq - 1 - col)


class Clock:
    def __init__(self):
        self.now = jnp.zeros((), i32)

    def wait(self, *arrays):
        *out, self.now = lax.optimization_barrier((*arrays, self.now))
        return out

    def tie(self, x):
        return self.wait(x)[0]


class Chain:
    def __init__(self, clock, way, pack, *blocks):
        block = pack(*clock.wait(*blocks))
        dp, seq = lax.axis_size("dp"), lax.axis_size("seq")
        self.clock, self.count = clock, dp * seq
        self.ringed = self.count <= RING
        rows = block.shape[0]
        if not self.ringed:
            self.lanes = [[lax.all_gather(block, ("dp", "seq"), axis=0, tiled=True)]]
            self.offsets = jnp.zeros((1,), i32)
            return
        order = [place_of(i, seq) for i in range(self.count)]
        up = [(order[i], order[(i + 1) % self.count]) for i in range(self.count)]
        down = [(j, i) for i, j in up]
        place = place_of_traced(lax.axis_index("dp") * seq + lax.axis_index("seq"), seq)
        steps = jnp.arange(self.count)
        came_up = place_of_traced((place - steps) % self.count, seq) * rows
        came_down = place_of_traced((place + steps) % self.count, seq) * rows
        if way:
            self.lanes, self.ways = [[block]], [up if way > 0 else down]
            self.offsets = (came_up if way > 0 else came_down).astype(i32)
        else:
            half = rows // 2
            self.lanes, self.ways = [[block[:half]], [block[half:]]], [up, down]
            self.offsets = jnp.concatenate([came_up, came_down + half]).astype(i32)

    def settle(self):
        if self.ringed:
            came = self.clock.wait(*[lane[-1] for lane in self.lanes])
            for lane, x in zip(self.lanes, came):
                lane[-1] = x

    def step(self):
        if self.ringed:
            for lane, way in zip(self.lanes, self.ways):
                (lane[-1],) = self.clock.wait(lane[-1])
                lane.append(lax.ppermute(lane[-1], ("dp", "seq"), way))

    def pieces(self):
        self.settle()
        return [piece for lane in self.lanes for piece in lane]


def load_pieces(pieces, offsets, held, sems, first=0):
    copies = [
        pltpu.make_async_copy(
            piece.at[:, pl.ds(first, held.shape[1])],
            held.at[pl.ds(pl.multiple_of(offsets[i], 16), piece.shape[0])],
            sems.at[i],
        )
        for i, piece in enumerate(pieces)
    ]
    for copy in copies:
        copy.start()
    for copy in copies:
        copy.wait()


def params(limit):
    return pltpu.CompilerParams(vmem_limit_bytes=limit * MIB)


SMALL = pl.CostEstimate(flops=1, bytes_accessed=1, transcendentals=0)


ANY = pl.BlockSpec(memory_space=pl.ANY)


def whole(shape):
    return pl.BlockSpec(shape, lambda *_: (0,) * len(shape))


def rope(x, cos, sin):
    width = 2 * cos.shape[0]
    half = width // 2
    out = []
    for at in range(0, x.shape[0], width):
        x1, x2 = x[at : at + half], x[at + half : at + width]
        out += [x1 * cos - x2 * sin, x2 * cos + x1 * sin]
    return jnp.concatenate(out, axis=0)


def hedgehog(a, width):
    out = []
    for at in range(0, a.shape[0], width):
        one = a[at : at + width]
        for e in (
            jnp.exp(one - jnp.max(one, axis=0, keepdims=True)),
            jnp.exp(jnp.min(one, axis=0, keepdims=True) - one),
        ):
            out.append(e * (1.0 / jnp.sum(e, axis=0, keepdims=True)))
    return jnp.concatenate(out, axis=0).astype(bf16)


def hedgehog_back(phi, grad, width):
    out = []
    for at in range(0, phi.shape[0], 2 * width):
        p1, p2 = phi[at : at + width].astype(f32), phi[at + width : at + 2 * width].astype(f32)
        d1, d2 = grad[at : at + width], grad[at + width : at + 2 * width]
        out.append(
            p1 * (d1 - jnp.sum(p1 * d1, axis=0, keepdims=True))
            - p2 * (d2 - jnp.sum(p2 * d2, axis=0, keepdims=True))
        )
    return jnp.concatenate(out, axis=0).astype(bf16)


def tables_body(seq, lengths, here, ladder, cos_q, sin_q, cos_k, sin_k, q_doc, doc_col, doc_row, last, before, after):
    rows, ext = q_doc.shape[1], doc_row.shape[1]
    ends = [lengths[0]]
    for i in range(1, lengths.shape[0]):
        ends.append(ends[-1] + lengths[i])

    def document(at):
        doc, start = 0, 0
        for end in ends:
            past = at >= end
            doc = doc + past.astype(i32)
            start = jnp.where(past, end, start)
        return jnp.where(at >= 0, doc, -1), at - start

    def angles(relative, cos, sin):
        angle = ladder[...] * relative.astype(f32)
        cos[...] = jnp.cos(angle)
        sin[...] = jnp.sin(angle)

    def passing(block):
        ahead = rows * block - WIN - 1
        return (document(ahead)[0] == document(ahead + rows)[0]).astype(f32)

    first = here[0] * rows
    q_doc[...], relative = document(first + lax.broadcasted_iota(i32, (1, rows), 1))
    angles(relative, cos_q, sin_q)
    index = lax.broadcasted_iota(i32, (1, ext), 1)
    doc, relative = document(first - WIN + index)
    doc_row[...] = jnp.where(index < rows + WIN, doc, -2)
    angles(relative, cos_k, sin_k)
    index = lax.broadcasted_iota(i32, (ext, 1), 0)
    doc_col[...] = jnp.where(index < rows + WIN, document(first - WIN + index)[0], -2)
    for i in range(last.shape[0]):
        last[i] = document(first - WIN - 1 + CHUNK * i)[0]
    earlier = later = jnp.float32(1.0)
    for by in range(seq - 1):
        before[by], after[by] = earlier, later
        earlier = earlier * passing(jnp.maximum(here[0] - by - 1, 0))
        later = later * passing(jnp.minimum(here[0] + by + 1, seq - 1))


def norm_body(tokens, halo, gain, downs, normed, low, held, sems):
    rows, window = tokens.shape[0], halo.shape[0]
    part = rows // 4

    def copy(i):
        return pltpu.make_async_copy(
            tokens.at[pl.ds(i * part, part)], held.at[pl.ds(window + i * part, part)], sems.at[i]
        )

    for i in range(4):
        copy(i).start()
    held[:window, :] = halo[...]
    held[window + rows :, :] = jnp.zeros((held.shape[0] - window - rows, held.shape[1]), bf16)
    for i in range(4):
        copy(i).wait()
        first = window + i * part if i else 0
        last = window + (i + 1) * part if i < 3 else held.shape[0]
        x = held[first:last, :].astype(f32)
        out = (x * rms_factor(x) * gain[...]).astype(bf16)
        normed[first:last, :] = out
        low[first:last, :] = nn(out, downs[...])


def pack_body(units, gate, up, down, q_up, k_up, v_up, map_q, map_k, o_up, *outs):
    packed, (ups, twice, maps_q, maps_k, o_up_out) = outs[:-5], outs[-5:]
    o_up_out[...] = o_up[...]
    at = 0
    for size, out in zip(units, packed):
        out[:, :size] = gate[:, at : at + size]
        out[:, size : 2 * size] = up[:, at : at + size]
        out[:, 2 * size :] = down[at : at + size, :].T
        at += size
    head, rank = q_up.shape[1:]
    at = 0
    for i, x in enumerate((q_up, k_up, v_up)):
        for h in range(x.shape[0]):
            row = jnp.concatenate(
                [jnp.zeros((head, rank), bf16)] * i + [x[h]] + [jnp.zeros((head, rank), bf16)] * (2 - i), axis=1
            )
            ups[at : at + head, :] = row
            twice[at : at + head, :] = jnp.concatenate([row, row], axis=1)
            at += head
    maps_q[...] = jnp.zeros(maps_q.shape, bf16)
    maps_k[...] = jnp.zeros(maps_k.shape, bf16)
    group = map_q.shape[0] // maps_q.shape[0]
    for h in range(map_q.shape[0]):
        mine = slice(h % group * head, (h % group + 1) * head)
        maps_q[h // group, mine, mine] = map_q[h].astype(f32).T.astype(bf16)
    for h in range(map_k.shape[0]):
        mine = slice(h * head, (h + 1) * head)
        maps_k[mine, mine] = map_k[h].astype(f32).T.astype(bf16)


def prep_body(dims, offsets, last_docs, nx, low, ups, cos_q, sin_q, cos_k, sin_k, map_q, map_k, doc_row, *rest):
    tokens, ext, q_width, kv_width, head, n_pieces, chunks = dims
    pieces, rest = rest[:n_pieces], rest[n_pieces:]
    q_t, phi_q, k_n, k_t, v_n, v_a, phi_kn, phi_kt, contrib, held, sems = rest
    load_pieces(pieces, offsets, held, sems)
    kv_heads = kv_width // head
    step = ext // 3
    v_a[...] = jnp.zeros(v_a.shape, bf16)
    for at in range(0, ext, step):
        rows = pl.ds(at, step)
        raw = nn(nx[rows, :], held[:, q_width:]) + nt(halves(low[rows, :], 1), ups[q_width:, :])
        v = raw[:, kv_width:].astype(bf16)
        v_n[rows, :] = v
        v_tr = raw[:, kv_width:].T.astype(bf16)
        for k in range(kv_heads):
            v_a[k * AUG : k * AUG + head, rows] = v_tr[k * head : (k + 1) * head]
            v_a[k * AUG + head : (k + 1) * AUG, rows] = (
                lax.broadcasted_iota(i32, (AUG - head, step), 0) < 2
            ).astype(f32).astype(bf16)
        k_rot = rope(raw[:, :kv_width].T, cos_k[:, rows], sin_k[:, rows])
        k_bf = k_rot.astype(bf16)
        k_t[:, rows] = k_bf
        k_n[rows, :] = k_rot.T.astype(bf16)
        phi = hedgehog(nn(map_k[...], k_bf), head)
        phi_kt[:, rows] = phi
        phi_kn[rows, :] = phi.astype(f32).T.astype(bf16)
    incl = (doc_row[:, :tokens] == last_docs[chunks]).astype(f32).astype(bf16)
    for k in range(kv_heads):
        masked = v_a[k * AUG : (k + 1) * AUG, :tokens] * incl
        contrib[k] = nn(masked, phi_kn[:tokens, k * 2 * head : (k + 1) * 2 * head])
    step = tokens // 2
    group = q_width // kv_heads
    for at in range(0, tokens, step):
        rows = pl.ds(at, step)
        raw = nn(nx[pl.ds(WIN + at, step), :], held[:, :q_width])
        raw = raw + nt(halves(low[pl.ds(WIN + at, step), :], 1), ups[:q_width, :])
        q_bf = rope(raw.T, cos_q[:, rows], sin_q[:, rows]).astype(bf16)
        q_t[:, rows] = q_bf
        for k in range(kv_heads):
            logits = nn(map_q[k], q_bf[k * group : (k + 1) * group])
            phi_q[2 * k * group : 2 * (k + 1) * group, rows] = hedgehog(logits, head)


def masks(q_doc, k_doc, heads):
    keys = CHUNK + WIN
    j = lax.broadcasted_iota(i32, (keys, CHUNK), 0)
    t = lax.broadcasted_iota(i32, (keys, CHUNK), 1)
    same = k_doc == q_doc
    win = same & (j > t) & (j <= t + WIN)
    lin = (same & (j <= t))[:CHUNK]
    win_f = jnp.concatenate([win.astype(f32)] * heads, axis=1)
    lin_f = jnp.concatenate([lin.astype(f32)] * heads, axis=1)
    return win_f > 0.5, lin_f > 0.5


def side(ref, first, count, size):
    return jnp.concatenate([ref[first + g * size : first + (g + 1) * size, :] for g in range(count)], axis=1)


def window_weights(q, phi_q, k_win, phi_k, win, lin, scale):
    scores = nn(k_win, q)
    weights_win = jnp.where(win, jnp.exp(scores * scale), 0.0)
    linear = jnp.where(lin, nn(phi_k, phi_q), 0.0)
    return weights_win, jnp.concatenate([weights_win[:CHUNK] + linear, weights_win[CHUNK:]], axis=0)


def forward_body(dims, last_docs, factors, q_t, phi_q, k_n, v_a, phi_kn, doc_col, doc_row, q_doc, *rest):
    kv_heads, group, head = dims
    earlier, (att, att_t, totals, states, state) = rest[:-5], rest[-5:]
    chunk = pl.program_id(0)
    start = pl.multiple_of(chunk * CHUNK, CHUNK)

    @pl.when(chunk == 0)
    def _():
        total = jnp.zeros(state.shape, f32)
        for i, x in enumerate(earlier):
            total = total + factors[i] * x[...]
        state[...] = total

    keys = CHUNK + WIN
    win, lin = masks(q_doc[...], doc_col[pl.ds(start, keys), :], group)
    use = (q_doc[...] == last_docs[chunk]).astype(f32)
    use = jnp.concatenate([use] * group, axis=1)
    incl = (doc_row[:, pl.ds(start, CHUNK)] == last_docs[chunk + 1]).astype(f32).astype(bf16)
    passing = (last_docs[chunk] == last_docs[chunk + 1]).astype(f32)
    scale = head**-0.5
    out = []
    for k in range(kv_heads):
        q = side(q_t, k * group * head, group, head)
        phi = side(phi_q, 2 * k * group * head, group, 2 * head)
        k_win = k_n[pl.ds(start, keys), k * head : (k + 1) * head]
        phi_k = phi_kn[pl.ds(start, CHUNK), 2 * k * head : 2 * (k + 1) * head]
        v_win = v_a[k * AUG : (k + 1) * AUG, pl.ds(start, 2 * CHUNK)]
        _, weights = window_weights(q, phi, k_win, phi_k, win, lin, scale)
        before = state[k]
        from_state = nn(before.astype(bf16), phi) * use
        total = jnp.sum(weights, axis=0, keepdims=True) + from_state[head : head + 1]
        numer = nn(v_win[:, :keys], weights.astype(bf16))[:head] + from_state[:head]
        attended = numer * (1.0 / total)
        for g in range(group):
            out.append(attended[:, g * CHUNK : (g + 1) * CHUNK])
            totals[k * group + g : k * group + g + 1, :] = total[:, g * CHUNK : (g + 1) * CHUNK]
        states[0, k] = before.T.astype(bf16)
        state[k] = nn(v_win[:, :CHUNK] * incl, phi_k) + passing * before
    attended = jnp.concatenate(out, axis=0)
    att_t[...] = attended
    att[...] = attended.T.astype(bf16)


def store_at(step, value, outs):
    for i, out in enumerate(outs):

        @pl.when(step == i)
        def _(out=out):
            out[...] = value.astype(out.dtype)


def o_body(n_pieces, first, offsets, nat, att, down, up, *rest):
    pieces, parts, (lowered, held, sems) = rest[:n_pieces], rest[n_pieces:-3], rest[-3:]
    step = pl.program_id(0)

    @pl.when(step == 0)
    def _():
        load_pieces(pieces, offsets, held, sems, first)

    low = nn(att[...], down[...])
    lowered[...] = low
    store_at(step, nt(att[...], held[...]) + nn(halves(low, 1), up[...]), parts)


def quarter_copies(quarters, held, sems, first=0):
    return [pltpu.make_async_copy(x, held.at[first + i], sems.at[first + i]) for i, x in enumerate(quarters)]


def quarter_of(step, quarters, held, sems):
    for i, copy in enumerate(quarter_copies(quarters, held, sems)):

        @pl.when(step == i)
        def _(copy=copy):
            copy.wait()

    return held[step]


def ffn_body(lots, units, summed, last, offsets, nat, cot, *rest):
    count, n_out = sum(lots), 4 if last else 2
    quarters, pieces, rest = rest[:2], rest[2 : 2 + count], rest[2 + count :]
    sums, outs, rest = rest[: 2 * summed], rest[2 * summed : 2 * summed + n_out], rest[2 * summed + n_out :]
    rows, rows_sems, held, sems, out_held, out_sems, *rest = rest
    step = pl.program_id(0)

    def at_first(act):
        pl.when(step == 0)(act)

    def copies(which):
        made, at, i = [], 0, 0
        for lot, size in zip(lots, units):
            for _ in range(lot):
                made.append(
                    pltpu.make_async_copy(
                        pieces[i].at[:, pl.ds(which * size, size)],
                        held.at[which, pl.ds(pl.multiple_of(offsets[i], 16), pieces[i].shape[0]), pl.ds(at, size)],
                        sems.at[which, i],
                    )
                )
                i += 1
            at += size
        return made

    def sum_copy(i, kind):
        return pltpu.make_async_copy(sums[kind].at[i], rest[0].at[i, kind], rest[1].at[i, kind])

    def out_copy(i, kind):
        out = outs[2 * (1 - kind) + i] if last else outs[kind].at[i]
        return pltpu.make_async_copy(out_held.at[i, kind], out, out_sems.at[i, kind])

    @at_first
    def _():
        first = copies(0)
        for copy in quarter_copies(quarters[:1], rows, rows_sems) + first:
            copy.start()
        for copy in quarter_copies(quarters[1:], rows, rows_sems, 1):
            copy.start()
        for copy in first:
            copy.wait()
        for copy in copies(1):
            copy.start()

    n2 = quarter_of(step, quarters, rows, rows_sems)
    gate = nn(n2, held[0])

    @at_first
    def _():
        for copy in copies(1):
            copy.wait()
        for copy in copies(2):
            copy.start()

    up = nn(n2, held[1])

    @at_first
    def _():
        for copy in copies(2):
            copy.wait()
        for i in range(2 if summed else 0):
            for kind in (1, 0):
                sum_copy(i, kind).start()

    grad_act = nn(cot[...], held[2])
    s = 1.0 / (1.0 + jnp.exp(-gate))
    silu = gate * s
    act = (silu * up).astype(bf16)
    grad_gate = (grad_act * up * s * (1.0 + gate * (1.0 - s))).astype(bf16)
    grad_up = (grad_act * silu).astype(bf16)

    def finish(kind, total):
        if summed:
            sum_copy(step, kind).wait()
            total = total + rest[0][step, kind]
        out_held[step, kind] = total.astype(out_held.dtype)
        for i in range(2):

            @pl.when(step == i)
            def _(i=i):
                out_copy(i, kind).start()

    finish(1, nt(grad_gate, held[0]) + nt(grad_up, held[1]))
    finish(0, nt(act, held[2]))

    @pl.when(step == 1)
    def _():
        for i in range(2):
            for kind in range(2):
                out_copy(i, kind).wait()


def go_body(dims, offsets, nat, before_doc, o_up, o_down, att_t, totals, phi_q, q_doc, *rest):
    n_pieces, first, kv_heads, group, head, later = dims
    quarters, pieces, rest = rest[:2], rest[2 : 2 + n_pieces], rest[2 + n_pieces :]
    earlier, rest = rest[: 4 * later], rest[4 * later :]
    numer, grad_totals, up_product, dstate, rows_held, rows_sems, held, sems = rest
    step = pl.program_id(0)

    @pl.when(step == 0)
    def _():
        for copy in quarter_copies(quarters, rows_held, rows_sems):
            copy.start()
        load_pieces(pieces, offsets, held, sems, first)
        dstate[...] = earlier[3][...] if later else jnp.zeros(dstate.shape, f32)

    branch = quarter_of(step, quarters, rows_held, rows_sems)
    up = nn(branch, o_up[...])
    up_product[...] = up
    grad = (nn(branch, held[...]) + nn(halves(up, 1), o_down[...])).T
    use = (q_doc[...] == before_doc[0]).astype(f32)
    columns = grad.shape[1]
    for k in range(kv_heads):
        total = jnp.zeros((2 * head, AUG), f32)
        for g in range(group):
            h = k * group + g
            rows = slice(h * head, (h + 1) * head)
            inverse = 1.0 / totals[h : h + 1, :]
            one = grad[rows]
            g_total = -jnp.sum(one * att_t[rows, :], axis=0, keepdims=True) * inverse
            g_numer = (one * inverse).astype(bf16)
            numer[rows, :] = g_numer
            grad_totals[h : h + 1, :] = g_total
            aug = augmented(g_numer, g_total * use, columns, head, use)
            total = total + nt(phi_q[2 * h * head : 2 * (h + 1) * head, :], aug)
        dstate[k] += total


def augmented(g_numer, g_total, columns, head, use=None):
    top = g_numer if use is None else g_numer * use.astype(bf16)
    high = g_total.astype(bf16).astype(f32)
    row = lax.broadcasted_iota(i32, (AUG - head, columns), 0)
    below = jnp.where(row == 0, high, jnp.where(row == 1, g_total - high, 0.0))
    return jnp.concatenate([top, below.astype(bf16)], axis=0)


def backward_body(
    dims, last_docs, q_t, phi_q, numer, grad_totals, k_n, k_t, v_n, v_a, phi_kn, phi_kt, doc_col, doc_row, q_doc,
    states, cos_q, sin_q, map_q,
    g_nat, g_kt, g_vt, acc_phi, g_map_q, later,
):
    kv_heads, group, head, chunks = dims
    step = pl.program_id(0)
    chunk = chunks - 1 - step
    start = pl.multiple_of(chunk * CHUNK, CHUNK)
    keys = CHUNK + WIN

    @pl.when(step == 0)
    def _():
        later[...] = jnp.zeros(later.shape, f32)
        g_kt[...] = jnp.zeros(g_kt.shape, f32)
        g_vt[...] = jnp.zeros(g_vt.shape, f32)
        acc_phi[...] = jnp.zeros(acc_phi.shape, f32)
        g_map_q[...] = jnp.zeros(g_map_q.shape, f32)

    win, lin = masks(q_doc[...], doc_col[pl.ds(start, keys), :], group)
    use1 = (q_doc[...] == last_docs[chunk]).astype(f32)
    use = jnp.concatenate([use1] * group, axis=1)
    incl = (doc_row[:, pl.ds(start, CHUNK)] == last_docs[chunk + 1]).astype(f32)
    passing = (last_docs[chunk] == last_docs[chunk + 1]).astype(f32)
    scale = head**-0.5
    two = pl.ds(start, 2 * CHUNK)
    one = pl.ds(start, CHUNK)
    pad = jnp.zeros((head, 2 * CHUNK - keys), f32)
    grads = []
    for k in range(kv_heads):
        lanes = slice(k * head, (k + 1) * head)
        wide = slice(2 * k * head, 2 * (k + 1) * head)
        q = side(q_t, k * group * head, group, head)
        phi = side(phi_q, 2 * k * group * head, group, 2 * head)
        gn = side(numer, k * group * head, group, head)
        gt = side(grad_totals, k * group, group, 1)
        weights_win, weights = window_weights(
            q, phi, k_n[pl.ds(start, keys), lanes], phi_kn[one, wide], win, lin, scale
        )
        grad_w = nn(v_n[pl.ds(start, keys), lanes], gn) + gt
        gs = (grad_w * weights_win).astype(bf16)
        gl = jnp.where(lin, grad_w[:CHUNK], 0.0).astype(bf16)
        gq = nn(k_t[lanes, two][:, :keys], gs) * scale
        gk = nt(q, gs) * scale
        gv = nt(gn, weights.astype(bf16))
        aug = augmented(gn, gt, group * CHUNK, head)
        gphi_q = nn(phi_kt[wide, one], gl) + use * nn(states[0, k], aug)
        gphi_k = nt(phi, gl)
        after = later[k]
        after_bf = after.astype(bf16)
        v_aug = v_a[k * AUG : (k + 1) * AUG, one]
        gphi_k = gphi_k + incl * nn(after_bf, v_aug)
        from_later = incl * nn(after.T.astype(bf16), phi_kt[wide, one])[:head]
        gv = gv + jnp.concatenate([from_later, jnp.zeros((head, keys - CHUNK), f32)], axis=1)
        later[k] = nt(phi, augmented(gn, gt * use, group * CHUNK, head, use)) + passing * after
        g_kt[lanes, two] += jnp.concatenate([gk, pad], axis=1)
        g_vt[lanes, two] += jnp.concatenate([gv, pad], axis=1)
        acc_phi[wide, one] += gphi_k
        heads = [slice(g * CHUNK, (g + 1) * CHUNK) for g in range(group)]
        rows = slice(k * group * head, (k + 1) * group * head)
        grad_phi = jnp.concatenate([gphi_q[:, at] for at in heads], axis=0)
        phi_rows = phi_q[2 * k * group * head : 2 * (k + 1) * group * head, :]
        ga = hedgehog_back(phi_rows, grad_phi, head)
        gq_rows = jnp.concatenate([gq[:, at] for at in heads], axis=0) + tn(map_q[k], ga)
        g_map_q[k] += nt(q_t[rows, :], ga)
        grads.append(rope(gq_rows, cos_q[...], -sin_q[...]))
    g_nat[...] = jnp.concatenate(grads, axis=0).T.astype(bf16)


def keys_back_body(dims, last_docs, factors, g_kt, g_vt, g_phi, v_a, phi_kt, k_t, doc_row, map_k, *rest):
    kv_heads, head, chunks, rows = dims
    later, (g_own, g_halo, g_map_k) = rest[:-3], rest[-3:]
    ext = g_kt.shape[1]
    incl = (doc_row[...] == last_docs[chunks]) & (lax.broadcasted_iota(i32, (1, ext), 1) < rows)
    incl = incl.astype(f32)
    phi_grads, v_grads = [], []
    for k in range(kv_heads):
        wide = slice(2 * k * head, 2 * (k + 1) * head)
        after = jnp.zeros(later[0].shape[1:], f32)
        for i, x in enumerate(later):
            after = after + factors[i] * x[k]
        phi_grads.append(g_phi[wide, :] + incl * nn(after.astype(bf16), v_a[k * AUG : (k + 1) * AUG, :]))
        from_later = nn(after.T.astype(bf16), phi_kt[wide, :])[:head]
        v_grads.append(g_vt[k * head : (k + 1) * head, :] + incl * from_later)
    ga = hedgehog_back(phi_kt[...], jnp.concatenate(phi_grads, axis=0), head)
    g_map_k[...] = nt(k_t[...], ga)
    g_k = g_kt[...] + tn(map_k[...], ga)
    for i, grad in enumerate((g_k, jnp.concatenate(v_grads, axis=0))):
        mine = slice(i * kv_heads * head, (i + 1) * kv_heads * head)
        g_own[mine, :] = grad[:, WIN : WIN + rows]
        g_halo[mine, :] = jnp.concatenate([jnp.zeros((kv_heads * head, CHUNK - WIN), f32), grad[:, :WIN]], axis=1)


def adapters_body(
    dims, g_q, g_own, g_halo, cos, sin, ups, low, normed, g_o_up, g_o_down, g_map_q, g_map_k, *outs
):
    rows, window, head, rank = dims
    half = g_own.shape[0] // 2
    kv = keys_values(g_own[...], g_halo[...], cos[...], sin[...], 1.0)
    q_width = g_q.shape[1]
    up = nn(g_q[...], ups[:q_width]) + nn(kv, ups[q_width:])
    up_halves = halves(up, 1)

    def joined(x, axis):
        one, other = jnp.split(x, 2, axis=axis)
        return one + other

    low_halves = halves(low[...], 1)
    g_q_up = joined(tn(g_q[...], low_halves), 1)[:, :rank]
    g_kv_up = joined(tn(kv, low_halves), 1)
    if len(outs) == 1:
        (slabs,) = outs
        slabs[...] = jnp.zeros(slabs.shape, f32)
        tall = slabs.shape[2]
    else:
        by_head, shared = outs
        by_head[...] = jnp.zeros(by_head.shape, f32)

    def put(h, first, x):
        if len(outs) == 2:
            by_head[h, :, first : first + x.shape[1]] = x
            return
        for r in range(slabs.shape[0]):
            slabs[r, h, :, first : first + x.shape[1]] = x[r * tall : (r + 1) * tall]

    def put_shared(first, x):
        if len(outs) == 2:
            shared[first : first + x.shape[0], :] = x
            return
        wide = x.shape[1] // slabs.shape[0] // 128
        for i in range(x.shape[0] // tall):
            for r in range(slabs.shape[0]):
                for j in range(wide):
                    at = (r * wide + j) * 128
                    tile = x[i * tall : (i + 1) * tall, at : at + 128]
                    slabs[r, q_heads + kv_heads + (first // tall + i) * wide + j] = tile

    q_heads, kv_heads = q_width // head, half // head
    group = q_heads // kv_heads
    for h in range(q_heads):
        mine, at = slice(h * head, (h + 1) * head), (h % group) * head
        put(h, 0, g_map_q[h // group, at : at + head, at : at + head])
        put(h, head, g_q_up[mine])
        put(h, head + rank, g_o_down[mine, :])
    for h in range(kv_heads):
        mine = slice(h * head, (h + 1) * head)
        put(q_heads + h, 0, g_map_k[mine, mine])
        put(q_heads + h, head, g_kv_up[mine, rank : 2 * rank])
        put(q_heads + h, head + rank, g_kv_up[half + h * head : half + (h + 1) * head, 2 * rank :])
    put_shared(0, joined(tn(up_halves, normed[window : window + rows, :]), 0))
    put_shared(3 * rank, g_o_up[...])


def adapter_o_body(nat, lowered, att, up_product, *rest):
    branch, (g_o_up, g_o_down) = rest[:4], rest[4:]

    def joined(x, axis):
        one, other = jnp.split(x, 2, axis=axis)
        return one + other

    g_o_down[...] = joined(tn(att[...], halves(up_product[...], 1)), 1)
    o_up = 0.0
    for i, x in enumerate(branch):
        part = lowered[pl.ds(pl.multiple_of(nat[i] * x.shape[0], x.shape[0]), x.shape[0]), :]
        o_up = o_up + tn(halves(part, 1), x[...])
    g_o_up[...] = joined(o_up, 0)


def keys_values(own, halo, cos, sin, last):
    half, wide = own.shape[0] // 2, own.shape[1] - halo.shape[1]
    total = jnp.concatenate([own[:, :wide], own[:, wide:] + halo * last], axis=1)
    return jnp.concatenate([rope(total[:half], cos, -sin), total[half:]], axis=0).T.astype(bf16)


def gn_body(n_pieces, offsets, nat, g_q, g_own, g_halo, cos, sin, ups, downs, *rest):
    pieces = rest[:n_pieces]
    parts, (held, sems) = rest[n_pieces:-2], rest[-2:]
    step = pl.program_id(0)

    @pl.when(step == 0)
    def _():
        load_pieces(pieces, offsets, held, sems)

    q_width = g_q.shape[1]
    kv = keys_values(g_own[...], g_halo[...], cos[...], sin[...], (nat[3 - step] == 3).astype(f32))
    up = nn(g_q[...], ups[:q_width]) + nn(kv, ups[q_width:])
    total = nt(g_q[...], held[:, :q_width]) + nt(kv, held[:, q_width:])
    store_at(step, total + nn(halves(up, 1), downs[...]), parts)


def rms_factor(x):
    return lax.rsqrt(jnp.mean(x * x, axis=-1, keepdims=True) + epsilon)


def rms_back(x, gain, grads):
    factor = rms_factor(x)
    unit = x * factor
    scaled = grads * gain
    return factor * (scaled - unit * jnp.mean(unit * scaled, axis=-1, keepdims=True))


def hidden_body(nat, near, beside, across, tokens, gain, hidden, normed):
    total = near[...].astype(f32) + beside[...].astype(f32) + across[...].astype(f32)
    hidden[...] = tokens[...].astype(f32) + total
    normed[...] = (hidden[...] * rms_factor(hidden[...]) * gain[...]).astype(bf16)


def grad_hidden_body(nat, near, beside, across, cotangent, hidden, gain, grad, rounded):
    total = near[...].astype(f32) + beside[...].astype(f32) + across[...].astype(f32)
    grad[...] = cotangent[...].astype(f32) + rms_back(hidden[...], gain[...], total)
    rounded[...] = grad[...].astype(bf16)


def grad_tokens_body(nat, near, beside, across, tokens, grad, gain, out):
    total = near[...].astype(f32) + beside[...].astype(f32) + across[...].astype(f32)
    out[...] = (grad[...] + rms_back(tokens[...].astype(f32), gain[...], total)).astype(bf16)


def on_own_rows(body, nat, near, beside, across, placed, owned, gain, out_types):
    rows, model = near.shape
    steps = 2
    block = pl.BlockSpec((rows // steps, model), lambda i, nat: (i, 0))
    return pl.pallas_call(
        body,
        grid_spec=pltpu.PrefetchScalarGridSpec(
            num_scalar_prefetch=1,
            grid=(steps,),
            in_specs=[block] * 3
            + [pl.BlockSpec((rows // steps, model), lambda i, nat: (nat[0] * steps + i, 0))]
            + [block] * len(owned)
            + [whole((1, model))],
            out_specs=[block] * len(out_types),
        ),
        out_shape=[jax.ShapeDtypeStruct((rows, model), x) for x in out_types],
        compiler_params=params(BIG),
        cost_estimate=SMALL,
        name="own_rows",
    )(nat, near, beside, across, placed, *owned, gain)


def place_body(count, nat, *refs):
    quarters, (out, held, sems) = refs[:count], refs[-3:]
    step = pl.program_id(0)

    @pl.when(step == 0)
    def _():
        for copy in quarter_copies(quarters, held, sems):
            copy.start()

    out[...] = quarter_of(step, quarters, held, sems).astype(out.dtype)


def place(quarters, first, nat, dtype, earlier=()):
    count, (rows, width) = len(quarters), quarters[0].shape
    return pl.pallas_call(
        lambda *refs: place_body(count, *refs),
        grid_spec=pltpu.PrefetchScalarGridSpec(
            num_scalar_prefetch=1,
            grid=(count,),
            in_specs=[ANY] * (count + len(earlier)),
            out_specs=pl.BlockSpec((rows, width), lambda i, nat: (nat[first + i], 0)),
            scratch_shapes=[pltpu.VMEM((count, rows, width), bf16), pltpu.SemaphoreType.DMA((count,))],
        ),
        out_shape=jax.ShapeDtypeStruct((4 * rows, width), dtype),
        input_output_aliases={1 + count: 0} if earlier else {},
        compiler_params=params(BIG),
        cost_estimate=SMALL,
        name="place",
    )(nat, *quarters, *earlier)


def per_device(
    tokens,
    sequence_lengths,
    output_cotangent,
    query_weight,
    key_weight,
    value_weight,
    output_weight,
    gate_weight,
    up_weight,
    down_weight,
    attention_norm_gain,
    feedforward_norm_gain,
    query_adapter_down,
    key_adapter_down,
    value_adapter_down,
    output_adapter_up,
    query_adapter_up,
    key_adapter_up,
    value_adapter_up,
    output_adapter_down,
    feature_map_query,
    feature_map_key,
):
    rows, model = tokens.shape
    heads, head, rank = query_adapter_up.shape
    kv_heads = key_adapter_up.shape[0]
    group = heads // kv_heads
    q_width, kv_width = heads * head, kv_heads * head
    seq, ring = lax.axis_size("seq"), lax.axis_size("dp") * lax.axis_size("seq")
    here = lax.axis_index("seq")
    chunks = rows // CHUNK
    ext = -(-(rows + WIN) // CHUNK) * CHUNK
    quarter = rows // 4

    core, far = lax.axis_index("tensor") % 2, lax.axis_index("tensor") // 2
    nat = jnp.stack([core * 2 + far, (1 - core) * 2 + far, core * 2 + 1 - far, (1 - core) * 2 + 1 - far]).astype(i32)

    clock = Clock()
    pack = lambda q, k, v, o: jnp.concatenate([q, k, v, o.T], axis=1)
    attn_chain = Chain(clock, 0, pack, query_weight, key_weight, value_weight, output_weight)
    attn_chain.step()
    offsets = attn_chain.offsets
    n_pieces = offsets.shape[0]
    assert sum(map(sum, FFN_UNITS)) == gate_weight.shape[1]

    def turn(part):
        for chain in chains[part]:
            chain.step()


    ladder = jnp.exp(jnp.arange(head // 2).astype(f32) * (-2.0 * math.log(rope_base) / head))[:, None]
    tables = [((head // 2, rows), f32)] * 2 + [((head // 2, ext), f32)] * 2
    tables += [((1, rows), i32), ((ext, 1), i32), ((1, ext), i32)]
    scalars = [((chunks + 1,), i32), ((seq - 1,), f32), ((seq - 1,), f32)]
    cos_q, sin_q, cos_k, sin_k, q_doc, doc_col, doc_row, last_docs, passed_before, passed_after = pl.pallas_call(
        lambda *refs: tables_body(seq, *refs),
        grid_spec=pltpu.PrefetchScalarGridSpec(
            num_scalar_prefetch=2,
            grid=(1,),
            in_specs=[whole(ladder.shape)],
            out_specs=[whole(x) for x, _ in tables] + [pl.BlockSpec(memory_space=pltpu.SMEM)] * 3,
        ),
        out_shape=[jax.ShapeDtypeStruct(x, d) for x, d in tables + scalars],
        compiler_params=params(32),
        cost_estimate=SMALL,
        name="tables",
    )(sequence_lengths[0], here[None].astype(i32), ladder)
    q_doc, doc_col, doc_row, last_docs, passed_before, passed_after = clock.wait(
        q_doc, doc_col, doc_row, last_docs, passed_before, passed_after
    )
    attn_chain.step()

    halo = shifted(clock.tie(tokens)[rows - WIN :], "seq", 1)
    attn_chain.step()
    (halo,) = clock.wait(halo)
    gain_attn = attention_norm_gain.astype(f32)[None, :]
    gain_mlp = feedforward_norm_gain.astype(f32)[None, :]
    downs = jnp.concatenate([query_adapter_down, key_adapter_down, value_adapter_down], axis=1)
    normed, low = pl.pallas_call(
        norm_body,
        grid_spec=pltpu.PrefetchScalarGridSpec(
            num_scalar_prefetch=0,
            grid=(1,),
            in_specs=[ANY, whole((WIN, model)), whole((1, model)), whole((model, 3 * rank))],
            out_specs=[whole((ext, model)), whole((ext, 3 * rank))],
            scratch_shapes=[pltpu.VMEM((ext, model), bf16), pltpu.SemaphoreType.DMA((4,))],
        ),
        out_shape=[jax.ShapeDtypeStruct((ext, model), bf16), jax.ShapeDtypeStruct((ext, 3 * rank), f32)],
        compiler_params=params(BIG),
        cost_estimate=SMALL,
        name="norm",
    )(clock.tie(tokens), halo, gain_attn, downs)
    normed, low = clock.wait(normed, low)
    attn_chain.step()
    all_units = [x for part in FFN_UNITS for x in part]
    pack_in = (
        gate_weight, up_weight, down_weight, query_adapter_up, key_adapter_up, value_adapter_up,
        feature_map_query, feature_map_key, output_adapter_up,
    )
    pack_out = [(gate_weight.shape[0], 3 * x) for x in all_units] + [
        (q_width + 2 * kv_width, 3 * rank),
        (q_width + 2 * kv_width, 6 * rank),
        (kv_heads, group * head, group * head),
        (kv_width, kv_width),
        (model, rank),
    ]
    packed = pl.pallas_call(
        lambda *refs: pack_body(all_units, *refs),
        grid_spec=pltpu.PrefetchScalarGridSpec(
            num_scalar_prefetch=0,
            grid=(1,),
            in_specs=[whole(x.shape) for x in pack_in],
            out_specs=[whole(x) for x in pack_out],
        ),
        out_shape=[jax.ShapeDtypeStruct(x, bf16) for x in pack_out],
        compiler_params=params(BIG),
        cost_estimate=SMALL,
        name="pack",
    )(clock.tie(gate_weight), *pack_in[1:])
    *packed, ups, ups_twice, maps_q, maps_k, o_up = clock.wait(*packed)
    chains = [[Chain(clock, 1, lambda x: x, packed[2 * i]), Chain(clock, -1, lambda x: x, packed[2 * i + 1])] for i in range(2)]
    for _ in range(ring - 5):
        attn_chain.step()
    attn_pieces = attn_chain.pieces()
    turn(0)

    sems = pltpu.SemaphoreType.DMA((n_pieces,))
    qkv_width = q_width + 2 * kv_width
    held_qkv = pltpu.VMEM((model, qkv_width), bf16)
    held_o = pltpu.VMEM((model, q_width), bf16)

    dims = (rows, ext, q_width, kv_width, head, n_pieces, chunks)
    shapes = [
        ((q_width, rows), bf16),
        ((2 * q_width, rows), bf16),
        ((ext, kv_width), bf16),
        ((kv_width, ext), bf16),
        ((ext, kv_width), bf16),
        ((kv_heads * AUG, ext), bf16),
        ((ext, 2 * kv_width), bf16),
        ((2 * kv_width, ext), bf16),
        ((kv_heads, AUG, 2 * head), f32),
    ]
    prep_in = (normed, low, ups_twice, cos_q, sin_q, cos_k, sin_k, maps_q, maps_k, doc_row)
    q_t, phi_q, k_n, k_t, v_n, v_a, phi_kn, phi_kt, contrib = pl.pallas_call(
        lambda *refs: prep_body(dims, *refs),
        grid_spec=pltpu.PrefetchScalarGridSpec(
            num_scalar_prefetch=2,
            grid=(1,),
            in_specs=[whole(x.shape) for x in prep_in] + [ANY] * n_pieces,
            out_specs=[whole(s) for s, _ in shapes],
            scratch_shapes=[held_qkv, sems],
        ),
        out_shape=[jax.ShapeDtypeStruct(s, d) for s, d in shapes],
        compiler_params=params(56),
        cost_estimate=SMALL,
        name="prep",
    )(clock.tie(offsets), last_docs, *prep_in, *attn_pieces)
    (contrib,) = clock.wait(contrib)
    turn(0)

    coming = clock.wait(*[shifted(contrib, "seq", by) for by in range(1, seq)])
    column = lambda r: pl.BlockSpec((r, CHUNK), lambda c, *_: (0, c))
    att, att_t, totals, states = pl.pallas_call(
        lambda *refs: forward_body((kv_heads, group, head), *refs),
        grid_spec=pltpu.PrefetchScalarGridSpec(
            num_scalar_prefetch=2,
            grid=(chunks,),
            in_specs=[
                column(q_width),
                column(2 * q_width),
                whole(k_n.shape),
                whole(v_a.shape),
                whole(phi_kn.shape),
                whole(doc_col.shape),
                whole(doc_row.shape),
                column(1),
            ]
            + [whole(contrib.shape)] * len(coming),
            out_specs=[
                pl.BlockSpec((CHUNK, q_width), lambda c, *_: (c, 0)),
                column(q_width),
                column(heads),
                pl.BlockSpec((1, kv_heads, 2 * head, AUG), lambda c, *_: (c, 0, 0, 0)),
            ],
            scratch_shapes=[pltpu.VMEM(contrib.shape, f32)],
        ),
        out_shape=[
            jax.ShapeDtypeStruct((rows, q_width), bf16),
            jax.ShapeDtypeStruct((q_width, rows), f32),
            jax.ShapeDtypeStruct((heads, rows), f32),
            jax.ShapeDtypeStruct((chunks, kv_heads, 2 * head, AUG), bf16),
        ],
        compiler_params=params(BIG),
        cost_estimate=SMALL,
        name="attend",
    )(clock.tie(last_docs), passed_before, q_t, phi_q, k_n, v_a, phi_kn, doc_col, doc_row, q_doc, *coming)
    att = clock.tie(att)
    turn(0)

    o_down = output_adapter_down.reshape(q_width, rank)
    o_up_t = jnp.concatenate([output_adapter_up.T, output_adapter_up.T], axis=0)
    one_quarter = jax.ShapeDtypeStruct((quarter, model), bf16)

    *o_parts, lowered = pl.pallas_call(
        lambda *refs: o_body(n_pieces, qkv_width, *refs),
        grid_spec=pltpu.PrefetchScalarGridSpec(
            num_scalar_prefetch=2,
            grid=(4,),
            in_specs=[
                pl.BlockSpec((quarter, q_width), lambda i, off, nat: (nat[3 - i], 0)),
                whole(o_down.shape),
                whole(o_up_t.shape),
            ]
            + [ANY] * n_pieces,
            out_specs=[whole((quarter, model))] * 4
            + [pl.BlockSpec((quarter, rank), lambda i, off, nat: (nat[3 - i], 0))],
            scratch_shapes=[held_o, sems],
        ),
        out_shape=[one_quarter] * 4 + [jax.ShapeDtypeStruct((rows, rank), f32)],
        compiler_params=params(BIG),
        cost_estimate=SMALL,
        name="project",
    )(clock.tie(offsets), nat, att, o_down, o_up_t, *attn_pieces)
    o_far0, o_far1, o_near0, o_near1 = clock.wait(*o_parts)
    turn(0)
    o_far0, o_near0 = clock.wait(o_far0, o_near0)
    beside = exchange(o_far0, "tensor", 1)
    beside_near = exchange(o_near0, "tensor", 1)
    beside, beside_near = clock.wait(beside, beside_near)
    o_far = clock.tie((o_far1.astype(f32) + beside.astype(f32)).astype(bf16))
    across = exchange(o_far, "tensor", 2)
    turn(0)
    (across,) = clock.wait(across)
    beside = beside_near
    hidden, normed_mlp = on_own_rows(
        hidden_body, clock.tie(nat), o_near1, beside, across, tokens, (), gain_mlp, (f32, bf16)
    )
    hidden, normed_mlp = clock.wait(hidden, normed_mlp)
    for _ in range(ring - 7):
        turn(0)
    normed_mlp = clock.tie(normed_mlp)
    across, beside = exchange(normed_mlp, "tensor", 2), exchange(normed_mlp, "tensor", 1)
    (beside,) = clock.wait(beside)
    turn(0)
    (across,) = clock.wait(across)
    for chain in chains[0]:
        chain.settle()
    turn(1)
    last = clock.tie(exchange(clock.tie(across), "tensor", 1))
    normed_mlp = [normed_mlp, beside, across, last]

    def ffn(part, which, quarters, sums):
        units, last = FFN_UNITS[part][which], part == len(FFN_UNITS) - 1
        lots = [chain.pieces() for chain in chains[part][which]]
        sizes = tuple(map(len, lots))
        pieces = [piece for lot in lots for piece in lot]
        ring_offsets = jnp.concatenate([chain.offsets for chain in chains[part][which]])
        first = quarters[0]
        summed = jax.ShapeDtypeStruct((2, quarter, model), f32)
        return pl.pallas_call(
            lambda *refs: ffn_body(sizes, units, bool(sums), last, *refs),
            grid_spec=pltpu.PrefetchScalarGridSpec(
                num_scalar_prefetch=2,
                grid=(2,),
                in_specs=[pl.BlockSpec((quarter, model), lambda i, off, nat: (nat[first - i], 0))]
                + [ANY] * (2 + len(pieces) + len(sums)),
                out_specs=[ANY] * (4 if last else 2),
                scratch_shapes=[
                    pltpu.VMEM((2, quarter, model), bf16),
                    pltpu.SemaphoreType.DMA((2,)),
                    pltpu.VMEM((3, model, sum(units)), bf16),
                    pltpu.SemaphoreType.DMA((3, len(pieces))),
                    pltpu.VMEM((2, 2, quarter, model), bf16 if last else f32),
                    pltpu.SemaphoreType.DMA((2, 2)),
                ]
                + [pltpu.VMEM((2, 2, quarter, model), f32), pltpu.SemaphoreType.DMA((2, 2))] * bool(sums),
            ),
            out_shape=[one_quarter] * 4 if last else [summed] * 2,
            compiler_params=params(BIG),
            cost_estimate=SMALL,
            name="feed_forward",
        )(clock.tie(ring_offsets), nat, output_cotangent, *[normed_mlp[q] for q in quarters], *pieces, *sums)

    sums_far = sums_near = ()
    up, down, both = slice(0, 1), slice(1, 2), slice(0, 2)
    for way in (up, down):
        sums_far = clock.wait(*ffn(0, way, (3, 2), sums_far))
        turn(1)
        sums_near = clock.wait(*ffn(0, way, (1, 0), sums_near))
        turn(1)
    for _ in range(ring - 6):
        turn(1)
    gn_far0, gn_far1, mlp_far0, mlp_far1 = ffn(1, both, (3, 2), sums_far)
    gn_far0, mlp_far0 = clock.wait(gn_far0, mlp_far0)
    beside = exchange(gn_far0, "tensor", 1)
    mlp_beside_far = exchange(mlp_far0, "tensor", 1)
    (beside,) = clock.wait(beside)
    across = exchange(clock.tie((gn_far1.astype(f32) + beside.astype(f32)).astype(bf16)), "tensor", 2)
    gn_near0, gn_near1, mlp_near0, mlp_near1 = ffn(1, both, (1, 0), sums_near)
    gn_near0, mlp_near0 = clock.wait(gn_near0, mlp_near0)
    across, gn_near0 = clock.wait(across, gn_near0)
    beside = exchange(gn_near0, "tensor", 1)
    (beside,) = clock.wait(beside)
    grad_hidden, branch = on_own_rows(
        grad_hidden_body, clock.tie(nat), gn_near1, beside, across, output_cotangent, (hidden,), gain_mlp, (f32, bf16)
    )
    grad_hidden, branch = clock.wait(grad_hidden, branch)
    across, beside = exchange(branch, "tensor", 2), exchange(branch, "tensor", 1)
    mlp_beside = exchange(clock.tie(mlp_near0), "tensor", 1)
    (beside,) = clock.wait(beside)

    o_down_t = jnp.concatenate([o_down.T, o_down.T], axis=0)
    sizes = [((q_width, rows), bf16), ((heads, rows), f32), ((rows, rank), f32), ((kv_heads, 2 * head, AUG), f32)]

    def go_part(first, quarters, earlier):
        by_quarter = lambda r: pl.BlockSpec((r, quarter), lambda i, off, nat, before: (0, nat[first + i]))
        late = bool(earlier)
        return pl.pallas_call(
            lambda *refs: go_body((n_pieces, qkv_width, kv_heads, group, head, late), *refs),
            grid_spec=pltpu.PrefetchScalarGridSpec(
                num_scalar_prefetch=3,
                grid=(2,),
                in_specs=[
                    whole((model, rank)),
                    whole(o_down_t.shape),
                    by_quarter(q_width),
                    by_quarter(heads),
                    by_quarter(2 * q_width),
                    by_quarter(1),
                ]
                + [ANY] * (2 + n_pieces)
                + ([ANY] * 3 + [whole(sizes[3][0])]) * late,
                out_specs=[
                    by_quarter(q_width),
                    by_quarter(heads),
                    pl.BlockSpec((quarter, rank), lambda i, off, nat, before: (nat[first + i], 0)),
                    whole(sizes[3][0]),
                ],
                scratch_shapes=[
                    pltpu.VMEM((2, quarter, model), bf16),
                    pltpu.SemaphoreType.DMA((2,)),
                    held_o,
                    sems,
                ],
            ),
            out_shape=[jax.ShapeDtypeStruct(s, d) for s, d in sizes],
            input_output_aliases={11 + n_pieces + i: i for i in range(3)} if late else {},
            compiler_params=params(BIG),
            cost_estimate=SMALL,
            name="project_back",
        )(
            clock.tie(offsets), nat, last_docs, o_up, o_down_t, att_t, totals, phi_q, q_doc,
            *quarters, *attn_pieces, *earlier,
        )

    near = clock.wait(*go_part(0, (branch, beside), ()))
    mlp_beside, mlp_beside_far = clock.wait(mlp_beside, mlp_beside_far)
    mlp_far = clock.tie((mlp_far1.astype(f32) + mlp_beside_far.astype(f32)).astype(bf16))
    mlp_near = clock.tie(hidden + (mlp_near1.astype(f32) + mlp_beside.astype(f32)))
    (across,) = clock.wait(across)
    last = clock.tie(exchange(across, "tensor", 1))
    mlp_across = exchange(clock.tie(mlp_far), "tensor", 2)
    branch = [branch, beside, across, last]
    numer, grad_totals, up_product, dstate = clock.wait(*go_part(2, branch[2:], near))

    coming = [shifted(dstate, "seq", -by) for by in range(1, seq)]

    back_column = lambda r: pl.BlockSpec((r, CHUNK), lambda c, *_: (0, chunks - 1 - c))
    back_in = (
        (q_t, back_column(q_width)),
        (phi_q, back_column(2 * q_width)),
        (numer, back_column(q_width)),
        (grad_totals, back_column(heads)),
        (k_n, None),
        (k_t, None),
        (v_n, None),
        (v_a, None),
        (phi_kn, None),
        (phi_kt, None),
        (doc_col, None),
        (doc_row, None),
        (q_doc, back_column(1)),
        (states, pl.BlockSpec((1, kv_heads, 2 * head, AUG), lambda c, *_: (chunks - 1 - c, 0, 0, 0))),
        (cos_q, back_column(head // 2)),
        (sin_q, back_column(head // 2)),
        (maps_q, None),
    )
    g_q, g_kt, g_vt, g_phi, g_map_q = pl.pallas_call(
        lambda *refs: backward_body((kv_heads, group, head, chunks), *refs),
        grid_spec=pltpu.PrefetchScalarGridSpec(
            num_scalar_prefetch=1,
            grid=(chunks,),
            in_specs=[whole(x.shape) if spec is None else spec for x, spec in back_in],
            out_specs=[
                pl.BlockSpec((CHUNK, q_width), lambda c, *_: (chunks - 1 - c, 0)),
                whole((kv_width, ext)),
                whole((kv_width, ext)),
                whole((2 * kv_width, ext)),
                whole((kv_heads, group * head, group * head)),
            ],
            scratch_shapes=[pltpu.VMEM(dstate.shape, f32)],
        ),
        out_shape=[
            jax.ShapeDtypeStruct((rows, q_width), bf16),
            jax.ShapeDtypeStruct((kv_width, ext), f32),
            jax.ShapeDtypeStruct((kv_width, ext), f32),
            jax.ShapeDtypeStruct((2 * kv_width, ext), f32),
            jax.ShapeDtypeStruct((kv_heads, group * head, group * head), f32),
        ],
        compiler_params=params(52),
        cost_estimate=SMALL,
        name="attend_back",
    )(clock.tie(last_docs), *[x for x, _ in back_in])

    g_q, g_kt, g_vt, g_phi, g_map_q = clock.wait(g_q, g_kt, g_vt, g_phi, g_map_q)
    coming = clock.wait(*coming)
    (mlp_across,) = clock.wait(mlp_across)
    out_rows = clock.tie((mlp_near + mlp_across.astype(f32)).astype(bf16))
    out_across, out_beside = exchange(out_rows, "tensor", 2), exchange(out_rows, "tensor", 1)
    g_own, g_halo, g_map_k = pl.pallas_call(
        lambda *refs: keys_back_body((kv_heads, head, chunks, rows), *refs),
        grid_spec=pltpu.PrefetchScalarGridSpec(
            num_scalar_prefetch=2,
            grid=(1,),
            in_specs=[whole(x.shape) for x in (g_kt, g_vt, g_phi, v_a, phi_kt, k_t, doc_row, maps_k, *coming)],
            out_specs=[whole((2 * kv_width, rows)), whole((2 * kv_width, CHUNK)), whole((kv_width, kv_width))],
        ),
        out_shape=[
            jax.ShapeDtypeStruct((2 * kv_width, rows), f32),
            jax.ShapeDtypeStruct((2 * kv_width, CHUNK), f32),
            jax.ShapeDtypeStruct((kv_width, kv_width), f32),
        ],
        compiler_params=params(BIG),
        cost_estimate=SMALL,
        name="keys_back",
    )(clock.tie(last_docs), passed_after, g_kt, g_vt, g_phi, v_a, phi_kt, k_t, doc_row, maps_k, *coming)

    g_own, g_halo, g_map_k = clock.wait(g_own, g_halo, g_map_k)
    g_halo = shifted(g_halo, "seq", -1)
    o_in = (lowered, att, up_product, *branch)
    g_o_up, g_o_down = pl.pallas_call(
        adapter_o_body,
        grid_spec=pltpu.PrefetchScalarGridSpec(
            num_scalar_prefetch=1,
            grid=(1,),
            in_specs=[whole(x.shape) for x in o_in],
            out_specs=[whole((rank, model)), whole((q_width, rank))],
        ),
        out_shape=[jax.ShapeDtypeStruct((rank, model), f32), jax.ShapeDtypeStruct((q_width, rank), f32)],
        compiler_params=params(BIG),
        cost_estimate=SMALL,
        name="adapter_o",
    )(clock.tie(nat), *o_in)
    g_o_up, g_o_down, g_halo = clock.wait(g_o_up, g_o_down, g_halo)

    downs_t = jnp.concatenate([downs.T, downs.T], axis=0)

    by_rows = lambda w: pl.BlockSpec((quarter, w), lambda i, off, nat: (nat[3 - i], 0))
    by_columns = lambda r: pl.BlockSpec((r, quarter), lambda i, off, nat: (0, nat[3 - i]))
    gn_parts = pl.pallas_call(
        lambda *refs: gn_body(n_pieces, *refs),
        grid_spec=pltpu.PrefetchScalarGridSpec(
            num_scalar_prefetch=2,
            grid=(4,),
            in_specs=[
                by_rows(q_width),
                by_columns(2 * kv_width),
                whole(g_halo.shape),
                by_columns(head // 2),
                by_columns(head // 2),
                whole(ups.shape),
                whole(downs_t.shape),
            ]
            + [ANY] * n_pieces,
            out_specs=[whole((quarter, model))] * 4,
            scratch_shapes=[held_qkv, sems],
        ),
        out_shape=[one_quarter] * 4,
        compiler_params=params(BIG),
        cost_estimate=SMALL,
        name="norm_back",
    )(clock.tie(offsets), nat, g_q, g_own, g_halo, cos_q, sin_q, ups, downs_t, *attn_pieces)
    gn_far0, gn_far1, gn_near0, gn_near1 = clock.wait(*gn_parts)
    out_across, out_beside, gn_far0, gn_near0 = clock.wait(out_across, out_beside, gn_far0, gn_near0)
    beside, beside_near = exchange(gn_far0, "tensor", 1), exchange(gn_near0, "tensor", 1)
    beside, beside_near = clock.wait(beside, beside_near)
    gn_far = clock.tie((gn_far1.astype(f32) + beside.astype(f32)).astype(bf16))
    across = exchange(gn_far, "tensor", 2)

    adapters_in = (g_q, g_own, g_halo, cos_q, sin_q, ups, low[WIN : WIN + rows], normed, g_o_up, g_o_down, g_map_q, g_map_k)
    tall = head // ring
    tiles = 4 * rank // 8 * (model // ring // 128)
    in_tiles = tall == 8 and rank == 8 and model // ring % 128 == 0 and 2 * head == 128
    if in_tiles:
        sizes = [((ring, heads + kv_heads + tiles, tall, 2 * head), f32)]
    else:
        sizes = [((heads + kv_heads, head, 2 * head), f32), ((4 * rank, model), f32)]
    parts = pl.pallas_call(
        lambda *refs: adapters_body((rows, WIN, head, rank), *refs),
        grid_spec=pltpu.PrefetchScalarGridSpec(
            num_scalar_prefetch=0,
            grid=(1,),
            in_specs=[whole(x.shape) for x in adapters_in],
            out_specs=[whole(x) for x, _ in sizes],
        ),
        out_shape=[jax.ShapeDtypeStruct(x, d) for x, d in sizes],
        compiler_params=params(BIG),
        cost_estimate=SMALL,
        name="adapters",
    )(clock.tie(adapters_in[0]), *adapters_in[1:])
    if not in_tiles:
        parts = [
            parts[0].reshape(heads + kv_heads, ring, tall, 2 * head).transpose(1, 0, 2, 3),
            parts[1].reshape(4 * rank, ring, model // ring).transpose(1, 0, 2),
        ]
    parts = clock.wait(*parts)

    def halved(x, axis, half, bit, over=0, sent_as=f32):
        x = x.reshape(x.shape[:over] + (2, half) + x.shape[over + 1 :])
        send = lax.dynamic_index_in_dim(x, 1 - bit, over, keepdims=False)
        return lax.dynamic_index_in_dim(x, bit, over, keepdims=False), exchange(send.astype(sent_as), axis, half)

    def summed_over(axis, size, xs):
        while size > 1:
            half = size // 2
            both = [halved(x, axis, half, (lax.axis_index(axis) // half) % 2, 0, bf16) for x in xs]
            coming = clock.wait(*[coming for _, coming in both])
            xs = [kept + x.astype(f32) for (kept, _), x in zip(both, coming)]
            size = half
            yield xs

    dp = ring // seq
    parts = [x.reshape((dp, seq) + x.shape[1:]) for x in parts]
    for parts in summed_over("dp", dp, parts):
        pass
    along_seq = summed_over("seq", seq, clock.wait(*[x[0] for x in parts]))
    parts = next(along_seq)
    (across,) = clock.wait(across)
    (grad_rows,) = on_own_rows(
        grad_tokens_body, clock.tie(nat), gn_near1, beside_near, across, tokens, (grad_hidden,), gain_attn, (bf16,)
    )
    (grad_rows,) = clock.wait(grad_rows)
    across, beside = exchange(grad_rows, "tensor", 2), exchange(grad_rows, "tensor", 1)
    out_last = clock.tie(exchange(out_across, "tensor", 1))
    (beside,) = clock.wait(beside)
    grad_tokens = clock.tie(place([grad_rows, beside], 0, nat, f32))
    for parts in along_seq:
        pass
    by_head, shared = parts[0][0], parts[-1][0]
    if in_tiles:
        by_head, shared = by_head[: heads + kv_heads], by_head[heads + kv_heads :]
        shared = shared.reshape(4 * rank // 8, -1, 8, 128).transpose(0, 2, 1, 3)
    kept, sent = halved(shared.reshape(4 * rank, 4, -1), "tensor", 2, far, 1)
    shared = kept.reshape(4 * rank, 2, -1)
    sent = sent.reshape(4 * rank, 2, -1)
    block_out = clock.tie(place([out_rows, out_beside, out_across, out_last], 0, nat, bf16))
    (across,) = clock.wait(across)
    last = exchange(across, "tensor", 1)
    kept, sent = halved(shared + clock.tie(sent), "tensor", 1, core, 1)
    (last,) = clock.wait(last)
    grad_tokens = clock.tie(place([across, last], 2, nat, f32, (grad_tokens,)))
    shared = (kept + clock.tie(sent)).reshape(4 * rank, -1).T
    of_q, of_kv = by_head[:heads], by_head[heads:]
    first, second = slice(head, head + rank), slice(head + rank, head + 2 * rank)
    out = [of_q[..., first], of_kv[..., first], of_kv[..., second], of_q[..., second], of_q[..., :head], of_kv[..., :head]]
    return (
        block_out,
        grad_tokens,
        shared[:, :rank] + clock.now.astype(f32),
        shared[:, rank : 2 * rank],
        shared[:, 2 * rank : 3 * rank],
        shared[:, 3 * rank :],
        *out,
    )


def solution(mesh):
    return jax.shard_map(
        per_device,
        mesh=mesh,
        in_specs=(
            P(("dp", "seq"), None),
            P("dp", None),
            P(("dp", "seq"), None),
            P(("dp", "seq"), "tensor"),
            P(("dp", "seq"), "tensor"),
            P(("dp", "seq"), "tensor"),
            P("tensor", ("dp", "seq")),
            P(("dp", "seq"), "tensor"),
            P(("dp", "seq"), "tensor"),
            P("tensor", ("dp", "seq")),
            P(),
            P(),
            P(),
            P(),
            P(),
            P(),
            P("tensor", None, None),
            P("tensor", None, None),
            P("tensor", None, None),
            P("tensor", None, None),
            P("tensor", None, None),
            P("tensor", None, None),
        ),
        out_specs=(
            P(("dp", "seq"), None),
            P(("dp", "seq"), None),
            P(("dp", "seq", "tensor"), None),
            P(("dp", "seq", "tensor"), None),
            P(("dp", "seq", "tensor"), None),
            P(("dp", "seq", "tensor"), None),
            P("tensor", ("dp", "seq"), None),
            P("tensor", ("dp", "seq"), None),
            P("tensor", ("dp", "seq"), None),
            P("tensor", ("dp", "seq"), None),
            P("tensor", ("dp", "seq"), None),
            P("tensor", ("dp", "seq"), None),
        ),
        check_vma=False,
    )
```

```python
import math

import jax
import jax.numpy as jnp
from jax import lax
from jax.experimental import pallas as pl
from jax.experimental.pallas import tpu as pltpu
from jax.sharding import PartitionSpec as P

WIN = 64
CHUNK = 128
AUG = 80
RING = 8
FFN_UNITS = ((512, 512), (512, 512))
BIG = 60

epsilon = 1e-05
rope_base = 500000.0
bf16, f32, i32 = jnp.bfloat16, jnp.float32, jnp.int32
MIB = 1 << 20


def nn(a, b):
    return lax.dot_general(a, b, (((1,), (0,)), ((), ())), preferred_element_type=f32)


def nt(a, b):
    return lax.dot_general(a, b, (((1,), (1,)), ((), ())), preferred_element_type=f32)


def tn(a, b):
    return lax.dot_general(a, b, (((0,), (0,)), ((), ())), preferred_element_type=f32)


def halves(x, axis):
    high = x.astype(bf16)
    return jnp.concatenate([high, (x - high.astype(f32)).astype(bf16)], axis=axis)


def exchange(x, axis, bit):
    count = lax.axis_size(axis)
    return lax.ppermute(x, axis, [(i, i ^ bit) for i in range(count)])


def shifted(x, axis, by):
    count = lax.axis_size(axis)
    return lax.ppermute(x, axis, [(i, i + by) for i in range(count) if 0 <= i + by < count])


def place_of(index, seq):
    row, col = index // seq, index % seq
    return row * seq + (col if row % 2 == 0 else seq - 1 - col)


def place_of_traced(index, seq):
    row, col = index // seq, index % seq
    return row * seq + jnp.where(row % 2 == 0, col, seq - 1 - col)


class Clock:
    def __init__(self):
        self.now = jnp.zeros((), i32)

    def wait(self, *arrays):
        *out, self.now = lax.optimization_barrier((*arrays, self.now))
        return out

    def tie(self, x):
        return self.wait(x)[0]


class Chain:
    def __init__(self, clock, way, pack, *blocks):
        block = pack(*clock.wait(*blocks))
        dp, seq = lax.axis_size("dp"), lax.axis_size("seq")
        self.clock, self.count = clock, dp * seq
        self.ringed = self.count <= RING
        rows = block.shape[0]
        if not self.ringed:
            self.lanes = [[lax.all_gather(block, ("dp", "seq"), axis=0, tiled=True)]]
            self.offsets = jnp.zeros((1,), i32)
            return
        order = [place_of(i, seq) for i in range(self.count)]
        up = [(order[i], order[(i + 1) % self.count]) for i in range(self.count)]
        down = [(j, i) for i, j in up]
        place = place_of_traced(lax.axis_index("dp") * seq + lax.axis_index("seq"), seq)
        steps = jnp.arange(self.count)
        came_up = place_of_traced((place - steps) % self.count, seq) * rows
        came_down = place_of_traced((place + steps) % self.count, seq) * rows
        if way:
            self.lanes, self.ways = [[block]], [up if way > 0 else down]
            self.offsets = (came_up if way > 0 else came_down).astype(i32)
        else:
            half = rows // 2
            self.lanes, self.ways = [[block[:half]], [block[half:]]], [up, down]
            self.offsets = jnp.concatenate([came_up, came_down + half]).astype(i32)

    def settle(self):
        if self.ringed:
            came = self.clock.wait(*[lane[-1] for lane in self.lanes])
            for lane, x in zip(self.lanes, came):
                lane[-1] = x

    def step(self):
        if self.ringed:
            for lane, way in zip(self.lanes, self.ways):
                (lane[-1],) = self.clock.wait(lane[-1])
                lane.append(lax.ppermute(lane[-1], ("dp", "seq"), way))

    def pieces(self):
        self.settle()
        return [piece for lane in self.lanes for piece in lane]


def load_pieces(pieces, offsets, held, sems, first=0):
    copies = [
        pltpu.make_async_copy(
            piece.at[:, pl.ds(first, held.shape[1])],
            held.at[pl.ds(pl.multiple_of(offsets[i], 16), piece.shape[0])],
            sems.at[i],
        )
        for i, piece in enumerate(pieces)
    ]
    for copy in copies:
        copy.start()
    for copy in copies:
        copy.wait()


def params(limit):
    return pltpu.CompilerParams(vmem_limit_bytes=limit * MIB)


SMALL = pl.CostEstimate(flops=1, bytes_accessed=1, transcendentals=0)


ANY = pl.BlockSpec(memory_space=pl.ANY)


def whole(shape):
    return pl.BlockSpec(shape, lambda *_: (0,) * len(shape))


def rope(x, cos, sin):
    width = 2 * cos.shape[0]
    half = width // 2
    out = []
    for at in range(0, x.shape[0], width):
        x1, x2 = x[at : at + half], x[at + half : at + width]
        out += [x1 * cos - x2 * sin, x2 * cos + x1 * sin]
    return jnp.concatenate(out, axis=0)


def hedgehog(a, width):
    out = []
    for at in range(0, a.shape[0], width):
        one = a[at : at + width]
        for e in (
            jnp.exp(one - jnp.max(one, axis=0, keepdims=True)),
            jnp.exp(jnp.min(one, axis=0, keepdims=True) - one),
        ):
            out.append(e * (1.0 / jnp.sum(e, axis=0, keepdims=True)))
    return jnp.concatenate(out, axis=0).astype(bf16)


def hedgehog_back(phi, grad, width):
    out = []
    for at in range(0, phi.shape[0], 2 * width):
        p1, p2 = phi[at : at + width].astype(f32), phi[at + width : at + 2 * width].astype(f32)
        d1, d2 = grad[at : at + width], grad[at + width : at + 2 * width]
        out.append(
            p1 * (d1 - jnp.sum(p1 * d1, axis=0, keepdims=True))
            - p2 * (d2 - jnp.sum(p2 * d2, axis=0, keepdims=True))
        )
    return jnp.concatenate(out, axis=0).astype(bf16)


def tables_body(seq, lengths, here, ladder, cos_q, sin_q, cos_k, sin_k, q_doc, doc_col, doc_row, last, before, after):
    rows, ext = q_doc.shape[1], doc_row.shape[1]
    ends = [lengths[0]]
    for i in range(1, lengths.shape[0]):
        ends.append(ends[-1] + lengths[i])

    def document(at):
        doc, start = 0, 0
        for end in ends:
            past = at >= end
            doc = doc + past.astype(i32)
            start = jnp.where(past, end, start)
        return jnp.where(at >= 0, doc, -1), at - start

    def angles(relative, cos, sin):
        angle = ladder[...] * relative.astype(f32)
        cos[...] = jnp.cos(angle)
        sin[...] = jnp.sin(angle)

    def passing(block):
        ahead = rows * block - WIN - 1
        return (document(ahead)[0] == document(ahead + rows)[0]).astype(f32)

    first = here[0] * rows
    q_doc[...], relative = document(first + lax.broadcasted_iota(i32, (1, rows), 1))
    angles(relative, cos_q, sin_q)
    index = lax.broadcasted_iota(i32, (1, ext), 1)
    doc, relative = document(first - WIN + index)
    doc_row[...] = jnp.where(index < rows + WIN, doc, -2)
    angles(relative, cos_k, sin_k)
    index = lax.broadcasted_iota(i32, (ext, 1), 0)
    doc_col[...] = jnp.where(index < rows + WIN, document(first - WIN + index)[0], -2)
    for i in range(last.shape[0]):
        last[i] = document(first - WIN - 1 + CHUNK * i)[0]
    earlier = later = jnp.float32(1.0)
    for by in range(seq - 1):
        before[by], after[by] = earlier, later
        earlier = earlier * passing(jnp.maximum(here[0] - by - 1, 0))
        later = later * passing(jnp.minimum(here[0] + by + 1, seq - 1))


def norm_body(tokens, halo, gain, downs, normed, low, held, sems):
    rows, window = tokens.shape[0], halo.shape[0]
    part = rows // 4

    def copy(i):
        return pltpu.make_async_copy(
            tokens.at[pl.ds(i * part, part)], held.at[pl.ds(window + i * part, part)], sems.at[i]
        )

    for i in range(4):
        copy(i).start()
    held[:window, :] = halo[...]
    held[window + rows :, :] = jnp.zeros((held.shape[0] - window - rows, held.shape[1]), bf16)
    for i in range(4):
        copy(i).wait()
        first = window + i * part if i else 0
        last = window + (i + 1) * part if i < 3 else held.shape[0]
        x = held[first:last, :].astype(f32)
        out = (x * rms_factor(x) * gain[...]).astype(bf16)
        normed[first:last, :] = out
        low[first:last, :] = nn(out, downs[...])


def pack_body(units, gate, up, down, q_up, k_up, v_up, map_q, map_k, o_up, *outs):
    packed, (ups, twice, maps_q, maps_k, o_up_out) = outs[:-5], outs[-5:]
    o_up_out[...] = o_up[...]
    at = 0
    for size, out in zip(units, packed):
        out[:, :size] = gate[:, at : at + size]
        out[:, size : 2 * size] = up[:, at : at + size]
        out[:, 2 * size :] = down[at : at + size, :].T
        at += size
    head, rank = q_up.shape[1:]
    at = 0
    for i, x in enumerate((q_up, k_up, v_up)):
        for h in range(x.shape[0]):
            row = jnp.concatenate(
                [jnp.zeros((head, rank), bf16)] * i + [x[h]] + [jnp.zeros((head, rank), bf16)] * (2 - i), axis=1
            )
            ups[at : at + head, :] = row
            twice[at : at + head, :] = jnp.concatenate([row, row], axis=1)
            at += head
    maps_q[...] = jnp.zeros(maps_q.shape, bf16)
    maps_k[...] = jnp.zeros(maps_k.shape, bf16)
    group = map_q.shape[0] // maps_q.shape[0]
    for h in range(map_q.shape[0]):
        mine = slice(h % group * head, (h % group + 1) * head)
        maps_q[h // group, mine, mine] = map_q[h].astype(f32).T.astype(bf16)
    for h in range(map_k.shape[0]):
        mine = slice(h * head, (h + 1) * head)
        maps_k[mine, mine] = map_k[h].astype(f32).T.astype(bf16)


def prep_body(dims, offsets, last_docs, nx, low, ups, cos_q, sin_q, cos_k, sin_k, map_q, map_k, doc_row, *rest):
    tokens, ext, q_width, kv_width, head, n_pieces, chunks = dims
    pieces, rest = rest[:n_pieces], rest[n_pieces:]
    q_t, phi_q, k_n, k_t, v_n, v_a, phi_kn, phi_kt, contrib, held, sems = rest
    load_pieces(pieces, offsets, held, sems)
    kv_heads = kv_width // head
    step = ext // 3
    v_a[...] = jnp.zeros(v_a.shape, bf16)
    for at in range(0, ext, step):
        rows = pl.ds(at, step)
        raw = nn(nx[rows, :], held[:, q_width:]) + nt(halves(low[rows, :], 1), ups[q_width:, :])
        v = raw[:, kv_width:].astype(bf16)
        v_n[rows, :] = v
        v_tr = raw[:, kv_width:].T.astype(bf16)
        for k in range(kv_heads):
            v_a[k * AUG : k * AUG + head, rows] = v_tr[k * head : (k + 1) * head]
            v_a[k * AUG + head : (k + 1) * AUG, rows] = (
                lax.broadcasted_iota(i32, (AUG - head, step), 0) < 2
            ).astype(f32).astype(bf16)
        k_rot = rope(raw[:, :kv_width].T, cos_k[:, rows], sin_k[:, rows])
        k_bf = k_rot.astype(bf16)
        k_t[:, rows] = k_bf
        k_n[rows, :] = k_rot.T.astype(bf16)
        phi = hedgehog(nn(map_k[...], k_bf), head)
        phi_kt[:, rows] = phi
        phi_kn[rows, :] = phi.astype(f32).T.astype(bf16)
    incl = (doc_row[:, :tokens] == last_docs[chunks]).astype(f32).astype(bf16)
    for k in range(kv_heads):
        masked = v_a[k * AUG : (k + 1) * AUG, :tokens] * incl
        contrib[k] = nn(masked, phi_kn[:tokens, k * 2 * head : (k + 1) * 2 * head])
    step = tokens // 2
    group = q_width // kv_heads
    for at in range(0, tokens, step):
        rows = pl.ds(at, step)
        raw = nn(nx[pl.ds(WIN + at, step), :], held[:, :q_width])
        raw = raw + nt(halves(low[pl.ds(WIN + at, step), :], 1), ups[:q_width, :])
        q_bf = rope(raw.T, cos_q[:, rows], sin_q[:, rows]).astype(bf16)
        q_t[:, rows] = q_bf
        for k in range(kv_heads):
            logits = nn(map_q[k], q_bf[k * group : (k + 1) * group])
            phi_q[2 * k * group : 2 * (k + 1) * group, rows] = hedgehog(logits, head)


def masks(q_doc, k_doc, heads):
    keys = CHUNK + WIN
    j = lax.broadcasted_iota(i32, (keys, CHUNK), 0)
    t = lax.broadcasted_iota(i32, (keys, CHUNK), 1)
    same = k_doc == q_doc
    win = same & (j > t) & (j <= t + WIN)
    lin = (same & (j <= t))[:CHUNK]
    win_f = jnp.concatenate([win.astype(f32)] * heads, axis=1)
    lin_f = jnp.concatenate([lin.astype(f32)] * heads, axis=1)
    return win_f > 0.5, lin_f > 0.5


def side(ref, first, count, size):
    return jnp.concatenate([ref[first + g * size : first + (g + 1) * size, :] for g in range(count)], axis=1)


def window_weights(q, phi_q, k_win, phi_k, win, lin, scale):
    scores = nn(k_win, q)
    weights_win = jnp.where(win, jnp.exp(scores * scale), 0.0)
    linear = jnp.where(lin, nn(phi_k, phi_q), 0.0)
    return weights_win, jnp.concatenate([weights_win[:CHUNK] + linear, weights_win[CHUNK:]], axis=0)


def forward_body(dims, last_docs, factors, q_t, phi_q, k_n, v_a, phi_kn, doc_col, doc_row, q_doc, *rest):
    kv_heads, group, head = dims
    earlier, (att, att_t, totals, states, state) = rest[:-5], rest[-5:]
    chunk = pl.program_id(0)
    start = pl.multiple_of(chunk * CHUNK, CHUNK)

    @pl.when(chunk == 0)
    def _():
        total = jnp.zeros(state.shape, f32)
        for i, x in enumerate(earlier):
            total = total + factors[i] * x[...]
        state[...] = total

    keys = CHUNK + WIN
    win, lin = masks(q_doc[...], doc_col[pl.ds(start, keys), :], group)
    use = (q_doc[...] == last_docs[chunk]).astype(f32)
    use = jnp.concatenate([use] * group, axis=1)
    incl = (doc_row[:, pl.ds(start, CHUNK)] == last_docs[chunk + 1]).astype(f32).astype(bf16)
    passing = (last_docs[chunk] == last_docs[chunk + 1]).astype(f32)
    scale = head**-0.5
    out = []
    for k in range(kv_heads):
        q = side(q_t, k * group * head, group, head)
        phi = side(phi_q, 2 * k * group * head, group, 2 * head)
        k_win = k_n[pl.ds(start, keys), k * head : (k + 1) * head]
        phi_k = phi_kn[pl.ds(start, CHUNK), 2 * k * head : 2 * (k + 1) * head]
        v_win = v_a[k * AUG : (k + 1) * AUG, pl.ds(start, 2 * CHUNK)]
        _, weights = window_weights(q, phi, k_win, phi_k, win, lin, scale)
        before = state[k]
        from_state = nn(before.astype(bf16), phi) * use
        total = jnp.sum(weights, axis=0, keepdims=True) + from_state[head : head + 1]
        numer = nn(v_win[:, :keys], weights.astype(bf16))[:head] + from_state[:head]
        attended = numer * (1.0 / total)
        for g in range(group):
            out.append(attended[:, g * CHUNK : (g + 1) * CHUNK])
            totals[k * group + g : k * group + g + 1, :] = total[:, g * CHUNK : (g + 1) * CHUNK]
        states[0, k] = before.T.astype(bf16)
        state[k] = nn(v_win[:, :CHUNK] * incl, phi_k) + passing * before
    attended = jnp.concatenate(out, axis=0)
    att_t[...] = attended
    att[...] = attended.T.astype(bf16)


def store_at(step, value, outs):
    for i, out in enumerate(outs):

        @pl.when(step == i)
        def _(out=out):
            out[...] = value.astype(out.dtype)


def o_body(n_pieces, first, offsets, nat, att, down, up, *rest):
    pieces, parts, (lowered, held, sems) = rest[:n_pieces], rest[n_pieces:-3], rest[-3:]
    step = pl.program_id(0)

    @pl.when(step == 0)
    def _():
        load_pieces(pieces, offsets, held, sems, first)

    low = nn(att[...], down[...])
    lowered[...] = low
    store_at(step, nt(att[...], held[...]) + nn(halves(low, 1), up[...]), parts)


def quarter_copies(quarters, held, sems, first=0):
    return [pltpu.make_async_copy(x, held.at[first + i], sems.at[first + i]) for i, x in enumerate(quarters)]


def quarter_of(step, quarters, held, sems):
    for i, copy in enumerate(quarter_copies(quarters, held, sems)):

        @pl.when(step == i)
        def _(copy=copy):
            copy.wait()

    return held[step]


def ffn_body(lots, units, summed, last, offsets, nat, cot, *rest):
    count, n_out = sum(lots), 4 if last else 2
    quarters, pieces, rest = rest[:2], rest[2 : 2 + count], rest[2 + count :]
    sums, outs, rest = rest[: 2 * summed], rest[2 * summed : 2 * summed + n_out], rest[2 * summed + n_out :]
    rows, rows_sems, held, sems, out_held, out_sems, *rest = rest
    step = pl.program_id(0)

    def at_first(act):
        pl.when(step == 0)(act)

    starts = [sum(units[:i]) for i in range(len(units))]
    blocks = [(which, lot) for which in range(3) for lot in range(len(lots))]

    def copies(block):
        which, lot = block
        size = units[lot]
        return [
            pltpu.make_async_copy(
                pieces[i].at[:, pl.ds(which * size, size)],
                held.at[which, pl.ds(pl.multiple_of(offsets[i], 16), pieces[i].shape[0]), pl.ds(starts[lot], size)],
                sems.at[which, i],
            )
            for i in range(sum(lots[:lot]), sum(lots[: lot + 1]))
        ]

    def sum_copy(i, kind):
        return pltpu.make_async_copy(sums[kind].at[i], rest[0].at[i, kind], rest[1].at[i, kind])

    def out_copy(i, kind):
        out = outs[2 * (1 - kind) + i] if last else outs[kind].at[i]
        return pltpu.make_async_copy(out_held.at[i, kind], out, out_sems.at[i, kind])

    @at_first
    def _():
        for copy in quarter_copies(quarters[:1], rows, rows_sems) + copies(blocks[0]) + copies(blocks[1]):
            copy.start()
        for copy in quarter_copies(quarters[1:], rows, rows_sems, 1):
            copy.start()

    def product(x, index):
        @at_first
        def _():
            for copy in copies(blocks[index]):
                copy.wait()
            if index + 2 < len(blocks):
                for copy in copies(blocks[index + 2]):
                    copy.start()
            elif index + 2 == len(blocks) and summed:
                for i in range(2):
                    for kind in (1, 0):
                        sum_copy(i, kind).start()

        which, lot = blocks[index]
        return nn(x, held[which, :, starts[lot] : starts[lot] + units[lot]])

    n2 = quarter_of(step, quarters, rows, rows_sems)
    count = len(lots)
    gates = [product(n2, i) for i in range(count)]
    ups = [product(n2, count + i) for i in range(count)]
    grads = [product(cot[...], 2 * count + i) for i in range(count)]
    parts = [[], [], []]
    for gate, up, grad_act in zip(gates, ups, grads):
        s = 1.0 / (1.0 + jnp.exp(-gate))
        silu = gate * s
        parts[0].append((silu * up).astype(bf16))
        parts[1].append((grad_act * up * s * (1.0 + gate * (1.0 - s))).astype(bf16))
        parts[2].append((grad_act * silu).astype(bf16))
    act, grad_gate, grad_up = [jnp.concatenate(x, axis=1) for x in parts]

    def finish(kind, total):
        if summed:
            sum_copy(step, kind).wait()
            total = total + rest[0][step, kind]
        out_held[step, kind] = total.astype(out_held.dtype)
        for i in range(2):

            @pl.when(step == i)
            def _(i=i):
                out_copy(i, kind).start()

    finish(1, nt(grad_gate, held[0]) + nt(grad_up, held[1]))
    finish(0, nt(act, held[2]))

    @pl.when(step == 1)
    def _():
        for i in range(2):
            for kind in range(2):
                out_copy(i, kind).wait()


def go_body(dims, offsets, nat, before_doc, o_up, o_down, att_t, totals, phi_q, q_doc, *rest):
    n_pieces, first, kv_heads, group, head, later = dims
    quarters, pieces, rest = rest[:2], rest[2 : 2 + n_pieces], rest[2 + n_pieces :]
    earlier, rest = rest[: 4 * later], rest[4 * later :]
    numer, grad_totals, up_product, dstate, rows_held, rows_sems, held, sems = rest
    step = pl.program_id(0)

    @pl.when(step == 0)
    def _():
        for copy in quarter_copies(quarters, rows_held, rows_sems):
            copy.start()
        load_pieces(pieces, offsets, held, sems, first)
        dstate[...] = earlier[3][...] if later else jnp.zeros(dstate.shape, f32)

    branch = quarter_of(step, quarters, rows_held, rows_sems)
    up = nn(branch, o_up[...])
    up_product[...] = up
    grad = (nn(branch, held[...]) + nn(halves(up, 1), o_down[...])).T
    use = (q_doc[...] == before_doc[0]).astype(f32)
    columns = grad.shape[1]
    for k in range(kv_heads):
        total = jnp.zeros((2 * head, AUG), f32)
        for g in range(group):
            h = k * group + g
            rows = slice(h * head, (h + 1) * head)
            inverse = 1.0 / totals[h : h + 1, :]
            one = grad[rows]
            g_total = -jnp.sum(one * att_t[rows, :], axis=0, keepdims=True) * inverse
            g_numer = (one * inverse).astype(bf16)
            numer[rows, :] = g_numer
            grad_totals[h : h + 1, :] = g_total
            aug = augmented(g_numer, g_total * use, columns, head, use)
            total = total + nt(phi_q[2 * h * head : 2 * (h + 1) * head, :], aug)
        dstate[k] += total


def augmented(g_numer, g_total, columns, head, use=None):
    top = g_numer if use is None else g_numer * use.astype(bf16)
    high = g_total.astype(bf16).astype(f32)
    row = lax.broadcasted_iota(i32, (AUG - head, columns), 0)
    below = jnp.where(row == 0, high, jnp.where(row == 1, g_total - high, 0.0))
    return jnp.concatenate([top, below.astype(bf16)], axis=0)


def backward_body(
    dims, last_docs, q_t, phi_q, numer, grad_totals, k_n, k_t, v_n, v_a, phi_kn, phi_kt, doc_col, doc_row, q_doc,
    states, cos_q, sin_q, map_q,
    g_nat, g_kt, g_vt, acc_phi, g_map_q, later,
):
    kv_heads, group, head, chunks = dims
    step = pl.program_id(0)
    chunk = chunks - 1 - step
    start = pl.multiple_of(chunk * CHUNK, CHUNK)
    keys = CHUNK + WIN

    @pl.when(step == 0)
    def _():
        later[...] = jnp.zeros(later.shape, f32)
        g_kt[...] = jnp.zeros(g_kt.shape, f32)
        g_vt[...] = jnp.zeros(g_vt.shape, f32)
        acc_phi[...] = jnp.zeros(acc_phi.shape, f32)
        g_map_q[...] = jnp.zeros(g_map_q.shape, f32)

    win, lin = masks(q_doc[...], doc_col[pl.ds(start, keys), :], group)
    use1 = (q_doc[...] == last_docs[chunk]).astype(f32)
    use = jnp.concatenate([use1] * group, axis=1)
    incl = (doc_row[:, pl.ds(start, CHUNK)] == last_docs[chunk + 1]).astype(f32)
    passing = (last_docs[chunk] == last_docs[chunk + 1]).astype(f32)
    scale = head**-0.5
    two = pl.ds(start, 2 * CHUNK)
    one = pl.ds(start, CHUNK)
    pad = jnp.zeros((head, 2 * CHUNK - keys), f32)
    grads = []
    for k in range(kv_heads):
        lanes = slice(k * head, (k + 1) * head)
        wide = slice(2 * k * head, 2 * (k + 1) * head)
        q = side(q_t, k * group * head, group, head)
        phi = side(phi_q, 2 * k * group * head, group, 2 * head)
        gn = side(numer, k * group * head, group, head)
        gt = side(grad_totals, k * group, group, 1)
        weights_win, weights = window_weights(
            q, phi, k_n[pl.ds(start, keys), lanes], phi_kn[one, wide], win, lin, scale
        )
        grad_w = nn(v_n[pl.ds(start, keys), lanes], gn) + gt
        gs = (grad_w * weights_win).astype(bf16)
        gl = jnp.where(lin, grad_w[:CHUNK], 0.0).astype(bf16)
        gq = nn(k_t[lanes, two][:, :keys], gs) * scale
        gk = nt(q, gs) * scale
        gv = nt(gn, weights.astype(bf16))
        aug = augmented(gn, gt, group * CHUNK, head)
        gphi_q = nn(phi_kt[wide, one], gl) + use * nn(states[0, k], aug)
        gphi_k = nt(phi, gl)
        after = later[k]
        after_bf = after.astype(bf16)
        v_aug = v_a[k * AUG : (k + 1) * AUG, one]
        gphi_k = gphi_k + incl * nn(after_bf, v_aug)
        from_later = incl * nn(after.T.astype(bf16), phi_kt[wide, one])[:head]
        gv = gv + jnp.concatenate([from_later, jnp.zeros((head, keys - CHUNK), f32)], axis=1)
        later[k] = nt(phi, augmented(gn, gt * use, group * CHUNK, head, use)) + passing * after
        g_kt[lanes, two] += jnp.concatenate([gk, pad], axis=1)
        g_vt[lanes, two] += jnp.concatenate([gv, pad], axis=1)
        acc_phi[wide, one] += gphi_k
        heads = [slice(g * CHUNK, (g + 1) * CHUNK) for g in range(group)]
        rows = slice(k * group * head, (k + 1) * group * head)
        grad_phi = jnp.concatenate([gphi_q[:, at] for at in heads], axis=0)
        phi_rows = phi_q[2 * k * group * head : 2 * (k + 1) * group * head, :]
        ga = hedgehog_back(phi_rows, grad_phi, head)
        gq_rows = jnp.concatenate([gq[:, at] for at in heads], axis=0) + tn(map_q[k], ga)
        g_map_q[k] += nt(q_t[rows, :], ga)
        grads.append(rope(gq_rows, cos_q[...], -sin_q[...]))
    g_nat[...] = jnp.concatenate(grads, axis=0).T.astype(bf16)


def keys_back_body(dims, last_docs, factors, g_kt, g_vt, g_phi, v_a, phi_kt, k_t, doc_row, map_k, *rest):
    kv_heads, head, chunks, rows = dims
    later, (g_own, g_halo, g_map_k) = rest[:-3], rest[-3:]
    ext = g_kt.shape[1]
    incl = (doc_row[...] == last_docs[chunks]) & (lax.broadcasted_iota(i32, (1, ext), 1) < rows)
    incl = incl.astype(f32)
    phi_grads, v_grads = [], []
    for k in range(kv_heads):
        wide = slice(2 * k * head, 2 * (k + 1) * head)
        after = jnp.zeros(later[0].shape[1:], f32)
        for i, x in enumerate(later):
            after = after + factors[i] * x[k]
        phi_grads.append(g_phi[wide, :] + incl * nn(after.astype(bf16), v_a[k * AUG : (k + 1) * AUG, :]))
        from_later = nn(after.T.astype(bf16), phi_kt[wide, :])[:head]
        v_grads.append(g_vt[k * head : (k + 1) * head, :] + incl * from_later)
    ga = hedgehog_back(phi_kt[...], jnp.concatenate(phi_grads, axis=0), head)
    g_map_k[...] = nt(k_t[...], ga)
    g_k = g_kt[...] + tn(map_k[...], ga)
    for i, grad in enumerate((g_k, jnp.concatenate(v_grads, axis=0))):
        mine = slice(i * kv_heads * head, (i + 1) * kv_heads * head)
        g_own[mine, :] = grad[:, WIN : WIN + rows]
        g_halo[mine, :] = jnp.concatenate([jnp.zeros((kv_heads * head, CHUNK - WIN), f32), grad[:, :WIN]], axis=1)


def adapters_body(
    dims, g_q, g_own, g_halo, cos, sin, ups, low, normed, g_o_up, g_o_down, g_map_q, g_map_k, *outs
):
    rows, window, head, rank = dims
    half = g_own.shape[0] // 2
    kv = keys_values(g_own[...], g_halo[...], cos[...], sin[...], 1.0)
    q_width = g_q.shape[1]
    up = nn(g_q[...], ups[:q_width]) + nn(kv, ups[q_width:])
    up_halves = halves(up, 1)

    def joined(x, axis):
        one, other = jnp.split(x, 2, axis=axis)
        return one + other

    low_halves = halves(low[...], 1)
    g_q_up = joined(tn(g_q[...], low_halves), 1)[:, :rank]
    g_kv_up = joined(tn(kv, low_halves), 1)
    if len(outs) == 1:
        (slabs,) = outs
        slabs[...] = jnp.zeros(slabs.shape, f32)
        tall = slabs.shape[2]
    else:
        by_head, shared = outs
        by_head[...] = jnp.zeros(by_head.shape, f32)

    def put(h, first, x):
        if len(outs) == 2:
            by_head[h, :, first : first + x.shape[1]] = x
            return
        for r in range(slabs.shape[0]):
            slabs[r, h, :, first : first + x.shape[1]] = x[r * tall : (r + 1) * tall]

    def put_shared(first, x):
        if len(outs) == 2:
            shared[first : first + x.shape[0], :] = x
            return
        wide = x.shape[1] // slabs.shape[0] // 128
        for i in range(x.shape[0] // tall):
            for r in range(slabs.shape[0]):
                for j in range(wide):
                    at = (r * wide + j) * 128
                    tile = x[i * tall : (i + 1) * tall, at : at + 128]
                    slabs[r, q_heads + kv_heads + (first // tall + i) * wide + j] = tile

    q_heads, kv_heads = q_width // head, half // head
    group = q_heads // kv_heads
    for h in range(q_heads):
        mine, at = slice(h * head, (h + 1) * head), (h % group) * head
        put(h, 0, g_map_q[h // group, at : at + head, at : at + head])
        put(h, head, g_q_up[mine])
        put(h, head + rank, g_o_down[mine, :])
    for h in range(kv_heads):
        mine = slice(h * head, (h + 1) * head)
        put(q_heads + h, 0, g_map_k[mine, mine])
        put(q_heads + h, head, g_kv_up[mine, rank : 2 * rank])
        put(q_heads + h, head + rank, g_kv_up[half + h * head : half + (h + 1) * head, 2 * rank :])
    put_shared(0, joined(tn(up_halves, normed[window : window + rows, :]), 0))
    put_shared(3 * rank, g_o_up[...])


def adapter_o_body(nat, lowered, att, up_product, *rest):
    branch, (g_o_up, g_o_down) = rest[:4], rest[4:]

    def joined(x, axis):
        one, other = jnp.split(x, 2, axis=axis)
        return one + other

    g_o_down[...] = joined(tn(att[...], halves(up_product[...], 1)), 1)
    o_up = 0.0
    for i, x in enumerate(branch):
        part = lowered[pl.ds(pl.multiple_of(nat[i] * x.shape[0], x.shape[0]), x.shape[0]), :]
        o_up = o_up + tn(halves(part, 1), x[...])
    g_o_up[...] = joined(o_up, 0)


def keys_values(own, halo, cos, sin, last):
    half, wide = own.shape[0] // 2, own.shape[1] - halo.shape[1]
    total = jnp.concatenate([own[:, :wide], own[:, wide:] + halo * last], axis=1)
    return jnp.concatenate([rope(total[:half], cos, -sin), total[half:]], axis=0).T.astype(bf16)


def gn_body(n_pieces, offsets, nat, g_q, g_own, g_halo, cos, sin, ups, downs, *rest):
    pieces = rest[:n_pieces]
    parts, (held, sems) = rest[n_pieces:-2], rest[-2:]
    step = pl.program_id(0)

    @pl.when(step == 0)
    def _():
        load_pieces(pieces, offsets, held, sems)

    q_width = g_q.shape[1]
    kv = keys_values(g_own[...], g_halo[...], cos[...], sin[...], (nat[3 - step] == 3).astype(f32))
    up = nn(g_q[...], ups[:q_width]) + nn(kv, ups[q_width:])
    total = nt(g_q[...], held[:, :q_width]) + nt(kv, held[:, q_width:])
    store_at(step, total + nn(halves(up, 1), downs[...]), parts)


def rms_factor(x):
    return lax.rsqrt(jnp.mean(x * x, axis=-1, keepdims=True) + epsilon)


def rms_back(x, gain, grads):
    factor = rms_factor(x)
    unit = x * factor
    scaled = grads * gain
    return factor * (scaled - unit * jnp.mean(unit * scaled, axis=-1, keepdims=True))


def hidden_body(nat, near, beside, across, tokens, gain, hidden, normed):
    total = near[...].astype(f32) + beside[...].astype(f32) + across[...].astype(f32)
    hidden[...] = tokens[...].astype(f32) + total
    normed[...] = (hidden[...] * rms_factor(hidden[...]) * gain[...]).astype(bf16)


def grad_hidden_body(nat, near, beside, across, cotangent, hidden, gain, grad, rounded):
    total = near[...].astype(f32) + beside[...].astype(f32) + across[...].astype(f32)
    grad[...] = cotangent[...].astype(f32) + rms_back(hidden[...], gain[...], total)
    rounded[...] = grad[...].astype(bf16)


def grad_tokens_body(nat, near, beside, across, tokens, grad, gain, out):
    total = near[...].astype(f32) + beside[...].astype(f32) + across[...].astype(f32)
    out[...] = (grad[...] + rms_back(tokens[...].astype(f32), gain[...], total)).astype(bf16)


def on_own_rows(body, nat, near, beside, across, placed, owned, gain, out_types):
    rows, model = near.shape
    steps = 2
    block = pl.BlockSpec((rows // steps, model), lambda i, nat: (i, 0))
    return pl.pallas_call(
        body,
        grid_spec=pltpu.PrefetchScalarGridSpec(
            num_scalar_prefetch=1,
            grid=(steps,),
            in_specs=[block] * 3
            + [pl.BlockSpec((rows // steps, model), lambda i, nat: (nat[0] * steps + i, 0))]
            + [block] * len(owned)
            + [whole((1, model))],
            out_specs=[block] * len(out_types),
        ),
        out_shape=[jax.ShapeDtypeStruct((rows, model), x) for x in out_types],
        compiler_params=params(BIG),
        cost_estimate=SMALL,
        name="own_rows",
    )(nat, near, beside, across, placed, *owned, gain)


def place_body(count, nat, *refs):
    quarters, (out, held, sems) = refs[:count], refs[-3:]
    step = pl.program_id(0)

    @pl.when(step == 0)
    def _():
        for copy in quarter_copies(quarters, held, sems):
            copy.start()

    out[...] = quarter_of(step, quarters, held, sems).astype(out.dtype)


def place(quarters, first, nat, dtype, earlier=()):
    count, (rows, width) = len(quarters), quarters[0].shape
    return pl.pallas_call(
        lambda *refs: place_body(count, *refs),
        grid_spec=pltpu.PrefetchScalarGridSpec(
            num_scalar_prefetch=1,
            grid=(count,),
            in_specs=[ANY] * (count + len(earlier)),
            out_specs=pl.BlockSpec((rows, width), lambda i, nat: (nat[first + i], 0)),
            scratch_shapes=[pltpu.VMEM((count, rows, width), bf16), pltpu.SemaphoreType.DMA((count,))],
        ),
        out_shape=jax.ShapeDtypeStruct((4 * rows, width), dtype),
        input_output_aliases={1 + count: 0} if earlier else {},
        compiler_params=params(BIG),
        cost_estimate=SMALL,
        name="place",
    )(nat, *quarters, *earlier)


def per_device(
    tokens,
    sequence_lengths,
    output_cotangent,
    query_weight,
    key_weight,
    value_weight,
    output_weight,
    gate_weight,
    up_weight,
    down_weight,
    attention_norm_gain,
    feedforward_norm_gain,
    query_adapter_down,
    key_adapter_down,
    value_adapter_down,
    output_adapter_up,
    query_adapter_up,
    key_adapter_up,
    value_adapter_up,
    output_adapter_down,
    feature_map_query,
    feature_map_key,
):
    rows, model = tokens.shape
    heads, head, rank = query_adapter_up.shape
    kv_heads = key_adapter_up.shape[0]
    group = heads // kv_heads
    q_width, kv_width = heads * head, kv_heads * head
    seq, ring = lax.axis_size("seq"), lax.axis_size("dp") * lax.axis_size("seq")
    here = lax.axis_index("seq")
    chunks = rows // CHUNK
    ext = -(-(rows + WIN) // CHUNK) * CHUNK
    quarter = rows // 4

    core, far = lax.axis_index("tensor") % 2, lax.axis_index("tensor") // 2
    nat = jnp.stack([core * 2 + far, (1 - core) * 2 + far, core * 2 + 1 - far, (1 - core) * 2 + 1 - far]).astype(i32)

    clock = Clock()
    pack = lambda q, k, v, o: jnp.concatenate([q, k, v, o.T], axis=1)
    attn_chain = Chain(clock, 0, pack, query_weight, key_weight, value_weight, output_weight)
    attn_chain.step()
    offsets = attn_chain.offsets
    n_pieces = offsets.shape[0]
    assert sum(map(sum, FFN_UNITS)) == gate_weight.shape[1]

    def turn(part):
        for chain in chains[part]:
            chain.step()


    ladder = jnp.exp(jnp.arange(head // 2).astype(f32) * (-2.0 * math.log(rope_base) / head))[:, None]
    tables = [((head // 2, rows), f32)] * 2 + [((head // 2, ext), f32)] * 2
    tables += [((1, rows), i32), ((ext, 1), i32), ((1, ext), i32)]
    scalars = [((chunks + 1,), i32), ((seq - 1,), f32), ((seq - 1,), f32)]
    cos_q, sin_q, cos_k, sin_k, q_doc, doc_col, doc_row, last_docs, passed_before, passed_after = pl.pallas_call(
        lambda *refs: tables_body(seq, *refs),
        grid_spec=pltpu.PrefetchScalarGridSpec(
            num_scalar_prefetch=2,
            grid=(1,),
            in_specs=[whole(ladder.shape)],
            out_specs=[whole(x) for x, _ in tables] + [pl.BlockSpec(memory_space=pltpu.SMEM)] * 3,
        ),
        out_shape=[jax.ShapeDtypeStruct(x, d) for x, d in tables + scalars],
        compiler_params=params(32),
        cost_estimate=SMALL,
        name="tables",
    )(sequence_lengths[0], here[None].astype(i32), ladder)
    q_doc, doc_col, doc_row, last_docs, passed_before, passed_after = clock.wait(
        q_doc, doc_col, doc_row, last_docs, passed_before, passed_after
    )
    attn_chain.step()

    halo = shifted(clock.tie(tokens)[rows - WIN :], "seq", 1)
    attn_chain.step()
    (halo,) = clock.wait(halo)
    gain_attn = attention_norm_gain.astype(f32)[None, :]
    gain_mlp = feedforward_norm_gain.astype(f32)[None, :]
    downs = jnp.concatenate([query_adapter_down, key_adapter_down, value_adapter_down], axis=1)
    normed, low = pl.pallas_call(
        norm_body,
        grid_spec=pltpu.PrefetchScalarGridSpec(
            num_scalar_prefetch=0,
            grid=(1,),
            in_specs=[ANY, whole((WIN, model)), whole((1, model)), whole((model, 3 * rank))],
            out_specs=[whole((ext, model)), whole((ext, 3 * rank))],
            scratch_shapes=[pltpu.VMEM((ext, model), bf16), pltpu.SemaphoreType.DMA((4,))],
        ),
        out_shape=[jax.ShapeDtypeStruct((ext, model), bf16), jax.ShapeDtypeStruct((ext, 3 * rank), f32)],
        compiler_params=params(BIG),
        cost_estimate=SMALL,
        name="norm",
    )(clock.tie(tokens), halo, gain_attn, downs)
    normed, low = clock.wait(normed, low)
    attn_chain.step()
    all_units = [x for part in FFN_UNITS for x in part]
    pack_in = (
        gate_weight, up_weight, down_weight, query_adapter_up, key_adapter_up, value_adapter_up,
        feature_map_query, feature_map_key, output_adapter_up,
    )
    pack_out = [(gate_weight.shape[0], 3 * x) for x in all_units] + [
        (q_width + 2 * kv_width, 3 * rank),
        (q_width + 2 * kv_width, 6 * rank),
        (kv_heads, group * head, group * head),
        (kv_width, kv_width),
        (model, rank),
    ]
    packed = pl.pallas_call(
        lambda *refs: pack_body(all_units, *refs),
        grid_spec=pltpu.PrefetchScalarGridSpec(
            num_scalar_prefetch=0,
            grid=(1,),
            in_specs=[whole(x.shape) for x in pack_in],
            out_specs=[whole(x) for x in pack_out],
        ),
        out_shape=[jax.ShapeDtypeStruct(x, bf16) for x in pack_out],
        compiler_params=params(BIG),
        cost_estimate=SMALL,
        name="pack",
    )(clock.tie(gate_weight), *pack_in[1:])
    *packed, ups, ups_twice, maps_q, maps_k, o_up = clock.wait(*packed)
    chains = [[Chain(clock, 1, lambda x: x, packed[2 * i]), Chain(clock, -1, lambda x: x, packed[2 * i + 1])] for i in range(2)]
    for _ in range(ring - 5):
        attn_chain.step()
    attn_pieces = attn_chain.pieces()
    turn(0)

    sems = pltpu.SemaphoreType.DMA((n_pieces,))
    qkv_width = q_width + 2 * kv_width
    held_qkv = pltpu.VMEM((model, qkv_width), bf16)
    held_o = pltpu.VMEM((model, q_width), bf16)

    dims = (rows, ext, q_width, kv_width, head, n_pieces, chunks)
    shapes = [
        ((q_width, rows), bf16),
        ((2 * q_width, rows), bf16),
        ((ext, kv_width), bf16),
        ((kv_width, ext), bf16),
        ((ext, kv_width), bf16),
        ((kv_heads * AUG, ext), bf16),
        ((ext, 2 * kv_width), bf16),
        ((2 * kv_width, ext), bf16),
        ((kv_heads, AUG, 2 * head), f32),
    ]
    prep_in = (normed, low, ups_twice, cos_q, sin_q, cos_k, sin_k, maps_q, maps_k, doc_row)
    q_t, phi_q, k_n, k_t, v_n, v_a, phi_kn, phi_kt, contrib = pl.pallas_call(
        lambda *refs: prep_body(dims, *refs),
        grid_spec=pltpu.PrefetchScalarGridSpec(
            num_scalar_prefetch=2,
            grid=(1,),
            in_specs=[whole(x.shape) for x in prep_in] + [ANY] * n_pieces,
            out_specs=[whole(s) for s, _ in shapes],
            scratch_shapes=[held_qkv, sems],
        ),
        out_shape=[jax.ShapeDtypeStruct(s, d) for s, d in shapes],
        compiler_params=params(56),
        cost_estimate=SMALL,
        name="prep",
    )(clock.tie(offsets), last_docs, *prep_in, *attn_pieces)
    (contrib,) = clock.wait(contrib)
    turn(0)

    coming = clock.wait(*[shifted(contrib, "seq", by) for by in range(1, seq)])
    column = lambda r: pl.BlockSpec((r, CHUNK), lambda c, *_: (0, c))
    att, att_t, totals, states = pl.pallas_call(
        lambda *refs: forward_body((kv_heads, group, head), *refs),
        grid_spec=pltpu.PrefetchScalarGridSpec(
            num_scalar_prefetch=2,
            grid=(chunks,),
            in_specs=[
                column(q_width),
                column(2 * q_width),
                whole(k_n.shape),
                whole(v_a.shape),
                whole(phi_kn.shape),
                whole(doc_col.shape),
                whole(doc_row.shape),
                column(1),
            ]
            + [whole(contrib.shape)] * len(coming),
            out_specs=[
                pl.BlockSpec((CHUNK, q_width), lambda c, *_: (c, 0)),
                column(q_width),
                column(heads),
                pl.BlockSpec((1, kv_heads, 2 * head, AUG), lambda c, *_: (c, 0, 0, 0)),
            ],
            scratch_shapes=[pltpu.VMEM(contrib.shape, f32)],
        ),
        out_shape=[
            jax.ShapeDtypeStruct((rows, q_width), bf16),
            jax.ShapeDtypeStruct((q_width, rows), f32),
            jax.ShapeDtypeStruct((heads, rows), f32),
            jax.ShapeDtypeStruct((chunks, kv_heads, 2 * head, AUG), bf16),
        ],
        compiler_params=params(BIG),
        cost_estimate=SMALL,
        name="attend",
    )(clock.tie(last_docs), passed_before, q_t, phi_q, k_n, v_a, phi_kn, doc_col, doc_row, q_doc, *coming)
    att = clock.tie(att)
    turn(0)

    o_down = output_adapter_down.reshape(q_width, rank)
    o_up_t = jnp.concatenate([output_adapter_up.T, output_adapter_up.T], axis=0)
    one_quarter = jax.ShapeDtypeStruct((quarter, model), bf16)

    *o_parts, lowered = pl.pallas_call(
        lambda *refs: o_body(n_pieces, qkv_width, *refs),
        grid_spec=pltpu.PrefetchScalarGridSpec(
            num_scalar_prefetch=2,
            grid=(4,),
            in_specs=[
                pl.BlockSpec((quarter, q_width), lambda i, off, nat: (nat[3 - i], 0)),
                whole(o_down.shape),
                whole(o_up_t.shape),
            ]
            + [ANY] * n_pieces,
            out_specs=[whole((quarter, model))] * 4
            + [pl.BlockSpec((quarter, rank), lambda i, off, nat: (nat[3 - i], 0))],
            scratch_shapes=[held_o, sems],
        ),
        out_shape=[one_quarter] * 4 + [jax.ShapeDtypeStruct((rows, rank), f32)],
        compiler_params=params(BIG),
        cost_estimate=SMALL,
        name="project",
    )(clock.tie(offsets), nat, att, o_down, o_up_t, *attn_pieces)
    o_far0, o_far1, o_near0, o_near1 = clock.wait(*o_parts)
    turn(0)
    o_far0, o_near0 = clock.wait(o_far0, o_near0)
    beside = exchange(o_far0, "tensor", 1)
    beside_near = exchange(o_near0, "tensor", 1)
    beside, beside_near = clock.wait(beside, beside_near)
    o_far = clock.tie((o_far1.astype(f32) + beside.astype(f32)).astype(bf16))
    across = exchange(o_far, "tensor", 2)
    turn(0)
    (across,) = clock.wait(across)
    beside = beside_near
    hidden, normed_mlp = on_own_rows(
        hidden_body, clock.tie(nat), o_near1, beside, across, tokens, (), gain_mlp, (f32, bf16)
    )
    hidden, normed_mlp = clock.wait(hidden, normed_mlp)
    for _ in range(ring - 7):
        turn(0)
    normed_mlp = clock.tie(normed_mlp)
    across, beside = exchange(normed_mlp, "tensor", 2), exchange(normed_mlp, "tensor", 1)
    (beside,) = clock.wait(beside)
    turn(0)
    (across,) = clock.wait(across)
    for chain in chains[0]:
        chain.settle()
    turn(1)
    last = clock.tie(exchange(clock.tie(across), "tensor", 1))
    normed_mlp = [normed_mlp, beside, across, last]

    def ffn(part, which, quarters, sums):
        units, last = FFN_UNITS[part][which], part == len(FFN_UNITS) - 1
        lots = [chain.pieces() for chain in chains[part][which]]
        sizes = tuple(map(len, lots))
        pieces = [piece for lot in lots for piece in lot]
        ring_offsets = jnp.concatenate([chain.offsets for chain in chains[part][which]])
        first = quarters[0]
        summed = jax.ShapeDtypeStruct((2, quarter, model), f32)
        return pl.pallas_call(
            lambda *refs: ffn_body(sizes, units, bool(sums), last, *refs),
            grid_spec=pltpu.PrefetchScalarGridSpec(
                num_scalar_prefetch=2,
                grid=(2,),
                in_specs=[pl.BlockSpec((quarter, model), lambda i, off, nat: (nat[first - i], 0))]
                + [ANY] * (2 + len(pieces) + len(sums)),
                out_specs=[ANY] * (4 if last else 2),
                scratch_shapes=[
                    pltpu.VMEM((2, quarter, model), bf16),
                    pltpu.SemaphoreType.DMA((2,)),
                    pltpu.VMEM((3, model, sum(units)), bf16),
                    pltpu.SemaphoreType.DMA((3, len(pieces))),
                    pltpu.VMEM((2, 2, quarter, model), bf16 if last else f32),
                    pltpu.SemaphoreType.DMA((2, 2)),
                ]
                + [pltpu.VMEM((2, 2, quarter, model), f32), pltpu.SemaphoreType.DMA((2, 2))] * bool(sums),
            ),
            out_shape=[one_quarter] * 4 if last else [summed] * 2,
            compiler_params=params(BIG),
            cost_estimate=SMALL,
            name="feed_forward",
        )(clock.tie(ring_offsets), nat, output_cotangent, *[normed_mlp[q] for q in quarters], *pieces, *sums)

    sums_far = sums_near = ()
    up, down, both = slice(0, 1), slice(1, 2), slice(0, 2)
    for way in (up, down):
        sums_far = clock.wait(*ffn(0, way, (3, 2), sums_far))
        turn(1)
        sums_near = clock.wait(*ffn(0, way, (1, 0), sums_near))
        turn(1)
    for _ in range(ring - 6):
        turn(1)
    gn_far0, gn_far1, mlp_far0, mlp_far1 = ffn(1, both, (3, 2), sums_far)
    gn_far0, mlp_far0 = clock.wait(gn_far0, mlp_far0)
    beside = exchange(gn_far0, "tensor", 1)
    mlp_beside_far = exchange(mlp_far0, "tensor", 1)
    (beside,) = clock.wait(beside)
    across = exchange(clock.tie((gn_far1.astype(f32) + beside.astype(f32)).astype(bf16)), "tensor", 2)
    gn_near0, gn_near1, mlp_near0, mlp_near1 = ffn(1, both, (1, 0), sums_near)
    gn_near0, mlp_near0 = clock.wait(gn_near0, mlp_near0)
    across, gn_near0 = clock.wait(across, gn_near0)
    beside = exchange(gn_near0, "tensor", 1)
    (beside,) = clock.wait(beside)
    grad_hidden, branch = on_own_rows(
        grad_hidden_body, clock.tie(nat), gn_near1, beside, across, output_cotangent, (hidden,), gain_mlp, (f32, bf16)
    )
    grad_hidden, branch = clock.wait(grad_hidden, branch)
    across, beside = exchange(branch, "tensor", 2), exchange(branch, "tensor", 1)
    mlp_beside = exchange(clock.tie(mlp_near0), "tensor", 1)
    (beside,) = clock.wait(beside)

    o_down_t = jnp.concatenate([o_down.T, o_down.T], axis=0)
    sizes = [((q_width, rows), bf16), ((heads, rows), f32), ((rows, rank), f32), ((kv_heads, 2 * head, AUG), f32)]

    def go_part(first, quarters, earlier):
        by_quarter = lambda r: pl.BlockSpec((r, quarter), lambda i, off, nat, before: (0, nat[first + i]))
        late = bool(earlier)
        return pl.pallas_call(
            lambda *refs: go_body((n_pieces, qkv_width, kv_heads, group, head, late), *refs),
            grid_spec=pltpu.PrefetchScalarGridSpec(
                num_scalar_prefetch=3,
                grid=(2,),
                in_specs=[
                    whole((model, rank)),
                    whole(o_down_t.shape),
                    by_quarter(q_width),
                    by_quarter(heads),
                    by_quarter(2 * q_width),
                    by_quarter(1),
                ]
                + [ANY] * (2 + n_pieces)
                + ([ANY] * 3 + [whole(sizes[3][0])]) * late,
                out_specs=[
                    by_quarter(q_width),
                    by_quarter(heads),
                    pl.BlockSpec((quarter, rank), lambda i, off, nat, before: (nat[first + i], 0)),
                    whole(sizes[3][0]),
                ],
                scratch_shapes=[
                    pltpu.VMEM((2, quarter, model), bf16),
                    pltpu.SemaphoreType.DMA((2,)),
                    held_o,
                    sems,
                ],
            ),
            out_shape=[jax.ShapeDtypeStruct(s, d) for s, d in sizes],
            input_output_aliases={11 + n_pieces + i: i for i in range(3)} if late else {},
            compiler_params=params(BIG),
            cost_estimate=SMALL,
            name="project_back",
        )(
            clock.tie(offsets), nat, last_docs, o_up, o_down_t, att_t, totals, phi_q, q_doc,
            *quarters, *attn_pieces, *earlier,
        )

    near = clock.wait(*go_part(0, (branch, beside), ()))
    mlp_beside, mlp_beside_far = clock.wait(mlp_beside, mlp_beside_far)
    mlp_far = clock.tie((mlp_far1.astype(f32) + mlp_beside_far.astype(f32)).astype(bf16))
    mlp_near = clock.tie(hidden + (mlp_near1.astype(f32) + mlp_beside.astype(f32)))
    (across,) = clock.wait(across)
    last = clock.tie(exchange(across, "tensor", 1))
    mlp_across = exchange(clock.tie(mlp_far), "tensor", 2)
    branch = [branch, beside, across, last]
    numer, grad_totals, up_product, dstate = clock.wait(*go_part(2, branch[2:], near))

    coming = [shifted(dstate, "seq", -by) for by in range(1, seq)]

    back_column = lambda r: pl.BlockSpec((r, CHUNK), lambda c, *_: (0, chunks - 1 - c))
    back_in = (
        (q_t, back_column(q_width)),
        (phi_q, back_column(2 * q_width)),
        (numer, back_column(q_width)),
        (grad_totals, back_column(heads)),
        (k_n, None),
        (k_t, None),
        (v_n, None),
        (v_a, None),
        (phi_kn, None),
        (phi_kt, None),
        (doc_col, None),
        (doc_row, None),
        (q_doc, back_column(1)),
        (states, pl.BlockSpec((1, kv_heads, 2 * head, AUG), lambda c, *_: (chunks - 1 - c, 0, 0, 0))),
        (cos_q, back_column(head // 2)),
        (sin_q, back_column(head // 2)),
        (maps_q, None),
    )
    g_q, g_kt, g_vt, g_phi, g_map_q = pl.pallas_call(
        lambda *refs: backward_body((kv_heads, group, head, chunks), *refs),
        grid_spec=pltpu.PrefetchScalarGridSpec(
            num_scalar_prefetch=1,
            grid=(chunks,),
            in_specs=[whole(x.shape) if spec is None else spec for x, spec in back_in],
            out_specs=[
                pl.BlockSpec((CHUNK, q_width), lambda c, *_: (chunks - 1 - c, 0)),
                whole((kv_width, ext)),
                whole((kv_width, ext)),
                whole((2 * kv_width, ext)),
                whole((kv_heads, group * head, group * head)),
            ],
            scratch_shapes=[pltpu.VMEM(dstate.shape, f32)],
        ),
        out_shape=[
            jax.ShapeDtypeStruct((rows, q_width), bf16),
            jax.ShapeDtypeStruct((kv_width, ext), f32),
            jax.ShapeDtypeStruct((kv_width, ext), f32),
            jax.ShapeDtypeStruct((2 * kv_width, ext), f32),
            jax.ShapeDtypeStruct((kv_heads, group * head, group * head), f32),
        ],
        compiler_params=params(52),
        cost_estimate=SMALL,
        name="attend_back",
    )(clock.tie(last_docs), *[x for x, _ in back_in])

    g_q, g_kt, g_vt, g_phi, g_map_q = clock.wait(g_q, g_kt, g_vt, g_phi, g_map_q)
    coming = clock.wait(*coming)
    (mlp_across,) = clock.wait(mlp_across)
    out_rows = clock.tie((mlp_near + mlp_across.astype(f32)).astype(bf16))
    out_across, out_beside = exchange(out_rows, "tensor", 2), exchange(out_rows, "tensor", 1)
    g_own, g_halo, g_map_k = pl.pallas_call(
        lambda *refs: keys_back_body((kv_heads, head, chunks, rows), *refs),
        grid_spec=pltpu.PrefetchScalarGridSpec(
            num_scalar_prefetch=2,
            grid=(1,),
            in_specs=[whole(x.shape) for x in (g_kt, g_vt, g_phi, v_a, phi_kt, k_t, doc_row, maps_k, *coming)],
            out_specs=[whole((2 * kv_width, rows)), whole((2 * kv_width, CHUNK)), whole((kv_width, kv_width))],
        ),
        out_shape=[
            jax.ShapeDtypeStruct((2 * kv_width, rows), f32),
            jax.ShapeDtypeStruct((2 * kv_width, CHUNK), f32),
            jax.ShapeDtypeStruct((kv_width, kv_width), f32),
        ],
        compiler_params=params(BIG),
        cost_estimate=SMALL,
        name="keys_back",
    )(clock.tie(last_docs), passed_after, g_kt, g_vt, g_phi, v_a, phi_kt, k_t, doc_row, maps_k, *coming)

    g_own, g_halo, g_map_k = clock.wait(g_own, g_halo, g_map_k)
    g_halo = shifted(g_halo, "seq", -1)
    o_in = (lowered, att, up_product, *branch)
    g_o_up, g_o_down = pl.pallas_call(
        adapter_o_body,
        grid_spec=pltpu.PrefetchScalarGridSpec(
            num_scalar_prefetch=1,
            grid=(1,),
            in_specs=[whole(x.shape) for x in o_in],
            out_specs=[whole((rank, model)), whole((q_width, rank))],
        ),
        out_shape=[jax.ShapeDtypeStruct((rank, model), f32), jax.ShapeDtypeStruct((q_width, rank), f32)],
        compiler_params=params(BIG),
        cost_estimate=SMALL,
        name="adapter_o",
    )(clock.tie(nat), *o_in)
    g_o_up, g_o_down, g_halo = clock.wait(g_o_up, g_o_down, g_halo)

    downs_t = jnp.concatenate([downs.T, downs.T], axis=0)

    by_rows = lambda w: pl.BlockSpec((quarter, w), lambda i, off, nat: (nat[3 - i], 0))
    by_columns = lambda r: pl.BlockSpec((r, quarter), lambda i, off, nat: (0, nat[3 - i]))
    gn_parts = pl.pallas_call(
        lambda *refs: gn_body(n_pieces, *refs),
        grid_spec=pltpu.PrefetchScalarGridSpec(
            num_scalar_prefetch=2,
            grid=(4,),
            in_specs=[
                by_rows(q_width),
                by_columns(2 * kv_width),
                whole(g_halo.shape),
                by_columns(head // 2),
                by_columns(head // 2),
                whole(ups.shape),
                whole(downs_t.shape),
            ]
            + [ANY] * n_pieces,
            out_specs=[whole((quarter, model))] * 4,
            scratch_shapes=[held_qkv, sems],
        ),
        out_shape=[one_quarter] * 4,
        compiler_params=params(BIG),
        cost_estimate=SMALL,
        name="norm_back",
    )(clock.tie(offsets), nat, g_q, g_own, g_halo, cos_q, sin_q, ups, downs_t, *attn_pieces)
    gn_far0, gn_far1, gn_near0, gn_near1 = clock.wait(*gn_parts)
    out_across, out_beside, gn_far0, gn_near0 = clock.wait(out_across, out_beside, gn_far0, gn_near0)
    beside, beside_near = exchange(gn_far0, "tensor", 1), exchange(gn_near0, "tensor", 1)
    beside, beside_near = clock.wait(beside, beside_near)
    gn_far = clock.tie((gn_far1.astype(f32) + beside.astype(f32)).astype(bf16))
    across = exchange(gn_far, "tensor", 2)

    adapters_in = (g_q, g_own, g_halo, cos_q, sin_q, ups, low[WIN : WIN + rows], normed, g_o_up, g_o_down, g_map_q, g_map_k)
    tall = head // ring
    tiles = 4 * rank // 8 * (model // ring // 128)
    in_tiles = tall == 8 and rank == 8 and model // ring % 128 == 0 and 2 * head == 128
    if in_tiles:
        sizes = [((ring, heads + kv_heads + tiles, tall, 2 * head), f32)]
    else:
        sizes = [((heads + kv_heads, head, 2 * head), f32), ((4 * rank, model), f32)]
    parts = pl.pallas_call(
        lambda *refs: adapters_body((rows, WIN, head, rank), *refs),
        grid_spec=pltpu.PrefetchScalarGridSpec(
            num_scalar_prefetch=0,
            grid=(1,),
            in_specs=[whole(x.shape) for x in adapters_in],
            out_specs=[whole(x) for x, _ in sizes],
        ),
        out_shape=[jax.ShapeDtypeStruct(x, d) for x, d in sizes],
        compiler_params=params(BIG),
        cost_estimate=SMALL,
        name="adapters",
    )(clock.tie(adapters_in[0]), *adapters_in[1:])
    if not in_tiles:
        parts = [
            parts[0].reshape(heads + kv_heads, ring, tall, 2 * head).transpose(1, 0, 2, 3),
            parts[1].reshape(4 * rank, ring, model // ring).transpose(1, 0, 2),
        ]
    parts = clock.wait(*parts)

    def halved(x, axis, half, bit, over=0, sent_as=f32):
        x = x.reshape(x.shape[:over] + (2, half) + x.shape[over + 1 :])
        send = lax.dynamic_index_in_dim(x, 1 - bit, over, keepdims=False)
        return lax.dynamic_index_in_dim(x, bit, over, keepdims=False), exchange(send.astype(sent_as), axis, half)

    def summed_over(axis, size, xs):
        while size > 1:
            half = size // 2
            both = [halved(x, axis, half, (lax.axis_index(axis) // half) % 2, 0, bf16) for x in xs]
            coming = clock.wait(*[coming for _, coming in both])
            xs = [kept + x.astype(f32) for (kept, _), x in zip(both, coming)]
            size = half
            yield xs

    dp = ring // seq
    parts = [x.reshape((dp, seq) + x.shape[1:]) for x in parts]
    for parts in summed_over("dp", dp, parts):
        pass
    along_seq = summed_over("seq", seq, clock.wait(*[x[0] for x in parts]))
    parts = next(along_seq)
    (across,) = clock.wait(across)
    (grad_rows,) = on_own_rows(
        grad_tokens_body, clock.tie(nat), gn_near1, beside_near, across, tokens, (grad_hidden,), gain_attn, (bf16,)
    )
    (grad_rows,) = clock.wait(grad_rows)
    across, beside = exchange(grad_rows, "tensor", 2), exchange(grad_rows, "tensor", 1)
    out_last = clock.tie(exchange(out_across, "tensor", 1))
    (beside,) = clock.wait(beside)
    grad_tokens = clock.tie(place([grad_rows, beside], 0, nat, f32))
    for parts in along_seq:
        pass
    by_head, shared = parts[0][0], parts[-1][0]
    if in_tiles:
        by_head, shared = by_head[: heads + kv_heads], by_head[heads + kv_heads :]
        shared = shared.reshape(4 * rank // 8, -1, 8, 128).transpose(0, 2, 1, 3)
    shared = shared.reshape(4 * rank, 2, 2, -1).transpose(2, 1, 0, 3)
    pick = lambda x, i: lax.dynamic_index_in_dim(x, i, 0, keepdims=False)
    shared = pick(shared, core) + clock.tie(exchange(pick(shared, 1 - core), "tensor", 1))
    shared = clock.tie(shared.reshape(2, 4 * rank, -1))
    block_out = clock.tie(place([out_rows, out_beside, out_across, out_last], 0, nat, bf16))
    (across,) = clock.wait(across)
    (last,) = clock.wait(exchange(across, "tensor", 1))
    shared = clock.tie(shared)
    sent = exchange(pick(shared, 1 - far), "tensor", 2)
    grad_tokens = clock.tie(place([across, last], 2, nat, f32, (grad_tokens,)))
    shared = (pick(shared, far) + clock.tie(sent)).T
    of_q, of_kv = by_head[:heads], by_head[heads:]
    first, second = slice(head, head + rank), slice(head + rank, head + 2 * rank)
    out = [of_q[..., first], of_kv[..., first], of_kv[..., second], of_q[..., second], of_q[..., :head], of_kv[..., :head]]
    return (
        block_out,
        grad_tokens,
        shared[:, :rank] + clock.now.astype(f32),
        shared[:, rank : 2 * rank],
        shared[:, 2 * rank : 3 * rank],
        shared[:, 3 * rank :],
        *out,
    )


def solution(mesh):
    return jax.shard_map(
        per_device,
        mesh=mesh,
        in_specs=(
            P(("dp", "seq"), None),
            P("dp", None),
            P(("dp", "seq"), None),
            P(("dp", "seq"), "tensor"),
            P(("dp", "seq"), "tensor"),
            P(("dp", "seq"), "tensor"),
            P("tensor", ("dp", "seq")),
            P(("dp", "seq"), "tensor"),
            P(("dp", "seq"), "tensor"),
            P("tensor", ("dp", "seq")),
            P(),
            P(),
            P(),
            P(),
            P(),
            P(),
            P("tensor", None, None),
            P("tensor", None, None),
            P("tensor", None, None),
            P("tensor", None, None),
            P("tensor", None, None),
            P("tensor", None, None),
        ),
        out_specs=(
            P(("dp", "seq"), None),
            P(("dp", "seq"), None),
            P(("dp", "seq", "tensor"), None),
            P(("dp", "seq", "tensor"), None),
            P(("dp", "seq", "tensor"), None),
            P(("dp", "seq", "tensor"), None),
            P("tensor", ("dp", "seq"), None),
            P("tensor", ("dp", "seq"), None),
            P("tensor", ("dp", "seq"), None),
            P("tensor", ("dp", "seq"), None),
            P("tensor", ("dp", "seq"), None),
            P("tensor", ("dp", "seq"), None),
        ),
        check_vma=False,
    )
```

```python
import math

import jax
import jax.numpy as jnp
from jax import lax
from jax.experimental import pallas as pl
from jax.experimental.pallas import tpu as pltpu
from jax.sharding import PartitionSpec as P

WIN = 64
CHUNK = 128
AUG = 80
RING = 8
FFN_UNITS = ((512, 512), (512, 512))
BIG = 60

epsilon = 1e-05
rope_base = 500000.0
bf16, f32, i32 = jnp.bfloat16, jnp.float32, jnp.int32
MIB = 1 << 20


def nn(a, b):
    return lax.dot_general(a, b, (((1,), (0,)), ((), ())), preferred_element_type=f32)


def nt(a, b):
    return lax.dot_general(a, b, (((1,), (1,)), ((), ())), preferred_element_type=f32)


def tn(a, b):
    return lax.dot_general(a, b, (((0,), (0,)), ((), ())), preferred_element_type=f32)


def halves(x, axis):
    high = x.astype(bf16)
    return jnp.concatenate([high, (x - high.astype(f32)).astype(bf16)], axis=axis)


def exchange(x, axis, bit):
    count = lax.axis_size(axis)
    return lax.ppermute(x, axis, [(i, i ^ bit) for i in range(count)])


def shifted(x, axis, by):
    count = lax.axis_size(axis)
    return lax.ppermute(x, axis, [(i, i + by) for i in range(count) if 0 <= i + by < count])


def place_of(index, seq):
    row, col = index // seq, index % seq
    return row * seq + (col if row % 2 == 0 else seq - 1 - col)


def place_of_traced(index, seq):
    row, col = index // seq, index % seq
    return row * seq + jnp.where(row % 2 == 0, col, seq - 1 - col)


class Clock:
    def __init__(self):
        self.now = jnp.zeros((), i32)

    def wait(self, *arrays):
        *out, self.now = lax.optimization_barrier((*arrays, self.now))
        return out

    def tie(self, x):
        return self.wait(x)[0]


class Chain:
    def __init__(self, clock, way, pack, *blocks):
        block = pack(*clock.wait(*blocks))
        dp, seq = lax.axis_size("dp"), lax.axis_size("seq")
        self.clock, self.count = clock, dp * seq
        self.ringed = self.count <= RING
        rows = block.shape[0]
        if not self.ringed:
            self.lanes = [[lax.all_gather(block, ("dp", "seq"), axis=0, tiled=True)]]
            self.offsets = jnp.zeros((1,), i32)
            return
        order = [place_of(i, seq) for i in range(self.count)]
        up = [(order[i], order[(i + 1) % self.count]) for i in range(self.count)]
        down = [(j, i) for i, j in up]
        place = place_of_traced(lax.axis_index("dp") * seq + lax.axis_index("seq"), seq)
        steps = jnp.arange(self.count)
        came_up = place_of_traced((place - steps) % self.count, seq) * rows
        came_down = place_of_traced((place + steps) % self.count, seq) * rows
        if way:
            self.lanes, self.ways = [[block]], [up if way > 0 else down]
            self.offsets = (came_up if way > 0 else came_down).astype(i32)
        else:
            half = rows // 2
            self.lanes, self.ways = [[block[:half]], [block[half:]]], [up, down]
            self.offsets = jnp.concatenate([came_up, came_down + half]).astype(i32)

    def settle(self):
        if self.ringed:
            came = self.clock.wait(*[lane[-1] for lane in self.lanes])
            for lane, x in zip(self.lanes, came):
                lane[-1] = x

    def step(self):
        if self.ringed:
            for lane, way in zip(self.lanes, self.ways):
                (lane[-1],) = self.clock.wait(lane[-1])
                lane.append(lax.ppermute(lane[-1], ("dp", "seq"), way))

    def pieces(self):
        self.settle()
        return [piece for lane in self.lanes for piece in lane]


def load_pieces(pieces, offsets, held, sems, first=0):
    copies = [
        pltpu.make_async_copy(
            piece.at[:, pl.ds(first, held.shape[1])],
            held.at[pl.ds(pl.multiple_of(offsets[i], 16), piece.shape[0])],
            sems.at[i],
        )
        for i, piece in enumerate(pieces)
    ]
    for copy in copies:
        copy.start()
    for copy in copies:
        copy.wait()


def params(limit):
    return pltpu.CompilerParams(vmem_limit_bytes=limit * MIB)


SMALL = pl.CostEstimate(flops=1, bytes_accessed=1, transcendentals=0)


ANY = pl.BlockSpec(memory_space=pl.ANY)


def whole(shape):
    return pl.BlockSpec(shape, lambda *_: (0,) * len(shape))


def rope(x, cos, sin):
    width = 2 * cos.shape[0]
    half = width // 2
    out = []
    for at in range(0, x.shape[0], width):
        x1, x2 = x[at : at + half], x[at + half : at + width]
        out += [x1 * cos - x2 * sin, x2 * cos + x1 * sin]
    return jnp.concatenate(out, axis=0)


def hedgehog(a, width):
    out = []
    for at in range(0, a.shape[0], width):
        one = a[at : at + width]
        for e in (
            jnp.exp(one - jnp.max(one, axis=0, keepdims=True)),
            jnp.exp(jnp.min(one, axis=0, keepdims=True) - one),
        ):
            out.append(e * (1.0 / jnp.sum(e, axis=0, keepdims=True)))
    return jnp.concatenate(out, axis=0).astype(bf16)


def hedgehog_back(phi, grad, width):
    out = []
    for at in range(0, phi.shape[0], 2 * width):
        p1, p2 = phi[at : at + width].astype(f32), phi[at + width : at + 2 * width].astype(f32)
        d1, d2 = grad[at : at + width], grad[at + width : at + 2 * width]
        out.append(
            p1 * (d1 - jnp.sum(p1 * d1, axis=0, keepdims=True))
            - p2 * (d2 - jnp.sum(p2 * d2, axis=0, keepdims=True))
        )
    return jnp.concatenate(out, axis=0).astype(bf16)


def tables_body(seq, lengths, here, ladder, cos_q, sin_q, cos_k, sin_k, q_doc, doc_col, doc_row, last, before, after):
    rows, ext = q_doc.shape[1], doc_row.shape[1]
    ends = [lengths[0]]
    for i in range(1, lengths.shape[0]):
        ends.append(ends[-1] + lengths[i])

    def document(at):
        doc, start = 0, 0
        for end in ends:
            past = at >= end
            doc = doc + past.astype(i32)
            start = jnp.where(past, end, start)
        return jnp.where(at >= 0, doc, -1), at - start

    def angles(relative, cos, sin):
        angle = ladder[...] * relative.astype(f32)
        cos[...] = jnp.cos(angle)
        sin[...] = jnp.sin(angle)

    def passing(block):
        ahead = rows * block - WIN - 1
        return (document(ahead)[0] == document(ahead + rows)[0]).astype(f32)

    first = here[0] * rows
    q_doc[...], relative = document(first + lax.broadcasted_iota(i32, (1, rows), 1))
    angles(relative, cos_q, sin_q)
    index = lax.broadcasted_iota(i32, (1, ext), 1)
    doc, relative = document(first - WIN + index)
    doc_row[...] = jnp.where(index < rows + WIN, doc, -2)
    angles(relative, cos_k, sin_k)
    index = lax.broadcasted_iota(i32, (ext, 1), 0)
    doc_col[...] = jnp.where(index < rows + WIN, document(first - WIN + index)[0], -2)
    for i in range(last.shape[0]):
        last[i] = document(first - WIN - 1 + CHUNK * i)[0]
    earlier = later = jnp.float32(1.0)
    for by in range(seq - 1):
        before[by], after[by] = earlier, later
        earlier = earlier * passing(jnp.maximum(here[0] - by - 1, 0))
        later = later * passing(jnp.minimum(here[0] + by + 1, seq - 1))


def norm_body(half, tokens, halo, gain, downs, *rest):
    normed, low, held, out_held, low_held, sems, out_sems = rest[-7:]
    rows, window, size = tokens.shape[0] // 2, halo.shape[0], held.shape[0]
    first = 0 if half else window
    part = rows // 2
    place = half * (window + rows)

    def copy(i):
        source = tokens.at[pl.ds(half * rows + i * part, part)]
        return pltpu.make_async_copy(source, held.at[pl.ds(first + i * part, part)], sems.at[i])

    def out_copies(i):
        at, count = spans[i][0], spans[i][1] - spans[i][0]
        return [
            pltpu.make_async_copy(x.at[pl.ds(at, count)], y.at[pl.ds(place + at, count)], out_sems.at[k, i])
            for k, (x, y) in enumerate(((out_held, normed), (low_held, low)))
        ]

    spans = [(0, first + part), (first + part, size)]
    for i in range(2):
        copy(i).start()
    if half:
        held[2 * part :, :] = jnp.zeros((size - 2 * part, held.shape[1]), bf16)
    else:
        held[:window, :] = halo[...]
    for i, (start, end) in enumerate(spans):
        copy(i).wait()
        x = held[start:end, :].astype(f32)
        out = (x * rms_factor(x) * gain[...]).astype(bf16)
        out_held[start:end, :] = out
        low_held[start:end, :] = nn(out, downs[...])
        for one in out_copies(i):
            one.start()
    for i in range(2):
        for one in out_copies(i):
            one.wait()


def pack_body(units, gate, up, down, q_up, k_up, v_up, map_q, map_k, o_up, *outs):
    packed, (ups, twice, maps_q, maps_k, o_up_out) = outs[:-5], outs[-5:]
    o_up_out[...] = o_up[...]
    at = 0
    for size, out in zip(units, packed):
        out[:, :size] = gate[:, at : at + size]
        out[:, size : 2 * size] = up[:, at : at + size]
        out[:, 2 * size :] = down[at : at + size, :].T
        at += size
    head, rank = q_up.shape[1:]
    at = 0
    for i, x in enumerate((q_up, k_up, v_up)):
        for h in range(x.shape[0]):
            row = jnp.concatenate(
                [jnp.zeros((head, rank), bf16)] * i + [x[h]] + [jnp.zeros((head, rank), bf16)] * (2 - i), axis=1
            )
            ups[at : at + head, :] = row
            twice[at : at + head, :] = jnp.concatenate([row, row], axis=1)
            at += head
    maps_q[...] = jnp.zeros(maps_q.shape, bf16)
    maps_k[...] = jnp.zeros(maps_k.shape, bf16)
    group = map_q.shape[0] // maps_q.shape[0]
    for h in range(map_q.shape[0]):
        mine = slice(h % group * head, (h % group + 1) * head)
        maps_q[h // group, mine, mine] = map_q[h].astype(f32).T.astype(bf16)
    for h in range(map_k.shape[0]):
        mine = slice(h * head, (h + 1) * head)
        maps_k[mine, mine] = map_k[h].astype(f32).T.astype(bf16)


def prep_body(dims, offsets, last_docs, nx, low, ups, cos_q, sin_q, cos_k, sin_k, map_q, map_k, doc_row, *rest):
    tokens, ext, q_width, kv_width, head, n_pieces, chunks = dims
    pieces, rest = rest[:n_pieces], rest[n_pieces:]
    q_t, phi_q, k_n, k_t, v_n, v_a, phi_kn, phi_kt, contrib, held, sems = rest
    load_pieces(pieces, offsets, held, sems)
    kv_heads = kv_width // head
    step = ext // 3
    v_a[...] = jnp.zeros(v_a.shape, bf16)
    for at in range(0, ext, step):
        rows = pl.ds(at, step)
        raw = nn(nx[rows, :], held[:, q_width:]) + nt(halves(low[rows, :], 1), ups[q_width:, :])
        v = raw[:, kv_width:].astype(bf16)
        v_n[rows, :] = v
        v_tr = raw[:, kv_width:].T.astype(bf16)
        for k in range(kv_heads):
            v_a[k * AUG : k * AUG + head, rows] = v_tr[k * head : (k + 1) * head]
            v_a[k * AUG + head : (k + 1) * AUG, rows] = (
                lax.broadcasted_iota(i32, (AUG - head, step), 0) < 2
            ).astype(f32).astype(bf16)
        k_rot = rope(raw[:, :kv_width].T, cos_k[:, rows], sin_k[:, rows])
        k_bf = k_rot.astype(bf16)
        k_t[:, rows] = k_bf
        k_n[rows, :] = k_rot.T.astype(bf16)
        phi = hedgehog(nn(map_k[...], k_bf), head)
        phi_kt[:, rows] = phi
        phi_kn[rows, :] = phi.astype(f32).T.astype(bf16)
    incl = (doc_row[:, :tokens] == last_docs[chunks]).astype(f32).astype(bf16)
    for k in range(kv_heads):
        masked = v_a[k * AUG : (k + 1) * AUG, :tokens] * incl
        contrib[k] = nn(masked, phi_kn[:tokens, k * 2 * head : (k + 1) * 2 * head])
    step = tokens // 2
    group = q_width // kv_heads
    for at in range(0, tokens, step):
        rows = pl.ds(at, step)
        raw = nn(nx[pl.ds(WIN + at, step), :], held[:, :q_width])
        raw = raw + nt(halves(low[pl.ds(WIN + at, step), :], 1), ups[:q_width, :])
        q_bf = rope(raw.T, cos_q[:, rows], sin_q[:, rows]).astype(bf16)
        q_t[:, rows] = q_bf
        for k in range(kv_heads):
            logits = nn(map_q[k], q_bf[k * group : (k + 1) * group])
            phi_q[2 * k * group : 2 * (k + 1) * group, rows] = hedgehog(logits, head)


def masks(q_doc, k_doc, heads):
    keys = CHUNK + WIN
    j = lax.broadcasted_iota(i32, (keys, CHUNK), 0)
    t = lax.broadcasted_iota(i32, (keys, CHUNK), 1)
    same = k_doc == q_doc
    win = same & (j > t) & (j <= t + WIN)
    lin = (same & (j <= t))[:CHUNK]
    win_f = jnp.concatenate([win.astype(f32)] * heads, axis=1)
    lin_f = jnp.concatenate([lin.astype(f32)] * heads, axis=1)
    return win_f > 0.5, lin_f > 0.5


def side(ref, first, count, size):
    return jnp.concatenate([ref[first + g * size : first + (g + 1) * size, :] for g in range(count)], axis=1)


def window_weights(q, phi_q, k_win, phi_k, win, lin, scale):
    scores = nn(k_win, q)
    weights_win = jnp.where(win, jnp.exp(scores * scale), 0.0)
    linear = jnp.where(lin, nn(phi_k, phi_q), 0.0)
    return weights_win, jnp.concatenate([weights_win[:CHUNK] + linear, weights_win[CHUNK:]], axis=0)


def forward_body(dims, last_docs, factors, q_t, phi_q, k_n, v_a, phi_kn, doc_col, doc_row, q_doc, *rest):
    kv_heads, group, head = dims
    earlier, (att, att_t, totals, states, state) = rest[:-5], rest[-5:]
    chunk = pl.program_id(0)
    start = pl.multiple_of(chunk * CHUNK, CHUNK)

    @pl.when(chunk == 0)
    def _():
        total = jnp.zeros(state.shape, f32)
        for i, x in enumerate(earlier):
            total = total + factors[i] * x[...]
        state[...] = total

    keys = CHUNK + WIN
    win, lin = masks(q_doc[...], doc_col[pl.ds(start, keys), :], group)
    use = (q_doc[...] == last_docs[chunk]).astype(f32)
    use = jnp.concatenate([use] * group, axis=1)
    incl = (doc_row[:, pl.ds(start, CHUNK)] == last_docs[chunk + 1]).astype(f32).astype(bf16)
    passing = (last_docs[chunk] == last_docs[chunk + 1]).astype(f32)
    scale = head**-0.5
    out = []
    for k in range(kv_heads):
        q = side(q_t, k * group * head, group, head)
        phi = side(phi_q, 2 * k * group * head, group, 2 * head)
        k_win = k_n[pl.ds(start, keys), k * head : (k + 1) * head]
        phi_k = phi_kn[pl.ds(start, CHUNK), 2 * k * head : 2 * (k + 1) * head]
        v_win = v_a[k * AUG : (k + 1) * AUG, pl.ds(start, 2 * CHUNK)]
        _, weights = window_weights(q, phi, k_win, phi_k, win, lin, scale)
        before = state[k]
        from_state = nn(before.astype(bf16), phi) * use
        total = jnp.sum(weights, axis=0, keepdims=True) + from_state[head : head + 1]
        numer = nn(v_win[:, :keys], weights.astype(bf16))[:head] + from_state[:head]
        attended = numer * (1.0 / total)
        for g in range(group):
            out.append(attended[:, g * CHUNK : (g + 1) * CHUNK])
            totals[k * group + g : k * group + g + 1, :] = total[:, g * CHUNK : (g + 1) * CHUNK]
        states[0, k] = before.T.astype(bf16)
        state[k] = nn(v_win[:, :CHUNK] * incl, phi_k) + passing * before
    attended = jnp.concatenate(out, axis=0)
    att_t[...] = attended
    att[...] = attended.T.astype(bf16)


def store_at(step, value, outs):
    for i, out in enumerate(outs):

        @pl.when(step == i)
        def _(out=out):
            out[...] = value.astype(out.dtype)


def o_body(n_pieces, first, offsets, nat, att, down, up, *rest):
    pieces, parts, (lowered, held, sems) = rest[:n_pieces], rest[n_pieces:-3], rest[-3:]
    step = pl.program_id(0)

    @pl.when(step == 0)
    def _():
        load_pieces(pieces, offsets, held, sems, first)

    low = nn(att[...], down[...])
    lowered[...] = low
    store_at(step, nt(att[...], held[...]) + nn(halves(low, 1), up[...]), parts)


def quarter_copies(quarters, held, sems, first=0):
    return [pltpu.make_async_copy(x, held.at[first + i], sems.at[first + i]) for i, x in enumerate(quarters)]


def quarter_of(step, quarters, held, sems):
    for i, copy in enumerate(quarter_copies(quarters, held, sems)):

        @pl.when(step == i)
        def _(copy=copy):
            copy.wait()

    return held[step]


def ffn_body(lots, units, summed, last, offsets, nat, cot, *rest):
    count, n_out = sum(lots), 4 if last else 2
    quarters, pieces, rest = rest[:2], rest[2 : 2 + count], rest[2 + count :]
    sums, outs, rest = rest[: 2 * summed], rest[2 * summed : 2 * summed + n_out], rest[2 * summed + n_out :]
    rows, rows_sems, held, sems, out_held, out_sems, *rest = rest
    step = pl.program_id(0)

    def at_first(act):
        pl.when(step == 0)(act)

    starts = [sum(units[:i]) for i in range(len(units))]
    blocks = [(which, lot) for which in range(3) for lot in range(len(lots))]

    def copies(block):
        which, lot = block
        size = units[lot]
        return [
            pltpu.make_async_copy(
                pieces[i].at[:, pl.ds(which * size, size)],
                held.at[which, pl.ds(pl.multiple_of(offsets[i], 16), pieces[i].shape[0]), pl.ds(starts[lot], size)],
                sems.at[which, i],
            )
            for i in range(sum(lots[:lot]), sum(lots[: lot + 1]))
        ]

    def sum_copy(i, kind):
        return pltpu.make_async_copy(sums[kind].at[i], rest[0].at[i, kind], rest[1].at[i, kind])

    def out_copy(i, kind):
        out = outs[2 * (1 - kind) + i] if last else outs[kind].at[i]
        return pltpu.make_async_copy(out_held.at[i, kind], out, out_sems.at[i, kind])

    @at_first
    def _():
        for copy in quarter_copies(quarters[:1], rows, rows_sems) + copies(blocks[0]) + copies(blocks[1]):
            copy.start()
        for copy in quarter_copies(quarters[1:], rows, rows_sems, 1):
            copy.start()

    def product(x, index):
        @at_first
        def _():
            for copy in copies(blocks[index]):
                copy.wait()
            if index + 2 < len(blocks):
                for copy in copies(blocks[index + 2]):
                    copy.start()
            elif index + 2 == len(blocks) and summed:
                for i in range(2):
                    for kind in (1, 0):
                        sum_copy(i, kind).start()

        which, lot = blocks[index]
        return nn(x, held[which, :, starts[lot] : starts[lot] + units[lot]])

    n2 = quarter_of(step, quarters, rows, rows_sems)
    count = len(lots)
    gates = [product(n2, i) for i in range(count)]
    ups = [product(n2, count + i) for i in range(count)]
    grads = [product(cot[...], 2 * count + i) for i in range(count)]
    parts = [[], [], []]
    for gate, up, grad_act in zip(gates, ups, grads):
        s = 1.0 / (1.0 + jnp.exp(-gate))
        silu = gate * s
        parts[0].append((silu * up).astype(bf16))
        parts[1].append((grad_act * up * s * (1.0 + gate * (1.0 - s))).astype(bf16))
        parts[2].append((grad_act * silu).astype(bf16))
    act, grad_gate, grad_up = [jnp.concatenate(x, axis=1) for x in parts]

    def finish(kind, total):
        if summed:
            sum_copy(step, kind).wait()
            total = total + rest[0][step, kind]
        out_held[step, kind] = total.astype(out_held.dtype)
        for i in range(2):

            @pl.when(step == i)
            def _(i=i):
                out_copy(i, kind).start()

    finish(1, nt(grad_gate, held[0]) + nt(grad_up, held[1]))
    finish(0, nt(act, held[2]))

    @pl.when(step == 1)
    def _():
        for i in range(2):
            for kind in range(2):
                out_copy(i, kind).wait()


def go_body(dims, offsets, nat, before_doc, o_up, o_down, att_t, totals, phi_q, q_doc, *rest):
    n_pieces, first, kv_heads, group, head, later = dims
    quarters, pieces, rest = rest[:2], rest[2 : 2 + n_pieces], rest[2 + n_pieces :]
    earlier, rest = rest[: 4 * later], rest[4 * later :]
    numer, grad_totals, up_product, dstate, rows_held, rows_sems, held, sems = rest
    step = pl.program_id(0)

    @pl.when(step == 0)
    def _():
        for copy in quarter_copies(quarters, rows_held, rows_sems):
            copy.start()
        load_pieces(pieces, offsets, held, sems, first)
        dstate[...] = earlier[3][...] if later else jnp.zeros(dstate.shape, f32)

    branch = quarter_of(step, quarters, rows_held, rows_sems)
    up = nn(branch, o_up[...])
    up_product[...] = up
    grad = (nn(branch, held[...]) + nn(halves(up, 1), o_down[...])).T
    use = (q_doc[...] == before_doc[0]).astype(f32)
    columns = grad.shape[1]
    for k in range(kv_heads):
        total = jnp.zeros((2 * head, AUG), f32)
        for g in range(group):
            h = k * group + g
            rows = slice(h * head, (h + 1) * head)
            inverse = 1.0 / totals[h : h + 1, :]
            one = grad[rows]
            g_total = -jnp.sum(one * att_t[rows, :], axis=0, keepdims=True) * inverse
            g_numer = (one * inverse).astype(bf16)
            numer[rows, :] = g_numer
            grad_totals[h : h + 1, :] = g_total
            aug = augmented(g_numer, g_total * use, columns, head, use)
            total = total + nt(phi_q[2 * h * head : 2 * (h + 1) * head, :], aug)
        dstate[k] += total


def augmented(g_numer, g_total, columns, head, use=None):
    top = g_numer if use is None else g_numer * use.astype(bf16)
    high = g_total.astype(bf16).astype(f32)
    row = lax.broadcasted_iota(i32, (AUG - head, columns), 0)
    below = jnp.where(row == 0, high, jnp.where(row == 1, g_total - high, 0.0))
    return jnp.concatenate([top, below.astype(bf16)], axis=0)


def backward_body(
    dims, last_docs, q_t, phi_q, numer, grad_totals, k_n, k_t, v_n, v_a, phi_kn, phi_kt, doc_col, doc_row, q_doc,
    states, cos_q, sin_q, map_q,
    g_nat, g_kt, g_vt, acc_phi, g_map_q, later,
):
    kv_heads, group, head, chunks = dims
    step = pl.program_id(0)
    chunk = chunks - 1 - step
    start = pl.multiple_of(chunk * CHUNK, CHUNK)
    keys = CHUNK + WIN

    @pl.when(step == 0)
    def _():
        later[...] = jnp.zeros(later.shape, f32)
        g_kt[...] = jnp.zeros(g_kt.shape, f32)
        g_vt[...] = jnp.zeros(g_vt.shape, f32)
        acc_phi[...] = jnp.zeros(acc_phi.shape, f32)
        g_map_q[...] = jnp.zeros(g_map_q.shape, f32)

    win, lin = masks(q_doc[...], doc_col[pl.ds(start, keys), :], group)
    use1 = (q_doc[...] == last_docs[chunk]).astype(f32)
    use = jnp.concatenate([use1] * group, axis=1)
    incl = (doc_row[:, pl.ds(start, CHUNK)] == last_docs[chunk + 1]).astype(f32)
    passing = (last_docs[chunk] == last_docs[chunk + 1]).astype(f32)
    scale = head**-0.5
    two = pl.ds(start, 2 * CHUNK)
    one = pl.ds(start, CHUNK)
    pad = jnp.zeros((head, 2 * CHUNK - keys), f32)
    grads = []
    for k in range(kv_heads):
        lanes = slice(k * head, (k + 1) * head)
        wide = slice(2 * k * head, 2 * (k + 1) * head)
        q = side(q_t, k * group * head, group, head)
        phi = side(phi_q, 2 * k * group * head, group, 2 * head)
        gn = side(numer, k * group * head, group, head)
        gt = side(grad_totals, k * group, group, 1)
        weights_win, weights = window_weights(
            q, phi, k_n[pl.ds(start, keys), lanes], phi_kn[one, wide], win, lin, scale
        )
        grad_w = nn(v_n[pl.ds(start, keys), lanes], gn) + gt
        gs = (grad_w * weights_win).astype(bf16)
        gl = jnp.where(lin, grad_w[:CHUNK], 0.0).astype(bf16)
        gq = nn(k_t[lanes, two][:, :keys], gs) * scale
        gk = nt(q, gs) * scale
        gv = nt(gn, weights.astype(bf16))
        aug = augmented(gn, gt, group * CHUNK, head)
        gphi_q = nn(phi_kt[wide, one], gl) + use * nn(states[0, k], aug)
        gphi_k = nt(phi, gl)
        after = later[k]
        after_bf = after.astype(bf16)
        v_aug = v_a[k * AUG : (k + 1) * AUG, one]
        gphi_k = gphi_k + incl * nn(after_bf, v_aug)
        from_later = incl * nn(after.T.astype(bf16), phi_kt[wide, one])[:head]
        gv = gv + jnp.concatenate([from_later, jnp.zeros((head, keys - CHUNK), f32)], axis=1)
        later[k] = nt(phi, augmented(gn, gt * use, group * CHUNK, head, use)) + passing * after
        g_kt[lanes, two] += jnp.concatenate([gk, pad], axis=1)
        g_vt[lanes, two] += jnp.concatenate([gv, pad], axis=1)
        acc_phi[wide, one] += gphi_k
        heads = [slice(g * CHUNK, (g + 1) * CHUNK) for g in range(group)]
        rows = slice(k * group * head, (k + 1) * group * head)
        grad_phi = jnp.concatenate([gphi_q[:, at] for at in heads], axis=0)
        phi_rows = phi_q[2 * k * group * head : 2 * (k + 1) * group * head, :]
        ga = hedgehog_back(phi_rows, grad_phi, head)
        gq_rows = jnp.concatenate([gq[:, at] for at in heads], axis=0) + tn(map_q[k], ga)
        g_map_q[k] += nt(q_t[rows, :], ga)
        grads.append(rope(gq_rows, cos_q[...], -sin_q[...]))
    g_nat[...] = jnp.concatenate(grads, axis=0).T.astype(bf16)


def keys_back_body(dims, last_docs, factors, g_kt, g_vt, g_phi, v_a, phi_kt, k_t, doc_row, map_k, *rest):
    kv_heads, head, chunks, rows = dims
    later, (g_own, g_halo, g_map_k) = rest[:-3], rest[-3:]
    ext = g_kt.shape[1]
    incl = (doc_row[...] == last_docs[chunks]) & (lax.broadcasted_iota(i32, (1, ext), 1) < rows)
    incl = incl.astype(f32)
    phi_grads, v_grads = [], []
    for k in range(kv_heads):
        wide = slice(2 * k * head, 2 * (k + 1) * head)
        after = jnp.zeros(later[0].shape[1:], f32)
        for i, x in enumerate(later):
            after = after + factors[i] * x[k]
        phi_grads.append(g_phi[wide, :] + incl * nn(after.astype(bf16), v_a[k * AUG : (k + 1) * AUG, :]))
        from_later = nn(after.T.astype(bf16), phi_kt[wide, :])[:head]
        v_grads.append(g_vt[k * head : (k + 1) * head, :] + incl * from_later)
    ga = hedgehog_back(phi_kt[...], jnp.concatenate(phi_grads, axis=0), head)
    g_map_k[...] = nt(k_t[...], ga)
    g_k = g_kt[...] + tn(map_k[...], ga)
    for i, grad in enumerate((g_k, jnp.concatenate(v_grads, axis=0))):
        mine = slice(i * kv_heads * head, (i + 1) * kv_heads * head)
        g_own[mine, :] = grad[:, WIN : WIN + rows]
        g_halo[mine, :] = jnp.concatenate([jnp.zeros((kv_heads * head, CHUNK - WIN), f32), grad[:, :WIN]], axis=1)


def adapters_body(
    dims, g_q, g_own, g_halo, cos, sin, ups, low, normed, g_o_up, g_o_down, g_map_q, g_map_k, *outs
):
    rows, window, head, rank = dims
    half = g_own.shape[0] // 2
    kv = keys_values(g_own[...], g_halo[...], cos[...], sin[...], 1.0)
    q_width = g_q.shape[1]
    up = nn(g_q[...], ups[:q_width]) + nn(kv, ups[q_width:])
    up_halves = halves(up, 1)

    def joined(x, axis):
        one, other = jnp.split(x, 2, axis=axis)
        return one + other

    low_halves = halves(low[...], 1)
    g_q_up = joined(tn(g_q[...], low_halves), 1)[:, :rank]
    g_kv_up = joined(tn(kv, low_halves), 1)
    if len(outs) == 1:
        (slabs,) = outs
        slabs[...] = jnp.zeros(slabs.shape, f32)
        tall = slabs.shape[2]
    else:
        by_head, shared = outs
        by_head[...] = jnp.zeros(by_head.shape, f32)

    def put(h, first, x):
        if len(outs) == 2:
            by_head[h, :, first : first + x.shape[1]] = x
            return
        for r in range(slabs.shape[0]):
            slabs[r, h, :, first : first + x.shape[1]] = x[r * tall : (r + 1) * tall]

    def put_shared(first, x):
        if len(outs) == 2:
            shared[first : first + x.shape[0], :] = x
            return
        wide = x.shape[1] // slabs.shape[0] // 128
        for i in range(x.shape[0] // tall):
            for r in range(slabs.shape[0]):
                for j in range(wide):
                    at = (r * wide + j) * 128
                    tile = x[i * tall : (i + 1) * tall, at : at + 128]
                    slabs[r, q_heads + kv_heads + (first // tall + i) * wide + j] = tile

    q_heads, kv_heads = q_width // head, half // head
    group = q_heads // kv_heads
    for h in range(q_heads):
        mine, at = slice(h * head, (h + 1) * head), (h % group) * head
        put(h, 0, g_map_q[h // group, at : at + head, at : at + head])
        put(h, head, g_q_up[mine])
        put(h, head + rank, g_o_down[mine, :])
    for h in range(kv_heads):
        mine = slice(h * head, (h + 1) * head)
        put(q_heads + h, 0, g_map_k[mine, mine])
        put(q_heads + h, head, g_kv_up[mine, rank : 2 * rank])
        put(q_heads + h, head + rank, g_kv_up[half + h * head : half + (h + 1) * head, 2 * rank :])
    put_shared(0, joined(tn(up_halves, normed[window : window + rows, :]), 0))
    put_shared(3 * rank, g_o_up[...])


def adapter_o_body(nat, lowered, att, up_product, *rest):
    branch, (g_o_up, g_o_down) = rest[:4], rest[4:]

    def joined(x, axis):
        one, other = jnp.split(x, 2, axis=axis)
        return one + other

    g_o_down[...] = joined(tn(att[...], halves(up_product[...], 1)), 1)
    o_up = 0.0
    for i, x in enumerate(branch):
        part = lowered[pl.ds(pl.multiple_of(nat[i] * x.shape[0], x.shape[0]), x.shape[0]), :]
        o_up = o_up + tn(halves(part, 1), x[...])
    g_o_up[...] = joined(o_up, 0)


def keys_values(own, halo, cos, sin, last):
    half, wide = own.shape[0] // 2, own.shape[1] - halo.shape[1]
    total = jnp.concatenate([own[:, :wide], own[:, wide:] + halo * last], axis=1)
    return jnp.concatenate([rope(total[:half], cos, -sin), total[half:]], axis=0).T.astype(bf16)


def gn_body(n_pieces, offsets, nat, g_q, g_own, g_halo, cos, sin, ups, downs, *rest):
    pieces = rest[:n_pieces]
    parts, (held, sems) = rest[n_pieces:-2], rest[-2:]
    step = pl.program_id(0)

    @pl.when(step == 0)
    def _():
        load_pieces(pieces, offsets, held, sems)

    q_width = g_q.shape[1]
    kv = keys_values(g_own[...], g_halo[...], cos[...], sin[...], (nat[3 - step] == 3).astype(f32))
    up = nn(g_q[...], ups[:q_width]) + nn(kv, ups[q_width:])
    total = nt(g_q[...], held[:, :q_width]) + nt(kv, held[:, q_width:])
    store_at(step, total + nn(halves(up, 1), downs[...]), parts)


def rms_factor(x):
    return lax.rsqrt(jnp.mean(x * x, axis=-1, keepdims=True) + epsilon)


def rms_back(x, gain, grads):
    factor = rms_factor(x)
    unit = x * factor
    scaled = grads * gain
    return factor * (scaled - unit * jnp.mean(unit * scaled, axis=-1, keepdims=True))


def hidden_body(nat, near, beside, across, tokens, gain, hidden, normed):
    total = near[...].astype(f32) + beside[...].astype(f32) + across[...].astype(f32)
    hidden[...] = tokens[...].astype(f32) + total
    normed[...] = (hidden[...] * rms_factor(hidden[...]) * gain[...]).astype(bf16)


def grad_hidden_body(nat, near, beside, across, cotangent, hidden, gain, grad, rounded):
    total = near[...].astype(f32) + beside[...].astype(f32) + across[...].astype(f32)
    grad[...] = cotangent[...].astype(f32) + rms_back(hidden[...], gain[...], total)
    rounded[...] = grad[...].astype(bf16)


def grad_tokens_body(nat, near, beside, across, tokens, grad, gain, out):
    total = near[...].astype(f32) + beside[...].astype(f32) + across[...].astype(f32)
    out[...] = (grad[...] + rms_back(tokens[...].astype(f32), gain[...], total)).astype(bf16)


def on_own_rows(body, nat, near, beside, across, placed, owned, gain, out_types):
    rows, model = near.shape
    steps = 2
    block = pl.BlockSpec((rows // steps, model), lambda i, nat: (i, 0))
    return pl.pallas_call(
        body,
        grid_spec=pltpu.PrefetchScalarGridSpec(
            num_scalar_prefetch=1,
            grid=(steps,),
            in_specs=[block] * 3
            + [pl.BlockSpec((rows // steps, model), lambda i, nat: (nat[0] * steps + i, 0))]
            + [block] * len(owned)
            + [whole((1, model))],
            out_specs=[block] * len(out_types),
        ),
        out_shape=[jax.ShapeDtypeStruct((rows, model), x) for x in out_types],
        compiler_params=params(BIG),
        cost_estimate=SMALL,
        name="own_rows",
    )(nat, near, beside, across, placed, *owned, gain)


def place_body(count, nat, *refs):
    quarters, (out, held, sems) = refs[:count], refs[-3:]
    step = pl.program_id(0)

    @pl.when(step == 0)
    def _():
        for copy in quarter_copies(quarters, held, sems):
            copy.start()

    out[...] = quarter_of(step, quarters, held, sems).astype(out.dtype)


def place(quarters, first, nat, dtype, earlier=()):
    count, (rows, width) = len(quarters), quarters[0].shape
    return pl.pallas_call(
        lambda *refs: place_body(count, *refs),
        grid_spec=pltpu.PrefetchScalarGridSpec(
            num_scalar_prefetch=1,
            grid=(count,),
            in_specs=[ANY] * (count + len(earlier)),
            out_specs=pl.BlockSpec((rows, width), lambda i, nat: (nat[first + i], 0)),
            scratch_shapes=[pltpu.VMEM((count, rows, width), bf16), pltpu.SemaphoreType.DMA((count,))],
        ),
        out_shape=jax.ShapeDtypeStruct((4 * rows, width), dtype),
        input_output_aliases={1 + count: 0} if earlier else {},
        compiler_params=params(BIG),
        cost_estimate=SMALL,
        name="place",
    )(nat, *quarters, *earlier)


def per_device(
    tokens,
    sequence_lengths,
    output_cotangent,
    query_weight,
    key_weight,
    value_weight,
    output_weight,
    gate_weight,
    up_weight,
    down_weight,
    attention_norm_gain,
    feedforward_norm_gain,
    query_adapter_down,
    key_adapter_down,
    value_adapter_down,
    output_adapter_up,
    query_adapter_up,
    key_adapter_up,
    value_adapter_up,
    output_adapter_down,
    feature_map_query,
    feature_map_key,
):
    rows, model = tokens.shape
    heads, head, rank = query_adapter_up.shape
    kv_heads = key_adapter_up.shape[0]
    group = heads // kv_heads
    q_width, kv_width = heads * head, kv_heads * head
    seq, ring = lax.axis_size("seq"), lax.axis_size("dp") * lax.axis_size("seq")
    here = lax.axis_index("seq")
    chunks = rows // CHUNK
    ext = -(-(rows + WIN) // CHUNK) * CHUNK
    quarter = rows // 4

    core, far = lax.axis_index("tensor") % 2, lax.axis_index("tensor") // 2
    nat = jnp.stack([core * 2 + far, (1 - core) * 2 + far, core * 2 + 1 - far, (1 - core) * 2 + 1 - far]).astype(i32)

    clock = Clock()
    pack = lambda q, k, v, o: jnp.concatenate([q, k, v, o.T], axis=1)
    attn_chain = Chain(clock, 0, pack, query_weight, key_weight, value_weight, output_weight)
    attn_chain.step()
    offsets = attn_chain.offsets
    n_pieces = offsets.shape[0]
    assert sum(map(sum, FFN_UNITS)) == gate_weight.shape[1]

    def turn(part):
        for chain in chains[part]:
            chain.step()


    ladder = jnp.exp(jnp.arange(head // 2).astype(f32) * (-2.0 * math.log(rope_base) / head))[:, None]
    tables = [((head // 2, rows), f32)] * 2 + [((head // 2, ext), f32)] * 2
    tables += [((1, rows), i32), ((ext, 1), i32), ((1, ext), i32)]
    scalars = [((chunks + 1,), i32), ((seq - 1,), f32), ((seq - 1,), f32)]
    cos_q, sin_q, cos_k, sin_k, q_doc, doc_col, doc_row, last_docs, passed_before, passed_after = pl.pallas_call(
        lambda *refs: tables_body(seq, *refs),
        grid_spec=pltpu.PrefetchScalarGridSpec(
            num_scalar_prefetch=2,
            grid=(1,),
            in_specs=[whole(ladder.shape)],
            out_specs=[whole(x) for x, _ in tables] + [pl.BlockSpec(memory_space=pltpu.SMEM)] * 3,
        ),
        out_shape=[jax.ShapeDtypeStruct(x, d) for x, d in tables + scalars],
        compiler_params=params(32),
        cost_estimate=SMALL,
        name="tables",
    )(sequence_lengths[0], here[None].astype(i32), ladder)
    q_doc, doc_col, doc_row, last_docs, passed_before, passed_after = clock.wait(
        q_doc, doc_col, doc_row, last_docs, passed_before, passed_after
    )
    attn_chain.step()

    halo = shifted(clock.tie(tokens)[rows - WIN :], "seq", 1)
    attn_chain.step()
    (halo,) = clock.wait(halo)
    gain_attn = attention_norm_gain.astype(f32)[None, :]
    gain_mlp = feedforward_norm_gain.astype(f32)[None, :]
    downs = jnp.concatenate([query_adapter_down, key_adapter_down, value_adapter_down], axis=1)
    low_shape = (ext, 3 * rank)

    def norm_half(half, earlier):
        size = rows // 2 + (ext - rows - WIN if half else WIN)
        return pl.pallas_call(
            lambda *refs: norm_body(half, *refs),
            grid_spec=pltpu.PrefetchScalarGridSpec(
                num_scalar_prefetch=0,
                grid=(1,),
                in_specs=[ANY, whole((WIN, model)), whole((1, model)), whole((model, 3 * rank))] + [ANY] * len(earlier),
                out_specs=[ANY, ANY],
                scratch_shapes=[
                    pltpu.VMEM((size, model), bf16),
                    pltpu.VMEM((size, model), bf16),
                    pltpu.VMEM((size, 3 * rank), f32),
                    pltpu.SemaphoreType.DMA((2,)),
                    pltpu.SemaphoreType.DMA((2, 2)),
                ],
            ),
            out_shape=[jax.ShapeDtypeStruct((ext, model), bf16), jax.ShapeDtypeStruct(low_shape, f32)],
            input_output_aliases={4: 0, 5: 1} if earlier else {},
            compiler_params=params(BIG),
            cost_estimate=SMALL,
            name="norm",
        )(clock.tie(tokens), halo, gain_attn, downs, *earlier)

    normed_low = clock.wait(*norm_half(0, ()))
    attn_chain.step()
    normed, low = clock.wait(*norm_half(1, normed_low))
    attn_chain.step()
    all_units = [x for part in FFN_UNITS for x in part]
    pack_in = (
        gate_weight, up_weight, down_weight, query_adapter_up, key_adapter_up, value_adapter_up,
        feature_map_query, feature_map_key, output_adapter_up,
    )
    pack_out = [(gate_weight.shape[0], 3 * x) for x in all_units] + [
        (q_width + 2 * kv_width, 3 * rank),
        (q_width + 2 * kv_width, 6 * rank),
        (kv_heads, group * head, group * head),
        (kv_width, kv_width),
        (model, rank),
    ]
    packed = pl.pallas_call(
        lambda *refs: pack_body(all_units, *refs),
        grid_spec=pltpu.PrefetchScalarGridSpec(
            num_scalar_prefetch=0,
            grid=(1,),
            in_specs=[whole(x.shape) for x in pack_in],
            out_specs=[whole(x) for x in pack_out],
        ),
        out_shape=[jax.ShapeDtypeStruct(x, bf16) for x in pack_out],
        compiler_params=params(BIG),
        cost_estimate=SMALL,
        name="pack",
    )(clock.tie(gate_weight), *pack_in[1:])
    *packed, ups, ups_twice, maps_q, maps_k, o_up = clock.wait(*packed)
    chains = [[Chain(clock, 1, lambda x: x, packed[2 * i]), Chain(clock, -1, lambda x: x, packed[2 * i + 1])] for i in range(2)]
    for _ in range(ring - 6):
        attn_chain.step()
    attn_pieces = attn_chain.pieces()
    turn(0)

    sems = pltpu.SemaphoreType.DMA((n_pieces,))
    qkv_width = q_width + 2 * kv_width
    held_qkv = pltpu.VMEM((model, qkv_width), bf16)
    held_o = pltpu.VMEM((model, q_width), bf16)

    dims = (rows, ext, q_width, kv_width, head, n_pieces, chunks)
    shapes = [
        ((q_width, rows), bf16),
        ((2 * q_width, rows), bf16),
        ((ext, kv_width), bf16),
        ((kv_width, ext), bf16),
        ((ext, kv_width), bf16),
        ((kv_heads * AUG, ext), bf16),
        ((ext, 2 * kv_width), bf16),
        ((2 * kv_width, ext), bf16),
        ((kv_heads, AUG, 2 * head), f32),
    ]
    prep_in = (normed, low, ups_twice, cos_q, sin_q, cos_k, sin_k, maps_q, maps_k, doc_row)
    q_t, phi_q, k_n, k_t, v_n, v_a, phi_kn, phi_kt, contrib = pl.pallas_call(
        lambda *refs: prep_body(dims, *refs),
        grid_spec=pltpu.PrefetchScalarGridSpec(
            num_scalar_prefetch=2,
            grid=(1,),
            in_specs=[whole(x.shape) for x in prep_in] + [ANY] * n_pieces,
            out_specs=[whole(s) for s, _ in shapes],
            scratch_shapes=[held_qkv, sems],
        ),
        out_shape=[jax.ShapeDtypeStruct(s, d) for s, d in shapes],
        compiler_params=params(56),
        cost_estimate=SMALL,
        name="prep",
    )(clock.tie(offsets), last_docs, *prep_in, *attn_pieces)
    (contrib,) = clock.wait(contrib)
    turn(0)

    coming = clock.wait(*[shifted(contrib, "seq", by) for by in range(1, seq)])
    column = lambda r: pl.BlockSpec((r, CHUNK), lambda c, *_: (0, c))
    att, att_t, totals, states = pl.pallas_call(
        lambda *refs: forward_body((kv_heads, group, head), *refs),
        grid_spec=pltpu.PrefetchScalarGridSpec(
            num_scalar_prefetch=2,
            grid=(chunks,),
            in_specs=[
                column(q_width),
                column(2 * q_width),
                whole(k_n.shape),
                whole(v_a.shape),
                whole(phi_kn.shape),
                whole(doc_col.shape),
                whole(doc_row.shape),
                column(1),
            ]
            + [whole(contrib.shape)] * len(coming),
            out_specs=[
                pl.BlockSpec((CHUNK, q_width), lambda c, *_: (c, 0)),
                column(q_width),
                column(heads),
                pl.BlockSpec((1, kv_heads, 2 * head, AUG), lambda c, *_: (c, 0, 0, 0)),
            ],
            scratch_shapes=[pltpu.VMEM(contrib.shape, f32)],
        ),
        out_shape=[
            jax.ShapeDtypeStruct((rows, q_width), bf16),
            jax.ShapeDtypeStruct((q_width, rows), f32),
            jax.ShapeDtypeStruct((heads, rows), f32),
            jax.ShapeDtypeStruct((chunks, kv_heads, 2 * head, AUG), bf16),
        ],
        compiler_params=params(BIG),
        cost_estimate=SMALL,
        name="attend",
    )(clock.tie(last_docs), passed_before, q_t, phi_q, k_n, v_a, phi_kn, doc_col, doc_row, q_doc, *coming)
    att = clock.tie(att)
    turn(0)

    o_down = output_adapter_down.reshape(q_width, rank)
    o_up_t = jnp.concatenate([output_adapter_up.T, output_adapter_up.T], axis=0)
    one_quarter = jax.ShapeDtypeStruct((quarter, model), bf16)

    *o_parts, lowered = pl.pallas_call(
        lambda *refs: o_body(n_pieces, qkv_width, *refs),
        grid_spec=pltpu.PrefetchScalarGridSpec(
            num_scalar_prefetch=2,
            grid=(4,),
            in_specs=[
                pl.BlockSpec((quarter, q_width), lambda i, off, nat: (nat[3 - i], 0)),
                whole(o_down.shape),
                whole(o_up_t.shape),
            ]
            + [ANY] * n_pieces,
            out_specs=[whole((quarter, model))] * 4
            + [pl.BlockSpec((quarter, rank), lambda i, off, nat: (nat[3 - i], 0))],
            scratch_shapes=[held_o, sems],
        ),
        out_shape=[one_quarter] * 4 + [jax.ShapeDtypeStruct((rows, rank), f32)],
        compiler_params=params(BIG),
        cost_estimate=SMALL,
        name="project",
    )(clock.tie(offsets), nat, att, o_down, o_up_t, *attn_pieces)
    o_far0, o_far1, o_near0, o_near1 = clock.wait(*o_parts)
    turn(0)
    o_far0, o_near0 = clock.wait(o_far0, o_near0)
    beside = exchange(o_far0, "tensor", 1)
    beside_near = exchange(o_near0, "tensor", 1)
    beside, beside_near = clock.wait(beside, beside_near)
    o_far = clock.tie((o_far1.astype(f32) + beside.astype(f32)).astype(bf16))
    across = exchange(o_far, "tensor", 2)
    turn(0)
    (across,) = clock.wait(across)
    beside = beside_near
    hidden, normed_mlp = on_own_rows(
        hidden_body, clock.tie(nat), o_near1, beside, across, tokens, (), gain_mlp, (f32, bf16)
    )
    hidden, normed_mlp = clock.wait(hidden, normed_mlp)
    for _ in range(ring - 7):
        turn(0)
    normed_mlp = clock.tie(normed_mlp)
    across, beside = exchange(normed_mlp, "tensor", 2), exchange(normed_mlp, "tensor", 1)
    (beside,) = clock.wait(beside)
    turn(0)
    (across,) = clock.wait(across)
    for chain in chains[0]:
        chain.settle()
    turn(1)
    last = clock.tie(exchange(clock.tie(across), "tensor", 1))
    normed_mlp = [normed_mlp, beside, across, last]

    def ffn(part, which, quarters, sums):
        units, last = FFN_UNITS[part][which], part == len(FFN_UNITS) - 1
        lots = [chain.pieces() for chain in chains[part][which]]
        sizes = tuple(map(len, lots))
        pieces = [piece for lot in lots for piece in lot]
        ring_offsets = jnp.concatenate([chain.offsets for chain in chains[part][which]])
        first = quarters[0]
        summed = jax.ShapeDtypeStruct((2, quarter, model), f32)
        return pl.pallas_call(
            lambda *refs: ffn_body(sizes, units, bool(sums), last, *refs),
            grid_spec=pltpu.PrefetchScalarGridSpec(
                num_scalar_prefetch=2,
                grid=(2,),
                in_specs=[pl.BlockSpec((quarter, model), lambda i, off, nat: (nat[first - i], 0))]
                + [ANY] * (2 + len(pieces) + len(sums)),
                out_specs=[ANY] * (4 if last else 2),
                scratch_shapes=[
                    pltpu.VMEM((2, quarter, model), bf16),
                    pltpu.SemaphoreType.DMA((2,)),
                    pltpu.VMEM((3, model, sum(units)), bf16),
                    pltpu.SemaphoreType.DMA((3, len(pieces))),
                    pltpu.VMEM((2, 2, quarter, model), bf16 if last else f32),
                    pltpu.SemaphoreType.DMA((2, 2)),
                ]
                + [pltpu.VMEM((2, 2, quarter, model), f32), pltpu.SemaphoreType.DMA((2, 2))] * bool(sums),
            ),
            out_shape=[one_quarter] * 4 if last else [summed] * 2,
            compiler_params=params(BIG),
            cost_estimate=SMALL,
            name="feed_forward",
        )(clock.tie(ring_offsets), nat, output_cotangent, *[normed_mlp[q] for q in quarters], *pieces, *sums)

    sums_far = sums_near = ()
    up, down, both = slice(0, 1), slice(1, 2), slice(0, 2)
    for way in (up, down):
        sums_far = clock.wait(*ffn(0, way, (3, 2), sums_far))
        turn(1)
        sums_near = clock.wait(*ffn(0, way, (1, 0), sums_near))
        turn(1)
    for _ in range(ring - 6):
        turn(1)
    gn_far0, gn_far1, mlp_far0, mlp_far1 = ffn(1, both, (3, 2), sums_far)
    gn_far0, mlp_far0 = clock.wait(gn_far0, mlp_far0)
    beside = exchange(gn_far0, "tensor", 1)
    mlp_beside_far = exchange(mlp_far0, "tensor", 1)
    (beside,) = clock.wait(beside)
    across = exchange(clock.tie((gn_far1.astype(f32) + beside.astype(f32)).astype(bf16)), "tensor", 2)
    gn_near0, gn_near1, mlp_near0, mlp_near1 = ffn(1, both, (1, 0), sums_near)
    gn_near0, mlp_near0 = clock.wait(gn_near0, mlp_near0)
    across, gn_near0 = clock.wait(across, gn_near0)
    beside = exchange(gn_near0, "tensor", 1)
    (beside,) = clock.wait(beside)
    grad_hidden, branch = on_own_rows(
        grad_hidden_body, clock.tie(nat), gn_near1, beside, across, output_cotangent, (hidden,), gain_mlp, (f32, bf16)
    )
    grad_hidden, branch = clock.wait(grad_hidden, branch)
    across, beside = exchange(branch, "tensor", 2), exchange(branch, "tensor", 1)
    mlp_beside = exchange(clock.tie(mlp_near0), "tensor", 1)
    (beside,) = clock.wait(beside)

    o_down_t = jnp.concatenate([o_down.T, o_down.T], axis=0)
    sizes = [((q_width, rows), bf16), ((heads, rows), f32), ((rows, rank), f32), ((kv_heads, 2 * head, AUG), f32)]

    def go_part(first, quarters, earlier):
        by_quarter = lambda r: pl.BlockSpec((r, quarter), lambda i, off, nat, before: (0, nat[first + i]))
        late = bool(earlier)
        return pl.pallas_call(
            lambda *refs: go_body((n_pieces, qkv_width, kv_heads, group, head, late), *refs),
            grid_spec=pltpu.PrefetchScalarGridSpec(
                num_scalar_prefetch=3,
                grid=(2,),
                in_specs=[
                    whole((model, rank)),
                    whole(o_down_t.shape),
                    by_quarter(q_width),
                    by_quarter(heads),
                    by_quarter(2 * q_width),
                    by_quarter(1),
                ]
                + [ANY] * (2 + n_pieces)
                + ([ANY] * 3 + [whole(sizes[3][0])]) * late,
                out_specs=[
                    by_quarter(q_width),
                    by_quarter(heads),
                    pl.BlockSpec((quarter, rank), lambda i, off, nat, before: (nat[first + i], 0)),
                    whole(sizes[3][0]),
                ],
                scratch_shapes=[
                    pltpu.VMEM((2, quarter, model), bf16),
                    pltpu.SemaphoreType.DMA((2,)),
                    held_o,
                    sems,
                ],
            ),
            out_shape=[jax.ShapeDtypeStruct(s, d) for s, d in sizes],
            input_output_aliases={11 + n_pieces + i: i for i in range(3)} if late else {},
            compiler_params=params(BIG),
            cost_estimate=SMALL,
            name="project_back",
        )(
            clock.tie(offsets), nat, last_docs, o_up, o_down_t, att_t, totals, phi_q, q_doc,
            *quarters, *attn_pieces, *earlier,
        )

    near = clock.wait(*go_part(0, (branch, beside), ()))
    mlp_beside, mlp_beside_far = clock.wait(mlp_beside, mlp_beside_far)
    mlp_far = clock.tie((mlp_far1.astype(f32) + mlp_beside_far.astype(f32)).astype(bf16))
    mlp_near = clock.tie(hidden + (mlp_near1.astype(f32) + mlp_beside.astype(f32)))
    (across,) = clock.wait(across)
    last = clock.tie(exchange(across, "tensor", 1))
    mlp_across = exchange(clock.tie(mlp_far), "tensor", 2)
    branch = [branch, beside, across, last]
    numer, grad_totals, up_product, dstate = clock.wait(*go_part(2, branch[2:], near))

    coming = [shifted(dstate, "seq", -by) for by in range(1, seq)]

    back_column = lambda r: pl.BlockSpec((r, CHUNK), lambda c, *_: (0, chunks - 1 - c))
    back_in = (
        (q_t, back_column(q_width)),
        (phi_q, back_column(2 * q_width)),
        (numer, back_column(q_width)),
        (grad_totals, back_column(heads)),
        (k_n, None),
        (k_t, None),
        (v_n, None),
        (v_a, None),
        (phi_kn, None),
        (phi_kt, None),
        (doc_col, None),
        (doc_row, None),
        (q_doc, back_column(1)),
        (states, pl.BlockSpec((1, kv_heads, 2 * head, AUG), lambda c, *_: (chunks - 1 - c, 0, 0, 0))),
        (cos_q, back_column(head // 2)),
        (sin_q, back_column(head // 2)),
        (maps_q, None),
    )
    g_q, g_kt, g_vt, g_phi, g_map_q = pl.pallas_call(
        lambda *refs: backward_body((kv_heads, group, head, chunks), *refs),
        grid_spec=pltpu.PrefetchScalarGridSpec(
            num_scalar_prefetch=1,
            grid=(chunks,),
            in_specs=[whole(x.shape) if spec is None else spec for x, spec in back_in],
            out_specs=[
                pl.BlockSpec((CHUNK, q_width), lambda c, *_: (chunks - 1 - c, 0)),
                whole((kv_width, ext)),
                whole((kv_width, ext)),
                whole((2 * kv_width, ext)),
                whole((kv_heads, group * head, group * head)),
            ],
            scratch_shapes=[pltpu.VMEM(dstate.shape, f32)],
        ),
        out_shape=[
            jax.ShapeDtypeStruct((rows, q_width), bf16),
            jax.ShapeDtypeStruct((kv_width, ext), f32),
            jax.ShapeDtypeStruct((kv_width, ext), f32),
            jax.ShapeDtypeStruct((2 * kv_width, ext), f32),
            jax.ShapeDtypeStruct((kv_heads, group * head, group * head), f32),
        ],
        compiler_params=params(52),
        cost_estimate=SMALL,
        name="attend_back",
    )(clock.tie(last_docs), *[x for x, _ in back_in])

    g_q, g_kt, g_vt, g_phi, g_map_q = clock.wait(g_q, g_kt, g_vt, g_phi, g_map_q)
    coming = clock.wait(*coming)
    (mlp_across,) = clock.wait(mlp_across)
    out_rows = clock.tie((mlp_near + mlp_across.astype(f32)).astype(bf16))
    out_across, out_beside = exchange(out_rows, "tensor", 2), exchange(out_rows, "tensor", 1)
    g_own, g_halo, g_map_k = pl.pallas_call(
        lambda *refs: keys_back_body((kv_heads, head, chunks, rows), *refs),
        grid_spec=pltpu.PrefetchScalarGridSpec(
            num_scalar_prefetch=2,
            grid=(1,),
            in_specs=[whole(x.shape) for x in (g_kt, g_vt, g_phi, v_a, phi_kt, k_t, doc_row, maps_k, *coming)],
            out_specs=[whole((2 * kv_width, rows)), whole((2 * kv_width, CHUNK)), whole((kv_width, kv_width))],
        ),
        out_shape=[
            jax.ShapeDtypeStruct((2 * kv_width, rows), f32),
            jax.ShapeDtypeStruct((2 * kv_width, CHUNK), f32),
            jax.ShapeDtypeStruct((kv_width, kv_width), f32),
        ],
        compiler_params=params(BIG),
        cost_estimate=SMALL,
        name="keys_back",
    )(clock.tie(last_docs), passed_after, g_kt, g_vt, g_phi, v_a, phi_kt, k_t, doc_row, maps_k, *coming)

    g_own, g_halo, g_map_k = clock.wait(g_own, g_halo, g_map_k)
    g_halo = shifted(g_halo, "seq", -1)
    o_in = (lowered, att, up_product, *branch)
    g_o_up, g_o_down = pl.pallas_call(
        adapter_o_body,
        grid_spec=pltpu.PrefetchScalarGridSpec(
            num_scalar_prefetch=1,
            grid=(1,),
            in_specs=[whole(x.shape) for x in o_in],
            out_specs=[whole((rank, model)), whole((q_width, rank))],
        ),
        out_shape=[jax.ShapeDtypeStruct((rank, model), f32), jax.ShapeDtypeStruct((q_width, rank), f32)],
        compiler_params=params(BIG),
        cost_estimate=SMALL,
        name="adapter_o",
    )(clock.tie(nat), *o_in)
    g_o_up, g_o_down, g_halo = clock.wait(g_o_up, g_o_down, g_halo)

    downs_t = jnp.concatenate([downs.T, downs.T], axis=0)

    by_rows = lambda w: pl.BlockSpec((quarter, w), lambda i, off, nat: (nat[3 - i], 0))
    by_columns = lambda r: pl.BlockSpec((r, quarter), lambda i, off, nat: (0, nat[3 - i]))
    gn_parts = pl.pallas_call(
        lambda *refs: gn_body(n_pieces, *refs),
        grid_spec=pltpu.PrefetchScalarGridSpec(
            num_scalar_prefetch=2,
            grid=(4,),
            in_specs=[
                by_rows(q_width),
                by_columns(2 * kv_width),
                whole(g_halo.shape),
                by_columns(head // 2),
                by_columns(head // 2),
                whole(ups.shape),
                whole(downs_t.shape),
            ]
            + [ANY] * n_pieces,
            out_specs=[whole((quarter, model))] * 4,
            scratch_shapes=[held_qkv, sems],
        ),
        out_shape=[one_quarter] * 4,
        compiler_params=params(BIG),
        cost_estimate=SMALL,
        name="norm_back",
    )(clock.tie(offsets), nat, g_q, g_own, g_halo, cos_q, sin_q, ups, downs_t, *attn_pieces)
    gn_far0, gn_far1, gn_near0, gn_near1 = clock.wait(*gn_parts)
    out_across, out_beside, gn_far0, gn_near0 = clock.wait(out_across, out_beside, gn_far0, gn_near0)
    beside, beside_near = exchange(gn_far0, "tensor", 1), exchange(gn_near0, "tensor", 1)
    beside, beside_near = clock.wait(beside, beside_near)
    gn_far = clock.tie((gn_far1.astype(f32) + beside.astype(f32)).astype(bf16))
    across = exchange(gn_far, "tensor", 2)

    adapters_in = (g_q, g_own, g_halo, cos_q, sin_q, ups, low[WIN : WIN + rows], normed, g_o_up, g_o_down, g_map_q, g_map_k)
    tall = head // ring
    tiles = 4 * rank // 8 * (model // ring // 128)
    in_tiles = tall == 8 and rank == 8 and model // ring % 128 == 0 and 2 * head == 128
    if in_tiles:
        sizes = [((ring, heads + kv_heads + tiles, tall, 2 * head), f32)]
    else:
        sizes = [((heads + kv_heads, head, 2 * head), f32), ((4 * rank, model), f32)]
    parts = pl.pallas_call(
        lambda *refs: adapters_body((rows, WIN, head, rank), *refs),
        grid_spec=pltpu.PrefetchScalarGridSpec(
            num_scalar_prefetch=0,
            grid=(1,),
            in_specs=[whole(x.shape) for x in adapters_in],
            out_specs=[whole(x) for x, _ in sizes],
        ),
        out_shape=[jax.ShapeDtypeStruct(x, d) for x, d in sizes],
        compiler_params=params(BIG),
        cost_estimate=SMALL,
        name="adapters",
    )(clock.tie(adapters_in[0]), *adapters_in[1:])
    if not in_tiles:
        parts = [
            parts[0].reshape(heads + kv_heads, ring, tall, 2 * head).transpose(1, 0, 2, 3),
            parts[1].reshape(4 * rank, ring, model // ring).transpose(1, 0, 2),
        ]
    parts = clock.wait(*parts)

    def halved(x, axis, half, bit, over=0, sent_as=f32):
        x = x.reshape(x.shape[:over] + (2, half) + x.shape[over + 1 :])
        send = lax.dynamic_index_in_dim(x, 1 - bit, over, keepdims=False)
        return lax.dynamic_index_in_dim(x, bit, over, keepdims=False), exchange(send.astype(sent_as), axis, half)

    def summed_over(axis, size, xs):
        while size > 1:
            half = size // 2
            both = [halved(x, axis, half, (lax.axis_index(axis) // half) % 2, 0, bf16) for x in xs]
            coming = clock.wait(*[coming for _, coming in both])
            xs = [kept + x.astype(f32) for (kept, _), x in zip(both, coming)]
            size = half
            yield xs

    dp = ring // seq
    parts = [x.reshape((dp, seq) + x.shape[1:]) for x in parts]
    for parts in summed_over("dp", dp, parts):
        pass
    along_seq = summed_over("seq", seq, clock.wait(*[x[0] for x in parts]))
    parts = next(along_seq)
    (across,) = clock.wait(across)
    (grad_rows,) = on_own_rows(
        grad_tokens_body, clock.tie(nat), gn_near1, beside_near, across, tokens, (grad_hidden,), gain_attn, (bf16,)
    )
    (grad_rows,) = clock.wait(grad_rows)
    across, beside = exchange(grad_rows, "tensor", 2), exchange(grad_rows, "tensor", 1)
    out_last = clock.tie(exchange(out_across, "tensor", 1))
    (beside,) = clock.wait(beside)
    grad_tokens = clock.tie(place([grad_rows, beside], 0, nat, f32))
    for parts in along_seq:
        pass
    by_head, shared = parts[0][0], parts[-1][0]
    if in_tiles:
        by_head, shared = by_head[: heads + kv_heads], by_head[heads + kv_heads :]
        shared = shared.reshape(4 * rank // 8, -1, 8, 128).transpose(0, 2, 1, 3)
    shared = shared.reshape(4 * rank, 2, 2, -1).transpose(2, 1, 0, 3)
    pick = lambda x, i: lax.dynamic_index_in_dim(x, i, 0, keepdims=False)
    shared = pick(shared, core) + clock.tie(exchange(pick(shared, 1 - core), "tensor", 1))
    shared = clock.tie(shared.reshape(2, 4 * rank, -1))
    block_out = clock.tie(place([out_rows, out_beside, out_across, out_last], 0, nat, bf16))
    (across,) = clock.wait(across)
    (last,) = clock.wait(exchange(across, "tensor", 1))
    shared = clock.tie(shared)
    sent = exchange(pick(shared, 1 - far), "tensor", 2)
    grad_tokens = clock.tie(place([across, last], 2, nat, f32, (grad_tokens,)))
    shared = (pick(shared, far) + clock.tie(sent)).T
    of_q, of_kv = by_head[:heads], by_head[heads:]
    first, second = slice(head, head + rank), slice(head + rank, head + 2 * rank)
    out = [of_q[..., first], of_kv[..., first], of_kv[..., second], of_q[..., second], of_q[..., :head], of_kv[..., :head]]
    return (
        block_out,
        grad_tokens,
        shared[:, :rank] + clock.now.astype(f32),
        shared[:, rank : 2 * rank],
        shared[:, 2 * rank : 3 * rank],
        shared[:, 3 * rank :],
        *out,
    )


def solution(mesh):
    return jax.shard_map(
        per_device,
        mesh=mesh,
        in_specs=(
            P(("dp", "seq"), None),
            P("dp", None),
            P(("dp", "seq"), None),
            P(("dp", "seq"), "tensor"),
            P(("dp", "seq"), "tensor"),
            P(("dp", "seq"), "tensor"),
            P("tensor", ("dp", "seq")),
            P(("dp", "seq"), "tensor"),
            P(("dp", "seq"), "tensor"),
            P("tensor", ("dp", "seq")),
            P(),
            P(),
            P(),
            P(),
            P(),
            P(),
            P("tensor", None, None),
            P("tensor", None, None),
            P("tensor", None, None),
            P("tensor", None, None),
            P("tensor", None, None),
            P("tensor", None, None),
        ),
        out_specs=(
            P(("dp", "seq"), None),
            P(("dp", "seq"), None),
            P(("dp", "seq", "tensor"), None),
            P(("dp", "seq", "tensor"), None),
            P(("dp", "seq", "tensor"), None),
            P(("dp", "seq", "tensor"), None),
            P("tensor", ("dp", "seq"), None),
            P("tensor", ("dp", "seq"), None),
            P("tensor", ("dp", "seq"), None),
            P("tensor", ("dp", "seq"), None),
            P("tensor", ("dp", "seq"), None),
            P("tensor", ("dp", "seq"), None),
        ),
        check_vma=False,
    )
```

```python
import math

import jax
import jax.numpy as jnp
from jax import lax
from jax.experimental import pallas as pl
from jax.experimental.pallas import tpu as pltpu
from jax.sharding import PartitionSpec as P

WIN = 64
CHUNK = 128
AUG = 80
RING = 8
FFN_UNITS = ((512, 512), (512, 512))
BIG = 60

epsilon = 1e-05
rope_base = 500000.0
bf16, f32, i32 = jnp.bfloat16, jnp.float32, jnp.int32
MIB = 1 << 20


def nn(a, b):
    return lax.dot_general(a, b, (((1,), (0,)), ((), ())), preferred_element_type=f32)


def nt(a, b):
    return lax.dot_general(a, b, (((1,), (1,)), ((), ())), preferred_element_type=f32)


def tn(a, b):
    return lax.dot_general(a, b, (((0,), (0,)), ((), ())), preferred_element_type=f32)


def halves(x, axis):
    high = x.astype(bf16)
    return jnp.concatenate([high, (x - high.astype(f32)).astype(bf16)], axis=axis)


def exchange(x, axis, bit):
    count = lax.axis_size(axis)
    return lax.ppermute(x, axis, [(i, i ^ bit) for i in range(count)])


def shifted(x, axis, by):
    count = lax.axis_size(axis)
    return lax.ppermute(x, axis, [(i, i + by) for i in range(count) if 0 <= i + by < count])


def place_of(index, seq):
    row, col = index // seq, index % seq
    return row * seq + (col if row % 2 == 0 else seq - 1 - col)


def place_of_traced(index, seq):
    row, col = index // seq, index % seq
    return row * seq + jnp.where(row % 2 == 0, col, seq - 1 - col)


class Clock:
    def __init__(self):
        self.now = jnp.zeros((), i32)

    def wait(self, *arrays):
        *out, self.now = lax.optimization_barrier((*arrays, self.now))
        return out

    def tie(self, x):
        return self.wait(x)[0]


class Chain:
    def __init__(self, clock, way, pack, *blocks):
        block = pack(*clock.wait(*blocks))
        dp, seq = lax.axis_size("dp"), lax.axis_size("seq")
        self.clock, self.count = clock, dp * seq
        self.ringed = self.count <= RING
        rows = block.shape[0]
        if not self.ringed:
            self.lanes = [[lax.all_gather(block, ("dp", "seq"), axis=0, tiled=True)]]
            self.offsets = jnp.zeros((1,), i32)
            return
        order = [place_of(i, seq) for i in range(self.count)]
        up = [(order[i], order[(i + 1) % self.count]) for i in range(self.count)]
        down = [(j, i) for i, j in up]
        place = place_of_traced(lax.axis_index("dp") * seq + lax.axis_index("seq"), seq)
        steps = jnp.arange(self.count)
        came_up = place_of_traced((place - steps) % self.count, seq) * rows
        came_down = place_of_traced((place + steps) % self.count, seq) * rows
        if way:
            self.lanes, self.ways = [[block]], [up if way > 0 else down]
            self.offsets = (came_up if way > 0 else came_down).astype(i32)
        else:
            half = rows // 2
            self.lanes, self.ways = [[block[:half]], [block[half:]]], [up, down]
            self.offsets = jnp.concatenate([came_up, came_down + half]).astype(i32)

    def settle(self):
        if self.ringed:
            came = self.clock.wait(*[lane[-1] for lane in self.lanes])
            for lane, x in zip(self.lanes, came):
                lane[-1] = x

    def step(self):
        if self.ringed:
            for lane, way in zip(self.lanes, self.ways):
                (lane[-1],) = self.clock.wait(lane[-1])
                lane.append(lax.ppermute(lane[-1], ("dp", "seq"), way))

    def pieces(self):
        self.settle()
        return [piece for lane in self.lanes for piece in lane]


def load_pieces(pieces, offsets, held, sems, first=0):
    copies = [
        pltpu.make_async_copy(
            piece.at[:, pl.ds(first, held.shape[1])],
            held.at[pl.ds(pl.multiple_of(offsets[i], 16), piece.shape[0])],
            sems.at[i],
        )
        for i, piece in enumerate(pieces)
    ]
    for copy in copies:
        copy.start()
    for copy in copies:
        copy.wait()


def params(limit):
    return pltpu.CompilerParams(vmem_limit_bytes=limit * MIB)


SMALL = pl.CostEstimate(flops=1, bytes_accessed=1, transcendentals=0)


ANY = pl.BlockSpec(memory_space=pl.ANY)


def whole(shape):
    return pl.BlockSpec(shape, lambda *_: (0,) * len(shape))


def rope(x, cos, sin):
    width = 2 * cos.shape[0]
    half = width // 2
    out = []
    for at in range(0, x.shape[0], width):
        x1, x2 = x[at : at + half], x[at + half : at + width]
        out += [x1 * cos - x2 * sin, x2 * cos + x1 * sin]
    return jnp.concatenate(out, axis=0)


def hedgehog(a, width):
    out = []
    for at in range(0, a.shape[0], width):
        one = a[at : at + width]
        for e in (
            jnp.exp(one - jnp.max(one, axis=0, keepdims=True)),
            jnp.exp(jnp.min(one, axis=0, keepdims=True) - one),
        ):
            out.append(e * (1.0 / jnp.sum(e, axis=0, keepdims=True)))
    return jnp.concatenate(out, axis=0).astype(bf16)


def hedgehog_back(phi, grad, width):
    out = []
    for at in range(0, phi.shape[0], 2 * width):
        p1, p2 = phi[at : at + width].astype(f32), phi[at + width : at + 2 * width].astype(f32)
        d1, d2 = grad[at : at + width], grad[at + width : at + 2 * width]
        out.append(
            p1 * (d1 - jnp.sum(p1 * d1, axis=0, keepdims=True))
            - p2 * (d2 - jnp.sum(p2 * d2, axis=0, keepdims=True))
        )
    return jnp.concatenate(out, axis=0).astype(bf16)


def tables_body(seq, lengths, here, ladder, cos_q, sin_q, cos_k, sin_k, q_doc, doc_col, doc_row, last, before, after):
    rows, ext = q_doc.shape[1], doc_row.shape[1]
    ends = [lengths[0]]
    for i in range(1, lengths.shape[0]):
        ends.append(ends[-1] + lengths[i])

    def document(at):
        doc, start = 0, 0
        for end in ends:
            past = at >= end
            doc = doc + past.astype(i32)
            start = jnp.where(past, end, start)
        return jnp.where(at >= 0, doc, -1), at - start

    def angles(relative, cos, sin):
        angle = ladder[...] * relative.astype(f32)
        cos[...] = jnp.cos(angle)
        sin[...] = jnp.sin(angle)

    def passing(block):
        ahead = rows * block - WIN - 1
        return (document(ahead)[0] == document(ahead + rows)[0]).astype(f32)

    first = here[0] * rows
    q_doc[...], relative = document(first + lax.broadcasted_iota(i32, (1, rows), 1))
    angles(relative, cos_q, sin_q)
    index = lax.broadcasted_iota(i32, (1, ext), 1)
    doc, relative = document(first - WIN + index)
    doc_row[...] = jnp.where(index < rows + WIN, doc, -2)
    angles(relative, cos_k, sin_k)
    index = lax.broadcasted_iota(i32, (ext, 1), 0)
    doc_col[...] = jnp.where(index < rows + WIN, document(first - WIN + index)[0], -2)
    for i in range(last.shape[0]):
        last[i] = document(first - WIN - 1 + CHUNK * i)[0]
    earlier = later = jnp.float32(1.0)
    for by in range(seq - 1):
        before[by], after[by] = earlier, later
        earlier = earlier * passing(jnp.maximum(here[0] - by - 1, 0))
        later = later * passing(jnp.minimum(here[0] + by + 1, seq - 1))


def norm_body(half, tokens, halo, gain, downs, *rest):
    normed, low, held, out_held, low_held, sems, out_sems = rest[-7:]
    rows, window, size = tokens.shape[0] // 2, halo.shape[0], held.shape[0]
    first = 0 if half else window
    part = rows // 2
    place = half * (window + rows)

    def copy(i):
        source = tokens.at[pl.ds(half * rows + i * part, part)]
        return pltpu.make_async_copy(source, held.at[pl.ds(first + i * part, part)], sems.at[i])

    def out_copies(i):
        at, count = spans[i][0], spans[i][1] - spans[i][0]
        return [
            pltpu.make_async_copy(x.at[pl.ds(at, count)], y.at[pl.ds(place + at, count)], out_sems.at[k, i])
            for k, (x, y) in enumerate(((out_held, normed), (low_held, low)))
        ]

    spans = [(0, first + part), (first + part, size)]
    for i in range(2):
        copy(i).start()
    if half:
        held[2 * part :, :] = jnp.zeros((size - 2 * part, held.shape[1]), bf16)
    else:
        held[:window, :] = halo[...]
    for i, (start, end) in enumerate(spans):
        copy(i).wait()
        x = held[start:end, :].astype(f32)
        out = (x * rms_factor(x) * gain[...]).astype(bf16)
        out_held[start:end, :] = out
        low_held[start:end, :] = nn(out, downs[...])
        for one in out_copies(i):
            one.start()
    for i in range(2):
        for one in out_copies(i):
            one.wait()


def pack_body(units, gate, up, down, q_up, k_up, v_up, map_q, map_k, o_up, *outs):
    packed, (ups, twice, maps_q, maps_k, o_up_out) = outs[:-5], outs[-5:]
    o_up_out[...] = o_up[...]
    at = 0
    for size, out in zip(units, packed):
        out[:, :size] = gate[:, at : at + size]
        out[:, size : 2 * size] = up[:, at : at + size]
        out[:, 2 * size :] = down[at : at + size, :].T
        at += size
    head, rank = q_up.shape[1:]
    at = 0
    for i, x in enumerate((q_up, k_up, v_up)):
        for h in range(x.shape[0]):
            row = jnp.concatenate(
                [jnp.zeros((head, rank), bf16)] * i + [x[h]] + [jnp.zeros((head, rank), bf16)] * (2 - i), axis=1
            )
            ups[at : at + head, :] = row
            twice[at : at + head, :] = jnp.concatenate([row, row], axis=1)
            at += head
    maps_q[...] = jnp.zeros(maps_q.shape, bf16)
    maps_k[...] = jnp.zeros(maps_k.shape, bf16)
    group = map_q.shape[0] // maps_q.shape[0]
    for h in range(map_q.shape[0]):
        mine = slice(h % group * head, (h % group + 1) * head)
        maps_q[h // group, mine, mine] = map_q[h].astype(f32).T.astype(bf16)
    for h in range(map_k.shape[0]):
        mine = slice(h * head, (h + 1) * head)
        maps_k[mine, mine] = map_k[h].astype(f32).T.astype(bf16)


def prep_body(dims, offsets, last_docs, nx, low, ups, cos_q, sin_q, cos_k, sin_k, map_q, map_k, doc_row, *rest):
    tokens, ext, q_width, kv_width, head, n_pieces, chunks = dims
    pieces, rest = rest[:n_pieces], rest[n_pieces:]
    q_t, phi_q, k_n, k_t, v_n, v_a, phi_kn, phi_kt, contrib, held, sems = rest
    load_pieces(pieces, offsets, held, sems)
    kv_heads = kv_width // head
    step = ext // 3
    v_a[...] = jnp.zeros(v_a.shape, bf16)
    for at in range(0, ext, step):
        rows = pl.ds(at, step)
        raw = nn(nx[rows, :], held[:, q_width:]) + nt(halves(low[rows, :], 1), ups[q_width:, :])
        v = raw[:, kv_width:].astype(bf16)
        v_n[rows, :] = v
        v_tr = raw[:, kv_width:].T.astype(bf16)
        for k in range(kv_heads):
            v_a[k * AUG : k * AUG + head, rows] = v_tr[k * head : (k + 1) * head]
            v_a[k * AUG + head : (k + 1) * AUG, rows] = (
                lax.broadcasted_iota(i32, (AUG - head, step), 0) < 2
            ).astype(f32).astype(bf16)
        k_rot = rope(raw[:, :kv_width].T, cos_k[:, rows], sin_k[:, rows])
        k_bf = k_rot.astype(bf16)
        k_t[:, rows] = k_bf
        k_n[rows, :] = k_rot.T.astype(bf16)
        phi = hedgehog(nn(map_k[...], k_bf), head)
        phi_kt[:, rows] = phi
        phi_kn[rows, :] = phi.astype(f32).T.astype(bf16)
    incl = (doc_row[:, :tokens] == last_docs[chunks]).astype(f32).astype(bf16)
    for k in range(kv_heads):
        masked = v_a[k * AUG : (k + 1) * AUG, :tokens] * incl
        contrib[k] = nn(masked, phi_kn[:tokens, k * 2 * head : (k + 1) * 2 * head])
    step = tokens // 2
    group = q_width // kv_heads
    for at in range(0, tokens, step):
        rows = pl.ds(at, step)
        raw = nn(nx[pl.ds(WIN + at, step), :], held[:, :q_width])
        raw = raw + nt(halves(low[pl.ds(WIN + at, step), :], 1), ups[:q_width, :])
        q_bf = rope(raw.T, cos_q[:, rows], sin_q[:, rows]).astype(bf16)
        q_t[:, rows] = q_bf
        for k in range(kv_heads):
            logits = nn(map_q[k], q_bf[k * group : (k + 1) * group])
            phi_q[2 * k * group : 2 * (k + 1) * group, rows] = hedgehog(logits, head)


def masks(q_doc, k_doc, heads):
    keys = CHUNK + WIN
    j = lax.broadcasted_iota(i32, (keys, CHUNK), 0)
    t = lax.broadcasted_iota(i32, (keys, CHUNK), 1)
    same = k_doc == q_doc
    win = same & (j > t) & (j <= t + WIN)
    lin = (same & (j <= t))[:CHUNK]
    win_f = jnp.concatenate([win.astype(f32)] * heads, axis=1)
    lin_f = jnp.concatenate([lin.astype(f32)] * heads, axis=1)
    return win_f > 0.5, lin_f > 0.5


def side(ref, first, count, size):
    return jnp.concatenate([ref[first + g * size : first + (g + 1) * size, :] for g in range(count)], axis=1)


def window_weights(q, phi_q, k_win, phi_k, win, lin, scale):
    scores = nn(k_win, q)
    weights_win = jnp.where(win, jnp.exp(scores * scale), 0.0)
    linear = jnp.where(lin, nn(phi_k, phi_q), 0.0)
    return weights_win, jnp.concatenate([weights_win[:CHUNK] + linear, weights_win[CHUNK:]], axis=0)


def forward_body(dims, last_docs, factors, q_t, phi_q, k_n, v_a, phi_kn, doc_col, doc_row, q_doc, *rest):
    kv_heads, group, head = dims
    earlier, (att, att_t, totals, states, state) = rest[:-5], rest[-5:]
    chunk = pl.program_id(0)
    start = pl.multiple_of(chunk * CHUNK, CHUNK)

    @pl.when(chunk == 0)
    def _():
        total = jnp.zeros(state.shape, f32)
        for i, x in enumerate(earlier):
            total = total + factors[i] * x[...]
        state[...] = total

    keys = CHUNK + WIN
    win, lin = masks(q_doc[...], doc_col[pl.ds(start, keys), :], group)
    use = (q_doc[...] == last_docs[chunk]).astype(f32)
    use = jnp.concatenate([use] * group, axis=1)
    incl = (doc_row[:, pl.ds(start, CHUNK)] == last_docs[chunk + 1]).astype(f32).astype(bf16)
    passing = (last_docs[chunk] == last_docs[chunk + 1]).astype(f32)
    scale = head**-0.5
    out = []
    for k in range(kv_heads):
        q = side(q_t, k * group * head, group, head)
        phi = side(phi_q, 2 * k * group * head, group, 2 * head)
        k_win = k_n[pl.ds(start, keys), k * head : (k + 1) * head]
        phi_k = phi_kn[pl.ds(start, CHUNK), 2 * k * head : 2 * (k + 1) * head]
        v_win = v_a[k * AUG : (k + 1) * AUG, pl.ds(start, 2 * CHUNK)]
        _, weights = window_weights(q, phi, k_win, phi_k, win, lin, scale)
        before = state[k]
        from_state = nn(before.astype(bf16), phi) * use
        total = jnp.sum(weights, axis=0, keepdims=True) + from_state[head : head + 1]
        numer = nn(v_win[:, :keys], weights.astype(bf16))[:head] + from_state[:head]
        attended = numer * (1.0 / total)
        for g in range(group):
            out.append(attended[:, g * CHUNK : (g + 1) * CHUNK])
            totals[k * group + g : k * group + g + 1, :] = total[:, g * CHUNK : (g + 1) * CHUNK]
        states[0, k] = before.T.astype(bf16)
        state[k] = nn(v_win[:, :CHUNK] * incl, phi_k) + passing * before
    attended = jnp.concatenate(out, axis=0)
    att_t[...] = attended
    att[...] = attended.T.astype(bf16)


def store_at(step, value, outs):
    for i, out in enumerate(outs):

        @pl.when(step == i)
        def _(out=out):
            out[...] = value.astype(out.dtype)


def o_body(n_pieces, first, offsets, nat, att, down, up, *rest):
    pieces, parts, (lowered, held, sems) = rest[:n_pieces], rest[n_pieces:-3], rest[-3:]
    step = pl.program_id(0)

    @pl.when(step == 0)
    def _():
        load_pieces(pieces, offsets, held, sems, first)

    low = nn(att[...], down[...])
    lowered[...] = low
    store_at(step, nt(att[...], held[...]) + nn(halves(low, 1), up[...]), parts)


def quarter_copies(quarters, held, sems, first=0):
    return [pltpu.make_async_copy(x, held.at[first + i], sems.at[first + i]) for i, x in enumerate(quarters)]


def quarter_of(step, quarters, held, sems):
    for i, copy in enumerate(quarter_copies(quarters, held, sems)):

        @pl.when(step == i)
        def _(copy=copy):
            copy.wait()

    return held[step]


def ffn_body(lots, units, summed, last, offsets, nat, cot, *rest):
    count, n_out = sum(lots), 4 if last else 2
    quarters, pieces, rest = rest[:2], rest[2 : 2 + count], rest[2 + count :]
    sums, outs, rest = rest[: 2 * summed], rest[2 * summed : 2 * summed + n_out], rest[2 * summed + n_out :]
    rows, rows_sems, held, sems, out_held, out_sems, *rest = rest
    step = pl.program_id(0)

    def at_first(act):
        pl.when(step == 0)(act)

    starts = [sum(units[:i]) for i in range(len(units))]
    blocks = [(which, lot) for which in range(3) for lot in range(len(lots))]

    def copies(block):
        which, lot = block
        size = units[lot]
        return [
            pltpu.make_async_copy(
                pieces[i].at[:, pl.ds(which * size, size)],
                held.at[which, pl.ds(pl.multiple_of(offsets[i], 16), pieces[i].shape[0]), pl.ds(starts[lot], size)],
                sems.at[which, i],
            )
            for i in range(sum(lots[:lot]), sum(lots[: lot + 1]))
        ]

    def sum_copy(i, kind):
        return pltpu.make_async_copy(sums[kind].at[i], rest[0].at[i, kind], rest[1].at[i, kind])

    def out_copy(i, kind):
        out = outs[2 * (1 - kind) + i] if last else outs[kind].at[i]
        return pltpu.make_async_copy(out_held.at[i, kind], out, out_sems.at[i, kind])

    @at_first
    def _():
        for copy in quarter_copies(quarters[:1], rows, rows_sems) + copies(blocks[0]) + copies(blocks[1]):
            copy.start()
        for copy in quarter_copies(quarters[1:], rows, rows_sems, 1):
            copy.start()

    def product(x, index):
        @at_first
        def _():
            for copy in copies(blocks[index]):
                copy.wait()
            if index + 2 < len(blocks):
                for copy in copies(blocks[index + 2]):
                    copy.start()
            elif index + 2 == len(blocks) and summed:
                for i in range(2):
                    for kind in (1, 0):
                        sum_copy(i, kind).start()

        which, lot = blocks[index]
        return nn(x, held[which, :, starts[lot] : starts[lot] + units[lot]])

    n2 = quarter_of(step, quarters, rows, rows_sems)
    count = len(lots)
    gates = [product(n2, i) for i in range(count)]
    ups = [product(n2, count + i) for i in range(count)]
    grads = [product(cot[...], 2 * count + i) for i in range(count)]
    parts = [[], [], []]
    for gate, up, grad_act in zip(gates, ups, grads):
        s = 1.0 / (1.0 + jnp.exp(-gate))
        silu = gate * s
        parts[0].append((silu * up).astype(bf16))
        parts[1].append((grad_act * up * s * (1.0 + gate * (1.0 - s))).astype(bf16))
        parts[2].append((grad_act * silu).astype(bf16))
    act, grad_gate, grad_up = [jnp.concatenate(x, axis=1) for x in parts]

    def finish(kind, total):
        if summed:
            sum_copy(step, kind).wait()
            total = total + rest[0][step, kind]
        out_held[step, kind] = total.astype(out_held.dtype)
        for i in range(2):

            @pl.when(step == i)
            def _(i=i):
                out_copy(i, kind).start()

    finish(1, nt(grad_gate, held[0]) + nt(grad_up, held[1]))
    finish(0, nt(act, held[2]))

    @pl.when(step == 1)
    def _():
        for i in range(2):
            for kind in range(2):
                out_copy(i, kind).wait()


def go_body(dims, offsets, nat, before_doc, o_up, o_down, att_t, totals, phi_q, q_doc, *rest):
    n_pieces, first, kv_heads, group, head, later = dims
    quarters, pieces, rest = rest[:2], rest[2 : 2 + n_pieces], rest[2 + n_pieces :]
    earlier, rest = rest[: 4 * later], rest[4 * later :]
    numer, grad_totals, up_product, dstate, rows_held, rows_sems, held, sems = rest
    step = pl.program_id(0)

    @pl.when(step == 0)
    def _():
        for copy in quarter_copies(quarters, rows_held, rows_sems):
            copy.start()
        load_pieces(pieces, offsets, held, sems, first)
        dstate[...] = earlier[3][...] if later else jnp.zeros(dstate.shape, f32)

    branch = quarter_of(step, quarters, rows_held, rows_sems)
    up = nn(branch, o_up[...])
    up_product[...] = up
    grad = (nn(branch, held[...]) + nn(halves(up, 1), o_down[...])).T
    use = (q_doc[...] == before_doc[0]).astype(f32)
    columns = grad.shape[1]
    for k in range(kv_heads):
        total = jnp.zeros((2 * head, AUG), f32)
        for g in range(group):
            h = k * group + g
            rows = slice(h * head, (h + 1) * head)
            inverse = 1.0 / totals[h : h + 1, :]
            one = grad[rows]
            g_total = -jnp.sum(one * att_t[rows, :], axis=0, keepdims=True) * inverse
            g_numer = (one * inverse).astype(bf16)
            numer[rows, :] = g_numer
            grad_totals[h : h + 1, :] = g_total
            aug = augmented(g_numer, g_total * use, columns, head, use)
            total = total + nt(phi_q[2 * h * head : 2 * (h + 1) * head, :], aug)
        dstate[k] += total


def augmented(g_numer, g_total, columns, head, use=None):
    top = g_numer if use is None else g_numer * use.astype(bf16)
    high = g_total.astype(bf16).astype(f32)
    row = lax.broadcasted_iota(i32, (AUG - head, columns), 0)
    below = jnp.where(row == 0, high, jnp.where(row == 1, g_total - high, 0.0))
    return jnp.concatenate([top, below.astype(bf16)], axis=0)


def backward_body(
    dims, last_docs, q_t, phi_q, numer, grad_totals, k_n, k_t, v_n, v_a, phi_kn, phi_kt, doc_col, doc_row, q_doc,
    states, cos_q, sin_q, map_q,
    g_nat, g_kt, g_vt, acc_phi, g_map_q, later,
):
    kv_heads, group, head, chunks = dims
    step = pl.program_id(0)
    chunk = chunks - 1 - step
    start = pl.multiple_of(chunk * CHUNK, CHUNK)
    keys = CHUNK + WIN

    @pl.when(step == 0)
    def _():
        later[...] = jnp.zeros(later.shape, f32)
        g_kt[...] = jnp.zeros(g_kt.shape, f32)
        g_vt[...] = jnp.zeros(g_vt.shape, f32)
        acc_phi[...] = jnp.zeros(acc_phi.shape, f32)
        g_map_q[...] = jnp.zeros(g_map_q.shape, f32)

    win, lin = masks(q_doc[...], doc_col[pl.ds(start, keys), :], group)
    use1 = (q_doc[...] == last_docs[chunk]).astype(f32)
    use = jnp.concatenate([use1] * group, axis=1)
    incl = (doc_row[:, pl.ds(start, CHUNK)] == last_docs[chunk + 1]).astype(f32)
    passing = (last_docs[chunk] == last_docs[chunk + 1]).astype(f32)
    scale = head**-0.5
    two = pl.ds(start, 2 * CHUNK)
    one = pl.ds(start, CHUNK)
    pad = jnp.zeros((head, 2 * CHUNK - keys), f32)
    grads = []
    for k in range(kv_heads):
        lanes = slice(k * head, (k + 1) * head)
        wide = slice(2 * k * head, 2 * (k + 1) * head)
        q = side(q_t, k * group * head, group, head)
        phi = side(phi_q, 2 * k * group * head, group, 2 * head)
        gn = side(numer, k * group * head, group, head)
        gt = side(grad_totals, k * group, group, 1)
        weights_win, weights = window_weights(
            q, phi, k_n[pl.ds(start, keys), lanes], phi_kn[one, wide], win, lin, scale
        )
        grad_w = nn(v_n[pl.ds(start, keys), lanes], gn) + gt
        gs = (grad_w * weights_win).astype(bf16)
        gl = jnp.where(lin, grad_w[:CHUNK], 0.0).astype(bf16)
        gq = nn(k_t[lanes, two][:, :keys], gs) * scale
        gk = nt(q, gs) * scale
        gv = nt(gn, weights.astype(bf16))
        aug = augmented(gn, gt, group * CHUNK, head)
        gphi_q = nn(phi_kt[wide, one], gl) + use * nn(states[0, k], aug)
        gphi_k = nt(phi, gl)
        after = later[k]
        after_bf = after.astype(bf16)
        v_aug = v_a[k * AUG : (k + 1) * AUG, one]
        gphi_k = gphi_k + incl * nn(after_bf, v_aug)
        from_later = incl * nn(after.T.astype(bf16), phi_kt[wide, one])[:head]
        gv = gv + jnp.concatenate([from_later, jnp.zeros((head, keys - CHUNK), f32)], axis=1)
        later[k] = nt(phi, augmented(gn, gt * use, group * CHUNK, head, use)) + passing * after
        g_kt[lanes, two] += jnp.concatenate([gk, pad], axis=1)
        g_vt[lanes, two] += jnp.concatenate([gv, pad], axis=1)
        acc_phi[wide, one] += gphi_k
        heads = [slice(g * CHUNK, (g + 1) * CHUNK) for g in range(group)]
        rows = slice(k * group * head, (k + 1) * group * head)
        grad_phi = jnp.concatenate([gphi_q[:, at] for at in heads], axis=0)
        phi_rows = phi_q[2 * k * group * head : 2 * (k + 1) * group * head, :]
        ga = hedgehog_back(phi_rows, grad_phi, head)
        gq_rows = jnp.concatenate([gq[:, at] for at in heads], axis=0) + tn(map_q[k], ga)
        g_map_q[k] += nt(q_t[rows, :], ga)
        grads.append(rope(gq_rows, cos_q[...], -sin_q[...]))
    g_nat[...] = jnp.concatenate(grads, axis=0).T.astype(bf16)


def keys_back_body(dims, last_docs, factors, g_kt, g_vt, g_phi, v_a, phi_kt, k_t, doc_row, map_k, *rest):
    kv_heads, head, chunks, rows = dims
    later, (g_own, g_halo, g_map_k) = rest[:-3], rest[-3:]
    ext = g_kt.shape[1]
    incl = (doc_row[...] == last_docs[chunks]) & (lax.broadcasted_iota(i32, (1, ext), 1) < rows)
    incl = incl.astype(f32)
    phi_grads, v_grads = [], []
    for k in range(kv_heads):
        wide = slice(2 * k * head, 2 * (k + 1) * head)
        after = jnp.zeros(later[0].shape[1:], f32)
        for i, x in enumerate(later):
            after = after + factors[i] * x[k]
        phi_grads.append(g_phi[wide, :] + incl * nn(after.astype(bf16), v_a[k * AUG : (k + 1) * AUG, :]))
        from_later = nn(after.T.astype(bf16), phi_kt[wide, :])[:head]
        v_grads.append(g_vt[k * head : (k + 1) * head, :] + incl * from_later)
    ga = hedgehog_back(phi_kt[...], jnp.concatenate(phi_grads, axis=0), head)
    g_map_k[...] = nt(k_t[...], ga)
    g_k = g_kt[...] + tn(map_k[...], ga)
    for i, grad in enumerate((g_k, jnp.concatenate(v_grads, axis=0))):
        mine = slice(i * kv_heads * head, (i + 1) * kv_heads * head)
        g_own[mine, :] = grad[:, WIN : WIN + rows]
        g_halo[mine, :] = jnp.concatenate([jnp.zeros((kv_heads * head, CHUNK - WIN), f32), grad[:, :WIN]], axis=1)


def adapters_body(
    dims, g_q, g_own, g_halo, cos, sin, ups, low, normed, g_o_up, g_o_down, g_map_q, g_map_k, *outs
):
    rows, window, head, rank = dims
    half = g_own.shape[0] // 2
    kv = keys_values(g_own[...], g_halo[...], cos[...], sin[...], 1.0)
    q_width = g_q.shape[1]
    up = nn(g_q[...], ups[:q_width]) + nn(kv, ups[q_width:])
    up_halves = halves(up, 1)

    def joined(x, axis):
        one, other = jnp.split(x, 2, axis=axis)
        return one + other

    low_halves = halves(low[...], 1)
    g_q_up = joined(tn(g_q[...], low_halves), 1)[:, :rank]
    g_kv_up = joined(tn(kv, low_halves), 1)
    if len(outs) == 1:
        (slabs,) = outs
        slabs[...] = jnp.zeros(slabs.shape, f32)
        tall = slabs.shape[2]
    else:
        by_head, shared = outs
        by_head[...] = jnp.zeros(by_head.shape, f32)

    def put(h, first, x):
        if len(outs) == 2:
            by_head[h, :, first : first + x.shape[1]] = x
            return
        for r in range(slabs.shape[0]):
            slabs[r, h, :, first : first + x.shape[1]] = x[r * tall : (r + 1) * tall]

    def put_shared(first, x):
        if len(outs) == 2:
            shared[first : first + x.shape[0], :] = x
            return
        wide = x.shape[1] // slabs.shape[0] // 128
        for i in range(x.shape[0] // tall):
            for r in range(slabs.shape[0]):
                for j in range(wide):
                    at = (r * wide + j) * 128
                    tile = x[i * tall : (i + 1) * tall, at : at + 128]
                    slabs[r, q_heads + kv_heads + (first // tall + i) * wide + j] = tile

    q_heads, kv_heads = q_width // head, half // head
    group = q_heads // kv_heads
    for h in range(q_heads):
        mine, at = slice(h * head, (h + 1) * head), (h % group) * head
        put(h, 0, g_map_q[h // group, at : at + head, at : at + head])
        put(h, head, g_q_up[mine])
        put(h, head + rank, g_o_down[mine, :])
    for h in range(kv_heads):
        mine = slice(h * head, (h + 1) * head)
        put(q_heads + h, 0, g_map_k[mine, mine])
        put(q_heads + h, head, g_kv_up[mine, rank : 2 * rank])
        put(q_heads + h, head + rank, g_kv_up[half + h * head : half + (h + 1) * head, 2 * rank :])
    put_shared(0, joined(tn(up_halves, normed[window : window + rows, :]), 0))
    put_shared(3 * rank, g_o_up[...])


def adapter_o_body(nat, lowered, att, up_product, *rest):
    branch, (g_o_up, g_o_down) = rest[:4], rest[4:]

    def joined(x, axis):
        one, other = jnp.split(x, 2, axis=axis)
        return one + other

    g_o_down[...] = joined(tn(att[...], halves(up_product[...], 1)), 1)
    o_up = 0.0
    for i, x in enumerate(branch):
        part = lowered[pl.ds(pl.multiple_of(nat[i] * x.shape[0], x.shape[0]), x.shape[0]), :]
        o_up = o_up + tn(halves(part, 1), x[...])
    g_o_up[...] = joined(o_up, 0)


def keys_values(own, halo, cos, sin, last):
    half, wide = own.shape[0] // 2, own.shape[1] - halo.shape[1]
    total = jnp.concatenate([own[:, :wide], own[:, wide:] + halo * last], axis=1)
    return jnp.concatenate([rope(total[:half], cos, -sin), total[half:]], axis=0).T.astype(bf16)


def gn_body(n_pieces, offsets, nat, g_q, g_own, g_halo, cos, sin, ups, downs, *rest):
    pieces = rest[:n_pieces]
    parts, (held, sems) = rest[n_pieces:-2], rest[-2:]
    step = pl.program_id(0)

    @pl.when(step == 0)
    def _():
        load_pieces(pieces, offsets, held, sems)

    q_width = g_q.shape[1]
    kv = keys_values(g_own[...], g_halo[...], cos[...], sin[...], (nat[3 - step] == 3).astype(f32))
    up = nn(g_q[...], ups[:q_width]) + nn(kv, ups[q_width:])
    total = nt(g_q[...], held[:, :q_width]) + nt(kv, held[:, q_width:])
    store_at(step, total + nn(halves(up, 1), downs[...]), parts)


def rms_factor(x):
    return lax.rsqrt(jnp.mean(x * x, axis=-1, keepdims=True) + epsilon)


def rms_back(x, gain, grads):
    factor = rms_factor(x)
    unit = x * factor
    scaled = grads * gain
    return factor * (scaled - unit * jnp.mean(unit * scaled, axis=-1, keepdims=True))


def hidden_body(nat, near, beside, across, tokens, gain, hidden, normed):
    total = near[...].astype(f32) + beside[...].astype(f32) + across[...].astype(f32)
    hidden[...] = tokens[...].astype(f32) + total
    normed[...] = (hidden[...] * rms_factor(hidden[...]) * gain[...]).astype(bf16)


def grad_hidden_body(nat, near, beside, across, cotangent, hidden, gain, grad, rounded):
    total = near[...].astype(f32) + beside[...].astype(f32) + across[...].astype(f32)
    grad[...] = cotangent[...].astype(f32) + rms_back(hidden[...], gain[...], total)
    rounded[...] = grad[...].astype(bf16)


def grad_tokens_body(nat, near, beside, across, tokens, grad, gain, out):
    total = near[...].astype(f32) + beside[...].astype(f32) + across[...].astype(f32)
    out[...] = (grad[...] + rms_back(tokens[...].astype(f32), gain[...], total)).astype(bf16)


def on_own_rows(body, nat, near, beside, across, placed, owned, gain, out_types):
    rows, model = near.shape
    steps = 2
    block = pl.BlockSpec((rows // steps, model), lambda i, nat: (i, 0))
    return pl.pallas_call(
        body,
        grid_spec=pltpu.PrefetchScalarGridSpec(
            num_scalar_prefetch=1,
            grid=(steps,),
            in_specs=[block] * 3
            + [pl.BlockSpec((rows // steps, model), lambda i, nat: (nat[0] * steps + i, 0))]
            + [block] * len(owned)
            + [whole((1, model))],
            out_specs=[block] * len(out_types),
        ),
        out_shape=[jax.ShapeDtypeStruct((rows, model), x) for x in out_types],
        compiler_params=params(BIG),
        cost_estimate=SMALL,
        name="own_rows",
    )(nat, near, beside, across, placed, *owned, gain)


def place_body(count, nat, *refs):
    quarters, (out, held, sems) = refs[:count], refs[-3:]
    step = pl.program_id(0)

    @pl.when(step == 0)
    def _():
        for copy in quarter_copies(quarters, held, sems):
            copy.start()

    out[...] = quarter_of(step, quarters, held, sems).astype(out.dtype)


def place(quarters, first, nat, dtype, earlier=()):
    count, (rows, width) = len(quarters), quarters[0].shape
    return pl.pallas_call(
        lambda *refs: place_body(count, *refs),
        grid_spec=pltpu.PrefetchScalarGridSpec(
            num_scalar_prefetch=1,
            grid=(count,),
            in_specs=[ANY] * (count + len(earlier)),
            out_specs=pl.BlockSpec((rows, width), lambda i, nat: (nat[first + i], 0)),
            scratch_shapes=[pltpu.VMEM((count, rows, width), bf16), pltpu.SemaphoreType.DMA((count,))],
        ),
        out_shape=jax.ShapeDtypeStruct((4 * rows, width), dtype),
        input_output_aliases={1 + count: 0} if earlier else {},
        compiler_params=params(BIG),
        cost_estimate=SMALL,
        name="place",
    )(nat, *quarters, *earlier)


def per_device(
    tokens,
    sequence_lengths,
    output_cotangent,
    query_weight,
    key_weight,
    value_weight,
    output_weight,
    gate_weight,
    up_weight,
    down_weight,
    attention_norm_gain,
    feedforward_norm_gain,
    query_adapter_down,
    key_adapter_down,
    value_adapter_down,
    output_adapter_up,
    query_adapter_up,
    key_adapter_up,
    value_adapter_up,
    output_adapter_down,
    feature_map_query,
    feature_map_key,
):
    rows, model = tokens.shape
    heads, head, rank = query_adapter_up.shape
    kv_heads = key_adapter_up.shape[0]
    group = heads // kv_heads
    q_width, kv_width = heads * head, kv_heads * head
    seq, ring = lax.axis_size("seq"), lax.axis_size("dp") * lax.axis_size("seq")
    here = lax.axis_index("seq")
    chunks = rows // CHUNK
    ext = -(-(rows + WIN) // CHUNK) * CHUNK
    quarter = rows // 4

    core, far = lax.axis_index("tensor") % 2, lax.axis_index("tensor") // 2
    nat = jnp.stack([core * 2 + far, (1 - core) * 2 + far, core * 2 + 1 - far, (1 - core) * 2 + 1 - far]).astype(i32)

    clock = Clock()
    pack = lambda q, k, v, o: jnp.concatenate([q, k, v, o.T], axis=1)
    attn_chain = Chain(clock, 0, pack, query_weight, key_weight, value_weight, output_weight)
    attn_chain.step()
    offsets = attn_chain.offsets
    n_pieces = offsets.shape[0]
    assert sum(map(sum, FFN_UNITS)) == gate_weight.shape[1]

    def turn(part):
        for chain in chains[part]:
            chain.step()


    ladder = jnp.exp(jnp.arange(head // 2).astype(f32) * (-2.0 * math.log(rope_base) / head))[:, None]
    tables = [((head // 2, rows), f32)] * 2 + [((head // 2, ext), f32)] * 2
    tables += [((1, rows), i32), ((ext, 1), i32), ((1, ext), i32)]
    scalars = [((chunks + 1,), i32), ((seq - 1,), f32), ((seq - 1,), f32)]
    cos_q, sin_q, cos_k, sin_k, q_doc, doc_col, doc_row, last_docs, passed_before, passed_after = pl.pallas_call(
        lambda *refs: tables_body(seq, *refs),
        grid_spec=pltpu.PrefetchScalarGridSpec(
            num_scalar_prefetch=2,
            grid=(1,),
            in_specs=[whole(ladder.shape)],
            out_specs=[whole(x) for x, _ in tables] + [pl.BlockSpec(memory_space=pltpu.SMEM)] * 3,
        ),
        out_shape=[jax.ShapeDtypeStruct(x, d) for x, d in tables + scalars],
        compiler_params=params(32),
        cost_estimate=SMALL,
        name="tables",
    )(sequence_lengths[0], here[None].astype(i32), ladder)
    q_doc, doc_col, doc_row, last_docs, passed_before, passed_after = clock.wait(
        q_doc, doc_col, doc_row, last_docs, passed_before, passed_after
    )
    attn_chain.step()

    halo = shifted(clock.tie(tokens)[rows - WIN :], "seq", 1)
    attn_chain.step()
    gain_attn = attention_norm_gain.astype(f32)[None, :]
    gain_mlp = feedforward_norm_gain.astype(f32)[None, :]
    downs = jnp.concatenate([query_adapter_down, key_adapter_down, value_adapter_down], axis=1)
    low_shape = (ext, 3 * rank)

    def norm_half(half, halo, earlier):
        size = rows // 2 + (ext - rows - WIN if half else WIN)
        return pl.pallas_call(
            lambda *refs: norm_body(half, *refs),
            grid_spec=pltpu.PrefetchScalarGridSpec(
                num_scalar_prefetch=0,
                grid=(1,),
                in_specs=[ANY, whole((WIN, model)), whole((1, model)), whole((model, 3 * rank))] + [ANY] * len(earlier),
                out_specs=[ANY, ANY],
                scratch_shapes=[
                    pltpu.VMEM((size, model), bf16),
                    pltpu.VMEM((size, model), bf16),
                    pltpu.VMEM((size, 3 * rank), f32),
                    pltpu.SemaphoreType.DMA((2,)),
                    pltpu.SemaphoreType.DMA((2, 2)),
                ],
            ),
            out_shape=[jax.ShapeDtypeStruct((ext, model), bf16), jax.ShapeDtypeStruct(low_shape, f32)],
            input_output_aliases={4: 0, 5: 1} if earlier else {},
            compiler_params=params(BIG),
            cost_estimate=SMALL,
            name="norm",
        )(clock.tie(tokens), halo, gain_attn, downs, *earlier)

    normed_low = clock.wait(*norm_half(1, jnp.zeros((WIN, model), bf16), ()))
    attn_chain.step()
    (halo,) = clock.wait(halo)
    normed, low = clock.wait(*norm_half(0, halo, normed_low))
    attn_chain.step()
    all_units = [x for part in FFN_UNITS for x in part]
    pack_in = (
        gate_weight, up_weight, down_weight, query_adapter_up, key_adapter_up, value_adapter_up,
        feature_map_query, feature_map_key, output_adapter_up,
    )
    pack_out = [(gate_weight.shape[0], 3 * x) for x in all_units] + [
        (q_width + 2 * kv_width, 3 * rank),
        (q_width + 2 * kv_width, 6 * rank),
        (kv_heads, group * head, group * head),
        (kv_width, kv_width),
        (model, rank),
    ]
    packed = pl.pallas_call(
        lambda *refs: pack_body(all_units, *refs),
        grid_spec=pltpu.PrefetchScalarGridSpec(
            num_scalar_prefetch=0,
            grid=(1,),
            in_specs=[whole(x.shape) for x in pack_in],
            out_specs=[whole(x) for x in pack_out],
        ),
        out_shape=[jax.ShapeDtypeStruct(x, bf16) for x in pack_out],
        compiler_params=params(BIG),
        cost_estimate=SMALL,
        name="pack",
    )(clock.tie(gate_weight), *pack_in[1:])
    *packed, ups, ups_twice, maps_q, maps_k, o_up = clock.wait(*packed)
    chains = [[Chain(clock, 1, lambda x: x, packed[2 * i]), Chain(clock, -1, lambda x: x, packed[2 * i + 1])] for i in range(2)]
    for _ in range(ring - 6):
        attn_chain.step()
    attn_pieces = attn_chain.pieces()
    turn(0)

    sems = pltpu.SemaphoreType.DMA((n_pieces,))
    qkv_width = q_width + 2 * kv_width
    held_qkv = pltpu.VMEM((model, qkv_width), bf16)
    held_o = pltpu.VMEM((model, q_width), bf16)

    dims = (rows, ext, q_width, kv_width, head, n_pieces, chunks)
    shapes = [
        ((q_width, rows), bf16),
        ((2 * q_width, rows), bf16),
        ((ext, kv_width), bf16),
        ((kv_width, ext), bf16),
        ((ext, kv_width), bf16),
        ((kv_heads * AUG, ext), bf16),
        ((ext, 2 * kv_width), bf16),
        ((2 * kv_width, ext), bf16),
        ((kv_heads, AUG, 2 * head), f32),
    ]
    prep_in = (normed, low, ups_twice, cos_q, sin_q, cos_k, sin_k, maps_q, maps_k, doc_row)
    q_t, phi_q, k_n, k_t, v_n, v_a, phi_kn, phi_kt, contrib = pl.pallas_call(
        lambda *refs: prep_body(dims, *refs),
        grid_spec=pltpu.PrefetchScalarGridSpec(
            num_scalar_prefetch=2,
            grid=(1,),
            in_specs=[whole(x.shape) for x in prep_in] + [ANY] * n_pieces,
            out_specs=[whole(s) for s, _ in shapes],
            scratch_shapes=[held_qkv, sems],
        ),
        out_shape=[jax.ShapeDtypeStruct(s, d) for s, d in shapes],
        compiler_params=params(56),
        cost_estimate=SMALL,
        name="prep",
    )(clock.tie(offsets), last_docs, *prep_in, *attn_pieces)
    (contrib,) = clock.wait(contrib)
    turn(0)

    coming = clock.wait(*[shifted(contrib, "seq", by) for by in range(1, seq)])
    column = lambda r: pl.BlockSpec((r, CHUNK), lambda c, *_: (0, c))
    att, att_t, totals, states = pl.pallas_call(
        lambda *refs: forward_body((kv_heads, group, head), *refs),
        grid_spec=pltpu.PrefetchScalarGridSpec(
            num_scalar_prefetch=2,
            grid=(chunks,),
            in_specs=[
                column(q_width),
                column(2 * q_width),
                whole(k_n.shape),
                whole(v_a.shape),
                whole(phi_kn.shape),
                whole(doc_col.shape),
                whole(doc_row.shape),
                column(1),
            ]
            + [whole(contrib.shape)] * len(coming),
            out_specs=[
                pl.BlockSpec((CHUNK, q_width), lambda c, *_: (c, 0)),
                column(q_width),
                column(heads),
                pl.BlockSpec((1, kv_heads, 2 * head, AUG), lambda c, *_: (c, 0, 0, 0)),
            ],
            scratch_shapes=[pltpu.VMEM(contrib.shape, f32)],
        ),
        out_shape=[
            jax.ShapeDtypeStruct((rows, q_width), bf16),
            jax.ShapeDtypeStruct((q_width, rows), f32),
            jax.ShapeDtypeStruct((heads, rows), f32),
            jax.ShapeDtypeStruct((chunks, kv_heads, 2 * head, AUG), bf16),
        ],
        compiler_params=params(BIG),
        cost_estimate=SMALL,
        name="attend",
    )(clock.tie(last_docs), passed_before, q_t, phi_q, k_n, v_a, phi_kn, doc_col, doc_row, q_doc, *coming)
    att = clock.tie(att)
    turn(0)

    o_down = output_adapter_down.reshape(q_width, rank)
    o_up_t = jnp.concatenate([output_adapter_up.T, output_adapter_up.T], axis=0)
    one_quarter = jax.ShapeDtypeStruct((quarter, model), bf16)

    *o_parts, lowered = pl.pallas_call(
        lambda *refs: o_body(n_pieces, qkv_width, *refs),
        grid_spec=pltpu.PrefetchScalarGridSpec(
            num_scalar_prefetch=2,
            grid=(4,),
            in_specs=[
                pl.BlockSpec((quarter, q_width), lambda i, off, nat: (nat[3 - i], 0)),
                whole(o_down.shape),
                whole(o_up_t.shape),
            ]
            + [ANY] * n_pieces,
            out_specs=[whole((quarter, model))] * 4
            + [pl.BlockSpec((quarter, rank), lambda i, off, nat: (nat[3 - i], 0))],
            scratch_shapes=[held_o, sems],
        ),
        out_shape=[one_quarter] * 4 + [jax.ShapeDtypeStruct((rows, rank), f32)],
        compiler_params=params(BIG),
        cost_estimate=SMALL,
        name="project",
    )(clock.tie(offsets), nat, att, o_down, o_up_t, *attn_pieces)
    o_far0, o_far1, o_near0, o_near1 = clock.wait(*o_parts)
    turn(0)
    o_far0, o_near0 = clock.wait(o_far0, o_near0)
    beside = exchange(o_far0, "tensor", 1)
    beside_near = exchange(o_near0, "tensor", 1)
    beside, beside_near = clock.wait(beside, beside_near)
    o_far = clock.tie((o_far1.astype(f32) + beside.astype(f32)).astype(bf16))
    across = exchange(o_far, "tensor", 2)
    turn(0)
    (across,) = clock.wait(across)
    beside = beside_near
    hidden, normed_mlp = on_own_rows(
        hidden_body, clock.tie(nat), o_near1, beside, across, tokens, (), gain_mlp, (f32, bf16)
    )
    hidden, normed_mlp = clock.wait(hidden, normed_mlp)
    for _ in range(ring - 7):
        turn(0)
    normed_mlp = clock.tie(normed_mlp)
    across, beside = exchange(normed_mlp, "tensor", 2), exchange(normed_mlp, "tensor", 1)
    (beside,) = clock.wait(beside)
    turn(0)
    (across,) = clock.wait(across)
    for chain in chains[0]:
        chain.settle()
    turn(1)
    last = clock.tie(exchange(clock.tie(across), "tensor", 1))
    normed_mlp = [normed_mlp, beside, across, last]

    def ffn(part, which, quarters, sums):
        units, last = FFN_UNITS[part][which], part == len(FFN_UNITS) - 1
        lots = [chain.pieces() for chain in chains[part][which]]
        sizes = tuple(map(len, lots))
        pieces = [piece for lot in lots for piece in lot]
        ring_offsets = jnp.concatenate([chain.offsets for chain in chains[part][which]])
        first = quarters[0]
        summed = jax.ShapeDtypeStruct((2, quarter, model), f32)
        return pl.pallas_call(
            lambda *refs: ffn_body(sizes, units, bool(sums), last, *refs),
            grid_spec=pltpu.PrefetchScalarGridSpec(
                num_scalar_prefetch=2,
                grid=(2,),
                in_specs=[pl.BlockSpec((quarter, model), lambda i, off, nat: (nat[first - i], 0))]
                + [ANY] * (2 + len(pieces) + len(sums)),
                out_specs=[ANY] * (4 if last else 2),
                scratch_shapes=[
                    pltpu.VMEM((2, quarter, model), bf16),
                    pltpu.SemaphoreType.DMA((2,)),
                    pltpu.VMEM((3, model, sum(units)), bf16),
                    pltpu.SemaphoreType.DMA((3, len(pieces))),
                    pltpu.VMEM((2, 2, quarter, model), bf16 if last else f32),
                    pltpu.SemaphoreType.DMA((2, 2)),
                ]
                + [pltpu.VMEM((2, 2, quarter, model), f32), pltpu.SemaphoreType.DMA((2, 2))] * bool(sums),
            ),
            out_shape=[one_quarter] * 4 if last else [summed] * 2,
            compiler_params=params(BIG),
            cost_estimate=SMALL,
            name="feed_forward",
        )(clock.tie(ring_offsets), nat, output_cotangent, *[normed_mlp[q] for q in quarters], *pieces, *sums)

    sums_far = sums_near = ()
    up, down, both = slice(0, 1), slice(1, 2), slice(0, 2)
    for way in (up, down):
        sums_far = clock.wait(*ffn(0, way, (3, 2), sums_far))
        turn(1)
        sums_near = clock.wait(*ffn(0, way, (1, 0), sums_near))
        turn(1)
    for _ in range(ring - 6):
        turn(1)
    gn_far0, gn_far1, mlp_far0, mlp_far1 = ffn(1, both, (3, 2), sums_far)
    gn_far0, mlp_far0 = clock.wait(gn_far0, mlp_far0)
    beside = exchange(gn_far0, "tensor", 1)
    mlp_beside_far = exchange(mlp_far0, "tensor", 1)
    (beside,) = clock.wait(beside)
    across = exchange(clock.tie((gn_far1.astype(f32) + beside.astype(f32)).astype(bf16)), "tensor", 2)
    gn_near0, gn_near1, mlp_near0, mlp_near1 = ffn(1, both, (1, 0), sums_near)
    gn_near0, mlp_near0 = clock.wait(gn_near0, mlp_near0)
    across, gn_near0 = clock.wait(across, gn_near0)
    beside = exchange(gn_near0, "tensor", 1)
    (beside,) = clock.wait(beside)
    grad_hidden, branch = on_own_rows(
        grad_hidden_body, clock.tie(nat), gn_near1, beside, across, output_cotangent, (hidden,), gain_mlp, (f32, bf16)
    )
    grad_hidden, branch = clock.wait(grad_hidden, branch)
    across, beside = exchange(branch, "tensor", 2), exchange(branch, "tensor", 1)
    mlp_beside = exchange(clock.tie(mlp_near0), "tensor", 1)
    (beside,) = clock.wait(beside)

    o_down_t = jnp.concatenate([o_down.T, o_down.T], axis=0)
    sizes = [((q_width, rows), bf16), ((heads, rows), f32), ((rows, rank), f32), ((kv_heads, 2 * head, AUG), f32)]

    def go_part(first, quarters, earlier):
        by_quarter = lambda r: pl.BlockSpec((r, quarter), lambda i, off, nat, before: (0, nat[first + i]))
        late = bool(earlier)
        return pl.pallas_call(
            lambda *refs: go_body((n_pieces, qkv_width, kv_heads, group, head, late), *refs),
            grid_spec=pltpu.PrefetchScalarGridSpec(
                num_scalar_prefetch=3,
                grid=(2,),
                in_specs=[
                    whole((model, rank)),
                    whole(o_down_t.shape),
                    by_quarter(q_width),
                    by_quarter(heads),
                    by_quarter(2 * q_width),
                    by_quarter(1),
                ]
                + [ANY] * (2 + n_pieces)
                + ([ANY] * 3 + [whole(sizes[3][0])]) * late,
                out_specs=[
                    by_quarter(q_width),
                    by_quarter(heads),
                    pl.BlockSpec((quarter, rank), lambda i, off, nat, before: (nat[first + i], 0)),
                    whole(sizes[3][0]),
                ],
                scratch_shapes=[
                    pltpu.VMEM((2, quarter, model), bf16),
                    pltpu.SemaphoreType.DMA((2,)),
                    held_o,
                    sems,
                ],
            ),
            out_shape=[jax.ShapeDtypeStruct(s, d) for s, d in sizes],
            input_output_aliases={11 + n_pieces + i: i for i in range(3)} if late else {},
            compiler_params=params(BIG),
            cost_estimate=SMALL,
            name="project_back",
        )(
            clock.tie(offsets), nat, last_docs, o_up, o_down_t, att_t, totals, phi_q, q_doc,
            *quarters, *attn_pieces, *earlier,
        )

    near = clock.wait(*go_part(0, (branch, beside), ()))
    mlp_beside, mlp_beside_far = clock.wait(mlp_beside, mlp_beside_far)
    mlp_far = clock.tie((mlp_far1.astype(f32) + mlp_beside_far.astype(f32)).astype(bf16))
    mlp_near = clock.tie(hidden + (mlp_near1.astype(f32) + mlp_beside.astype(f32)))
    (across,) = clock.wait(across)
    last = clock.tie(exchange(across, "tensor", 1))
    mlp_across = exchange(clock.tie(mlp_far), "tensor", 2)
    branch = [branch, beside, across, last]
    numer, grad_totals, up_product, dstate = clock.wait(*go_part(2, branch[2:], near))

    coming = [shifted(dstate, "seq", -by) for by in range(1, seq)]

    back_column = lambda r: pl.BlockSpec((r, CHUNK), lambda c, *_: (0, chunks - 1 - c))
    back_in = (
        (q_t, back_column(q_width)),
        (phi_q, back_column(2 * q_width)),
        (numer, back_column(q_width)),
        (grad_totals, back_column(heads)),
        (k_n, None),
        (k_t, None),
        (v_n, None),
        (v_a, None),
        (phi_kn, None),
        (phi_kt, None),
        (doc_col, None),
        (doc_row, None),
        (q_doc, back_column(1)),
        (states, pl.BlockSpec((1, kv_heads, 2 * head, AUG), lambda c, *_: (chunks - 1 - c, 0, 0, 0))),
        (cos_q, back_column(head // 2)),
        (sin_q, back_column(head // 2)),
        (maps_q, None),
    )
    g_q, g_kt, g_vt, g_phi, g_map_q = pl.pallas_call(
        lambda *refs: backward_body((kv_heads, group, head, chunks), *refs),
        grid_spec=pltpu.PrefetchScalarGridSpec(
            num_scalar_prefetch=1,
            grid=(chunks,),
            in_specs=[whole(x.shape) if spec is None else spec for x, spec in back_in],
            out_specs=[
                pl.BlockSpec((CHUNK, q_width), lambda c, *_: (chunks - 1 - c, 0)),
                whole((kv_width, ext)),
                whole((kv_width, ext)),
                whole((2 * kv_width, ext)),
                whole((kv_heads, group * head, group * head)),
            ],
            scratch_shapes=[pltpu.VMEM(dstate.shape, f32)],
        ),
        out_shape=[
            jax.ShapeDtypeStruct((rows, q_width), bf16),
            jax.ShapeDtypeStruct((kv_width, ext), f32),
            jax.ShapeDtypeStruct((kv_width, ext), f32),
            jax.ShapeDtypeStruct((2 * kv_width, ext), f32),
            jax.ShapeDtypeStruct((kv_heads, group * head, group * head), f32),
        ],
        compiler_params=params(52),
        cost_estimate=SMALL,
        name="attend_back",
    )(clock.tie(last_docs), *[x for x, _ in back_in])

    g_q, g_kt, g_vt, g_phi, g_map_q = clock.wait(g_q, g_kt, g_vt, g_phi, g_map_q)
    coming = clock.wait(*coming)
    (mlp_across,) = clock.wait(mlp_across)
    out_rows = clock.tie((mlp_near + mlp_across.astype(f32)).astype(bf16))
    out_across, out_beside = exchange(out_rows, "tensor", 2), exchange(out_rows, "tensor", 1)
    g_own, g_halo, g_map_k = pl.pallas_call(
        lambda *refs: keys_back_body((kv_heads, head, chunks, rows), *refs),
        grid_spec=pltpu.PrefetchScalarGridSpec(
            num_scalar_prefetch=2,
            grid=(1,),
            in_specs=[whole(x.shape) for x in (g_kt, g_vt, g_phi, v_a, phi_kt, k_t, doc_row, maps_k, *coming)],
            out_specs=[whole((2 * kv_width, rows)), whole((2 * kv_width, CHUNK)), whole((kv_width, kv_width))],
        ),
        out_shape=[
            jax.ShapeDtypeStruct((2 * kv_width, rows), f32),
            jax.ShapeDtypeStruct((2 * kv_width, CHUNK), f32),
            jax.ShapeDtypeStruct((kv_width, kv_width), f32),
        ],
        compiler_params=params(BIG),
        cost_estimate=SMALL,
        name="keys_back",
    )(clock.tie(last_docs), passed_after, g_kt, g_vt, g_phi, v_a, phi_kt, k_t, doc_row, maps_k, *coming)

    g_own, g_halo, g_map_k = clock.wait(g_own, g_halo, g_map_k)
    g_halo = shifted(g_halo, "seq", -1)
    o_in = (lowered, att, up_product, *branch)
    g_o_up, g_o_down = pl.pallas_call(
        adapter_o_body,
        grid_spec=pltpu.PrefetchScalarGridSpec(
            num_scalar_prefetch=1,
            grid=(1,),
            in_specs=[whole(x.shape) for x in o_in],
            out_specs=[whole((rank, model)), whole((q_width, rank))],
        ),
        out_shape=[jax.ShapeDtypeStruct((rank, model), f32), jax.ShapeDtypeStruct((q_width, rank), f32)],
        compiler_params=params(BIG),
        cost_estimate=SMALL,
        name="adapter_o",
    )(clock.tie(nat), *o_in)
    g_o_up, g_o_down, g_halo = clock.wait(g_o_up, g_o_down, g_halo)

    downs_t = jnp.concatenate([downs.T, downs.T], axis=0)

    by_rows = lambda w: pl.BlockSpec((quarter, w), lambda i, off, nat: (nat[3 - i], 0))
    by_columns = lambda r: pl.BlockSpec((r, quarter), lambda i, off, nat: (0, nat[3 - i]))
    gn_parts = pl.pallas_call(
        lambda *refs: gn_body(n_pieces, *refs),
        grid_spec=pltpu.PrefetchScalarGridSpec(
            num_scalar_prefetch=2,
            grid=(4,),
            in_specs=[
                by_rows(q_width),
                by_columns(2 * kv_width),
                whole(g_halo.shape),
                by_columns(head // 2),
                by_columns(head // 2),
                whole(ups.shape),
                whole(downs_t.shape),
            ]
            + [ANY] * n_pieces,
            out_specs=[whole((quarter, model))] * 4,
            scratch_shapes=[held_qkv, sems],
        ),
        out_shape=[one_quarter] * 4,
        compiler_params=params(BIG),
        cost_estimate=SMALL,
        name="norm_back",
    )(clock.tie(offsets), nat, g_q, g_own, g_halo, cos_q, sin_q, ups, downs_t, *attn_pieces)
    gn_far0, gn_far1, gn_near0, gn_near1 = clock.wait(*gn_parts)
    out_across, out_beside, gn_far0, gn_near0 = clock.wait(out_across, out_beside, gn_far0, gn_near0)
    beside, beside_near = exchange(gn_far0, "tensor", 1), exchange(gn_near0, "tensor", 1)
    beside, beside_near = clock.wait(beside, beside_near)
    gn_far = clock.tie((gn_far1.astype(f32) + beside.astype(f32)).astype(bf16))
    across = exchange(gn_far, "tensor", 2)

    adapters_in = (g_q, g_own, g_halo, cos_q, sin_q, ups, low[WIN : WIN + rows], normed, g_o_up, g_o_down, g_map_q, g_map_k)
    tall = head // ring
    tiles = 4 * rank // 8 * (model // ring // 128)
    in_tiles = tall == 8 and rank == 8 and model // ring % 128 == 0 and 2 * head == 128
    if in_tiles:
        sizes = [((ring, heads + kv_heads + tiles, tall, 2 * head), f32)]
    else:
        sizes = [((heads + kv_heads, head, 2 * head), f32), ((4 * rank, model), f32)]
    parts = pl.pallas_call(
        lambda *refs: adapters_body((rows, WIN, head, rank), *refs),
        grid_spec=pltpu.PrefetchScalarGridSpec(
            num_scalar_prefetch=0,
            grid=(1,),
            in_specs=[whole(x.shape) for x in adapters_in],
            out_specs=[whole(x) for x, _ in sizes],
        ),
        out_shape=[jax.ShapeDtypeStruct(x, d) for x, d in sizes],
        compiler_params=params(BIG),
        cost_estimate=SMALL,
        name="adapters",
    )(clock.tie(adapters_in[0]), *adapters_in[1:])
    if not in_tiles:
        parts = [
            parts[0].reshape(heads + kv_heads, ring, tall, 2 * head).transpose(1, 0, 2, 3),
            parts[1].reshape(4 * rank, ring, model // ring).transpose(1, 0, 2),
        ]
    parts = clock.wait(*parts)

    def halved(x, axis, half, bit, over=0, sent_as=f32):
        x = x.reshape(x.shape[:over] + (2, half) + x.shape[over + 1 :])
        send = lax.dynamic_index_in_dim(x, 1 - bit, over, keepdims=False)
        return lax.dynamic_index_in_dim(x, bit, over, keepdims=False), exchange(send.astype(sent_as), axis, half)

    def summed_over(axis, size, xs):
        while size > 1:
            half = size // 2
            both = [halved(x, axis, half, (lax.axis_index(axis) // half) % 2, 0, bf16) for x in xs]
            coming = clock.wait(*[coming for _, coming in both])
            xs = [kept + x.astype(f32) for (kept, _), x in zip(both, coming)]
            size = half
            yield xs

    dp = ring // seq
    parts = [x.reshape((dp, seq) + x.shape[1:]) for x in parts]
    for parts in summed_over("dp", dp, parts):
        pass
    along_seq = summed_over("seq", seq, clock.wait(*[x[0] for x in parts]))
    parts = next(along_seq)
    (across,) = clock.wait(across)
    (grad_rows,) = on_own_rows(
        grad_tokens_body, clock.tie(nat), gn_near1, beside_near, across, tokens, (grad_hidden,), gain_attn, (bf16,)
    )
    (grad_rows,) = clock.wait(grad_rows)
    across, beside = exchange(grad_rows, "tensor", 2), exchange(grad_rows, "tensor", 1)
    out_last = clock.tie(exchange(out_across, "tensor", 1))
    (beside,) = clock.wait(beside)
    grad_tokens = clock.tie(place([grad_rows, beside], 0, nat, f32))
    for parts in along_seq:
        pass
    by_head, shared = parts[0][0], parts[-1][0]
    if in_tiles:
        by_head, shared = by_head[: heads + kv_heads], by_head[heads + kv_heads :]
        shared = shared.reshape(4 * rank // 8, -1, 8, 128).transpose(0, 2, 1, 3)
    shared = shared.reshape(4 * rank, 2, 2, -1).transpose(2, 1, 0, 3)
    pick = lambda x, i: lax.dynamic_index_in_dim(x, i, 0, keepdims=False)
    shared = pick(shared, core) + clock.tie(exchange(pick(shared, 1 - core), "tensor", 1))
    shared = clock.tie(shared.reshape(2, 4 * rank, -1))
    block_out = clock.tie(place([out_rows, out_beside, out_across, out_last], 0, nat, bf16))
    (across,) = clock.wait(across)
    (last,) = clock.wait(exchange(across, "tensor", 1))
    shared = clock.tie(shared)
    sent = exchange(pick(shared, 1 - far), "tensor", 2)
    grad_tokens = clock.tie(place([across, last], 2, nat, f32, (grad_tokens,)))
    shared = (pick(shared, far) + clock.tie(sent)).T
    of_q, of_kv = by_head[:heads], by_head[heads:]
    first, second = slice(head, head + rank), slice(head + rank, head + 2 * rank)
    out = [of_q[..., first], of_kv[..., first], of_kv[..., second], of_q[..., second], of_q[..., :head], of_kv[..., :head]]
    return (
        block_out,
        grad_tokens,
        shared[:, :rank] + clock.now.astype(f32),
        shared[:, rank : 2 * rank],
        shared[:, 2 * rank : 3 * rank],
        shared[:, 3 * rank :],
        *out,
    )


def solution(mesh):
    return jax.shard_map(
        per_device,
        mesh=mesh,
        in_specs=(
            P(("dp", "seq"), None),
            P("dp", None),
            P(("dp", "seq"), None),
            P(("dp", "seq"), "tensor"),
            P(("dp", "seq"), "tensor"),
            P(("dp", "seq"), "tensor"),
            P("tensor", ("dp", "seq")),
            P(("dp", "seq"), "tensor"),
            P(("dp", "seq"), "tensor"),
            P("tensor", ("dp", "seq")),
            P(),
            P(),
            P(),
            P(),
            P(),
            P(),
            P("tensor", None, None),
            P("tensor", None, None),
            P("tensor", None, None),
            P("tensor", None, None),
            P("tensor", None, None),
            P("tensor", None, None),
        ),
        out_specs=(
            P(("dp", "seq"), None),
            P(("dp", "seq"), None),
            P(("dp", "seq", "tensor"), None),
            P(("dp", "seq", "tensor"), None),
            P(("dp", "seq", "tensor"), None),
            P(("dp", "seq", "tensor"), None),
            P("tensor", ("dp", "seq"), None),
            P("tensor", ("dp", "seq"), None),
            P("tensor", ("dp", "seq"), None),
            P("tensor", ("dp", "seq"), None),
            P("tensor", ("dp", "seq"), None),
            P("tensor", ("dp", "seq"), None),
        ),
        check_vma=False,
    )
```
